32 devices in a mesh: groups: 2 (over x), tile: 16 (over z, y, core).
Axes of the slice: x: 2, y: 2, z: 4, core: 2. Of those that a mesh axis runs over, the one named last changes fastest.
Arguments:
- inputs: bfloat16 [64, 16, 16, 256], P(('groups', 'tile')), parts along dimension 0, may hold values from -6 to 6
- out_grad: bfloat16 [64, 16, 16, 256], P(('groups', 'tile')), parts along dimension 0, may hold values from -4 to 4
- kernel: float32 [2, 7, 7, 256], replicated, may hold values from -0.875 to 0.875
- norm_gain: float32 [2, 256], replicated, may hold values from 0.5 to 1.5
- up_weight: bfloat16 [2, 256, 1024], replicated, may hold values from -0.375 to 0.375
- down_weight: bfloat16 [2, 1024, 256], replicated, may hold values from -0.1875 to 0.1875
- layer_scale: float32 [2, 256], replicated, may hold values from 0.3 to 1
- seam_table: int32 [32, 4, 2], replicated, may hold values from 0 to 31, as said below
- corner_table: int32 [32, 4, 2], replicated, may hold values from 0 to 31, as said below
Outputs:
- output: bfloat16 [64, 16, 16, 256], P(('groups', 'tile')), parts along dimension 0
- in_grad: bfloat16 [64, 16, 16, 256], P(('groups', 'tile')), parts along dimension 0
- grad_kernel: float32 [4, 7, 7, 256], P('groups'), parts along dimension 0
- grad_gain: float32 [4, 256], P('groups'), parts along dimension 0
- grad_up: float32 [4, 256, 1024], P('groups'), parts along dimension 0
- grad_down: float32 [4, 1024, 256], P('groups'), parts along dimension 0
- grad_scale: float32 [4, 256], P('groups'), parts along dimension 0
The draws below stay inside these ranges and needn't reach their ends.
There are 2 independent parts, one for each index of `groups`. The reference program is written for one: setup_inputs(seed, part) draws one part's arguments, and reference() takes and returns one part's arrays. A program takes and returns all parts, laid end to end along the dimension named above; an argument that names none is the same for every part. Nothing has to cross between parts.
Inputs may be any that keep to these rules, and one draw needn't show every extreme that they name: `seam_table`: tile q is held by device q // 2 of the tile axis. Entry [q, e] names a tile and one of its sides (0 to 3); every side of every tile is named exactly once. The named tile lies on the device of q or on one of the two devices beside it along the tile axis, counted cyclically. From one device beside it a device needs at most 4 strips, and some devices need exactly that many. `corner_table`: entry [q, e] names a tile and one of its corners (0 to 3), lying on the device of q or on one of the two devices beside it along the tile axis, counted cyclically. From one device beside it a device needs at most 6 corner blocks, and some devices need exactly that many.
All inputs are finite; a program needn't handle non-finite values.
Results may differ from the reference program's by a relative error of at most 0.0085.
Values may be sent and summed in bfloat16 or wider, within the bound.
No kernel may reach another device: no remote copies, remote signals or barrier semaphores. Data moves between devices by JAX's collectives and lax.ppermute only.
A program may use at most 192 MiB of HBM per device.

```python
import math
import jax
import jax.numpy as jnp
from jax import lax

C = 256
HIDDEN_SIZE = 1024
S = 16
TPD = 2
BLOCKS = 2
NT = 32
N_TILE = 16


def build_table(sources, stored, quarter_turns):
    table = jnp.zeros((NT, 4, 2), jnp.int32)
    targets = stored.reshape(-1)
    for geo_side in range(4):
        source_row, source_column, source_side = sources[geo_side]
        side_here = ((geo_side - quarter_turns) % 4).reshape(-1)
        source_slot = stored[source_row, source_column].reshape(-1)
        source_edge = ((source_side - quarter_turns[source_row, source_column]) % 4).reshape(-1)
        table = table.at[targets, side_here].set(jnp.stack([source_slot, source_edge], axis=-1).astype(jnp.int32))
    return table


def seam_geometry(key):
    columns = NT // TPD
    slot_key, turn_key = jax.random.split(key)
    slot_order = jax.vmap(lambda subkey: jax.random.permutation(subkey, TPD))(jax.random.split(slot_key, columns))
    quarter_turns = jax.random.randint(turn_key, (TPD, columns), 0, 4)
    row_index = jnp.broadcast_to(jnp.arange(TPD, dtype=jnp.int32)[:, None], (TPD, columns))
    column_index = jnp.broadcast_to(jnp.arange(columns, dtype=jnp.int32)[None, :], (TPD, columns))
    stored = column_index * TPD + slot_order.T.astype(jnp.int32)
    partner = jnp.bitwise_xor(column_index, 1)
    east_column = (column_index + 1) % columns
    west_column = (column_index + columns - 1) % columns
    has_above = row_index > 0
    has_below = row_index < TPD - 1
    row_above = jnp.where(has_above, row_index - 1, 0)
    row_below = jnp.where(has_below, row_index + 1, TPD - 1)
    edge_sources = [(row_above, jnp.where(has_above, column_index, partner), jnp.where(has_above, 2, 0)), (row_index, east_column, jnp.full((TPD, columns), 3, jnp.int32)), (row_below, jnp.where(has_below, column_index, partner), jnp.where(has_below, 0, 2)), (row_index, west_column, jnp.full((TPD, columns), 1, jnp.int32))]
    corner_sources = [(row_above, jnp.where(has_above, west_column, partner), jnp.where(has_above, 2, 1)), (row_above, jnp.where(has_above, east_column, partner), jnp.where(has_above, 3, 0)), (row_below, jnp.where(has_below, east_column, partner), jnp.where(has_below, 0, 3)), (row_below, jnp.where(has_below, west_column, partner), jnp.where(has_below, 1, 2))]
    return (build_table(edge_sources, stored, quarter_turns), build_table(corner_sources, stored, quarter_turns))


def draw_seam_table(key, part):
    return seam_geometry(key)[0]


def draw_corner_table(key, part):
    return seam_geometry(key)[1]


def shard_levels(stream_key, shape, shards, low, high):
    loudness = 1.0
    for axis_at, shards_of in shards:
        draws = jax.random.uniform(jax.random.fold_in(jax.random.fold_in(stream_key, 6), axis_at), (shards_of,), jnp.float32, low / len(shards), high / len(shards))
        loudness = loudness * jnp.repeat(jnp.exp(draws), shape[axis_at] // shards_of).reshape((-1,) + (1,) * (len(shape) - 1 - axis_at))
    return loudness


def normal_values(rng, shape, width, bound, cuts=(), held_as=jnp.bfloat16):
    values = jax.random.normal(rng, shape, jnp.float32) * width
    if len(cuts) > 0:
        values = shard_levels(rng, shape, cuts, -0.22, 0.18) * values
    return jnp.clip(values, min=-bound, max=bound).astype(held_as)


def setup_inputs(seed: int = 0, part: int = 0) -> dict:
    arg_keys = jax.random.split(jax.random.key(seed), 10)
    own_keys = jax.random.split(jax.random.fold_in(arg_keys[9], part), 10)
    return {
        "inputs": normal_values(own_keys[0], (NT, S, S, C), 1.0, 6.0, ((0, 16),)),
        "out_grad": normal_values(own_keys[1], (NT, S, S, C), 0.5, 4.0, ((0, 16),)),
        "kernel": normal_values(arg_keys[2], (BLOCKS, 7, 7, C), 49 ** -0.5, 0.875, (), jnp.float32),
        "norm_gain": jnp.clip(1.0 + 0.1 * jax.random.normal(arg_keys[3], (BLOCKS, C), jnp.float32), 0.5, 1.5),
        "up_weight": normal_values(arg_keys[4], (BLOCKS, C, HIDDEN_SIZE), C ** -0.5, 0.375),
        "down_weight": normal_values(arg_keys[5], (BLOCKS, HIDDEN_SIZE, C), HIDDEN_SIZE ** -0.5, 0.1875),
        "layer_scale": jnp.clip(jnp.exp(jax.random.uniform(arg_keys[6], (BLOCKS, C), jnp.float32, math.log(0.3), math.log(1.0))), 0.3, 1.0),
        "seam_table": draw_seam_table(jax.random.fold_in(arg_keys[9], 71), part),
        "corner_table": draw_corner_table(jax.random.fold_in(arg_keys[9], 71), part),
    }


epsilon = 1e-06
inverse_root_two = 0.7071067811865476
inverse_root_tau = 0.3989422804014327

def seam_parts(blocks):
    tile_edge = blocks.shape[1]
    channels = blocks.shape[3]
    strips = jnp.stack([jnp.rot90(blocks, quarter, axes=(1, 2))[:, 0:3] for quarter in range(4)], axis=1)
    corners = jnp.stack([jnp.rot90(blocks, quarter, axes=(1, 2))[:, 0:3, 0:3] for quarter in range(4)], axis=1)
    pieces = blocks.shape[0] * 4
    return (strips.reshape((pieces, 3, tile_edge, channels)), corners.reshape((pieces, 3, 3, channels)))

def fill_margin(blocks, pool_strips, pool_corners, strip_index, corner_index):
    tile_count = blocks.shape[0]
    tile_edge = blocks.shape[1]
    channels = blocks.shape[3]
    halo_strips = jnp.take(pool_strips, strip_index, axis=0).reshape((tile_count, 4, 3, tile_edge, channels))[:, :, ::-1, ::-1]
    halo_corners = jnp.take(pool_corners, corner_index, axis=0).reshape((tile_count, 4, 3, 3, channels))[:, :, ::-1, ::-1]
    padded = jnp.pad(blocks, ((0, 0), (3, 3), (3, 3), (0, 0)))
    for quarter in range(4):
        turned = jnp.rot90(padded, quarter, axes=(1, 2))
        turned = turned.at[:, 0:3, 3:tile_edge + 3].set(halo_strips[:, quarter])
        turned = turned.at[:, 0:3, 0:3].set(halo_corners[:, quarter])
        padded = jnp.rot90(turned, -quarter, axes=(1, 2))
    return padded

def depthwise(padded, kernel):
    inner_edge = padded.shape[1] - 6
    summed = jnp.zeros((padded.shape[0], inner_edge, inner_edge, padded.shape[3]), jnp.float32)
    for row_tap in range(7):
        for column_tap in range(7):
            window = padded[:, row_tap:row_tap + inner_edge, column_tap:column_tap + inner_edge].astype(jnp.float32)
            summed = summed + window * kernel[row_tap, column_tap]
    return summed

def depthwise_grad(padded, grad_conv, kernel):
    inner_edge = grad_conv.shape[1]
    outer_edge = inner_edge + 6
    grown_grad = jnp.pad(grad_conv, ((0, 0), (6, 6), (6, 6), (0, 0)))
    grad_pad = jnp.zeros((grad_conv.shape[0], outer_edge, outer_edge, grad_conv.shape[3]), jnp.float32)
    tap_sums = []
    for row_tap in range(7):
        for column_tap in range(7):
            moved = grown_grad[:, 6 - row_tap:6 - row_tap + outer_edge, 6 - column_tap:6 - column_tap + outer_edge]
            grad_pad = grad_pad + moved * kernel[row_tap, column_tap]
            window = padded[:, row_tap:row_tap + inner_edge, column_tap:column_tap + inner_edge].astype(jnp.float32)
            tap_sums.append(lax.optimization_barrier(jnp.sum(window * grad_conv, axis=(0, 1, 2))))
    return (grad_pad, jnp.stack(tap_sums).reshape((7, 7, grad_conv.shape[3])))

def block_forward(blocks, padded, kernel, norm_gain, up_weight, down_weight, layer_scale):
    channels = blocks.shape[3]
    conv_out = depthwise(padded, kernel).reshape((-1, channels))
    center = conv_out - lax.optimization_barrier(jnp.mean(conv_out, axis=-1, keepdims=True))
    inverse = lax.rsqrt(lax.optimization_barrier(jnp.mean(center * center, axis=-1, keepdims=True)) + epsilon)
    normal = center * inverse
    normed = (normal * norm_gain).astype(jnp.bfloat16)
    upward = jnp.dot(normed, up_weight, preferred_element_type=jnp.float32)
    active = jax.nn.gelu(upward, approximate=False).astype(jnp.bfloat16)
    branch = jnp.dot(active, down_weight, preferred_element_type=jnp.float32)
    result = (blocks.reshape((-1, channels)).astype(jnp.float32) + branch * layer_scale).astype(jnp.bfloat16)
    return (result.reshape(blocks.shape), (normal, inverse, normed, upward, active, branch))

def block_backward(padded, cache, grad_out, kernel, norm_gain, up_weight, down_weight, layer_scale):
    normal, inverse, normed, upward, active, branch = cache
    channels = grad_out.shape[3]
    outer_grad = grad_out.reshape((-1, channels)).astype(jnp.float32)
    grad_scale = lax.optimization_barrier(jnp.sum(outer_grad * branch, axis=0))
    down_in = (outer_grad * layer_scale).astype(jnp.bfloat16)
    grad_down = lax.dot_general(active, down_in, (((0,), (0,)), ((), ())), preferred_element_type=jnp.float32)
    grad_active = lax.dot_general(down_in, down_weight, (((1,), (1,)), ((), ())), preferred_element_type=jnp.float32)
    gelu_slope = 0.5 * (1.0 + jax.scipy.special.erf(upward * inverse_root_two)) + upward * jnp.exp(-0.5 * upward * upward) * inverse_root_tau
    up_in = (grad_active * gelu_slope).astype(jnp.bfloat16)
    grad_up = lax.dot_general(normed, up_in, (((0,), (0,)), ((), ())), preferred_element_type=jnp.float32)
    grad_normed = lax.dot_general(up_in, up_weight, (((1,), (1,)), ((), ())), preferred_element_type=jnp.float32)
    grad_gain = lax.optimization_barrier(jnp.sum(grad_normed * normal, axis=0))
    scaled = grad_normed * norm_gain
    grad_conv = inverse * (scaled - lax.optimization_barrier(jnp.mean(scaled, axis=-1, keepdims=True)) - normal * lax.optimization_barrier(jnp.mean(scaled * normal, axis=-1, keepdims=True)))
    grad_conv = grad_conv.reshape(grad_out.shape)
    grad_pad, grad_kernel = depthwise_grad(padded, grad_conv, kernel)
    return (grad_pad, outer_grad, (grad_kernel, grad_gain, grad_up, grad_down, grad_scale))

def reference(inputs, out_grad, kernel, norm_gain, up_weight, down_weight, layer_scale, seam_table, corner_table):
    strip_index = (seam_table[:, :, 0] * 4 + seam_table[:, :, 1]).reshape(-1).astype(jnp.int32)
    corner_index = (corner_table[:, :, 0] * 4 + corner_table[:, :, 1]).reshape(-1).astype(jnp.int32)

    def margin(blocks):
        strips, corners = seam_parts(blocks)
        return fill_margin(blocks, strips, corners, strip_index, corner_index)

    def grouped(array):
        return array.reshape((N_TILE, TPD) + array.shape[1:])
    layers = kernel.shape[0]
    states = []
    pads = []
    current = inputs
    for layer_index in range(layers):
        padded = margin(current)

        def forward_step(running, members):
            result, cache = block_forward(members[0], members[1], kernel[layer_index], norm_gain[layer_index], up_weight[layer_index], down_weight[layer_index], layer_scale[layer_index])
            return (running, result)
        running, results = lax.scan(forward_step, jnp.zeros((), jnp.float32), (grouped(current), grouped(padded)))
        states.append(current)
        pads.append(padded)
        current = results.reshape(inputs.shape)
    output = current
    grad_now = out_grad
    collected = [None] * layers
    for layer_index in reversed(range(layers)):
        blocks = states[layer_index]
        padded = pads[layer_index]

        def backward_step(running, members):
            result, cache = block_forward(members[0], members[1], kernel[layer_index], norm_gain[layer_index], up_weight[layer_index], down_weight[layer_index], layer_scale[layer_index])
            grad_pad, outer_grad, grad_parts = block_backward(members[1], cache, members[2], kernel[layer_index], norm_gain[layer_index], up_weight[layer_index], down_weight[layer_index], layer_scale[layer_index])
            running = jax.tree.map(lambda earlier, addend: earlier + addend, running, grad_parts)
            return (running, (grad_pad, outer_grad))
        channels = inputs.shape[3]
        hidden_units = up_weight.shape[2]
        start = (jnp.zeros((7, 7, channels), jnp.float32), jnp.zeros((channels,), jnp.float32), jnp.zeros((channels, hidden_units), jnp.float32), jnp.zeros((hidden_units, channels), jnp.float32), jnp.zeros((channels,), jnp.float32))
        grad_parts, pair_out = lax.scan(backward_step, start, (grouped(blocks), grouped(padded), grouped(grad_now)))
        grad_pads, outer_grads = pair_out
        seam_pull = jax.vjp(margin, jnp.zeros(inputs.shape, jnp.float32))[1]
        seam_grad = seam_pull(grad_pads.reshape(padded.shape))[0]
        grad_now = (outer_grads.reshape(inputs.shape) + seam_grad).astype(jnp.bfloat16)
        collected[layer_index] = grad_parts
    return (output, grad_now, jnp.stack([collected[layer_index][0] for layer_index in range(layers)]), jnp.stack([collected[layer_index][1] for layer_index in range(layers)]), jnp.stack([collected[layer_index][2] for layer_index in range(layers)]), jnp.stack([collected[layer_index][3] for layer_index in range(layers)]), jnp.stack([collected[layer_index][4] for layer_index in range(layers)]))
```

```python
import functools

import jax
import jax.numpy as jnp
from jax import lax
from jax.experimental import pallas as pl
from jax.experimental.pallas import tpu as pltpu
from jax.sharding import PartitionSpec as P

epsilon = 1e-06
inverse_root_two = 0.7071067811865476
inverse_root_tau = 0.3989422804014327

LANES = 128
TAPS = 7
REACH = 3
PITCH = 24
GRAD_PITCH = 32
SMALL_ROWS = 64
F32 = jnp.float32
BF16 = jnp.bfloat16


def flip_rows(value):
    rows = value.shape[0]
    order = 7 - lax.broadcasted_iota(jnp.int32, (8, LANES), 0)
    parts = [
        jnp.take_along_axis(value[at : at + 8], order, axis=0, mode="promise_in_bounds")
        for at in range(0, rows, 8)
    ]
    return jnp.concatenate(parts[::-1], axis=0)


def halves(value):
    return [value[:, at : at + LANES] for at in range(0, value.shape[1], LANES)]


class Sizes:
    def __init__(self, tiles, edge, channels, hidden):
        self.tiles = tiles
        self.edge = edge
        self.channels = channels
        self.hidden = hidden
        self.lanes = channels // LANES
        self.cells = edge * edge
        self.rows = tiles * edge * edge
        self.pieces = tiles * 4
        self.outer = edge + 2 * REACH
        self.slabs = tiles * self.lanes

    def key(self):
        return (self.tiles, self.edge, self.channels, self.hidden)


def strip_window(edge, side, row):
    if side == 0:
        return pl.ds(row * edge, edge), False
    if side == 1:
        return pl.ds(edge - 1 - row, edge, stride=edge), False
    if side == 2:
        return pl.ds((edge - 1 - row) * edge, edge), True
    return pl.ds(row, edge, stride=edge), True


def margin_window(edge, side, row):
    last = edge + 2 * REACH - 1
    if side == 0:
        return pl.ds((2 - row) * PITCH + REACH, edge), True
    if side == 1:
        return pl.ds(REACH * PITCH + last - 2 + row, edge, stride=PITCH), True
    if side == 2:
        return pl.ds((last - 2 + row) * PITCH + REACH, edge), False
    return pl.ds(REACH * PITCH + 2 - row, edge, stride=PITCH), False


def corner_cell(edge, corner, row, column):
    last = edge + 2 * REACH - 1
    r, x = 2 - row, 2 - column
    if corner == 0:
        at = (r, x)
    elif corner == 1:
        at = (x, last - r)
    elif corner == 2:
        at = (last - r, last - x)
    else:
        at = (last - x, r)
    return at[0] * PITCH + at[1]


def write_strips(sz, flat, strips_ref):
    for q in range(sz.tiles):
        for side in range(4):
            for row in range(REACH):
                window, turned = strip_window(sz.edge, side, row)
                parts = [flat[q * sz.lanes + h, window, :] for h in range(sz.lanes)]
                if turned:
                    parts = [flip_rows(part) for part in parts]
                strips_ref[q * 4 + side, row] = jnp.concatenate(parts, axis=1).astype(BF16)


def surround(sz, strip_at, corner_at, cur, own, below, above, pool, pad):
    pool[0 : sz.pieces] = own[...]
    pool[sz.pieces : 2 * sz.pieces] = below[...]
    pool[2 * sz.pieces : 3 * sz.pieces] = above[...]
    for q in range(sz.tiles):
        for i in range(sz.edge):
            for h, part in enumerate(halves(cur[q, i].astype(F32))):
                pad[q * sz.lanes + h, pl.ds((i + REACH) * PITCH + REACH, sz.edge), :] = part
    for q in range(sz.tiles):
        for side in range(4):
            piece = strip_at[q * 4 + side]
            for row in range(REACH):
                window, turned = margin_window(sz.edge, side, row)
                for h, part in enumerate(halves(pool[piece, row].astype(F32))):
                    pad[q * sz.lanes + h, window, :] = flip_rows(part) if turned else part
            piece = corner_at[q * 4 + side]
            for row in range(REACH):
                for h, part in enumerate(halves(pool[piece, row].astype(F32))):
                    for column in range(REACH):
                        at = corner_cell(sz.edge, side, row, column)
                        pad[q * sz.lanes + h, pl.ds(at, 1), :] = part[column : column + 1]


def hold_taps(sz, kern, layer, taps):
    for a in range(TAPS):
        for h, part in enumerate(halves(kern[layer, a])):
            taps[h, pl.ds(a * 8, TAPS), :] = part


def tap(taps, h, a, b):
    return jnp.broadcast_to(taps[h, pl.ds(a * 8 + b, 1), :], (8, LANES))


def convolve(sz, pad, taps, conv):
    @pl.loop(0, sz.slabs)
    def _(slab):
        h = lax.rem(slab, sz.lanes)
        for g in range(sz.edge // 8):
            acc = [None] * sz.edge
            for b in range(TAPS):
                weights = [tap(taps, h, a, b) for a in range(TAPS)]
                for r in range(sz.outer):
                    x = pad[slab, pl.ds(r * PITCH + b + 8 * g, 8), :]
                    for a in range(TAPS):
                        i = r - a
                        if 0 <= i < sz.edge:
                            term = x * weights[a]
                            acc[i] = term if acc[i] is None else acc[i] + term
            for i in range(sz.edge):
                conv[slab, pl.ds(i * sz.edge + 8 * g, 8), :] = acc[i]


def normalise(sz, conv, gain, layer, normal, inverse, normed):
    scale = 1.0 / sz.channels
    for q in range(sz.tiles):

        @pl.loop(0, sz.edge, unroll=2)
        def _(i):
            at = pl.ds(pl.multiple_of(i * sz.edge, sz.edge), sz.edge)
            parts = [conv[q * sz.lanes + h, at, :] for h in range(sz.lanes)]
            mean = jnp.sum(sum(parts[1:], parts[0]), axis=-1, keepdims=True) * scale
            parts = [part - mean for part in parts]
            squares = [part * part for part in parts]
            variance = jnp.sum(sum(squares[1:], squares[0]), axis=-1, keepdims=True) * scale
            root = lax.rsqrt(variance + epsilon)
            inverse[q, at, :] = jnp.broadcast_to(root, (sz.edge, LANES))
            flat_at = pl.ds(pl.multiple_of(q * sz.cells + i * sz.edge, sz.edge), sz.edge)
            for h, part in enumerate(parts):
                part = part * root
                normal[q * sz.lanes + h, at, :] = part
                gains = gain[layer : layer + 1, h * LANES : (h + 1) * LANES]
                normed[flat_at, h * LANES : (h + 1) * LANES] = (part * gains).astype(BF16)


def activate(sz, upward, active, slope):
    width = 512

    @pl.loop(0, sz.rows // 16)
    def _(t):
        at = pl.ds(pl.multiple_of(t * 16, 16), 16)
        for start in range(0, sz.hidden, width):
            u = upward[at, start : start + width]
            chance = 0.5 * (1.0 + lax.erf(u * inverse_root_two))
            active[at, start : start + width] = (u * chance).astype(BF16)
            slope[at, start : start + width] = (
                chance + u * jnp.exp(-0.5 * u * u) * inverse_root_tau
            ).astype(slope.dtype)


def multiply(a, b, ca=1, cb=0):
    return lax.dot_general(a, b, (((ca,), (cb,)), ((), ())), preferred_element_type=F32)


def finish_forward(sz, cur, branch, lscale, layer, out, flat):
    for q in range(sz.tiles):

        @pl.loop(0, sz.edge, unroll=2)
        def _(i):
            at = pl.ds(pl.multiple_of(q * sz.cells + i * sz.edge, sz.edge), sz.edge)
            value = cur[q, i].astype(F32) + branch[at, :] * lscale[layer : layer + 1, :]
            value = value.astype(BF16)
            out[q, i] = value
            if flat is not None:
                local = pl.ds(pl.multiple_of(i * sz.edge, sz.edge), sz.edge)
                for h, part in enumerate(halves(value.astype(F32))):
                    flat[q * sz.lanes + h, local, :] = part


def scale_rows(sz, grad_row, branch, lscale, layer, down_in, sums):
    sums[...] = jnp.zeros_like(sums)
    for q in range(sz.tiles):

        @pl.loop(0, sz.edge, unroll=2)
        def _(i):
            at = pl.ds(pl.multiple_of(q * sz.cells + i * sz.edge, sz.edge), sz.edge)
            g = grad_row(q, i)
            down_in[at, :] = (g * lscale[layer : layer + 1, :]).astype(BF16)
            sums[...] += g * branch[at, :]


def slope_rows(sz, grad_active, slope, up_in):
    @pl.loop(0, sz.rows // 16, unroll=2)
    def _(t):
        at = pl.ds(pl.multiple_of(t * 16, 16), 16)
        up_in[at, :] = (grad_active[at, :] * slope[at, :].astype(F32)).astype(BF16)


def weight_gradients(sz, active, down_in, normed, up_in, weights_out):
    weights_out[0 : sz.hidden, :] = multiply(active[...], down_in[...], 0, 0).astype(BF16)
    for k in range(sz.hidden // sz.channels):
        part = multiply(
            normed[...], up_in[:, k * sz.channels : (k + 1) * sz.channels], 0, 0
        ).astype(BF16)
        start = sz.hidden + k * sz.channels
        weights_out[start : start + sz.channels, :] = part


def norm_gradients(sz, grad_normed, normal, inverse, gain, layer, grad_conv, sums):
    scale = 1.0 / sz.channels
    sums[...] = jnp.zeros_like(sums)
    blank = jnp.zeros((8, LANES), F32)
    for q in range(sz.tiles):

        @pl.loop(0, sz.edge, unroll=2)
        def _(i):
            at = pl.ds(pl.multiple_of(q * sz.cells + i * sz.edge, sz.edge), sz.edge)
            local = pl.ds(pl.multiple_of(i * sz.edge, sz.edge), sz.edge)
            g = halves(grad_normed[at, :])
            n = [normal[q * sz.lanes + h, local, :] for h in range(sz.lanes)]
            sums[...] += jnp.concatenate([a * b for a, b in zip(g, n)], axis=1)
            s = [
                part * gain[layer : layer + 1, h * LANES : (h + 1) * LANES]
                for h, part in enumerate(g)
            ]
            products = [a * b for a, b in zip(s, n)]
            mean = jnp.sum(sum(s[1:], s[0]), axis=-1, keepdims=True) * scale
            slant = jnp.sum(sum(products[1:], products[0]), axis=-1, keepdims=True) * scale
            root = inverse[q, local, :]
            for h in range(sz.lanes):
                slab = q * sz.lanes + h
                base = pl.multiple_of(i * GRAD_PITCH, GRAD_PITCH)
                grad_conv[slab, pl.ds(base, 8), :] = blank
                grad_conv[slab, pl.ds(base + 8, sz.edge), :] = root * (s[h] - mean - n[h] * slant)
                grad_conv[slab, pl.ds(base + 8 + sz.edge, 8), :] = blank


def tap_gradients(sz, pad, grad_conv, tap_sums, small):
    tap_sums[...] = jnp.zeros_like(tap_sums)

    @pl.loop(0, sz.slabs)
    def _(slab):
        h = lax.rem(slab, sz.lanes)
        for b in range(TAPS):
            acc = [None] * TAPS
            for g in range(sz.edge // 8):
                grads = [
                    grad_conv[slab, pl.ds(i * GRAD_PITCH + 8 + 8 * g, 8), :]
                    for i in range(sz.edge)
                ]
                for r in range(sz.outer):
                    x = pad[slab, pl.ds(r * PITCH + b + 8 * g, 8), :]
                    for a in range(TAPS):
                        i = r - a
                        if 0 <= i < sz.edge:
                            term = x * grads[i]
                            acc[a] = term if acc[a] is None else acc[a] + term
            for a in range(TAPS):
                tap_sums[h, a * TAPS + b] += acc[a]

    for h in range(sz.lanes):
        for k in range(TAPS * TAPS):
            row = k // TAPS * 8 + k % TAPS
            small[row : row + 1, h * LANES : (h + 1) * LANES] = jnp.sum(
                tap_sums[h, k], axis=0, keepdims=True
            )


def spread_gradients(sz, grad_conv, taps, grad_pad):
    @pl.loop(0, sz.slabs)
    def _(slab):
        h = lax.rem(slab, sz.lanes)
        for g in range(PITCH // 8):
            acc = [None] * sz.outer
            for b in range(TAPS):
                start = 8 * g - b + 8
                if start >= 8 + sz.edge:
                    continue
                weights = [tap(taps, h, a, b) for a in range(TAPS)]
                for i in range(sz.edge):
                    x = grad_conv[slab, pl.ds(i * GRAD_PITCH + start, 8), :]
                    for a in range(TAPS):
                        term = x * weights[a]
                        acc[i + a] = term if acc[i + a] is None else acc[i + a] + term
            for p in range(sz.outer):
                grad_pad[slab, pl.ds(p * PITCH + 8 * g, 8), :] = acc[p]


def return_margins(sz, strip_at, corner_at, grad_pad, pool):
    pool[...] = jnp.zeros_like(pool)
    for q in range(sz.tiles):
        for side in range(4):
            piece = strip_at[q * 4 + side]
            for row in range(REACH):
                window, turned = margin_window(sz.edge, side, row)
                for h in range(sz.lanes):
                    part = grad_pad[q * sz.lanes + h, window, :]
                    pool[piece, row, h] = flip_rows(part) if turned else part
    for q in range(sz.tiles):
        for side in range(4):
            piece = corner_at[q * 4 + side]
            for row in range(REACH):
                for column in range(REACH):
                    at = corner_cell(sz.edge, side, row, column)
                    for h in range(sz.lanes):
                        pool[piece, row, h, pl.ds(column, 1), :] += grad_pad[
                            q * sz.lanes + h, pl.ds(at, 1), :
                        ]


def send_margins(sz, pool, own, below, above):
    own[...] = pool[0 : sz.pieces]
    for piece in range(sz.pieces):
        for row in range(REACH):
            for offset, ref in ((1, below), (2, above)):
                parts = [pool[offset * sz.pieces + piece, row, h] for h in range(sz.lanes)]
                ref[piece, row] = jnp.concatenate(parts, axis=1).astype(BF16)


def gather_inner(sz, grad_row, grad_pad, base):
    for q in range(sz.tiles):
        for i in range(sz.edge):
            for h, part in enumerate(halves(grad_row(q, i))):
                slab = q * sz.lanes + h
                base[slab, pl.ds(i * sz.edge, sz.edge), :] = (
                    part + grad_pad[slab, pl.ds((i + REACH) * PITCH + REACH, sz.edge), :]
                )


def add_strips(sz, base, own, first, second, flat):
    flat[...] = base[...]
    for q in range(sz.tiles):
        for side in range(4):
            piece = q * 4 + side
            for row in range(REACH):
                window, turned = strip_window(sz.edge, side, row)
                came = first[piece, row].astype(F32) + second[piece, row].astype(F32)
                for h, part in enumerate(halves(came)):
                    part = part + own[piece, row, h]
                    flat[q * sz.lanes + h, window, :] += flip_rows(part) if turned else part


def fill_small(sz, small, gain_sums, scale_sums, weights_out):
    small[TAPS * 8 : TAPS * 8 + 1, :] = jnp.sum(gain_sums[...], axis=0, keepdims=True)
    small[TAPS * 8 + 1 : TAPS * 8 + 2, :] = jnp.sum(scale_sums[...], axis=0, keepdims=True)
    weights_out[2 * sz.hidden : 2 * sz.hidden + SMALL_ROWS, :] = small[...].astype(BF16)


def flat_grad_row(sz, flat):
    def row(q, i):
        at = pl.ds(i * sz.edge, sz.edge)
        parts = [flat[q * sz.lanes + h, at, :] for h in range(sz.lanes)]
        return jnp.concatenate(parts, axis=1)

    return row


def strips_kernel(sz, cur, strips, flat):
    for q in range(sz.tiles):
        for i in range(sz.edge):
            for h, part in enumerate(halves(cur[q, i].astype(F32))):
                flat[q * sz.lanes + h, pl.ds(i * sz.edge, sz.edge), :] = part
    write_strips(sz, flat, strips)


def forward_kernel(
    sz, layer, strip_at, corner_at, cur, own, below, above, kern, gain, lscale, up, down,
    out, strips, pad, normal, inverse, normed, slope, active, branch,
    pool, taps, conv, upward, flat,
):
    hold_taps(sz, kern, layer, taps)
    surround(sz, strip_at, corner_at, cur, own, below, above, pool, pad)
    convolve(sz, pad, taps, conv)
    normalise(sz, conv, gain, layer, normal, inverse, normed)
    upward[...] = multiply(normed[...], up[...])
    activate(sz, upward, active, slope)
    branch[...] = multiply(active[...], down[...])
    finish_forward(sz, cur, branch, lscale, layer, out, flat)
    write_strips(sz, flat, strips)


def backward_steps(
    sz, layer, strip_at, corner_at, grad_row, kern, gain, lscale, up, down,
    pad, normal, inverse, normed, slope, active, branch,
    weights_out, base, grad_own, grad_below, grad_above,
    grad_pool, taps, hidden, up_in, down_in, grad_conv, grad_pad, tap_sums, small,
    gain_sums, scale_sums,
):
    small[...] = jnp.zeros_like(small)
    scale_rows(sz, grad_row, branch, lscale, layer, down_in, scale_sums)
    hidden[...] = multiply(down_in[...], down[...], 1, 1)
    slope_rows(sz, hidden, slope, up_in)
    branch_grad = hidden.at[:, 0 : sz.channels]
    branch_grad[...] = multiply(up_in[...], up[...], 1, 1)
    norm_gradients(sz, branch_grad, normal, inverse, gain, layer, grad_conv, gain_sums)
    weight_gradients(sz, active, down_in, normed, up_in, weights_out)
    spread_gradients(sz, grad_conv, taps, grad_pad)
    return_margins(sz, strip_at, corner_at, grad_pad, grad_pool)
    send_margins(sz, grad_pool, grad_own, grad_below, grad_above)
    gather_inner(sz, grad_row, grad_pad, base)
    tap_gradients(sz, pad, grad_conv, tap_sums, small)
    fill_small(sz, small, gain_sums, scale_sums, weights_out)


def turn_kernel(
    sz, layer, strip_at, corner_at, cur, own, below, above, kern, gain, lscale, up, down, out_grad,
    out, weights_out, base, grad_own, grad_below, grad_above,
    pool, taps, conv, upward, pad, normal, inverse, normed, slope, active, branch,
    *rest,
):
    hold_taps(sz, kern, layer, taps)
    surround(sz, strip_at, corner_at, cur, own, below, above, pool, pad)
    convolve(sz, pad, taps, conv)
    normalise(sz, conv, gain, layer, normal, inverse, normed)
    upward[...] = multiply(normed[...], up[...])
    activate(sz, upward, active, slope)
    branch[...] = multiply(active[...], down[...])
    finish_forward(sz, cur, branch, lscale, layer, out, None)

    def grad_row(q, i):
        return out_grad[q, i].astype(F32)

    backward_steps(
        sz, layer, strip_at, corner_at, grad_row, kern, gain, lscale, up, down,
        pad, normal, inverse, normed, slope, active, branch,
        weights_out, base, grad_own, grad_below, grad_above,
        rest[0], taps, upward, *rest[1:],
    )


def backward_kernel(
    sz, layer, strip_at, corner_at, base_in, own_in, first, second, kern, gain, lscale, up, down,
    pad, normal, inverse, normed, slope, active, branch,
    weights_out, base, grad_own, grad_below, grad_above,
    flat, taps, hidden, grad_pool, *rest,
):
    hold_taps(sz, kern, layer, taps)
    add_strips(sz, base_in, own_in, first, second, flat)
    for q in range(sz.slabs):
        flat[q] = flat[q].astype(BF16).astype(F32)
    grad_row = flat_grad_row(sz, flat)
    backward_steps(
        sz, layer, strip_at, corner_at, grad_row, kern, gain, lscale, up, down,
        pad, normal, inverse, normed, slope, active, branch,
        weights_out, base, grad_own, grad_below, grad_above,
        grad_pool, taps, hidden, *rest,
    )


def last_kernel(sz, base, own, first, second, out, flat):
    add_strips(sz, base, own, first, second, flat)
    row = flat_grad_row(sz, flat)
    for q in range(sz.tiles):
        for i in range(sz.edge):
            out[q, i] = row(q, i).astype(BF16)


def call(body, outs, scratch, scalars, arrays, name):
    specs = [pl.BlockSpec(memory_space=pltpu.SMEM) for _ in scalars]
    values = list(scalars)
    for array in arrays:
        if isinstance(array, tuple):
            array, layer = array
            specs.append(
                pl.BlockSpec((None,) + array.shape[1:], lambda _, layer=layer: (layer, 0, 0))
            )
        else:
            rank = len(array.shape)
            specs.append(pl.BlockSpec(array.shape, lambda _, rank=rank: (0,) * rank))
        values.append(array)
    out_specs = [
        pl.BlockSpec(out.shape, lambda _, rank=len(out.shape): (0,) * rank) for out in outs
    ]
    return pl.pallas_call(
        body,
        grid=(1,),
        in_specs=specs,
        out_specs=out_specs,
        out_shape=outs,
        scratch_shapes=scratch,
        compiler_params=pltpu.CompilerParams(vmem_limit_bytes=48 * 1024 * 1024),
        name=name,
    )(*values)


def pass_on(shard, by):
    length = lax.axis_size("tile")
    return lax.ppermute(shard, "tile", [(i, (i + by) % length) for i in range(length)])


def margin_plan(table, tile_count, columns, device):
    pieces = tile_count * 4
    entries = lax.dynamic_slice_in_dim(table, device * tile_count, tile_count, 0).reshape(
        (pieces, 2)
    )
    source = entries[:, 0]
    source_device = source // tile_count
    local_piece = (source - source_device * tile_count) * 4 + entries[:, 1]
    below_device = (device + columns - 1) % columns
    return jnp.where(
        source_device == device,
        local_piece,
        jnp.where(source_device == below_device, pieces + local_piece, 2 * pieces + local_piece),
    )


def on_device(
    inputs,
    out_grad,
    kernel,
    norm_gain,
    up_weight,
    down_weight,
    layer_scale,
    seam_table,
    corner_table,
):
    tiles, edge, _, channels = inputs.shape
    hidden = up_weight.shape[2]
    sz = Sizes(tiles, edge, channels, hidden)
    columns = lax.axis_size("tile")
    device = lax.axis_index("tile")
    strip_at = margin_plan(seam_table, tiles, columns, device)
    corner_at = margin_plan(corner_table, tiles, columns, device)
    scalars = (strip_at, corner_at)

    def shape(dims, dtype=F32):
        return jax.ShapeDtypeStruct(dims, dtype)

    image = shape(inputs.shape, BF16)
    strips_shape = shape((sz.pieces, REACH, edge, channels), BF16)
    slab_dims = (sz.slabs, sz.cells, LANES)
    pad_dims = (sz.slabs, sz.outer * PITCH, LANES)
    saved = [
        shape(pad_dims),
        shape(slab_dims),
        shape((tiles, sz.cells, LANES)),
        shape((sz.rows, channels), BF16),
        shape((sz.rows, hidden), BF16),
        shape((sz.rows, hidden), BF16),
        shape((sz.rows, channels)),
    ]
    returned = [
        shape((2 * hidden + SMALL_ROWS, channels), BF16),
        shape(slab_dims),
        shape((sz.pieces, REACH, sz.lanes, edge, LANES)),
        strips_shape,
        strips_shape,
    ]
    flat = pltpu.VMEM(slab_dims, F32)
    taps = pltpu.VMEM((sz.lanes, TAPS * 8, LANES), F32)
    pool = pltpu.VMEM((3 * sz.pieces, REACH, edge, channels), BF16)
    wide = pltpu.VMEM((sz.rows, hidden), F32)
    grad_pool = pltpu.VMEM((3 * sz.pieces, REACH, sz.lanes, edge, LANES), F32)
    backward_scratch = [
        grad_pool,
        pltpu.VMEM((sz.rows, hidden), BF16),
        pltpu.VMEM((sz.rows, channels), BF16),
        pltpu.VMEM((sz.slabs, edge * GRAD_PITCH, LANES), F32),
        pltpu.VMEM(pad_dims, F32),
        pltpu.VMEM((sz.lanes, TAPS * TAPS, 8, LANES), F32),
        pltpu.VMEM((SMALL_ROWS, channels), F32),
        pltpu.VMEM((edge, channels), F32),
        pltpu.VMEM((edge, channels), F32),
    ]
    common = (kernel, norm_gain, layer_scale)

    (strips,) = call(
        functools.partial(strips_kernel, sz), [strips_shape], [flat], (), (inputs,), "strips"
    )
    below, above = pass_on(strips, 1), pass_on(strips, -1)
    first = call(
        functools.partial(forward_kernel, sz, 0),
        [image, strips_shape] + saved,
        [pool, taps, flat, wide, flat],
        scalars,
        (inputs, strips, below, above) + common + ((up_weight, 0), (down_weight, 0)),
        "forward",
    )
    middle, strips = first[:2]
    kept = first[2:]
    below, above = pass_on(strips, 1), pass_on(strips, -1)
    result, weights_one, base, grad_own, grad_below, grad_above = call(
        functools.partial(turn_kernel, sz, 1),
        [image] + returned,
        [pool, taps, flat, wide] + [pltpu.VMEM(one.shape, one.dtype) for one in saved]
        + backward_scratch,
        scalars,
        (middle, strips, below, above) + common
        + ((up_weight, 1), (down_weight, 1), out_grad),
        "turn",
    )
    weights_one = lax.psum(weights_one, "tile")
    from_below, from_above = pass_on(grad_above, 1), pass_on(grad_below, -1)
    weights_zero, base, grad_own, grad_below, grad_above = call(
        functools.partial(backward_kernel, sz, 0),
        returned,
        [flat, taps, wide] + backward_scratch,
        scalars,
        (base, grad_own, from_below, from_above) + common
        + ((up_weight, 0), (down_weight, 0)) + tuple(kept),
        "backward",
    )
    weights_zero = lax.psum(weights_zero, "tile")
    from_below, from_above = pass_on(grad_above, 1), pass_on(grad_below, -1)
    (in_grad,) = call(
        functools.partial(last_kernel, sz),
        [image],
        [flat],
        (),
        (base, grad_own, from_below, from_above),
        "last",
    )

    both = [weights_zero, weights_one]
    grad_down = jnp.stack([one[:hidden] for one in both]).astype(F32)
    grad_up = jnp.stack(
        [
            one[hidden : 2 * hidden]
            .reshape((hidden // channels, channels, channels))
            .transpose((1, 0, 2))
            .reshape((channels, hidden))
            for one in both
        ]
    ).astype(F32)
    small = jnp.stack([one[2 * hidden :] for one in both]).astype(F32)
    grad_kernel = small[:, : TAPS * 8].reshape((-1, TAPS, 8, channels))[:, :, :TAPS]
    grad_gain = small[:, TAPS * 8]
    grad_scale = small[:, TAPS * 8 + 1]
    return (result, in_grad, grad_kernel, grad_gain, grad_up, grad_down, grad_scale)


def solution(mesh):
    placed = (
        P(("groups", "tile"), None, None, None),
        P(("groups", "tile"), None, None, None),
        P(),
        P(),
        P(),
        P(),
        P(),
        P(),
        P(),
    )
    return jax.shard_map(
        on_device,
        mesh=mesh,
        in_specs=placed,
        out_specs=(
            P(("groups", "tile"), None, None, None),
            P(("groups", "tile"), None, None, None),
            P("groups", None, None, None),
            P("groups", None),
            P("groups", None, None),
            P("groups", None, None),
            P("groups", None),
        ),
        check_vma=False,
    )
```

```python
import functools

import jax
import jax.numpy as jnp
from jax import lax
from jax.experimental import pallas as pl
from jax.experimental.pallas import tpu as pltpu
from jax.sharding import PartitionSpec as P

epsilon = 1e-06
inverse_root_two = 0.7071067811865476
inverse_root_tau = 0.3989422804014327

LANES = 128
TAPS = 7
REACH = 3
PITCH = 24
GRAD_PITCH = 32
SMALL_ROWS = 64
F32 = jnp.float32
BF16 = jnp.bfloat16


def flip_rows(value):
    rows = value.shape[0]
    order = 7 - lax.broadcasted_iota(jnp.int32, (8, LANES), 0)
    parts = [
        jnp.take_along_axis(value[at : at + 8], order, axis=0, mode="promise_in_bounds")
        for at in range(0, rows, 8)
    ]
    return jnp.concatenate(parts[::-1], axis=0)


def halves(value):
    return [value[:, at : at + LANES] for at in range(0, value.shape[1], LANES)]


class Sizes:
    def __init__(self, tiles, edge, channels, hidden):
        self.tiles = tiles
        self.edge = edge
        self.channels = channels
        self.hidden = hidden
        self.lanes = channels // LANES
        self.cells = edge * edge
        self.rows = tiles * edge * edge
        self.pieces = tiles * 4
        self.outer = edge + 2 * REACH
        self.slabs = tiles * self.lanes

    def key(self):
        return (self.tiles, self.edge, self.channels, self.hidden)


def strip_window(edge, side, row):
    if side == 0:
        return pl.ds(row * edge, edge), False
    if side == 1:
        return pl.ds(edge - 1 - row, edge, stride=edge), False
    if side == 2:
        return pl.ds((edge - 1 - row) * edge, edge), True
    return pl.ds(row, edge, stride=edge), True


def margin_window(edge, side, row):
    last = edge + 2 * REACH - 1
    if side == 0:
        return pl.ds((2 - row) * PITCH + REACH, edge), True
    if side == 1:
        return pl.ds(REACH * PITCH + last - 2 + row, edge, stride=PITCH), True
    if side == 2:
        return pl.ds((last - 2 + row) * PITCH + REACH, edge), False
    return pl.ds(REACH * PITCH + 2 - row, edge, stride=PITCH), False


def corner_cell(edge, corner, row, column):
    last = edge + 2 * REACH - 1
    r, x = 2 - row, 2 - column
    if corner == 0:
        at = (r, x)
    elif corner == 1:
        at = (x, last - r)
    elif corner == 2:
        at = (last - r, last - x)
    else:
        at = (last - x, r)
    return at[0] * PITCH + at[1]


def write_strips(sz, flat, strips_ref):
    for q in range(sz.tiles):
        for side in range(4):
            for row in range(REACH):
                window, turned = strip_window(sz.edge, side, row)
                parts = [flat[q * sz.lanes + h, window, :] for h in range(sz.lanes)]
                if turned:
                    parts = [flip_rows(part) for part in parts]
                strips_ref[q * 4 + side, row] = jnp.concatenate(parts, axis=1).astype(BF16)


def surround(sz, strip_at, corner_at, cur, own, below, above, pool, pad):
    pool[0 : sz.pieces] = own[...]
    pool[sz.pieces : 2 * sz.pieces] = below[...]
    pool[2 * sz.pieces : 3 * sz.pieces] = above[...]
    for q in range(sz.tiles):
        for i in range(sz.edge):
            for h, part in enumerate(halves(cur[q, i].astype(F32))):
                pad[q * sz.lanes + h, pl.ds((i + REACH) * PITCH + REACH, sz.edge), :] = part
    for q in range(sz.tiles):
        for side in range(4):
            piece = strip_at[q * 4 + side]
            for row in range(REACH):
                window, turned = margin_window(sz.edge, side, row)
                for h, part in enumerate(halves(pool[piece, row].astype(F32))):
                    pad[q * sz.lanes + h, window, :] = flip_rows(part) if turned else part
            piece = corner_at[q * 4 + side]
            for row in range(REACH):
                for h, part in enumerate(halves(pool[piece, row].astype(F32))):
                    for column in range(REACH):
                        at = corner_cell(sz.edge, side, row, column)
                        pad[q * sz.lanes + h, pl.ds(at, 1), :] = part[column : column + 1]


def hold_taps(sz, kern, layer, taps):
    for a in range(TAPS):
        for b in range(TAPS):
            for h, part in enumerate(halves(kern[a, b, layer : layer + 1])):
                taps[h, pl.ds(a * 8 + b, 1), :] = part


def tap(taps, h, a, b):
    return jnp.broadcast_to(taps[h, pl.ds(a * 8 + b, 1), :], (8, LANES))


def convolve(sz, pad, taps, conv):
    @pl.loop(0, sz.slabs)
    def _(slab):
        h = lax.rem(slab, sz.lanes)
        for g in range(sz.edge // 8):
            acc = [None] * sz.edge
            for b in range(TAPS):
                weights = [tap(taps, h, a, b) for a in range(TAPS)]
                for r in range(sz.outer):
                    x = pad[slab, pl.ds(r * PITCH + b + 8 * g, 8), :]
                    for a in range(TAPS):
                        i = r - a
                        if 0 <= i < sz.edge:
                            term = x * weights[a]
                            acc[i] = term if acc[i] is None else acc[i] + term
            for i in range(sz.edge):
                conv[slab, pl.ds(i * sz.edge + 8 * g, 8), :] = acc[i]


def normalise(sz, conv, gain, layer, normal, inverse, normed):
    scale = 1.0 / sz.channels
    for q in range(sz.tiles):

        @pl.loop(0, sz.edge, unroll=2)
        def _(i):
            at = pl.ds(pl.multiple_of(i * sz.edge, sz.edge), sz.edge)
            parts = [conv[q * sz.lanes + h, at, :] for h in range(sz.lanes)]
            mean = jnp.sum(sum(parts[1:], parts[0]), axis=-1, keepdims=True) * scale
            parts = [part - mean for part in parts]
            squares = [part * part for part in parts]
            variance = jnp.sum(sum(squares[1:], squares[0]), axis=-1, keepdims=True) * scale
            root = lax.rsqrt(variance + epsilon)
            inverse[q, at, :] = jnp.broadcast_to(root, (sz.edge, LANES))
            flat_at = pl.ds(pl.multiple_of(q * sz.cells + i * sz.edge, sz.edge), sz.edge)
            for h, part in enumerate(parts):
                part = part * root
                normal[q * sz.lanes + h, at, :] = part
                gains = gain[layer : layer + 1, h * LANES : (h + 1) * LANES]
                normed[flat_at, h * LANES : (h + 1) * LANES] = (part * gains).astype(BF16)


def activate(sz, upward, active, slope):
    width = 512

    @pl.loop(0, sz.rows // 16)
    def _(t):
        at = pl.ds(pl.multiple_of(t * 16, 16), 16)
        for start in range(0, sz.hidden, width):
            u = upward[at, start : start + width]
            chance = 0.5 * (1.0 + lax.erf(u * inverse_root_two))
            active[at, start : start + width] = (u * chance).astype(BF16)
            slope[at, start : start + width] = (
                chance + u * jnp.exp(-0.5 * u * u) * inverse_root_tau
            ).astype(slope.dtype)


def multiply(a, b, ca=1, cb=0):
    return lax.dot_general(a, b, (((ca,), (cb,)), ((), ())), preferred_element_type=F32)


def finish_forward(sz, cur, branch, lscale, layer, out, flat):
    for q in range(sz.tiles):

        @pl.loop(0, sz.edge, unroll=2)
        def _(i):
            at = pl.ds(pl.multiple_of(q * sz.cells + i * sz.edge, sz.edge), sz.edge)
            value = cur[q, i].astype(F32) + branch[at, :] * lscale[layer : layer + 1, :]
            value = value.astype(BF16)
            out[q, i] = value
            if flat is not None:
                local = pl.ds(pl.multiple_of(i * sz.edge, sz.edge), sz.edge)
                for h, part in enumerate(halves(value.astype(F32))):
                    flat[q * sz.lanes + h, local, :] = part


def scale_rows(sz, grad_row, branch, lscale, layer, down_in, sums):
    sums[...] = jnp.zeros_like(sums)
    for q in range(sz.tiles):

        @pl.loop(0, sz.edge, unroll=2)
        def _(i):
            at = pl.ds(pl.multiple_of(q * sz.cells + i * sz.edge, sz.edge), sz.edge)
            g = grad_row(q, i)
            down_in[at, :] = (g * lscale[layer : layer + 1, :]).astype(BF16)
            sums[...] += g * branch[at, :]


def slope_rows(sz, grad_active, slope, up_in):
    @pl.loop(0, sz.rows // 16, unroll=2)
    def _(t):
        at = pl.ds(pl.multiple_of(t * 16, 16), 16)
        up_in[at, :] = (grad_active[at, :] * slope[at, :].astype(F32)).astype(BF16)


def weight_gradients(sz, active, down_in, normed, up_in, weights_out):
    weights_out[0 : sz.hidden, :] = multiply(active[...], down_in[...], 0, 0).astype(BF16)
    for k in range(sz.hidden // sz.channels):
        part = multiply(
            normed[...], up_in[:, k * sz.channels : (k + 1) * sz.channels], 0, 0
        ).astype(BF16)
        start = sz.hidden + k * sz.channels
        weights_out[start : start + sz.channels, :] = part


def norm_gradients(sz, grad_normed, normal, inverse, gain, layer, grad_conv, sums):
    scale = 1.0 / sz.channels
    sums[...] = jnp.zeros_like(sums)
    blank = jnp.zeros((8, LANES), F32)
    for q in range(sz.tiles):

        @pl.loop(0, sz.edge, unroll=2)
        def _(i):
            at = pl.ds(pl.multiple_of(q * sz.cells + i * sz.edge, sz.edge), sz.edge)
            local = pl.ds(pl.multiple_of(i * sz.edge, sz.edge), sz.edge)
            g = halves(grad_normed[at, :])
            n = [normal[q * sz.lanes + h, local, :] for h in range(sz.lanes)]
            sums[...] += jnp.concatenate([a * b for a, b in zip(g, n)], axis=1)
            s = [
                part * gain[layer : layer + 1, h * LANES : (h + 1) * LANES]
                for h, part in enumerate(g)
            ]
            products = [a * b for a, b in zip(s, n)]
            mean = jnp.sum(sum(s[1:], s[0]), axis=-1, keepdims=True) * scale
            slant = jnp.sum(sum(products[1:], products[0]), axis=-1, keepdims=True) * scale
            root = inverse[q, local, :]
            for h in range(sz.lanes):
                slab = q * sz.lanes + h
                base = pl.multiple_of(i * GRAD_PITCH, GRAD_PITCH)
                grad_conv[slab, pl.ds(base, 8), :] = blank
                grad_conv[slab, pl.ds(base + 8, sz.edge), :] = root * (s[h] - mean - n[h] * slant)
                grad_conv[slab, pl.ds(base + 8 + sz.edge, 8), :] = blank


def tap_gradients(sz, pad, grad_conv, tap_sums, small):
    tap_sums[...] = jnp.zeros_like(tap_sums)

    @pl.loop(0, sz.slabs)
    def _(slab):
        h = lax.rem(slab, sz.lanes)
        for b in range(TAPS):
            acc = [None] * TAPS
            for g in range(sz.edge // 8):
                grads = [
                    grad_conv[slab, pl.ds(i * GRAD_PITCH + 8 + 8 * g, 8), :]
                    for i in range(sz.edge)
                ]
                for r in range(sz.outer):
                    x = pad[slab, pl.ds(r * PITCH + b + 8 * g, 8), :]
                    for a in range(TAPS):
                        i = r - a
                        if 0 <= i < sz.edge:
                            term = x * grads[i]
                            acc[a] = term if acc[a] is None else acc[a] + term
            for a in range(TAPS):
                tap_sums[h, a * TAPS + b] += acc[a]

    for h in range(sz.lanes):
        for k in range(TAPS * TAPS):
            row = k // TAPS * 8 + k % TAPS
            small[row : row + 1, h * LANES : (h + 1) * LANES] = jnp.sum(
                tap_sums[h, k], axis=0, keepdims=True
            )


def spread_gradients(sz, grad_conv, taps, grad_pad):
    @pl.loop(0, sz.slabs)
    def _(slab):
        h = lax.rem(slab, sz.lanes)
        for g in range(PITCH // 8):
            acc = [None] * sz.outer
            for b in range(TAPS):
                start = 8 * g - b + 8
                if start >= 8 + sz.edge:
                    continue
                weights = [tap(taps, h, a, b) for a in range(TAPS)]
                for i in range(sz.edge):
                    x = grad_conv[slab, pl.ds(i * GRAD_PITCH + start, 8), :]
                    for a in range(TAPS):
                        term = x * weights[a]
                        acc[i + a] = term if acc[i + a] is None else acc[i + a] + term
            for p in range(sz.outer):
                grad_pad[slab, pl.ds(p * PITCH + 8 * g, 8), :] = acc[p]


def return_margins(sz, strip_at, corner_at, grad_pad, pool):
    pool[...] = jnp.zeros_like(pool)
    for q in range(sz.tiles):
        for side in range(4):
            piece = strip_at[q * 4 + side]
            for row in range(REACH):
                window, turned = margin_window(sz.edge, side, row)
                for h in range(sz.lanes):
                    part = grad_pad[q * sz.lanes + h, window, :]
                    pool[piece, row, h] = flip_rows(part) if turned else part
    for q in range(sz.tiles):
        for side in range(4):
            piece = corner_at[q * 4 + side]
            for row in range(REACH):
                for column in range(REACH):
                    at = corner_cell(sz.edge, side, row, column)
                    for h in range(sz.lanes):
                        pool[piece, row, h, pl.ds(column, 1), :] += grad_pad[
                            q * sz.lanes + h, pl.ds(at, 1), :
                        ]


def send_margins(sz, pool, own, below, above):
    own[...] = pool[0 : sz.pieces]
    for piece in range(sz.pieces):
        for row in range(REACH):
            for offset, ref in ((1, below), (2, above)):
                parts = [pool[offset * sz.pieces + piece, row, h] for h in range(sz.lanes)]
                ref[piece, row] = jnp.concatenate(parts, axis=1).astype(BF16)


def gather_inner(sz, grad_row, grad_pad, base):
    for q in range(sz.tiles):
        for i in range(sz.edge):
            for h, part in enumerate(halves(grad_row(q, i))):
                slab = q * sz.lanes + h
                base[slab, pl.ds(i * sz.edge, sz.edge), :] = (
                    part + grad_pad[slab, pl.ds((i + REACH) * PITCH + REACH, sz.edge), :]
                )


def add_strips(sz, base, own, first, second, flat):
    flat[...] = base[...]
    for q in range(sz.tiles):
        for side in range(4):
            piece = q * 4 + side
            for row in range(REACH):
                window, turned = strip_window(sz.edge, side, row)
                came = first[piece, row].astype(F32) + second[piece, row].astype(F32)
                for h, part in enumerate(halves(came)):
                    part = part + own[piece, row, h]
                    flat[q * sz.lanes + h, window, :] += flip_rows(part) if turned else part


def fill_small(small, gain_sums, scale_sums):
    small[TAPS * 8 : TAPS * 8 + 1, :] = jnp.sum(gain_sums[...], axis=0, keepdims=True)
    small[TAPS * 8 + 1 : TAPS * 8 + 2, :] = jnp.sum(scale_sums[...], axis=0, keepdims=True)


def flat_grad_row(sz, flat):
    def row(q, i):
        at = pl.ds(i * sz.edge, sz.edge)
        parts = [flat[q * sz.lanes + h, at, :] for h in range(sz.lanes)]
        return jnp.concatenate(parts, axis=1)

    return row


class Loads:
    def __init__(self, pairs, sems):
        self.copies = [
            pltpu.make_async_copy(source, target, sems.at[k])
            for k, (source, target) in enumerate(pairs)
        ]
        for copy in self.copies:
            copy.start()

    def wait(self, *which):
        for k in which:
            self.copies[k].wait()


def strips_kernel(sz, cur_hbm, strips, flat, cur, sems):
    loads = Loads([(cur_hbm, cur)], sems)
    loads.wait(0)
    for q in range(sz.tiles):
        for i in range(sz.edge):
            for h, part in enumerate(halves(cur[q, i].astype(F32))):
                flat[q * sz.lanes + h, pl.ds(i * sz.edge, sz.edge), :] = part
    write_strips(sz, flat, strips)


def forward_kernel(
    sz, layer, strip_at, corner_at, cur_hbm, own, below, above,
    kern_hbm, gain_hbm, lscale_hbm, up_hbm, down_hbm,
    out, strips, pad, normal, inverse, normed, slope, active, branch,
    pool, taps, conv, upward, flat, cur, kern, gain, lscale, up, down, sems,
):
    loads = Loads(
        [
            (cur_hbm, cur), (kern_hbm, kern), (gain_hbm, gain), (lscale_hbm, lscale),
            (up_hbm.at[layer], up), (down_hbm.at[layer], down),
        ],
        sems,
    )
    loads.wait(0)
    surround(sz, strip_at, corner_at, cur, own, below, above, pool, pad)
    loads.wait(1)
    hold_taps(sz, kern, layer, taps)
    convolve(sz, pad, taps, conv)
    loads.wait(2)
    normalise(sz, conv, gain, layer, normal, inverse, normed)
    loads.wait(4)
    upward[...] = multiply(normed[...], up[...])
    activate(sz, upward, active, slope)
    loads.wait(5)
    branch[...] = multiply(active[...], down[...])
    loads.wait(3)
    finish_forward(sz, cur, branch, lscale, layer, out, flat)
    write_strips(sz, flat, strips)


def turn_kernel(
    sz, layer, strip_at, corner_at, cur, own, below, above,
    kern_hbm, gain_hbm, lscale_hbm, up_hbm, down_hbm, out_grad_hbm,
    out_hbm, base, grad_own, grad_below, grad_above,
    pad, grad_conv, normed, active, down_in, up_in, gain_sums, scale_sums,
    pool, taps, conv, upward, kern, gain, lscale, up, down, sems,
    out_grad, out, normal, inverse, slope, branch, grad_pool, grad_pad, out_sem,
):
    loads = Loads(
        [
            (kern_hbm, kern), (gain_hbm, gain), (lscale_hbm, lscale),
            (up_hbm.at[layer], up), (down_hbm.at[layer], down), (out_grad_hbm, out_grad),
        ],
        sems,
    )
    surround(sz, strip_at, corner_at, cur, own, below, above, pool, pad)
    loads.wait(0)
    hold_taps(sz, kern, layer, taps)
    convolve(sz, pad, taps, conv)
    loads.wait(1)
    normalise(sz, conv, gain, layer, normal, inverse, normed)
    loads.wait(3)
    upward[...] = multiply(normed[...], up[...])
    activate(sz, upward, active, slope)
    loads.wait(4)
    branch[...] = multiply(active[...], down[...])
    loads.wait(2, 5)
    finish_forward(sz, cur, branch, lscale, layer, out, None)
    store = pltpu.make_async_copy(out, out_hbm, out_sem.at[0])
    store.start()

    def grad_row(q, i):
        return out_grad[q, i].astype(F32)

    scale_rows(sz, grad_row, branch, lscale, layer, down_in, scale_sums)
    upward[...] = multiply(down_in[...], down[...], 1, 1)
    slope_rows(sz, upward, slope, up_in)
    branch[...] = multiply(up_in[...], up[...], 1, 1)
    norm_gradients(sz, branch, normal, inverse, gain, layer, grad_conv, gain_sums)
    spread_gradients(sz, grad_conv, taps, grad_pad)
    return_margins(sz, strip_at, corner_at, grad_pad, grad_pool)
    send_margins(sz, grad_pool, grad_own, grad_below, grad_above)
    gather_inner(sz, grad_row, grad_pad, base)
    store.wait()


def weights_kernel(
    sz, pad, grad_conv, normed, active, down_in, up_in, gain_sums, scale_sums,
    weights_out, small, tap_sums,
):
    small[...] = jnp.zeros_like(small)
    weight_gradients(sz, active, down_in, normed, up_in, weights_out)
    tap_gradients(sz, pad, grad_conv, tap_sums, small)
    fill_small(small, gain_sums, scale_sums)


def backward_kernel(
    sz, layer, base, own, first, second, lscale_hbm, down_hbm, normed, slope, active, branch,
    weights_out, flat, up_in, scale_sums,
    hidden, down_in, lscale, down, sems,
):
    loads = Loads([(lscale_hbm, lscale), (down_hbm.at[layer], down)], sems)
    add_strips(sz, base, own, first, second, flat)
    for slab in range(sz.slabs):
        flat[slab] = flat[slab].astype(BF16).astype(F32)
    loads.wait(0)
    scale_rows(sz, flat_grad_row(sz, flat), branch, lscale, layer, down_in, scale_sums)
    loads.wait(1)
    hidden[...] = multiply(down_in[...], down[...], 1, 1)
    slope_rows(sz, hidden, slope, up_in)
    weight_gradients(sz, active, down_in, normed, up_in, weights_out)


def spread_kernel(
    sz, layer, strip_at, corner_at, kern_hbm, gain_hbm, up_hbm, flat, up_in, normal, inverse,
    base, grad_own, grad_below, grad_above, grad_conv, gain_sums,
    taps, branch, kern, gain, up, sems, grad_pool, grad_pad,
):
    loads = Loads([(up_hbm.at[layer], up), (gain_hbm, gain), (kern_hbm, kern)], sems)
    loads.wait(0)
    branch[...] = multiply(up_in[...], up[...], 1, 1)
    loads.wait(1)
    norm_gradients(sz, branch, normal, inverse, gain, layer, grad_conv, gain_sums)
    loads.wait(2)
    hold_taps(sz, kern, layer, taps)
    spread_gradients(sz, grad_conv, taps, grad_pad)
    return_margins(sz, strip_at, corner_at, grad_pad, grad_pool)
    send_margins(sz, grad_pool, grad_own, grad_below, grad_above)
    gather_inner(sz, flat_grad_row(sz, flat), grad_pad, base)


def taps_kernel(sz, pad, grad_conv, gain_sums, scale_sums, other, both, tap_sums, small):
    small[...] = jnp.zeros_like(small)
    tap_gradients(sz, pad, grad_conv, tap_sums, small)
    fill_small(small, gain_sums, scale_sums)
    both[0:SMALL_ROWS] = small[...]
    both[SMALL_ROWS : 2 * SMALL_ROWS] = other[...]


def last_kernel(sz, base, own, first, second, out_hbm, flat, out, sems):
    add_strips(sz, base, own, first, second, flat)
    row = flat_grad_row(sz, flat)
    for q in range(sz.tiles):
        for i in range(sz.edge):
            out[q, i] = row(q, i).astype(BF16)
    store = pltpu.make_async_copy(out, out_hbm, sems.at[0])
    store.start()
    store.wait()


def sum_rows(pieces, out):
    devices, rows, _ = pieces.shape
    for start in range(0, rows, 16):
        total = pieces[0, start : start + 16].astype(F32)
        for j in range(1, devices):
            total = total + pieces[j, start : start + 16].astype(F32)
        out[start : start + 16] = total.astype(BF16)


def sum_kernel(pieces, out):
    sum_rows(pieces, out)


def sum_both_kernel(pieces, small, out, held):
    rows = pieces.shape[1]
    sum_rows(pieces, out)
    total = small[0]
    for j in range(1, small.shape[0]):
        total = total + small[j]
    held[...] = jnp.zeros_like(held)
    held[0 : small.shape[1]] = total
    out[rows : rows + 16] = held[...].astype(BF16)


def unpack_kernel(
    sz, small_rows, zero, one, up_hbm, down_hbm, kernel_out, gain_out, scale_out,
    up, down, small, sems,
):
    devices, rows, channels = one.shape
    copies = []
    for layer, pieces in ((1, one), (0, zero)):
        for j in range(devices):
            value = pieces[j, 0:rows].astype(F32)
            start = j * rows
            if start < sz.hidden:
                down[layer, start : start + rows] = value
            else:
                k, c = divmod(start - sz.hidden, channels)
                up[layer, c : c + rows, k * channels : (k + 1) * channels] = value
            if start + rows == sz.hidden:
                copies.append((down.at[layer], down_hbm.at[layer]))
            elif start + rows == 2 * sz.hidden:
                copies.append((up.at[layer], up_hbm.at[layer]))
            else:
                continue
            k = len(copies) - 1
            copies[k] = pltpu.make_async_copy(*copies[k], sems.at[k])
            copies[k].start()
    for j in range(devices):
        value = zero[j, rows : rows + 16].astype(F32)
        small[j * small_rows : (j + 1) * small_rows] = value[0:small_rows]
    for layer in range(2):
        at = layer * SMALL_ROWS
        for a in range(TAPS):
            for b in range(TAPS):
                row = at + a * 8 + b
                kernel_out[a, b, layer : layer + 1] = small[row : row + 1]
        at = at + TAPS * 8
        gain_out[layer : layer + 1] = small[at : at + 1]
        scale_out[layer : layer + 1] = small[at + 1 : at + 2]
    for copy in copies:
        copy.wait()


IN_VMEM = pl.BlockSpec(memory_space=pltpu.VMEM)
IN_SMEM = pl.BlockSpec(memory_space=pltpu.SMEM)
IN_HBM = pl.BlockSpec(memory_space=pltpu.HBM)


def call(body, name, ins, outs, scratch):
    return pl.pallas_call(
        body,
        in_specs=[spec for spec, _ in ins],
        out_specs=[spec for spec, _ in outs],
        out_shape=[out for _, out in outs],
        scratch_shapes=scratch,
        compiler_params=pltpu.CompilerParams(vmem_limit_bytes=24 * 1024 * 1024),
        name=name,
    )(*[array for _, array in ins])


def near(*arrays):
    return [(IN_VMEM, array) for array in arrays]


def far(*arrays):
    return [(IN_HBM, array) for array in arrays]


def pass_on(shard, by):
    length = lax.axis_size("tile")
    return lax.ppermute(shard, "tile", [(i, (i + by) % length) for i in range(length)])


def to_owners(rows):
    devices = lax.axis_size("tile")
    shared = rows.reshape((devices, rows.shape[0] // devices, rows.shape[1]))
    return lax.all_to_all(shared, "tile", 0, 0)


def margin_plan(table, tile_count, columns, device):
    pieces = tile_count * 4
    entries = lax.dynamic_slice_in_dim(table, device * tile_count, tile_count, 0).reshape(
        (pieces, 2)
    )
    source = entries[:, 0]
    source_device = source // tile_count
    local_piece = (source - source_device * tile_count) * 4 + entries[:, 1]
    below_device = (device + columns - 1) % columns
    return jnp.where(
        source_device == device,
        local_piece,
        jnp.where(source_device == below_device, pieces + local_piece, 2 * pieces + local_piece),
    )


def on_device(
    inputs,
    out_grad,
    kernel,
    norm_gain,
    up_weight,
    down_weight,
    layer_scale,
    seam_table,
    corner_table,
):
    tiles, edge, _, channels = inputs.shape
    layers, _, hidden = up_weight.shape
    sz = Sizes(tiles, edge, channels, hidden)
    columns = lax.axis_size("tile")
    device = lax.axis_index("tile")
    strip_at = margin_plan(seam_table, tiles, columns, device)
    corner_at = margin_plan(corner_table, tiles, columns, device)
    plan = [(IN_SMEM, strip_at), (IN_SMEM, corner_at)]
    kernel_turned = kernel.transpose((1, 2, 0, 3))

    shape = jax.ShapeDtypeStruct
    image = shape(inputs.shape, BF16)
    strips_shape = shape((sz.pieces, REACH, edge, channels), BF16)
    slabs = shape((sz.slabs, sz.cells, LANES), F32)
    padded = shape((sz.slabs, sz.outer * PITCH, LANES), F32)
    inverses = shape((tiles, sz.cells, LANES), F32)
    narrow_short = shape((sz.rows, channels), BF16)
    wide_short = shape((sz.rows, hidden), BF16)
    narrow = shape((sz.rows, channels), F32)
    wide = shape((sz.rows, hidden), F32)
    sums = shape((edge, channels), F32)
    grad_slabs = shape((sz.slabs, edge * GRAD_PITCH, LANES), F32)
    own_shape = shape((sz.pieces, REACH, sz.lanes, edge, LANES), F32)
    pool = shape((3 * sz.pieces, REACH, edge, channels), BF16)
    grad_pool = shape((3 * sz.pieces, REACH, sz.lanes, edge, LANES), F32)
    taps = shape((sz.lanes, TAPS * 8, LANES), F32)
    tap_sums = shape((sz.lanes, TAPS * TAPS, 8, LANES), F32)
    small = shape((SMALL_ROWS, channels), F32)
    weights_shape = shape((2 * hidden, channels), BF16)
    held_kernel = shape(kernel_turned.shape, F32)
    vector = shape(norm_gain.shape, F32)
    held_up = shape(up_weight.shape[1:], BF16)
    held_down = shape(down_weight.shape[1:], BF16)
    held_weights = [held_kernel, vector, vector, held_up, held_down]

    def vmem(*shapes):
        return [pltpu.VMEM(one.shape, one.dtype) for one in shapes]

    def sems(count):
        return [pltpu.SemaphoreType.DMA((count,))]

    (strips,) = call(
        functools.partial(strips_kernel, sz),
        "strips",
        far(inputs),
        near(strips_shape),
        vmem(slabs, image) + sems(1),
    )
    below, above = pass_on(strips, 1), pass_on(strips, -1)
    middle, strips, pad_zero, normal, inverse, normed, slope, active, branch = call(
        functools.partial(forward_kernel, sz, 0),
        "forward",
        plan
        + far(inputs)
        + near(strips, below, above)
        + far(kernel_turned, norm_gain, layer_scale, up_weight, down_weight),
        near(
            image, strips_shape, padded, slabs, inverses,
            narrow_short, wide_short, wide_short, narrow,
        ),
        vmem(pool, taps, slabs, wide, slabs, image, *held_weights) + sems(6),
    )
    below, above = pass_on(strips, 1), pass_on(strips, -1)
    result, base, grad_own, grad_below, grad_above, *for_weights = call(
        functools.partial(turn_kernel, sz, 1),
        "turn",
        plan
        + near(middle, strips, below, above)
        + far(kernel_turned, norm_gain, layer_scale, up_weight, down_weight, out_grad),
        far(image)
        + near(
            slabs, own_shape, strips_shape, strips_shape,
            padded, grad_slabs, narrow_short, wide_short, narrow_short, wide_short, sums, sums,
        ),
        vmem(pool, taps, slabs, wide, *held_weights)
        + sems(6)
        + vmem(image, image, slabs, inverses, wide_short, narrow, grad_pool, padded)
        + sems(1),
    )
    from_below, from_above = pass_on(grad_above, 1), pass_on(grad_below, -1)
    weights_one, small_one = call(
        functools.partial(weights_kernel, sz),
        "weights",
        near(*for_weights),
        near(weights_shape, small),
        vmem(tap_sums),
    )
    pieces_one = to_owners(weights_one)
    weights_zero, flat, up_in, scale_sums = call(
        functools.partial(backward_kernel, sz, 0),
        "backward",
        near(base, grad_own, from_below, from_above)
        + far(layer_scale, down_weight)
        + near(normed, slope, active, branch),
        near(weights_shape, slabs, wide_short, sums),
        vmem(wide, narrow_short, vector, held_down) + sems(2),
    )
    pieces_zero = to_owners(weights_zero)
    base, grad_own, grad_below, grad_above, grad_conv, gain_sums = call(
        functools.partial(spread_kernel, sz, 0),
        "spread",
        plan + far(kernel_turned, norm_gain, up_weight) + near(flat, up_in, normal, inverse),
        near(slabs, own_shape, strips_shape, strips_shape, grad_slabs, sums),
        vmem(taps, narrow, held_kernel, vector, held_up) + sems(3) + vmem(grad_pool, padded),
    )
    from_below, from_above = pass_on(grad_above, 1), pass_on(grad_below, -1)
    both_rows = -(-2 * SMALL_ROWS // columns) * columns
    (small_both,) = call(
        functools.partial(taps_kernel, sz),
        "taps",
        near(pad_zero, grad_conv, gain_sums, scale_sums, small_one),
        near(shape((both_rows, channels), F32)),
        vmem(tap_sums, small),
    )
    pieces_small = to_owners(small_both)
    (in_grad,) = call(
        functools.partial(last_kernel, sz),
        "last",
        near(base, grad_own, from_below, from_above),
        far(image),
        vmem(slabs, image) + sems(1),
    )
    share = 2 * hidden // columns
    (sum_one,) = call(
        sum_kernel, "sum_one", near(pieces_one), near(shape((share, channels), BF16)), []
    )
    all_one = lax.all_gather(sum_one, "tile")
    (sum_zero,) = call(
        sum_both_kernel,
        "sum_zero",
        near(pieces_zero, pieces_small),
        near(shape((share + 16, channels), BF16)),
        vmem(shape((16, channels), F32)),
    )
    all_zero = lax.all_gather(sum_zero, "tile")
    grad_up, grad_down, grad_kernel, grad_gain, grad_scale = call(
        functools.partial(unpack_kernel, sz, both_rows // columns),
        "unpack",
        near(all_zero, all_one),
        far(shape(up_weight.shape, F32), shape(down_weight.shape, F32))
        + near(held_kernel, vector, vector),
        vmem(
            shape(up_weight.shape, F32),
            shape(down_weight.shape, F32),
            shape((both_rows, channels), F32),
        )
        + sems(4),
    )
    return (
        result, in_grad, grad_kernel.transpose((2, 0, 1, 3)),
        grad_gain, grad_up, grad_down, grad_scale,
    )


def solution(mesh):
    placed = (
        P(("groups", "tile"), None, None, None),
        P(("groups", "tile"), None, None, None),
        P(),
        P(),
        P(),
        P(),
        P(),
        P(),
        P(),
    )
    return jax.shard_map(
        on_device,
        mesh=mesh,
        in_specs=placed,
        out_specs=(
            P(("groups", "tile"), None, None, None),
            P(("groups", "tile"), None, None, None),
            P("groups", None, None, None),
            P("groups", None),
            P("groups", None, None),
            P("groups", None, None),
            P("groups", None),
        ),
        check_vma=False,
    )
```

```python
import functools

import jax
import jax.numpy as jnp
from jax import lax
from jax.experimental import pallas as pl
from jax.experimental.pallas import tpu as pltpu
from jax.sharding import PartitionSpec as P

epsilon = 1e-06
inverse_root_two = 0.7071067811865476
inverse_root_tau = 0.3989422804014327

LANES = 128
TAPS = 7
REACH = 3
PITCH = 24
GRAD_PITCH = 32
SMALL_ROWS = 64
F32 = jnp.float32
BF16 = jnp.bfloat16


def flip_rows(value):
    rows = value.shape[0]
    order = 7 - lax.broadcasted_iota(jnp.int32, (8, LANES), 0)
    parts = [
        jnp.take_along_axis(value[at : at + 8], order, axis=0, mode="promise_in_bounds")
        for at in range(0, rows, 8)
    ]
    return jnp.concatenate(parts[::-1], axis=0)


def halves(value):
    return [value[:, at : at + LANES] for at in range(0, value.shape[1], LANES)]


class Sizes:
    def __init__(self, tiles, edge, channels, hidden):
        self.tiles = tiles
        self.edge = edge
        self.channels = channels
        self.hidden = hidden
        self.lanes = channels // LANES
        self.cells = edge * edge
        self.rows = tiles * edge * edge
        self.pieces = tiles * 4
        self.outer = edge + 2 * REACH
        self.slabs = tiles * self.lanes

    def key(self):
        return (self.tiles, self.edge, self.channels, self.hidden)


def strip_window(edge, side, row):
    if side == 0:
        return pl.ds(row * edge, edge), False
    if side == 1:
        return pl.ds(edge - 1 - row, edge, stride=edge), False
    if side == 2:
        return pl.ds((edge - 1 - row) * edge, edge), True
    return pl.ds(row, edge, stride=edge), True


def margin_window(edge, side, row):
    last = edge + 2 * REACH - 1
    if side == 0:
        return pl.ds((2 - row) * PITCH + REACH, edge), True
    if side == 1:
        return pl.ds(REACH * PITCH + last - 2 + row, edge, stride=PITCH), True
    if side == 2:
        return pl.ds((last - 2 + row) * PITCH + REACH, edge), False
    return pl.ds(REACH * PITCH + 2 - row, edge, stride=PITCH), False


def corner_cell(edge, corner, row, column):
    last = edge + 2 * REACH - 1
    r, x = 2 - row, 2 - column
    if corner == 0:
        at = (r, x)
    elif corner == 1:
        at = (x, last - r)
    elif corner == 2:
        at = (last - r, last - x)
    else:
        at = (last - x, r)
    return at[0] * PITCH + at[1]


def write_strips(sz, flat, strips_ref):
    for q in range(sz.tiles):
        for side in range(4):
            for row in range(REACH):
                window, turned = strip_window(sz.edge, side, row)
                parts = [flat[q * sz.lanes + h, window, :] for h in range(sz.lanes)]
                if turned:
                    parts = [flip_rows(part) for part in parts]
                strips_ref[q * 4 + side, row] = jnp.concatenate(parts, axis=1).astype(BF16)


def surround(sz, strip_at, corner_at, cur, own, below, above, pool, pad):
    pool[0 : sz.pieces] = own[...]
    pool[sz.pieces : 2 * sz.pieces] = below[...]
    pool[2 * sz.pieces : 3 * sz.pieces] = above[...]
    for q in range(sz.tiles):
        for i in range(sz.edge):
            for h, part in enumerate(halves(cur[q, i].astype(F32))):
                pad[q * sz.lanes + h, pl.ds((i + REACH) * PITCH + REACH, sz.edge), :] = part
    for q in range(sz.tiles):
        for side in range(4):
            piece = strip_at[q * 4 + side]
            for row in range(REACH):
                window, turned = margin_window(sz.edge, side, row)
                for h, part in enumerate(halves(pool[piece, row].astype(F32))):
                    pad[q * sz.lanes + h, window, :] = flip_rows(part) if turned else part
            piece = corner_at[q * 4 + side]
            for row in range(REACH):
                for h, part in enumerate(halves(pool[piece, row].astype(F32))):
                    for column in range(REACH):
                        at = corner_cell(sz.edge, side, row, column)
                        pad[q * sz.lanes + h, pl.ds(at, 1), :] = part[column : column + 1]


def hold_taps(sz, kern, layer, taps):
    for a in range(TAPS):
        for b in range(TAPS):
            for h, part in enumerate(halves(kern[a, b, layer : layer + 1])):
                taps[h, pl.ds(a * 8 + b, 1), :] = part


def tap(taps, h, a, b):
    return jnp.broadcast_to(taps[h, pl.ds(a * 8 + b, 1), :], (8, LANES))


def convolve(sz, pad, taps, conv):
    @pl.loop(0, sz.slabs)
    def _(slab):
        h = lax.rem(slab, sz.lanes)
        for g in range(sz.edge // 8):
            acc = [None] * sz.edge
            for b in range(TAPS):
                weights = [tap(taps, h, a, b) for a in range(TAPS)]
                for r in range(sz.outer):
                    x = pad[slab, pl.ds(r * PITCH + b + 8 * g, 8), :]
                    for a in range(TAPS):
                        i = r - a
                        if 0 <= i < sz.edge:
                            term = x * weights[a]
                            acc[i] = term if acc[i] is None else acc[i] + term
            for i in range(sz.edge):
                conv[slab, pl.ds(i * sz.edge + 8 * g, 8), :] = acc[i]


def normalise(sz, conv, gain, layer, normal, inverse, normed):
    scale = 1.0 / sz.channels
    for q in range(sz.tiles):

        @pl.loop(0, sz.edge, unroll=2)
        def _(i):
            at = pl.ds(pl.multiple_of(i * sz.edge, sz.edge), sz.edge)
            parts = [conv[q * sz.lanes + h, at, :] for h in range(sz.lanes)]
            mean = jnp.sum(sum(parts[1:], parts[0]), axis=-1, keepdims=True) * scale
            parts = [part - mean for part in parts]
            squares = [part * part for part in parts]
            variance = jnp.sum(sum(squares[1:], squares[0]), axis=-1, keepdims=True) * scale
            root = lax.rsqrt(variance + epsilon)
            inverse[q, at, :] = jnp.broadcast_to(root, (sz.edge, LANES))
            flat_at = pl.ds(pl.multiple_of(q * sz.cells + i * sz.edge, sz.edge), sz.edge)
            for h, part in enumerate(parts):
                part = part * root
                normal[q * sz.lanes + h, at, :] = part
                gains = gain[layer : layer + 1, h * LANES : (h + 1) * LANES]
                normed[flat_at, h * LANES : (h + 1) * LANES] = (part * gains).astype(BF16)


def activate(sz, upward, active, slope):
    width = 512

    @pl.loop(0, sz.rows // 16)
    def _(t):
        at = pl.ds(pl.multiple_of(t * 16, 16), 16)
        for start in range(0, sz.hidden, width):
            u = upward[at, start : start + width]
            chance = 0.5 * (1.0 + lax.erf(u * inverse_root_two))
            active[at, start : start + width] = (u * chance).astype(BF16)
            slope[at, start : start + width] = (
                chance + u * jnp.exp(-0.5 * u * u) * inverse_root_tau
            ).astype(slope.dtype)


def multiply(a, b, ca=1, cb=0):
    return lax.dot_general(a, b, (((ca,), (cb,)), ((), ())), preferred_element_type=F32)


def finish_forward(sz, cur, branch, lscale, layer, out, flat):
    for q in range(sz.tiles):

        @pl.loop(0, sz.edge, unroll=2)
        def _(i):
            at = pl.ds(pl.multiple_of(q * sz.cells + i * sz.edge, sz.edge), sz.edge)
            value = cur[q, i].astype(F32) + branch[at, :] * lscale[layer : layer + 1, :]
            value = value.astype(BF16)
            out[q, i] = value
            if flat is not None:
                local = pl.ds(pl.multiple_of(i * sz.edge, sz.edge), sz.edge)
                for h, part in enumerate(halves(value.astype(F32))):
                    flat[q * sz.lanes + h, local, :] = part


def scale_rows(sz, grad_row, branch, lscale, layer, down_in, sums):
    sums[...] = jnp.zeros_like(sums)
    for q in range(sz.tiles):

        @pl.loop(0, sz.edge, unroll=2)
        def _(i):
            at = pl.ds(pl.multiple_of(q * sz.cells + i * sz.edge, sz.edge), sz.edge)
            g = grad_row(q, i)
            down_in[at, :] = (g * lscale[layer : layer + 1, :]).astype(BF16)
            sums[...] += g * branch[at, :]


def slope_rows(sz, grad_active, slope, up_in):
    @pl.loop(0, sz.rows // 16, unroll=2)
    def _(t):
        at = pl.ds(pl.multiple_of(t * 16, 16), 16)
        up_in[at, :] = (grad_active[at, :] * slope[at, :].astype(F32)).astype(BF16)


def weight_gradients(sz, core, active, down_in, normed, up_in, both, keep, send):
    both[0] = multiply(active[...], down_in[...], 0, 0).astype(BF16)
    for k in range(sz.hidden // sz.channels):
        part = multiply(normed[...], up_in[:, k * sz.channels : (k + 1) * sz.channels], 0, 0)
        both[1, k * sz.channels : (k + 1) * sz.channels, :] = part.astype(BF16)
    keep[...] = both[core]
    send[...] = both[1 - core]


def norm_gradients(sz, grad_normed, normal, inverse, gain, layer, grad_conv, sums):
    scale = 1.0 / sz.channels
    sums[...] = jnp.zeros_like(sums)
    blank = jnp.zeros((8, LANES), F32)
    for q in range(sz.tiles):

        @pl.loop(0, sz.edge, unroll=2)
        def _(i):
            at = pl.ds(pl.multiple_of(q * sz.cells + i * sz.edge, sz.edge), sz.edge)
            local = pl.ds(pl.multiple_of(i * sz.edge, sz.edge), sz.edge)
            g = halves(grad_normed[at, :])
            n = [normal[q * sz.lanes + h, local, :] for h in range(sz.lanes)]
            sums[...] += jnp.concatenate([a * b for a, b in zip(g, n)], axis=1)
            s = [
                part * gain[layer : layer + 1, h * LANES : (h + 1) * LANES]
                for h, part in enumerate(g)
            ]
            products = [a * b for a, b in zip(s, n)]
            mean = jnp.sum(sum(s[1:], s[0]), axis=-1, keepdims=True) * scale
            slant = jnp.sum(sum(products[1:], products[0]), axis=-1, keepdims=True) * scale
            root = inverse[q, local, :]
            for h in range(sz.lanes):
                slab = q * sz.lanes + h
                base = pl.multiple_of(i * GRAD_PITCH, GRAD_PITCH)
                grad_conv[slab, pl.ds(base, 8), :] = blank
                grad_conv[slab, pl.ds(base + 8, sz.edge), :] = root * (s[h] - mean - n[h] * slant)
                grad_conv[slab, pl.ds(base + 8 + sz.edge, 8), :] = blank


def tap_gradients(sz, pad, grad_conv, tap_sums, small):
    tap_sums[...] = jnp.zeros_like(tap_sums)

    @pl.loop(0, sz.slabs)
    def _(slab):
        h = lax.rem(slab, sz.lanes)
        for b in range(TAPS):
            acc = [None] * TAPS
            for g in range(sz.edge // 8):
                grads = [
                    grad_conv[slab, pl.ds(i * GRAD_PITCH + 8 + 8 * g, 8), :]
                    for i in range(sz.edge)
                ]
                for r in range(sz.outer):
                    x = pad[slab, pl.ds(r * PITCH + b + 8 * g, 8), :]
                    for a in range(TAPS):
                        i = r - a
                        if 0 <= i < sz.edge:
                            term = x * grads[i]
                            acc[a] = term if acc[a] is None else acc[a] + term
            for a in range(TAPS):
                tap_sums[h, a * TAPS + b] += acc[a]

    for h in range(sz.lanes):
        for k in range(TAPS * TAPS):
            row = k // TAPS * 8 + k % TAPS
            small[row : row + 1, h * LANES : (h + 1) * LANES] = jnp.sum(
                tap_sums[h, k], axis=0, keepdims=True
            )


def spread_gradients(sz, grad_conv, taps, grad_pad):
    @pl.loop(0, sz.slabs)
    def _(slab):
        h = lax.rem(slab, sz.lanes)
        for g in range(PITCH // 8):
            acc = [None] * sz.outer
            for b in range(TAPS):
                start = 8 * g - b + 8
                if start >= 8 + sz.edge:
                    continue
                weights = [tap(taps, h, a, b) for a in range(TAPS)]
                for i in range(sz.edge):
                    x = grad_conv[slab, pl.ds(i * GRAD_PITCH + start, 8), :]
                    for a in range(TAPS):
                        term = x * weights[a]
                        acc[i + a] = term if acc[i + a] is None else acc[i + a] + term
            for p in range(sz.outer):
                grad_pad[slab, pl.ds(p * PITCH + 8 * g, 8), :] = acc[p]


def return_margins(sz, strip_at, corner_at, grad_pad, pool):
    pool[...] = jnp.zeros_like(pool)
    for q in range(sz.tiles):
        for side in range(4):
            piece = strip_at[q * 4 + side]
            for row in range(REACH):
                window, turned = margin_window(sz.edge, side, row)
                for h in range(sz.lanes):
                    part = grad_pad[q * sz.lanes + h, window, :]
                    pool[piece, row, h] = flip_rows(part) if turned else part
    for q in range(sz.tiles):
        for side in range(4):
            piece = corner_at[q * 4 + side]
            for row in range(REACH):
                for column in range(REACH):
                    at = corner_cell(sz.edge, side, row, column)
                    for h in range(sz.lanes):
                        pool[piece, row, h, pl.ds(column, 1), :] += grad_pad[
                            q * sz.lanes + h, pl.ds(at, 1), :
                        ]


def send_margins(sz, pool, own, below, above):
    own[...] = pool[0 : sz.pieces]
    for piece in range(sz.pieces):
        for row in range(REACH):
            for offset, ref in ((1, below), (2, above)):
                parts = [pool[offset * sz.pieces + piece, row, h] for h in range(sz.lanes)]
                ref[piece, row] = jnp.concatenate(parts, axis=1).astype(BF16)


def gather_inner(sz, grad_row, grad_pad, base):
    for q in range(sz.tiles):
        for i in range(sz.edge):
            for h, part in enumerate(halves(grad_row(q, i))):
                slab = q * sz.lanes + h
                base[slab, pl.ds(i * sz.edge, sz.edge), :] = (
                    part + grad_pad[slab, pl.ds((i + REACH) * PITCH + REACH, sz.edge), :]
                )


def add_strips(sz, base, own, first, second, flat):
    flat[...] = base[...]
    for q in range(sz.tiles):
        for side in range(4):
            piece = q * 4 + side
            for row in range(REACH):
                window, turned = strip_window(sz.edge, side, row)
                came = first[piece, row].astype(F32) + second[piece, row].astype(F32)
                for h, part in enumerate(halves(came)):
                    part = part + own[piece, row, h]
                    flat[q * sz.lanes + h, window, :] += flip_rows(part) if turned else part


def fill_small(small, gain_sums, scale_sums):
    small[TAPS * 8 : TAPS * 8 + 1, :] = jnp.sum(gain_sums[...], axis=0, keepdims=True)
    small[TAPS * 8 + 1 : TAPS * 8 + 2, :] = jnp.sum(scale_sums[...], axis=0, keepdims=True)


def flat_grad_row(sz, flat):
    def row(q, i):
        at = pl.ds(i * sz.edge, sz.edge)
        parts = [flat[q * sz.lanes + h, at, :] for h in range(sz.lanes)]
        return jnp.concatenate(parts, axis=1)

    return row


def fetch_kernel(*refs):
    count = (len(refs) - 1) // 2
    copies = [
        pltpu.make_async_copy(refs[k], refs[count + k], refs[-1].at[k]) for k in range(count)
    ]
    for copy in copies:
        copy.start()
    for copy in copies:
        copy.wait()


def strips_kernel(sz, cur, strips, flat):
    for q in range(sz.tiles):
        for i in range(sz.edge):
            for h, part in enumerate(halves(cur[q, i].astype(F32))):
                flat[q * sz.lanes + h, pl.ds(i * sz.edge, sz.edge), :] = part
    write_strips(sz, flat, strips)


def forward_kernel(
    sz, layer, strip_at, corner_at, cur, own, below, above, kern, gain, lscale, up, down,
    out, strips, pad, normal, inverse, normed, slope, active, branch,
    pool, taps, conv, upward, flat,
):
    surround(sz, strip_at, corner_at, cur, own, below, above, pool, pad)
    hold_taps(sz, kern, layer, taps)
    convolve(sz, pad, taps, conv)
    normalise(sz, conv, gain, layer, normal, inverse, normed)
    upward[...] = multiply(normed[...], up[layer])
    activate(sz, upward, active, slope)
    branch[...] = multiply(active[...], down[layer])
    finish_forward(sz, cur, branch, lscale, layer, out, flat)
    write_strips(sz, flat, strips)


def turn_kernel(
    sz, layer, strip_at, corner_at, cur, own, below, above, kern, gain, lscale, up, down, out_grad,
    out_hbm, base, grad_own, grad_below, grad_above,
    pad, grad_conv, normed, active, down_in, up_in, gain_sums, scale_sums,
    pool, taps, conv, upward, out, normal, inverse, slope, branch, grad_pool, grad_pad, out_sem,
):
    surround(sz, strip_at, corner_at, cur, own, below, above, pool, pad)
    hold_taps(sz, kern, layer, taps)
    convolve(sz, pad, taps, conv)
    normalise(sz, conv, gain, layer, normal, inverse, normed)
    upward[...] = multiply(normed[...], up[layer])
    activate(sz, upward, active, slope)
    branch[...] = multiply(active[...], down[layer])
    finish_forward(sz, cur, branch, lscale, layer, out, None)
    store = pltpu.make_async_copy(out, out_hbm, out_sem.at[0])
    store.start()

    def grad_row(q, i):
        return out_grad[q, i].astype(F32)

    scale_rows(sz, grad_row, branch, lscale, layer, down_in, scale_sums)
    upward[...] = multiply(down_in[...], down[layer], 1, 1)
    slope_rows(sz, upward, slope, up_in)
    branch[...] = multiply(up_in[...], up[layer], 1, 1)
    norm_gradients(sz, branch, normal, inverse, gain, layer, grad_conv, gain_sums)
    spread_gradients(sz, grad_conv, taps, grad_pad)
    return_margins(sz, strip_at, corner_at, grad_pad, grad_pool)
    send_margins(sz, grad_pool, grad_own, grad_below, grad_above)
    gather_inner(sz, grad_row, grad_pad, base)
    store.wait()


def weights_kernel(
    sz, place, pad, grad_conv, normed, active, down_in, up_in, gain_sums, scale_sums,
    keep, send, small, tap_sums, both,
):
    small[...] = jnp.zeros_like(small)
    weight_gradients(sz, place[0], active, down_in, normed, up_in, both, keep, send)
    tap_gradients(sz, pad, grad_conv, tap_sums, small)
    fill_small(small, gain_sums, scale_sums)


def backward_kernel(
    sz, layer, place, base, own, first, second, lscale, down, normed, slope, active, branch,
    keep, send, flat, up_in, scale_sums,
    hidden, down_in, both,
):
    add_strips(sz, base, own, first, second, flat)
    for slab in range(sz.slabs):
        flat[slab] = flat[slab].astype(BF16).astype(F32)
    scale_rows(sz, flat_grad_row(sz, flat), branch, lscale, layer, down_in, scale_sums)
    hidden[...] = multiply(down_in[...], down[layer], 1, 1)
    slope_rows(sz, hidden, slope, up_in)
    weight_gradients(sz, place[0], active, down_in, normed, up_in, both, keep, send)


def spread_kernel(
    sz, layer, strip_at, corner_at, kern, gain, up, flat, up_in, normal, inverse,
    base, grad_own, grad_below, grad_above, grad_conv, gain_sums,
    taps, branch, grad_pool, grad_pad,
):
    branch[...] = multiply(up_in[...], up[layer], 1, 1)
    norm_gradients(sz, branch, normal, inverse, gain, layer, grad_conv, gain_sums)
    hold_taps(sz, kern, layer, taps)
    spread_gradients(sz, grad_conv, taps, grad_pad)
    return_margins(sz, strip_at, corner_at, grad_pad, grad_pool)
    send_margins(sz, grad_pool, grad_own, grad_below, grad_above)
    gather_inner(sz, flat_grad_row(sz, flat), grad_pad, base)


def taps_kernel(sz, pad, grad_conv, gain_sums, scale_sums, other, both, tap_sums, small):
    small[...] = jnp.zeros_like(small)
    tap_gradients(sz, pad, grad_conv, tap_sums, small)
    fill_small(small, gain_sums, scale_sums)
    both[0:SMALL_ROWS] = small[...].astype(BF16)
    both[SMALL_ROWS : 2 * SMALL_ROWS] = other[...].astype(BF16)


def last_kernel(sz, base, own, first, second, out_hbm, flat, out, sems):
    add_strips(sz, base, own, first, second, flat)
    row = flat_grad_row(sz, flat)
    for q in range(sz.tiles):
        for i in range(sz.edge):
            out[q, i] = row(q, i).astype(BF16)
    store = pltpu.make_async_copy(out, out_hbm, sems.at[0])
    store.start()
    store.wait()


def add_rows(out, parts):
    for start in range(0, out.shape[0], 16):
        rows = slice(start, start + 16)
        values = [part(rows).astype(F32) for part in parts]
        out[rows] = sum(values[1:], values[0]).astype(BF16)


def share_kernel(digit, *refs):
    place, refs = refs[0], refs[1:]
    count = refs[0].shape[0]
    arrays, outs = refs[:-count], refs[-count:]
    for k, out in enumerate(outs):
        piece = place[digit] ^ k
        add_rows(out, [lambda rows, array=array: array[piece, rows] for array in arrays])


def total_kernel(*refs):
    add_rows(refs[-1], [lambda rows, array=array: array[rows] for array in refs[:-1]])


def order_kernel(digit, place, *refs):
    for k, piece in enumerate(refs[:-1]):
        refs[-1][place[digit] ^ k] = piece[...]


def unpack_kernel(
    sz, place, mine_zero, theirs_zero, mine_one, theirs_one, small,
    up_hbm, down_hbm, kernel_out, gain_out, scale_out, up, down, sems,
):
    even = place[0] == 0
    copies = []
    step = 32
    for layer, mine, theirs in ((1, mine_one, theirs_one), (0, mine_zero, theirs_zero)):
        for start in range(0, sz.hidden, step):
            rows = slice(start, start + step)
            down[layer, rows] = jnp.where(even, mine[rows], theirs[rows]).astype(F32)
        copies.append((down.at[layer], down_hbm.at[layer]))
        for start in range(0, sz.hidden, step):
            rows = slice(start, start + step)
            k, c = divmod(start, sz.channels)
            up[layer, c : c + step, k * sz.channels : (k + 1) * sz.channels] = jnp.where(
                even, theirs[rows], mine[rows]
            ).astype(F32)
        copies.append((up.at[layer], up_hbm.at[layer]))
        for k in range(len(copies) - 2, len(copies)):
            copies[k] = pltpu.make_async_copy(*copies[k], sems.at[k])
            copies[k].start()
    for layer in range(2):
        at = layer * SMALL_ROWS
        for a in range(TAPS):
            part = small[at + a * 8 - a % 2 * 8 : at + a * 8 - a % 2 * 8 + 16].astype(F32)
            part = part[a % 2 * 8 : a % 2 * 8 + 8]
            for b in range(TAPS):
                kernel_out[a, b, layer : layer + 1] = part[b : b + 1]
        last = small[at + SMALL_ROWS - 16 : at + SMALL_ROWS].astype(F32)
        gain_out[layer : layer + 1] = last[8:9]
        scale_out[layer : layer + 1] = last[9:10]
    for copy in copies:
        copy.wait()


IN_VMEM = pl.BlockSpec(memory_space=pltpu.VMEM)
IN_SMEM = pl.BlockSpec(memory_space=pltpu.SMEM)
IN_HBM = pl.BlockSpec(memory_space=pltpu.HBM)


def call(body, name, micros, ins, outs, scratch):
    return pl.pallas_call(
        body,
        in_specs=[spec for spec, _ in ins],
        out_specs=[spec for spec, _ in outs],
        out_shape=[out for _, out in outs],
        scratch_shapes=scratch,
        compiler_params=pltpu.CompilerParams(vmem_limit_bytes=24 * 1024 * 1024),
        cost_estimate=pl.CostEstimate(
            flops=0, bytes_accessed=int(micros * 3.5e6), transcendentals=0
        ),
        name=name,
    )(*[array for _, array in ins])


def near(*arrays):
    return [(IN_VMEM, array) for array in arrays]


def far(*arrays):
    return [(IN_HBM, array) for array in arrays]


def pass_on(shard, by):
    length = lax.axis_size("tile")
    return lax.ppermute(shard, "tile", [(i, (i + by) % length) for i in range(length)])


def partners(array, masks):
    length = lax.axis_size("tile")
    return [
        lax.ppermute(array, "tile", [(i, i ^ mask) for i in range(length)]) for mask in masks
    ]


def swap(arrays, masks):
    length = lax.axis_size("tile")
    return [
        lax.ppermute(array, "tile", [(i, i ^ mask) for i in range(length)])
        for array, mask in zip(arrays, masks)
    ]


class Reduction:
    def __init__(self, place, devices):
        self.place = [(IN_SMEM, place)]
        self.rest = devices // 8
        self.near_masks = [2 * k for k in range(1, 4)]
        self.rest_masks = [8 * k for k in range(1, self.rest)]

    def scatter(self, keep, send):
        rows, channels = keep.shape
        (came,) = swap([send], [1])
        quarter = rows // 4
        parts = (4, quarter, channels)
        shape = jax.ShapeDtypeStruct((quarter, channels), BF16)
        pieces = call(
            functools.partial(share_kernel, 1), "share_near", 0.7,
            self.place + near(keep.reshape(parts), came.reshape(parts)), near(*[shape] * 4), [],
        )
        arrived = swap(pieces[1:], self.near_masks)
        parts = (self.rest, quarter // self.rest, channels)
        shape = jax.ShapeDtypeStruct(parts[1:], BF16)
        arrays = [piece.reshape(parts) for piece in [pieces[0]] + arrived]
        pieces = call(
            functools.partial(share_kernel, 2), "share_far", 0.5,
            self.place + near(*arrays), near(*[shape] * self.rest), [],
        )
        arrived = swap(pieces[1:], self.rest_masks)
        (total,) = call(
            total_kernel, "total", 0.3, near(pieces[0], *arrived), near(shape), []
        )
        return total

    def gather(self, total):
        rows, channels = total.shape
        for digit, masks, name in ((2, self.rest_masks, "order_far"), (1, self.near_masks, "order_near")):
            pieces = [total] + partners(total, masks)
            shape = jax.ShapeDtypeStruct((len(pieces),) + total.shape, BF16)
            (total,) = call(
                functools.partial(order_kernel, digit), name, 0.3,
                self.place + near(*pieces), near(shape), [],
            )
            total = total.reshape((-1, channels))
        return total, partners(total, [1])[0]

    def whole(self, array):
        for masks in ([1], self.near_masks, self.rest_masks):
            shape = jax.ShapeDtypeStruct(array.shape, BF16)
            (array,) = call(
                total_kernel, "total_small", 0.3,
                near(array, *partners(array, masks)), near(shape), [],
            )
        return array


def margin_plan(table, tile_count, columns, device):
    pieces = tile_count * 4
    entries = lax.dynamic_slice_in_dim(table, device * tile_count, tile_count, 0).reshape(
        (pieces, 2)
    )
    source = entries[:, 0]
    source_device = source // tile_count
    local_piece = (source - source_device * tile_count) * 4 + entries[:, 1]
    below_device = (device + columns - 1) % columns
    return jnp.where(
        source_device == device,
        local_piece,
        jnp.where(source_device == below_device, pieces + local_piece, 2 * pieces + local_piece),
    )


def on_device(
    inputs,
    out_grad,
    kernel,
    norm_gain,
    up_weight,
    down_weight,
    layer_scale,
    seam_table,
    corner_table,
):
    tiles, edge, _, channels = inputs.shape
    layers, _, hidden = up_weight.shape
    sz = Sizes(tiles, edge, channels, hidden)
    columns = lax.axis_size("tile")
    device = lax.axis_index("tile")
    strip_at = margin_plan(seam_table, tiles, columns, device)
    corner_at = margin_plan(corner_table, tiles, columns, device)
    plan = [(IN_SMEM, strip_at), (IN_SMEM, corner_at)]
    kernel_turned = kernel.transpose((1, 2, 0, 3))

    place = jnp.stack([device % 2, device // 2 % 4, device // 8]).astype(jnp.int32)
    where = [(IN_SMEM, place)]
    reduction = Reduction(place, columns)

    shape = jax.ShapeDtypeStruct
    image = shape(inputs.shape, BF16)
    strips_shape = shape((sz.pieces, REACH, edge, channels), BF16)
    slabs = shape((sz.slabs, sz.cells, LANES), F32)
    padded = shape((sz.slabs, sz.outer * PITCH, LANES), F32)
    inverses = shape((tiles, sz.cells, LANES), F32)
    narrow_short = shape((sz.rows, channels), BF16)
    wide_short = shape((sz.rows, hidden), BF16)
    narrow = shape((sz.rows, channels), F32)
    wide = shape((sz.rows, hidden), F32)
    sums = shape((edge, channels), F32)
    grad_slabs = shape((sz.slabs, edge * GRAD_PITCH, LANES), F32)
    own_shape = shape((sz.pieces, REACH, sz.lanes, edge, LANES), F32)
    pool = shape((3 * sz.pieces, REACH, edge, channels), BF16)
    grad_pool = shape((3 * sz.pieces, REACH, sz.lanes, edge, LANES), F32)
    taps = shape((sz.lanes, TAPS * 8, LANES), F32)
    tap_sums = shape((sz.lanes, TAPS * TAPS, 8, LANES), F32)
    small = shape((SMALL_ROWS, channels), F32)
    half = shape((hidden, channels), BF16)
    two_halves = shape((2, hidden, channels), BF16)

    def vmem(*shapes):
        return [pltpu.VMEM(one.shape, one.dtype) for one in shapes]

    def sems(count):
        return [pltpu.SemaphoreType.DMA((count,))]

    (strips,) = call(
        functools.partial(strips_kernel, sz),
        "strips", 0.3,
        near(inputs),
        near(strips_shape),
        vmem(slabs),
    )
    below, above = pass_on(strips, 1), pass_on(strips, -1)
    fetched = (inputs, out_grad, kernel_turned, norm_gain, layer_scale, up_weight, down_weight)
    inputs, out_grad, kern, gain, lscale, up, down = call(
        fetch_kernel,
        "fetch", 2.0,
        far(*fetched),
        near(*[shape(one.shape, one.dtype) for one in fetched]),
        sems(len(fetched)),
    )
    middle, strips, pad_zero, normal, inverse, normed, slope, active, branch = call(
        functools.partial(forward_kernel, sz, 0),
        "forward", 8.7,
        plan + near(inputs, strips, below, above, kern, gain, lscale, up, down),
        near(
            image, strips_shape, padded, slabs, inverses,
            narrow_short, wide_short, wide_short, narrow,
        ),
        vmem(pool, taps, slabs, wide, slabs),
    )
    below, above = pass_on(strips, 1), pass_on(strips, -1)
    result, base, grad_own, grad_below, grad_above, *for_weights = call(
        functools.partial(turn_kernel, sz, 1),
        "turn", 15.4,
        plan + near(middle, strips, below, above, kern, gain, lscale, up, down, out_grad),
        far(image)
        + near(
            slabs, own_shape, strips_shape, strips_shape,
            padded, grad_slabs, narrow_short, wide_short, narrow_short, wide_short, sums, sums,
        ),
        vmem(
            pool, taps, slabs, wide, image, slabs, inverses, wide_short, narrow, grad_pool, padded
        )
        + sems(1),
    )
    from_below, from_above = pass_on(grad_above, 1), pass_on(grad_below, -1)
    keep_one, send_one, small_one = call(
        functools.partial(weights_kernel, sz),
        "weights", 2.8,
        where + near(*for_weights),
        near(half, half, small),
        vmem(tap_sums, two_halves),
    )
    sum_one = reduction.scatter(keep_one, send_one)
    keep_zero, send_zero, flat, up_in, scale_sums = call(
        functools.partial(backward_kernel, sz, 0),
        "backward", 2.9,
        where
        + near(
            base, grad_own, from_below, from_above, lscale, down, normed, slope, active, branch
        ),
        near(half, half, slabs, wide_short, sums),
        vmem(wide, narrow_short, two_halves),
    )
    sum_zero = reduction.scatter(keep_zero, send_zero)
    base, grad_own, grad_below, grad_above, grad_conv, gain_sums = call(
        functools.partial(spread_kernel, sz, 0),
        "spread", 6.0,
        plan + near(kern, gain, up, flat, up_in, normal, inverse),
        near(slabs, own_shape, strips_shape, strips_shape, grad_slabs, sums),
        vmem(taps, narrow, grad_pool, padded),
    )
    from_below, from_above = pass_on(grad_above, 1), pass_on(grad_below, -1)
    (small_both,) = call(
        functools.partial(taps_kernel, sz),
        "taps", 2.1,
        near(pad_zero, grad_conv, gain_sums, scale_sums, small_one),
        near(shape((2 * SMALL_ROWS, channels), BF16)),
        vmem(tap_sums, small),
    )
    (in_grad,) = call(
        functools.partial(last_kernel, sz),
        "last", 1.0,
        near(base, grad_own, from_below, from_above),
        far(image),
        vmem(slabs, image) + sems(1),
    )
    grad_up, grad_down, grad_kernel, grad_gain, grad_scale = call(
        functools.partial(unpack_kernel, sz),
        "unpack", 2.7,
        where
        + near(
            *reduction.gather(sum_zero), *reduction.gather(sum_one), reduction.whole(small_both)
        ),
        far(shape(up_weight.shape, F32), shape(down_weight.shape, F32))
        + near(
            shape(kernel_turned.shape, F32), shape(norm_gain.shape, F32),
            shape(norm_gain.shape, F32),
        ),
        vmem(shape(up_weight.shape, F32), shape(down_weight.shape, F32)) + sems(4),
    )
    return (
        result, in_grad, grad_kernel.transpose((2, 0, 1, 3)),
        grad_gain, grad_up, grad_down, grad_scale,
    )


def solution(mesh):
    placed = (
        P(("groups", "tile"), None, None, None),
        P(("groups", "tile"), None, None, None),
        P(),
        P(),
        P(),
        P(),
        P(),
        P(),
        P(),
    )
    return jax.shard_map(
        on_device,
        mesh=mesh,
        in_specs=placed,
        out_specs=(
            P(("groups", "tile"), None, None, None),
            P(("groups", "tile"), None, None, None),
            P("groups", None, None, None),
            P("groups", None),
            P("groups", None, None),
            P("groups", None, None),
            P("groups", None),
        ),
        check_vma=False,
    )
```

```python
import functools

import jax
import jax.numpy as jnp
from jax import lax
from jax.experimental import pallas as pl
from jax.experimental.pallas import tpu as pltpu
from jax.sharding import PartitionSpec as P

epsilon = 1e-06
inverse_root_two = 0.7071067811865476
inverse_root_tau = 0.3989422804014327

LANES = 128
TAPS = 7
REACH = 3
PITCH = 24
GRAD_PITCH = 32
SMALL_ROWS = 64
F32 = jnp.float32
BF16 = jnp.bfloat16


def flip_rows(value):
    rows = value.shape[0]
    order = 7 - lax.broadcasted_iota(jnp.int32, (8, LANES), 0)
    parts = [
        jnp.take_along_axis(value[at : at + 8], order, axis=0, mode="promise_in_bounds")
        for at in range(0, rows, 8)
    ]
    return jnp.concatenate(parts[::-1], axis=0)


def halves(value):
    return [value[:, at : at + LANES] for at in range(0, value.shape[1], LANES)]


class Sizes:
    def __init__(self, tiles, edge, channels, hidden):
        self.tiles = tiles
        self.edge = edge
        self.channels = channels
        self.hidden = hidden
        self.lanes = channels // LANES
        self.cells = edge * edge
        self.rows = tiles * edge * edge
        self.pieces = tiles * 4
        self.outer = edge + 2 * REACH
        self.slabs = tiles * self.lanes

    def key(self):
        return (self.tiles, self.edge, self.channels, self.hidden)


def strip_window(edge, side, row):
    if side == 0:
        return pl.ds(row * edge, edge), False
    if side == 1:
        return pl.ds(edge - 1 - row, edge, stride=edge), False
    if side == 2:
        return pl.ds((edge - 1 - row) * edge, edge), True
    return pl.ds(row, edge, stride=edge), True


def margin_window(edge, side, row):
    last = edge + 2 * REACH - 1
    if side == 0:
        return pl.ds((2 - row) * PITCH + REACH, edge), True
    if side == 1:
        return pl.ds(REACH * PITCH + last - 2 + row, edge, stride=PITCH), True
    if side == 2:
        return pl.ds((last - 2 + row) * PITCH + REACH, edge), False
    return pl.ds(REACH * PITCH + 2 - row, edge, stride=PITCH), False


def corner_cell(edge, corner, row, column):
    last = edge + 2 * REACH - 1
    r, x = 2 - row, 2 - column
    if corner == 0:
        at = (r, x)
    elif corner == 1:
        at = (x, last - r)
    elif corner == 2:
        at = (last - r, last - x)
    else:
        at = (last - x, r)
    return at[0] * PITCH + at[1]


def read_plan(sz, table):
    columns = lax.axis_size("tile")
    device = lax.axis_index("tile")
    below = lax.rem(device + columns - 1, columns)
    plan = []
    for q in range(sz.tiles):
        for side in range(4):
            source = table[side, 0, device * sz.tiles + q]
            owner = lax.div(source, sz.tiles)
            local = (source - owner * sz.tiles) * 4 + table[side, 1, device * sz.tiles + q]
            shift = jnp.where(
                owner == device, 0, jnp.where(owner == below, sz.pieces, 2 * sz.pieces)
            )
            plan.append(shift + local)
    return plan


def digit_of(level):
    device = lax.axis_index("tile")
    if level == 0:
        return lax.rem(device, 2)
    if level == 1:
        return lax.rem(lax.div(device, 2), 4)
    return lax.div(device, 8)


def write_strips(sz, flat, strips_ref):
    for q in range(sz.tiles):
        for side in range(4):
            for row in range(REACH):
                window, turned = strip_window(sz.edge, side, row)
                parts = [flat[q * sz.lanes + h, window, :] for h in range(sz.lanes)]
                if turned:
                    parts = [flip_rows(part) for part in parts]
                strips_ref[q * 4 + side, row] = jnp.concatenate(parts, axis=1).astype(BF16)


def surround(sz, strip_at, corner_at, cur, own, below, above, pool, pad):
    pool[0 : sz.pieces] = own[...]
    pool[sz.pieces : 2 * sz.pieces] = below[...]
    pool[2 * sz.pieces : 3 * sz.pieces] = above[...]
    for q in range(sz.tiles):
        for i in range(sz.edge):
            for h, part in enumerate(halves(cur[q, i].astype(F32))):
                pad[q * sz.lanes + h, pl.ds((i + REACH) * PITCH + REACH, sz.edge), :] = part
    for q in range(sz.tiles):
        for side in range(4):
            piece = strip_at[q * 4 + side]
            for row in range(REACH):
                window, turned = margin_window(sz.edge, side, row)
                for h, part in enumerate(halves(pool[piece, row].astype(F32))):
                    pad[q * sz.lanes + h, window, :] = flip_rows(part) if turned else part
            piece = corner_at[q * 4 + side]
            for row in range(REACH):
                for h, part in enumerate(halves(pool[piece, row].astype(F32))):
                    for column in range(REACH):
                        at = corner_cell(sz.edge, side, row, column)
                        pad[q * sz.lanes + h, pl.ds(at, 1), :] = part[column : column + 1]


def hold_taps(sz, kern, layer, taps):
    for a in range(TAPS):
        for b in range(TAPS):
            for h, part in enumerate(halves(kern[a, b, layer : layer + 1])):
                taps[h, pl.ds(a * 8 + b, 1), :] = part


def tap(taps, h, a, b):
    return jnp.broadcast_to(taps[h, pl.ds(a * 8 + b, 1), :], (8, LANES))


def convolve(sz, pad, taps, conv):
    @pl.loop(0, sz.slabs)
    def _(slab):
        h = lax.rem(slab, sz.lanes)
        for g in range(sz.edge // 8):
            acc = [None] * sz.edge
            for b in range(TAPS):
                weights = [tap(taps, h, a, b) for a in range(TAPS)]
                for r in range(sz.outer):
                    x = pad[slab, pl.ds(r * PITCH + b + 8 * g, 8), :]
                    for a in range(TAPS):
                        i = r - a
                        if 0 <= i < sz.edge:
                            term = x * weights[a]
                            acc[i] = term if acc[i] is None else acc[i] + term
            for i in range(sz.edge):
                conv[slab, pl.ds(i * sz.edge + 8 * g, 8), :] = acc[i]


def normalise(sz, conv, gain, layer, normal, inverse, normed):
    scale = 1.0 / sz.channels
    for q in range(sz.tiles):

        @pl.loop(0, sz.edge, unroll=2)
        def _(i):
            at = pl.ds(pl.multiple_of(i * sz.edge, sz.edge), sz.edge)
            parts = [conv[q * sz.lanes + h, at, :] for h in range(sz.lanes)]
            mean = jnp.sum(sum(parts[1:], parts[0]), axis=-1, keepdims=True) * scale
            parts = [part - mean for part in parts]
            squares = [part * part for part in parts]
            variance = jnp.sum(sum(squares[1:], squares[0]), axis=-1, keepdims=True) * scale
            root = lax.rsqrt(variance + epsilon)
            inverse[q, at, :] = jnp.broadcast_to(root, (sz.edge, LANES))
            flat_at = pl.ds(pl.multiple_of(q * sz.cells + i * sz.edge, sz.edge), sz.edge)
            for h, part in enumerate(parts):
                part = part * root
                normal[q * sz.lanes + h, at, :] = part
                gains = gain[layer : layer + 1, h * LANES : (h + 1) * LANES]
                normed[flat_at, h * LANES : (h + 1) * LANES] = (part * gains).astype(BF16)


def activate(sz, upward, active, slope):
    width = 512

    @pl.loop(0, sz.rows // 16)
    def _(t):
        at = pl.ds(pl.multiple_of(t * 16, 16), 16)
        for start in range(0, sz.hidden, width):
            u = upward[at, start : start + width]
            chance = 0.5 * (1.0 + lax.erf(u * inverse_root_two))
            active[at, start : start + width] = (u * chance).astype(BF16)
            slope[at, start : start + width] = (
                chance + u * jnp.exp(-0.5 * u * u) * inverse_root_tau
            ).astype(slope.dtype)


def multiply(a, b, ca=1, cb=0):
    return lax.dot_general(a, b, (((ca,), (cb,)), ((), ())), preferred_element_type=F32)


def finish_forward(sz, cur, branch, lscale, layer, out, flat):
    for q in range(sz.tiles):

        @pl.loop(0, sz.edge, unroll=2)
        def _(i):
            at = pl.ds(pl.multiple_of(q * sz.cells + i * sz.edge, sz.edge), sz.edge)
            value = cur[q, i].astype(F32) + branch[at, :] * lscale[layer : layer + 1, :]
            value = value.astype(BF16)
            out[q, i] = value
            if flat is not None:
                local = pl.ds(pl.multiple_of(i * sz.edge, sz.edge), sz.edge)
                for h, part in enumerate(halves(value.astype(F32))):
                    flat[q * sz.lanes + h, local, :] = part


def scale_rows(sz, grad_row, branch, lscale, layer, down_in, sums):
    sums[...] = jnp.zeros_like(sums)
    for q in range(sz.tiles):

        @pl.loop(0, sz.edge, unroll=2)
        def _(i):
            at = pl.ds(pl.multiple_of(q * sz.cells + i * sz.edge, sz.edge), sz.edge)
            g = grad_row(q, i)
            down_in[at, :] = (g * lscale[layer : layer + 1, :]).astype(BF16)
            sums[...] += g * branch[at, :]


def slope_rows(sz, grad_active, slope, up_in):
    @pl.loop(0, sz.rows // 16, unroll=2)
    def _(t):
        at = pl.ds(pl.multiple_of(t * 16, 16), 16)
        up_in[at, :] = (grad_active[at, :] * slope[at, :].astype(F32)).astype(BF16)


def weight_gradients(sz, core, active, down_in, normed, up_in, both, keep, send):
    both[0] = multiply(active[...], down_in[...], 0, 0).astype(BF16)
    for k in range(sz.hidden // sz.channels):
        part = multiply(normed[...], up_in[:, k * sz.channels : (k + 1) * sz.channels], 0, 0)
        both[1, k * sz.channels : (k + 1) * sz.channels, :] = part.astype(BF16)
    keep[...] = both[core]
    send[...] = both[1 - core]


def norm_gradients(sz, grad_normed, normal, inverse, gain, layer, grad_conv, sums):
    scale = 1.0 / sz.channels
    sums[...] = jnp.zeros_like(sums)
    blank = jnp.zeros((8, LANES), F32)
    for q in range(sz.tiles):

        @pl.loop(0, sz.edge, unroll=2)
        def _(i):
            at = pl.ds(pl.multiple_of(q * sz.cells + i * sz.edge, sz.edge), sz.edge)
            local = pl.ds(pl.multiple_of(i * sz.edge, sz.edge), sz.edge)
            g = halves(grad_normed[at, :])
            n = [normal[q * sz.lanes + h, local, :] for h in range(sz.lanes)]
            sums[...] += jnp.concatenate([a * b for a, b in zip(g, n)], axis=1)
            s = [
                part * gain[layer : layer + 1, h * LANES : (h + 1) * LANES]
                for h, part in enumerate(g)
            ]
            products = [a * b for a, b in zip(s, n)]
            mean = jnp.sum(sum(s[1:], s[0]), axis=-1, keepdims=True) * scale
            slant = jnp.sum(sum(products[1:], products[0]), axis=-1, keepdims=True) * scale
            root = inverse[q, local, :]
            for h in range(sz.lanes):
                slab = q * sz.lanes + h
                base = pl.multiple_of(i * GRAD_PITCH, GRAD_PITCH)
                grad_conv[slab, pl.ds(base, 8), :] = blank
                grad_conv[slab, pl.ds(base + 8, sz.edge), :] = root * (s[h] - mean - n[h] * slant)
                grad_conv[slab, pl.ds(base + 8 + sz.edge, 8), :] = blank


def tap_gradients(sz, pad, grad_conv, tap_sums, small):
    tap_sums[...] = jnp.zeros_like(tap_sums)

    @pl.loop(0, sz.slabs)
    def _(slab):
        h = lax.rem(slab, sz.lanes)
        for b in range(TAPS):
            acc = [None] * TAPS
            for g in range(sz.edge // 8):
                grads = [
                    grad_conv[slab, pl.ds(i * GRAD_PITCH + 8 + 8 * g, 8), :]
                    for i in range(sz.edge)
                ]
                for r in range(sz.outer):
                    x = pad[slab, pl.ds(r * PITCH + b + 8 * g, 8), :]
                    for a in range(TAPS):
                        i = r - a
                        if 0 <= i < sz.edge:
                            term = x * grads[i]
                            acc[a] = term if acc[a] is None else acc[a] + term
            for a in range(TAPS):
                tap_sums[h, a * TAPS + b] += acc[a]

    for h in range(sz.lanes):
        for k in range(TAPS * TAPS):
            row = k // TAPS * 8 + k % TAPS
            small[row : row + 1, h * LANES : (h + 1) * LANES] = jnp.sum(
                tap_sums[h, k], axis=0, keepdims=True
            )


def spread_gradients(sz, grad_conv, taps, grad_pad):
    @pl.loop(0, sz.slabs)
    def _(slab):
        h = lax.rem(slab, sz.lanes)
        for g in range(PITCH // 8):
            acc = [None] * sz.outer
            for b in range(TAPS):
                start = 8 * g - b + 8
                if start >= 8 + sz.edge:
                    continue
                weights = [tap(taps, h, a, b) for a in range(TAPS)]
                for i in range(sz.edge):
                    x = grad_conv[slab, pl.ds(i * GRAD_PITCH + start, 8), :]
                    for a in range(TAPS):
                        term = x * weights[a]
                        acc[i + a] = term if acc[i + a] is None else acc[i + a] + term
            for p in range(sz.outer):
                grad_pad[slab, pl.ds(p * PITCH + 8 * g, 8), :] = acc[p]


def return_margins(sz, strip_at, corner_at, grad_pad, pool):
    pool[...] = jnp.zeros_like(pool)
    for q in range(sz.tiles):
        for side in range(4):
            piece = strip_at[q * 4 + side]
            for row in range(REACH):
                window, turned = margin_window(sz.edge, side, row)
                for h in range(sz.lanes):
                    part = grad_pad[q * sz.lanes + h, window, :]
                    pool[piece, row, h] = flip_rows(part) if turned else part
    for q in range(sz.tiles):
        for side in range(4):
            piece = corner_at[q * 4 + side]
            for row in range(REACH):
                for column in range(REACH):
                    at = corner_cell(sz.edge, side, row, column)
                    for h in range(sz.lanes):
                        pool[piece, row, h, pl.ds(column, 1), :] += grad_pad[
                            q * sz.lanes + h, pl.ds(at, 1), :
                        ]


def send_margins(sz, pool, own, below, above):
    own[...] = pool[0 : sz.pieces]
    for piece in range(sz.pieces):
        for row in range(REACH):
            for offset, ref in ((1, below), (2, above)):
                parts = [pool[offset * sz.pieces + piece, row, h] for h in range(sz.lanes)]
                ref[piece, row] = jnp.concatenate(parts, axis=1).astype(BF16)


def gather_inner(sz, grad_row, grad_pad, base):
    for q in range(sz.tiles):
        for i in range(sz.edge):
            for h, part in enumerate(halves(grad_row(q, i))):
                slab = q * sz.lanes + h
                base[slab, pl.ds(i * sz.edge, sz.edge), :] = (
                    part + grad_pad[slab, pl.ds((i + REACH) * PITCH + REACH, sz.edge), :]
                )


def add_strips(sz, base, own, first, second, flat):
    flat[...] = base[...]
    for q in range(sz.tiles):
        for side in range(4):
            piece = q * 4 + side
            for row in range(REACH):
                window, turned = strip_window(sz.edge, side, row)
                came = first[piece, row].astype(F32) + second[piece, row].astype(F32)
                for h, part in enumerate(halves(came)):
                    part = part + own[piece, row, h]
                    flat[q * sz.lanes + h, window, :] += flip_rows(part) if turned else part


def fill_small(small, gain_sums, scale_sums):
    small[TAPS * 8 : TAPS * 8 + 1, :] = jnp.sum(gain_sums[...], axis=0, keepdims=True)
    small[TAPS * 8 + 1 : TAPS * 8 + 2, :] = jnp.sum(scale_sums[...], axis=0, keepdims=True)


def flat_grad_row(sz, flat):
    def row(q, i):
        at = pl.ds(i * sz.edge, sz.edge)
        parts = [flat[q * sz.lanes + h, at, :] for h in range(sz.lanes)]
        return jnp.concatenate(parts, axis=1)

    return row


def fetch_kernel(*refs):
    count = (len(refs) - 1) // 2
    copies = [
        pltpu.make_async_copy(refs[k], refs[count + k], refs[-1].at[k]) for k in range(count)
    ]
    for copy in copies:
        copy.start()
    for copy in copies:
        copy.wait()


def strips_kernel(sz, cur, strips, flat):
    for q in range(sz.tiles):
        for i in range(sz.edge):
            for h, part in enumerate(halves(cur[q, i].astype(F32))):
                flat[q * sz.lanes + h, pl.ds(i * sz.edge, sz.edge), :] = part
    write_strips(sz, flat, strips)


def forward_kernel(
    sz, layer, seams, corners, cur, own, below, above, kern, gain, lscale, up, down,
    out, strips, pad, normal, inverse, normed, slope, active, branch,
    pool, taps, conv, upward, flat,
):
    strip_at, corner_at = read_plan(sz, seams), read_plan(sz, corners)
    surround(sz, strip_at, corner_at, cur, own, below, above, pool, pad)
    hold_taps(sz, kern, layer, taps)
    convolve(sz, pad, taps, conv)
    normalise(sz, conv, gain, layer, normal, inverse, normed)
    upward[...] = multiply(normed[...], up[layer])
    activate(sz, upward, active, slope)
    branch[...] = multiply(active[...], down[layer])
    finish_forward(sz, cur, branch, lscale, layer, out, flat)
    write_strips(sz, flat, strips)


def turn_kernel(
    sz, layer, seams, corners, cur, own, below, above, kern, gain, lscale, up, down, out_grad,
    out_hbm, base, grad_own, grad_below, grad_above,
    pad, grad_conv, normed, active, down_in, up_in, gain_sums, scale_sums,
    pool, taps, conv, upward, out, normal, inverse, slope, branch, grad_pool, grad_pad, out_sem,
):
    strip_at, corner_at = read_plan(sz, seams), read_plan(sz, corners)
    surround(sz, strip_at, corner_at, cur, own, below, above, pool, pad)
    hold_taps(sz, kern, layer, taps)
    convolve(sz, pad, taps, conv)
    normalise(sz, conv, gain, layer, normal, inverse, normed)
    upward[...] = multiply(normed[...], up[layer])
    activate(sz, upward, active, slope)
    branch[...] = multiply(active[...], down[layer])
    finish_forward(sz, cur, branch, lscale, layer, out, None)
    store = pltpu.make_async_copy(out, out_hbm, out_sem.at[0])
    store.start()

    def grad_row(q, i):
        return out_grad[q, i].astype(F32)

    scale_rows(sz, grad_row, branch, lscale, layer, down_in, scale_sums)
    upward[...] = multiply(down_in[...], down[layer], 1, 1)
    slope_rows(sz, upward, slope, up_in)
    branch[...] = multiply(up_in[...], up[layer], 1, 1)
    norm_gradients(sz, branch, normal, inverse, gain, layer, grad_conv, gain_sums)
    spread_gradients(sz, grad_conv, taps, grad_pad)
    return_margins(sz, strip_at, corner_at, grad_pad, grad_pool)
    send_margins(sz, grad_pool, grad_own, grad_below, grad_above)
    gather_inner(sz, grad_row, grad_pad, base)
    store.wait()


def weights_kernel(
    sz, pad, grad_conv, normed, active, down_in, up_in, gain_sums, scale_sums,
    keep, send, small, tap_sums, both,
):
    small[...] = jnp.zeros_like(small)
    weight_gradients(sz, digit_of(0), active, down_in, normed, up_in, both, keep, send)
    tap_gradients(sz, pad, grad_conv, tap_sums, small)
    fill_small(small, gain_sums, scale_sums)


def backward_kernel(
    sz, layer, base, own, first, second, lscale, down, normed, slope, active, branch,
    keep, send, flat, up_in, scale_sums,
    hidden, down_in, both,
):
    add_strips(sz, base, own, first, second, flat)
    for slab in range(sz.slabs):
        flat[slab] = flat[slab].astype(BF16).astype(F32)
    scale_rows(sz, flat_grad_row(sz, flat), branch, lscale, layer, down_in, scale_sums)
    hidden[...] = multiply(down_in[...], down[layer], 1, 1)
    slope_rows(sz, hidden, slope, up_in)
    weight_gradients(sz, digit_of(0), active, down_in, normed, up_in, both, keep, send)


def spread_kernel(
    sz, layer, seams, corners, kern, gain, up, flat, up_in, normal, inverse,
    base, grad_own, grad_below, grad_above, grad_conv, gain_sums,
    taps, branch, grad_pool, grad_pad,
):
    strip_at, corner_at = read_plan(sz, seams), read_plan(sz, corners)
    branch[...] = multiply(up_in[...], up[layer], 1, 1)
    norm_gradients(sz, branch, normal, inverse, gain, layer, grad_conv, gain_sums)
    hold_taps(sz, kern, layer, taps)
    spread_gradients(sz, grad_conv, taps, grad_pad)
    return_margins(sz, strip_at, corner_at, grad_pad, grad_pool)
    send_margins(sz, grad_pool, grad_own, grad_below, grad_above)
    gather_inner(sz, flat_grad_row(sz, flat), grad_pad, base)


def taps_kernel(sz, pad, grad_conv, gain_sums, scale_sums, other, both, tap_sums, small):
    small[...] = jnp.zeros_like(small)
    tap_gradients(sz, pad, grad_conv, tap_sums, small)
    fill_small(small, gain_sums, scale_sums)
    both[0:SMALL_ROWS] = small[...].astype(BF16)
    both[SMALL_ROWS : 2 * SMALL_ROWS] = other[...].astype(BF16)


def last_kernel(sz, base, own, first, second, out_hbm, flat, out, sems):
    add_strips(sz, base, own, first, second, flat)
    row = flat_grad_row(sz, flat)
    for q in range(sz.tiles):
        for i in range(sz.edge):
            out[q, i] = row(q, i).astype(BF16)
    store = pltpu.make_async_copy(out, out_hbm, sems.at[0])
    store.start()
    store.wait()


def add_rows(out, parts):
    for start in range(0, out.shape[0], 16):
        rows = slice(start, start + 16)
        values = [part(rows).astype(F32) for part in parts]
        out[rows] = sum(values[1:], values[0]).astype(BF16)


def share_near_kernel(*refs):
    arrays, outs = refs[:2], refs[2:]
    for k, out in enumerate(outs):
        piece = digit_of(1) ^ k
        add_rows(out, [lambda rows, array=array: array[piece, rows] for array in arrays])


def share_far_kernel(*refs):
    rest, share = refs[0].shape[:2]
    arrays, outs = refs[:-rest], refs[-rest:]
    for k, out in enumerate(outs):
        piece = digit_of(2) ^ k
        for layer in range(2):
            parts = arrays[4 * layer : 4 * layer + 4]
            add_rows(
                out.at[layer],
                [lambda rows, array=array: array[piece, rows] for array in parts],
            )


def total_kernel(*refs):
    out = refs[-1]
    if len(out.shape) == 2:
        add_rows(out, [lambda rows, array=array: array[rows] for array in refs[:-1]])
        return
    for layer in range(out.shape[0]):
        add_rows(
            out.at[layer],
            [lambda rows, array=array: array[layer, rows] for array in refs[:-1]],
        )


def order_kernel(level, *refs):
    for k, piece in enumerate(refs[:-1]):
        refs[-1][digit_of(level) ^ k] = piece[...]


def unpack_kernel(
    sz, mine, theirs, small, up_hbm, down_hbm, kernel_out, gain_out, scale_out, up, down, sems,
):
    even = digit_of(0) == 0
    pieces, _, share, _ = mine.shape
    copies = []
    for layer in range(2):
        for j in range(pieces):
            start = j * share
            down[layer, start : start + share] = jnp.where(
                even, mine[j, layer], theirs[j, layer]
            ).astype(F32)
        copies.append((down.at[layer], down_hbm.at[layer]))
        for j in range(pieces):
            k, c = divmod(j * share, sz.channels)
            up[layer, c : c + share, k * sz.channels : (k + 1) * sz.channels] = jnp.where(
                even, theirs[j, layer], mine[j, layer]
            ).astype(F32)
        copies.append((up.at[layer], up_hbm.at[layer]))
        for k in range(len(copies) - 2, len(copies)):
            copies[k] = pltpu.make_async_copy(*copies[k], sems.at[k])
            copies[k].start()
    for layer in range(2):
        at = layer * SMALL_ROWS
        for a in range(TAPS):
            part = small[at + a * 8 - a % 2 * 8 : at + a * 8 - a % 2 * 8 + 16].astype(F32)
            part = part[a % 2 * 8 : a % 2 * 8 + 8]
            for b in range(TAPS):
                kernel_out[a, b, layer : layer + 1] = part[b : b + 1]
        last = small[at + SMALL_ROWS - 16 : at + SMALL_ROWS].astype(F32)
        gain_out[layer : layer + 1] = last[8:9]
        scale_out[layer : layer + 1] = last[9:10]
    for copy in copies:
        copy.wait()


IN_VMEM = pl.BlockSpec(memory_space=pltpu.VMEM)
IN_SMEM = pl.BlockSpec(memory_space=pltpu.SMEM)
IN_HBM = pl.BlockSpec(memory_space=pltpu.HBM)


def call(body, name, micros, ins, outs, scratch, after=()):
    count = len(ins)

    def run(*refs):
        body(*refs[:count], *refs[count + len(after) :])

    return pl.pallas_call(
        run,
        in_specs=[spec for spec, _ in ins] + [pl.BlockSpec(memory_space=pl.ANY)] * len(after),
        out_specs=[spec for spec, _ in outs],
        out_shape=[out for _, out in outs],
        scratch_shapes=scratch,
        compiler_params=pltpu.CompilerParams(vmem_limit_bytes=24 * 1024 * 1024),
        cost_estimate=pl.CostEstimate(
            flops=0, bytes_accessed=int(micros * 3.5e6), transcendentals=0
        ),
        name=name,
    )(*[array for _, array in ins], *after)


def near(*arrays):
    return [(IN_VMEM, array) for array in arrays]


def far(*arrays):
    return [(IN_HBM, array) for array in arrays]


def pass_on(shard, by):
    length = lax.axis_size("tile")
    return lax.ppermute(shard, "tile", [(i, (i + by) % length) for i in range(length)])


def partners(array, masks):
    length = lax.axis_size("tile")
    return [
        lax.ppermute(array, "tile", [(i, i ^ mask) for i in range(length)]) for mask in masks
    ]


def swap(arrays, masks):
    length = lax.axis_size("tile")
    return [
        lax.ppermute(array, "tile", [(i, i ^ mask) for i in range(length)])
        for array, mask in zip(arrays, masks)
    ]


class Reduction:
    def __init__(self, devices):
        self.devices = devices
        self.rest = devices // 8
        self.near_masks = [2 * k for k in range(1, 4)]
        self.rest_masks = [8 * k for k in range(1, self.rest)]

    def start(self, keep, send):
        rows, channels = keep.shape
        (came,) = swap([send], [1])
        quarter = rows // 4
        parts = (4, quarter, channels)
        shape = jax.ShapeDtypeStruct((quarter, channels), BF16)
        pieces = call(
            share_near_kernel, "share_near", 0.7,
            near(keep.reshape(parts), came.reshape(parts)), near(*[shape] * 4), [],
        )
        return [pieces[0]] + swap(pieces[1:], self.near_masks)

    def finish(self, parts, after):
        quarter, channels = parts[0][0].shape
        dims = (self.rest, quarter // self.rest, channels)
        arrays = [part.reshape(dims) for layer in parts for part in layer]
        shape = jax.ShapeDtypeStruct((2,) + dims[1:], BF16)
        pieces = call(
            share_far_kernel, "share_far", 0.9,
            near(*arrays), near(*[shape] * self.rest), [], after,
        )
        arrived = swap(pieces[1:], self.rest_masks)
        (total,) = call(
            total_kernel, "total", 0.4, near(pieces[0], *arrived), near(shape), []
        )
        return pieces[0], total

    def gather(self, total, after):
        for level, masks, name in (
            (2, self.rest_masks, "order_far"),
            (1, self.near_masks, "order_near"),
        ):
            pieces = [total] + partners(total, masks)
            shape = jax.ShapeDtypeStruct((len(pieces),) + total.shape, BF16)
            (total,) = call(
                functools.partial(order_kernel, level), name, 0.5,
                near(*pieces), near(shape), [], after,
            )
            after = ()
        total = total.reshape((4 * self.rest,) + total.shape[2:])
        return total, partners(total, [1])[0]

    def whole(self, array):
        mask = 1
        while mask < self.devices:
            shape = jax.ShapeDtypeStruct(array.shape, BF16)
            (array,) = call(
                total_kernel, "total_small", 0.3,
                near(array, *partners(array, [mask])), near(shape), [],
            )
            mask *= 2
        return array


def on_device(
    inputs,
    out_grad,
    kernel,
    norm_gain,
    up_weight,
    down_weight,
    layer_scale,
    seam_table,
    corner_table,
):
    tiles, edge, _, channels = inputs.shape
    layers, _, hidden = up_weight.shape
    sz = Sizes(tiles, edge, channels, hidden)
    columns = lax.axis_size("tile")
    plan = [(IN_SMEM, table.transpose((1, 2, 0))) for table in (seam_table, corner_table)]
    kern = kernel.transpose((1, 2, 0, 3))
    gain, lscale, up, down = norm_gain, layer_scale, up_weight, down_weight
    reduction = Reduction(columns)

    shape = jax.ShapeDtypeStruct
    image = shape(inputs.shape, BF16)
    strips_shape = shape((sz.pieces, REACH, edge, channels), BF16)
    slabs = shape((sz.slabs, sz.cells, LANES), F32)
    padded = shape((sz.slabs, sz.outer * PITCH, LANES), F32)
    inverses = shape((tiles, sz.cells, LANES), F32)
    narrow_short = shape((sz.rows, channels), BF16)
    wide_short = shape((sz.rows, hidden), BF16)
    narrow = shape((sz.rows, channels), F32)
    wide = shape((sz.rows, hidden), F32)
    sums = shape((edge, channels), F32)
    grad_slabs = shape((sz.slabs, edge * GRAD_PITCH, LANES), F32)
    own_shape = shape((sz.pieces, REACH, sz.lanes, edge, LANES), F32)
    pool = shape((3 * sz.pieces, REACH, edge, channels), BF16)
    grad_pool = shape((3 * sz.pieces, REACH, sz.lanes, edge, LANES), F32)
    taps = shape((sz.lanes, TAPS * 8, LANES), F32)
    tap_sums = shape((sz.lanes, TAPS * TAPS, 8, LANES), F32)
    small = shape((SMALL_ROWS, channels), F32)
    half = shape((hidden, channels), BF16)
    two_halves = shape((2, hidden, channels), BF16)

    def vmem(*shapes):
        return [pltpu.VMEM(one.shape, one.dtype) for one in shapes]

    def sems(count):
        return [pltpu.SemaphoreType.DMA((count,))]

    (strips,) = call(
        functools.partial(strips_kernel, sz),
        "strips", 0.3,
        near(inputs),
        near(strips_shape),
        vmem(slabs),
    )
    below, above = pass_on(strips, 1), pass_on(strips, -1)
    fetched = (inputs, out_grad, kern, gain, lscale, up, down)
    inputs, out_grad, kern, gain, lscale, up, down = call(
        fetch_kernel,
        "fetch", 2.0,
        far(*fetched),
        near(*[shape(one.shape, one.dtype) for one in fetched]),
        sems(len(fetched)),
        (strips,),
    )
    middle, strips, pad_zero, normal, inverse, normed, slope, active, branch = call(
        functools.partial(forward_kernel, sz, 0),
        "forward", 8.7,
        plan + near(inputs, strips, below, above, kern, gain, lscale, up, down),
        near(
            image, strips_shape, padded, slabs, inverses,
            narrow_short, wide_short, wide_short, narrow,
        ),
        vmem(pool, taps, slabs, wide, slabs),
    )
    below, above = pass_on(strips, 1), pass_on(strips, -1)
    result, base, grad_own, grad_below, grad_above, *for_weights = call(
        functools.partial(turn_kernel, sz, 1),
        "turn", 15.4,
        plan + near(middle, strips, below, above, kern, gain, lscale, up, down, out_grad),
        far(image)
        + near(
            slabs, own_shape, strips_shape, strips_shape,
            padded, grad_slabs, narrow_short, wide_short, narrow_short, wide_short, sums, sums,
        ),
        vmem(
            pool, taps, slabs, wide, image, slabs, inverses, wide_short, narrow, grad_pool, padded
        )
        + sems(1),
    )
    from_below, from_above = pass_on(grad_above, 1), pass_on(grad_below, -1)
    keep_one, send_one, small_one = call(
        functools.partial(weights_kernel, sz),
        "weights", 2.8,
        near(*for_weights),
        near(half, half, small),
        vmem(tap_sums, two_halves),
    )
    parts_one = reduction.start(keep_one, send_one)
    keep_zero, send_zero, flat, up_in, scale_sums = call(
        functools.partial(backward_kernel, sz, 0),
        "backward", 2.9,
        near(
            base, grad_own, from_below, from_above, lscale, down, normed, slope, active, branch
        ),
        near(half, half, slabs, wide_short, sums),
        vmem(wide, narrow_short, two_halves),
    )
    parts_zero = reduction.start(keep_zero, send_zero)
    base, grad_own, grad_below, grad_above, grad_conv, gain_sums = call(
        functools.partial(spread_kernel, sz, 0),
        "spread", 6.0,
        plan + near(kern, gain, up, flat, up_in, normal, inverse),
        near(slabs, own_shape, strips_shape, strips_shape, grad_slabs, sums),
        vmem(taps, narrow, grad_pool, padded),
        (parts_zero[0],),
    )
    share, total = reduction.finish((parts_zero, parts_one), (gain_sums,))
    from_below, from_above = pass_on(grad_above, 1), pass_on(grad_below, -1)
    (small_both,) = call(
        functools.partial(taps_kernel, sz),
        "taps", 2.1,
        near(pad_zero, grad_conv, gain_sums, scale_sums, small_one),
        near(shape((2 * SMALL_ROWS, channels), BF16)),
        vmem(tap_sums, small),
        (share,),
    )
    (in_grad,) = call(
        functools.partial(last_kernel, sz),
        "last", 1.0,
        near(base, grad_own, from_below, from_above),
        far(image),
        vmem(slabs, image) + sems(1),
    )
    grad_up, grad_down, grad_kernel, grad_gain, grad_scale = call(
        functools.partial(unpack_kernel, sz),
        "unpack", 2.7,
        near(*reduction.gather(total, (in_grad,)), reduction.whole(small_both)),
        far(shape(up_weight.shape, F32), shape(down_weight.shape, F32))
        + near(
            shape(kern.shape, F32), shape(norm_gain.shape, F32),
            shape(norm_gain.shape, F32),
        ),
        vmem(shape(up_weight.shape, F32), shape(down_weight.shape, F32)) + sems(4),
    )
    return (
        result, in_grad, grad_kernel.transpose((2, 0, 1, 3)),
        grad_gain, grad_up, grad_down, grad_scale,
    )


def solution(mesh):
    placed = (
        P(("groups", "tile"), None, None, None),
        P(("groups", "tile"), None, None, None),
        P(),
        P(),
        P(),
        P(),
        P(),
        P(),
        P(),
    )
    return jax.shard_map(
        on_device,
        mesh=mesh,
        in_specs=placed,
        out_specs=(
            P(("groups", "tile"), None, None, None),
            P(("groups", "tile"), None, None, None),
            P("groups", None, None, None),
            P("groups", None),
            P("groups", None, None),
            P("groups", None, None),
            P("groups", None),
        ),
        check_vma=False,
    )
```

```python
import functools

import jax
import jax.numpy as jnp
from jax import lax
from jax.experimental import pallas as pl
from jax.experimental.pallas import tpu as pltpu
from jax.sharding import PartitionSpec as P

epsilon = 1e-06
inverse_root_two = 0.7071067811865476
inverse_root_tau = 0.3989422804014327

LANES = 128
TAPS = 7
REACH = 3
PITCH = 24
GRAD_PITCH = 32
SMALL_ROWS = 64
F32 = jnp.float32
BF16 = jnp.bfloat16


def flip_rows(value):
    rows = value.shape[0]
    order = 7 - lax.broadcasted_iota(jnp.int32, (8, LANES), 0)
    parts = [
        jnp.take_along_axis(value[at : at + 8], order, axis=0, mode="promise_in_bounds")
        for at in range(0, rows, 8)
    ]
    return jnp.concatenate(parts[::-1], axis=0)


def halves(value):
    return [value[:, at : at + LANES] for at in range(0, value.shape[1], LANES)]


class Sizes:
    def __init__(self, tiles, edge, channels, hidden):
        self.tiles = tiles
        self.edge = edge
        self.channels = channels
        self.hidden = hidden
        self.lanes = channels // LANES
        self.cells = edge * edge
        self.rows = tiles * edge * edge
        self.pieces = tiles * 4
        self.outer = edge + 2 * REACH
        self.slabs = tiles * self.lanes

    def key(self):
        return (self.tiles, self.edge, self.channels, self.hidden)


def strip_window(edge, side, row):
    if side == 0:
        return pl.ds(row * edge, edge), False
    if side == 1:
        return pl.ds(edge - 1 - row, edge, stride=edge), False
    if side == 2:
        return pl.ds((edge - 1 - row) * edge, edge), True
    return pl.ds(row, edge, stride=edge), True


def margin_window(edge, side, row):
    last = edge + 2 * REACH - 1
    if side == 0:
        return pl.ds((2 - row) * PITCH + REACH, edge), True
    if side == 1:
        return pl.ds(REACH * PITCH + last - 2 + row, edge, stride=PITCH), True
    if side == 2:
        return pl.ds((last - 2 + row) * PITCH + REACH, edge), False
    return pl.ds(REACH * PITCH + 2 - row, edge, stride=PITCH), False


def corner_cell(edge, corner, row, column):
    last = edge + 2 * REACH - 1
    r, x = 2 - row, 2 - column
    if corner == 0:
        at = (r, x)
    elif corner == 1:
        at = (x, last - r)
    elif corner == 2:
        at = (last - r, last - x)
    else:
        at = (last - x, r)
    return at[0] * PITCH + at[1]


def read_plan(sz, table):
    columns = lax.axis_size("tile")
    device = lax.axis_index("tile")
    below = lax.rem(device + columns - 1, columns)
    plan = []
    for q in range(sz.tiles):
        for side in range(4):
            source = table[side, 0, device * sz.tiles + q]
            owner = lax.div(source, sz.tiles)
            local = (source - owner * sz.tiles) * 4 + table[side, 1, device * sz.tiles + q]
            shift = jnp.where(
                owner == device, 0, jnp.where(owner == below, sz.pieces, 2 * sz.pieces)
            )
            plan.append(shift + local)
    return plan


def digit_of(level):
    device = lax.axis_index("tile")
    if level == 0:
        return lax.rem(device, 2)
    if level == 1:
        return lax.rem(lax.div(device, 2), 4)
    return lax.div(device, 8)


def write_strips(sz, flat, strips_ref):
    for q in range(sz.tiles):
        for side in range(4):
            for row in range(REACH):
                window, turned = strip_window(sz.edge, side, row)
                parts = [flat[q * sz.lanes + h, window, :] for h in range(sz.lanes)]
                if turned:
                    parts = [flip_rows(part) for part in parts]
                strips_ref[q * 4 + side, row] = jnp.concatenate(parts, axis=1).astype(BF16)


def surround(sz, strip_at, corner_at, cur, own, below, above, pool, pad):
    pool[0 : sz.pieces] = own[...]
    pool[sz.pieces : 2 * sz.pieces] = below[...]
    pool[2 * sz.pieces : 3 * sz.pieces] = above[...]
    for q in range(sz.tiles):
        for i in range(sz.edge):
            for h, part in enumerate(halves(cur[q, i].astype(F32))):
                pad[q * sz.lanes + h, pl.ds((i + REACH) * PITCH + REACH, sz.edge), :] = part
    for q in range(sz.tiles):
        for side in range(4):
            piece = strip_at[q * 4 + side]
            for row in range(REACH):
                window, turned = margin_window(sz.edge, side, row)
                for h, part in enumerate(halves(pool[piece, row].astype(F32))):
                    pad[q * sz.lanes + h, window, :] = flip_rows(part) if turned else part
            piece = corner_at[q * 4 + side]
            for row in range(REACH):
                for h, part in enumerate(halves(pool[piece, row].astype(F32))):
                    for column in range(REACH):
                        at = corner_cell(sz.edge, side, row, column)
                        pad[q * sz.lanes + h, pl.ds(at, 1), :] = part[column : column + 1]


def hold_taps(sz, kern, layer, taps):
    for a in range(TAPS):
        for b in range(TAPS):
            for h, part in enumerate(halves(kern[a, b, layer : layer + 1])):
                taps[h, pl.ds(a * 8 + b, 1), :] = part


def tap(taps, h, a, b):
    return jnp.broadcast_to(taps[h, pl.ds(a * 8 + b, 1), :], (8, LANES))


def convolve(sz, pad, taps, conv):
    @pl.loop(0, sz.slabs)
    def _(slab):
        h = lax.rem(slab, sz.lanes)
        for g in range(sz.edge // 8):
            acc = [None] * sz.edge
            for b in range(TAPS):
                weights = [tap(taps, h, a, b) for a in range(TAPS)]
                for r in range(sz.outer):
                    x = pad[slab, pl.ds(r * PITCH + b + 8 * g, 8), :]
                    for a in range(TAPS):
                        i = r - a
                        if 0 <= i < sz.edge:
                            term = x * weights[a]
                            acc[i] = term if acc[i] is None else acc[i] + term
            for i in range(sz.edge):
                conv[slab, pl.ds(i * sz.edge + 8 * g, 8), :] = acc[i]


def normalise(sz, conv, gain, layer, normal, inverse, normed):
    scale = 1.0 / sz.channels
    for q in range(sz.tiles):

        @pl.loop(0, sz.edge, unroll=2)
        def _(i):
            at = pl.ds(pl.multiple_of(i * sz.edge, sz.edge), sz.edge)
            parts = [conv[q * sz.lanes + h, at, :] for h in range(sz.lanes)]
            mean = jnp.sum(sum(parts[1:], parts[0]), axis=-1, keepdims=True) * scale
            parts = [part - mean for part in parts]
            squares = [part * part for part in parts]
            variance = jnp.sum(sum(squares[1:], squares[0]), axis=-1, keepdims=True) * scale
            root = lax.rsqrt(variance + epsilon)
            inverse[q, at, :] = jnp.broadcast_to(root, (sz.edge, LANES))
            flat_at = pl.ds(pl.multiple_of(q * sz.cells + i * sz.edge, sz.edge), sz.edge)
            for h, part in enumerate(parts):
                part = part * root
                normal[q * sz.lanes + h, at, :] = part
                gains = gain[layer : layer + 1, h * LANES : (h + 1) * LANES]
                normed[flat_at, h * LANES : (h + 1) * LANES] = (part * gains).astype(BF16)


def activate(sz, upward, active, slope):
    width = 512

    @pl.loop(0, sz.rows // 16)
    def _(t):
        at = pl.ds(pl.multiple_of(t * 16, 16), 16)
        for start in range(0, sz.hidden, width):
            u = upward[at, start : start + width]
            chance = 0.5 * (1.0 + lax.erf(u * inverse_root_two))
            active[at, start : start + width] = (u * chance).astype(BF16)
            slope[at, start : start + width] = (
                chance + u * jnp.exp(-0.5 * u * u) * inverse_root_tau
            ).astype(slope.dtype)


def multiply(a, b, ca=1, cb=0):
    return lax.dot_general(a, b, (((ca,), (cb,)), ((), ())), preferred_element_type=F32)


def finish_forward(sz, cur, branch, lscale, layer, out, flat):
    for q in range(sz.tiles):

        @pl.loop(0, sz.edge, unroll=2)
        def _(i):
            at = pl.ds(pl.multiple_of(q * sz.cells + i * sz.edge, sz.edge), sz.edge)
            value = cur[q, i].astype(F32) + branch[at, :] * lscale[layer : layer + 1, :]
            value = value.astype(BF16)
            out[q, i] = value
            if flat is not None:
                local = pl.ds(pl.multiple_of(i * sz.edge, sz.edge), sz.edge)
                for h, part in enumerate(halves(value.astype(F32))):
                    flat[q * sz.lanes + h, local, :] = part


def scale_rows(sz, grad_row, branch, lscale, layer, down_in, sums):
    sums[...] = jnp.zeros_like(sums)
    for q in range(sz.tiles):

        @pl.loop(0, sz.edge, unroll=2)
        def _(i):
            at = pl.ds(pl.multiple_of(q * sz.cells + i * sz.edge, sz.edge), sz.edge)
            g = grad_row(q, i)
            down_in[at, :] = (g * lscale[layer : layer + 1, :]).astype(BF16)
            sums[...] += g * branch[at, :]


def slope_rows(sz, grad_active, slope, up_in):
    @pl.loop(0, sz.rows // 16, unroll=2)
    def _(t):
        at = pl.ds(pl.multiple_of(t * 16, 16), 16)
        up_in[at, :] = (grad_active[at, :] * slope[at, :].astype(F32)).astype(BF16)


def weight_gradients(sz, core, active, down_in, normed, up_in, both, keep, send):
    both[0] = multiply(active[...], down_in[...], 0, 0).astype(BF16)
    for k in range(sz.hidden // sz.channels):
        part = multiply(normed[...], up_in[:, k * sz.channels : (k + 1) * sz.channels], 0, 0)
        both[1, k * sz.channels : (k + 1) * sz.channels, :] = part.astype(BF16)
    keep[...] = both[core]
    send[...] = both[1 - core]


def norm_gradients(sz, grad_normed, normal, inverse, gain, layer, grad_conv, sums):
    scale = 1.0 / sz.channels
    sums[...] = jnp.zeros_like(sums)
    blank = jnp.zeros((8, LANES), F32)
    for q in range(sz.tiles):

        @pl.loop(0, sz.edge, unroll=2)
        def _(i):
            at = pl.ds(pl.multiple_of(q * sz.cells + i * sz.edge, sz.edge), sz.edge)
            local = pl.ds(pl.multiple_of(i * sz.edge, sz.edge), sz.edge)
            g = halves(grad_normed[at, :])
            n = [normal[q * sz.lanes + h, local, :] for h in range(sz.lanes)]
            sums[...] += jnp.concatenate([a * b for a, b in zip(g, n)], axis=1)
            s = [
                part * gain[layer : layer + 1, h * LANES : (h + 1) * LANES]
                for h, part in enumerate(g)
            ]
            products = [a * b for a, b in zip(s, n)]
            mean = jnp.sum(sum(s[1:], s[0]), axis=-1, keepdims=True) * scale
            slant = jnp.sum(sum(products[1:], products[0]), axis=-1, keepdims=True) * scale
            root = inverse[q, local, :]
            for h in range(sz.lanes):
                slab = q * sz.lanes + h
                base = pl.multiple_of(i * GRAD_PITCH, GRAD_PITCH)
                grad_conv[slab, pl.ds(base, 8), :] = blank
                grad_conv[slab, pl.ds(base + 8, sz.edge), :] = root * (s[h] - mean - n[h] * slant)
                grad_conv[slab, pl.ds(base + 8 + sz.edge, 8), :] = blank


def tap_gradients(sz, pad, grad_conv, tap_sums, small):
    tap_sums[...] = jnp.zeros_like(tap_sums)

    @pl.loop(0, sz.slabs)
    def _(slab):
        h = lax.rem(slab, sz.lanes)
        for b in range(TAPS):
            acc = [None] * TAPS
            for g in range(sz.edge // 8):
                grads = [
                    grad_conv[slab, pl.ds(i * GRAD_PITCH + 8 + 8 * g, 8), :]
                    for i in range(sz.edge)
                ]
                for r in range(sz.outer):
                    x = pad[slab, pl.ds(r * PITCH + b + 8 * g, 8), :]
                    for a in range(TAPS):
                        i = r - a
                        if 0 <= i < sz.edge:
                            term = x * grads[i]
                            acc[a] = term if acc[a] is None else acc[a] + term
            for a in range(TAPS):
                tap_sums[h, a * TAPS + b] += acc[a]

    for h in range(sz.lanes):
        for k in range(TAPS * TAPS):
            row = k // TAPS * 8 + k % TAPS
            small[row : row + 1, h * LANES : (h + 1) * LANES] = jnp.sum(
                tap_sums[h, k], axis=0, keepdims=True
            )


def spread_gradients(sz, grad_conv, taps, grad_pad):
    @pl.loop(0, sz.slabs)
    def _(slab):
        h = lax.rem(slab, sz.lanes)
        for g in range(PITCH // 8):
            acc = [None] * sz.outer
            for b in range(TAPS):
                start = 8 * g - b + 8
                if start >= 8 + sz.edge:
                    continue
                weights = [tap(taps, h, a, b) for a in range(TAPS)]
                for i in range(sz.edge):
                    x = grad_conv[slab, pl.ds(i * GRAD_PITCH + start, 8), :]
                    for a in range(TAPS):
                        term = x * weights[a]
                        acc[i + a] = term if acc[i + a] is None else acc[i + a] + term
            for p in range(sz.outer):
                grad_pad[slab, pl.ds(p * PITCH + 8 * g, 8), :] = acc[p]


def return_margins(sz, strip_at, corner_at, grad_pad, pool):
    pool[...] = jnp.zeros_like(pool)
    for q in range(sz.tiles):
        for side in range(4):
            piece = strip_at[q * 4 + side]
            for row in range(REACH):
                window, turned = margin_window(sz.edge, side, row)
                for h in range(sz.lanes):
                    part = grad_pad[q * sz.lanes + h, window, :]
                    pool[piece, row, h] = flip_rows(part) if turned else part
    for q in range(sz.tiles):
        for side in range(4):
            piece = corner_at[q * 4 + side]
            for row in range(REACH):
                for column in range(REACH):
                    at = corner_cell(sz.edge, side, row, column)
                    for h in range(sz.lanes):
                        pool[piece, row, h, pl.ds(column, 1), :] += grad_pad[
                            q * sz.lanes + h, pl.ds(at, 1), :
                        ]


def send_margins(sz, pool, own, below, above):
    own[...] = pool[0 : sz.pieces]
    for piece in range(sz.pieces):
        for row in range(REACH):
            for offset, ref in ((1, below), (2, above)):
                parts = [pool[offset * sz.pieces + piece, row, h] for h in range(sz.lanes)]
                ref[piece, row] = jnp.concatenate(parts, axis=1).astype(BF16)


def gather_inner(sz, grad_row, grad_pad, base):
    for q in range(sz.tiles):
        for i in range(sz.edge):
            for h, part in enumerate(halves(grad_row(q, i))):
                slab = q * sz.lanes + h
                base[slab, pl.ds(i * sz.edge, sz.edge), :] = (
                    part + grad_pad[slab, pl.ds((i + REACH) * PITCH + REACH, sz.edge), :]
                )


def add_strips(sz, base, own, first, second, flat):
    flat[...] = base[...]
    for q in range(sz.tiles):
        for side in range(4):
            piece = q * 4 + side
            for row in range(REACH):
                window, turned = strip_window(sz.edge, side, row)
                came = first[piece, row].astype(F32) + second[piece, row].astype(F32)
                for h, part in enumerate(halves(came)):
                    part = part + own[piece, row, h]
                    flat[q * sz.lanes + h, window, :] += flip_rows(part) if turned else part


def fill_small(small, gain_sums, scale_sums):
    small[TAPS * 8 : TAPS * 8 + 1, :] = jnp.sum(gain_sums[...], axis=0, keepdims=True)
    small[TAPS * 8 + 1 : TAPS * 8 + 2, :] = jnp.sum(scale_sums[...], axis=0, keepdims=True)


def flat_grad_row(sz, flat):
    def row(q, i):
        at = pl.ds(i * sz.edge, sz.edge)
        parts = [flat[q * sz.lanes + h, at, :] for h in range(sz.lanes)]
        return jnp.concatenate(parts, axis=1)

    return row


def fetch_kernel(*refs):
    count = (len(refs) - 1) // 2
    copies = [
        pltpu.make_async_copy(refs[k], refs[count + k], refs[-1].at[k]) for k in range(count)
    ]
    for copy in copies:
        copy.start()
    for copy in copies:
        copy.wait()


def strips_kernel(sz, cur, strips, held, flat):
    held[...] = cur[...]
    for q in range(sz.tiles):
        for i in range(sz.edge):
            for h, part in enumerate(halves(cur[q, i].astype(F32))):
                flat[q * sz.lanes + h, pl.ds(i * sz.edge, sz.edge), :] = part
    write_strips(sz, flat, strips)


def forward_kernel(
    sz, layer, seams, corners, cur, own, below, above, kern, gain, lscale, up, down,
    out, strips, pad, normal, inverse, normed, slope, active, branch,
    pool, taps, conv, upward, flat,
):
    strip_at, corner_at = read_plan(sz, seams), read_plan(sz, corners)
    surround(sz, strip_at, corner_at, cur, own, below, above, pool, pad)
    hold_taps(sz, kern, layer, taps)
    convolve(sz, pad, taps, conv)
    normalise(sz, conv, gain, layer, normal, inverse, normed)
    upward[...] = multiply(normed[...], up[layer])
    activate(sz, upward, active, slope)
    branch[...] = multiply(active[...], down[layer])
    finish_forward(sz, cur, branch, lscale, layer, out, flat)
    write_strips(sz, flat, strips)


def turn_kernel(
    sz, layer, seams, corners, cur, own, below, above, kern, gain, lscale, up, down, out_grad,
    out_hbm, base, grad_own, grad_below, grad_above,
    pad, grad_conv, normed, active, down_in, up_in, gain_sums, scale_sums,
    pool, taps, conv, upward, out, normal, inverse, slope, branch, grad_pool, grad_pad, out_sem,
):
    strip_at, corner_at = read_plan(sz, seams), read_plan(sz, corners)
    surround(sz, strip_at, corner_at, cur, own, below, above, pool, pad)
    hold_taps(sz, kern, layer, taps)
    convolve(sz, pad, taps, conv)
    normalise(sz, conv, gain, layer, normal, inverse, normed)
    upward[...] = multiply(normed[...], up[layer])
    activate(sz, upward, active, slope)
    branch[...] = multiply(active[...], down[layer])
    finish_forward(sz, cur, branch, lscale, layer, out, None)
    store = pltpu.make_async_copy(out, out_hbm, out_sem.at[0])
    store.start()

    def grad_row(q, i):
        return out_grad[q, i].astype(F32)

    scale_rows(sz, grad_row, branch, lscale, layer, down_in, scale_sums)
    upward[...] = multiply(down_in[...], down[layer], 1, 1)
    slope_rows(sz, upward, slope, up_in)
    branch[...] = multiply(up_in[...], up[layer], 1, 1)
    norm_gradients(sz, branch, normal, inverse, gain, layer, grad_conv, gain_sums)
    spread_gradients(sz, grad_conv, taps, grad_pad)
    return_margins(sz, strip_at, corner_at, grad_pad, grad_pool)
    send_margins(sz, grad_pool, grad_own, grad_below, grad_above)
    gather_inner(sz, grad_row, grad_pad, base)
    store.wait()


def weights_kernel(
    sz, pad, grad_conv, normed, active, down_in, up_in, gain_sums, scale_sums,
    keep, send, small, tap_sums, both,
):
    small[...] = jnp.zeros_like(small)
    weight_gradients(sz, digit_of(0), active, down_in, normed, up_in, both, keep, send)
    tap_gradients(sz, pad, grad_conv, tap_sums, small)
    fill_small(small, gain_sums, scale_sums)


def backward_kernel(
    sz, layer, base, own, first, second, lscale, down, normed, slope, active, branch,
    keep, send, flat, up_in, scale_sums,
    hidden, down_in, both,
):
    add_strips(sz, base, own, first, second, flat)
    for slab in range(sz.slabs):
        flat[slab] = flat[slab].astype(BF16).astype(F32)
    scale_rows(sz, flat_grad_row(sz, flat), branch, lscale, layer, down_in, scale_sums)
    hidden[...] = multiply(down_in[...], down[layer], 1, 1)
    slope_rows(sz, hidden, slope, up_in)
    weight_gradients(sz, digit_of(0), active, down_in, normed, up_in, both, keep, send)


def spread_kernel(
    sz, layer, seams, corners, kern, gain, up, flat, up_in, normal, inverse,
    base, grad_own, grad_below, grad_above, grad_conv, gain_sums,
    taps, branch, grad_pool, grad_pad,
):
    strip_at, corner_at = read_plan(sz, seams), read_plan(sz, corners)
    branch[...] = multiply(up_in[...], up[layer], 1, 1)
    norm_gradients(sz, branch, normal, inverse, gain, layer, grad_conv, gain_sums)
    hold_taps(sz, kern, layer, taps)
    spread_gradients(sz, grad_conv, taps, grad_pad)
    return_margins(sz, strip_at, corner_at, grad_pad, grad_pool)
    send_margins(sz, grad_pool, grad_own, grad_below, grad_above)
    gather_inner(sz, flat_grad_row(sz, flat), grad_pad, base)


def taps_kernel(sz, pad, grad_conv, gain_sums, scale_sums, other, both, tap_sums, small):
    small[...] = jnp.zeros_like(small)
    tap_gradients(sz, pad, grad_conv, tap_sums, small)
    fill_small(small, gain_sums, scale_sums)
    both[0:SMALL_ROWS] = small[...].astype(BF16)
    both[SMALL_ROWS : 2 * SMALL_ROWS] = other[...].astype(BF16)


def last_kernel(sz, base, own, first, second, out_hbm, token, flat, out, sems):
    token[...] = jnp.zeros_like(token)
    add_strips(sz, base, own, first, second, flat)
    row = flat_grad_row(sz, flat)
    for q in range(sz.tiles):
        for i in range(sz.edge):
            out[q, i] = row(q, i).astype(BF16)
    store = pltpu.make_async_copy(out, out_hbm, sems.at[0])
    store.start()
    store.wait()


def add_rows(out, parts):
    for start in range(0, out.shape[0], 16):
        rows = slice(start, start + 16)
        values = [part(rows).astype(F32) for part in parts]
        out[rows] = sum(values[1:], values[0]).astype(BF16)


def share_near_kernel(*refs):
    arrays, outs = refs[:2], refs[2:]
    for k, out in enumerate(outs):
        piece = digit_of(1) ^ k
        add_rows(out, [lambda rows, array=array: array[piece, rows] for array in arrays])


def share_far_kernel(*refs):
    rest, share = refs[0].shape[:2]
    arrays, outs = refs[:-rest], refs[-rest:]
    for k, out in enumerate(outs):
        piece = digit_of(2) ^ k
        for layer in range(2):
            parts = arrays[4 * layer : 4 * layer + 4]
            add_rows(
                out.at[layer],
                [lambda rows, array=array: array[piece, rows] for array in parts],
            )


def total_kernel(*refs):
    out, small = refs[-1], refs[-2]
    for layer in range(2):
        add_rows(
            out.at[layer],
            [lambda rows, array=array: array[layer, rows] for array in refs[:-2]],
        )
    out[2:] = small[...]


def order_kernel(level, small_units, *refs):
    pieces, out = refs[:-1], refs[-1]
    units = pieces[0].shape[0] - small_units
    for k, piece in enumerate(pieces):
        at = (digit_of(level) ^ k) * units
        for j in range(units):
            out[at + j] = piece[j]
    for j in range(small_units):
        add_rows(
            out.at[len(pieces) * units + j],
            [lambda rows, piece=piece: piece[units + j, rows] for piece in pieces],
        )


def unpack_half(sz, half, source, staged, up_hbm, down_hbm, sems):
    share = source.shape[1]
    target = (down_hbm, up_hbm)[half]
    pieces = sz.hidden // share
    copies = []
    for layer in range(2):
        for j in range(pieces):
            value = source[2 * j + layer].astype(F32)
            if half == 0:
                staged[layer, j * share : (j + 1) * share] = value
            else:
                k, c = divmod(j * share, sz.channels)
                staged[layer, k * sz.channels + c : k * sz.channels + c + share] = value
        for k in range(sz.hidden // sz.channels):
            rows = pl.ds(k * sz.channels, sz.channels)
            place = target.at[layer, rows] if half == 0 else target.at[layer, :, rows]
            copy = pltpu.make_async_copy(
                staged.at[layer, rows], place, sems.at[half, len(copies)]
            )
            copy.start()
            copies.append(copy)
    for copy in copies:
        copy.wait()


def unpack_mine_kernel(sz, mine, up_hbm, down_hbm, staged, sems):
    for half in range(2):

        @pl.when(digit_of(0) == half)
        def _(half=half):
            unpack_half(sz, half, mine, staged, up_hbm, down_hbm, sems)


def unpack_theirs_kernel(
    sz, mine, theirs, _up, _down, up_hbm, down_hbm, kernel_out, gain_out, scale_out,
    staged, small, sems,
):
    for half in range(2):

        @pl.when(digit_of(0) == 1 - half)
        def _(half=half):
            unpack_half(sz, half, theirs, staged, up_hbm, down_hbm, sems)

    share = mine.shape[1]
    start = 2 * sz.hidden // share
    for j in range(start, mine.shape[0]):
        rows = pl.ds((j - start) * share, share)
        small[rows, :] = mine[j].astype(F32) + theirs[j].astype(F32)
    for layer in range(2):
        at = layer * SMALL_ROWS
        for a in range(TAPS):
            for b in range(TAPS):
                kernel_out[a, b, layer : layer + 1] = small[pl.ds(at + a * 8 + b, 1), :]
        at = at + TAPS * 8
        gain_out[layer : layer + 1] = small[pl.ds(at, 1), :]
        scale_out[layer : layer + 1] = small[pl.ds(at + 1, 1), :]


IN_VMEM = pl.BlockSpec(memory_space=pltpu.VMEM)
IN_SMEM = pl.BlockSpec(memory_space=pltpu.SMEM)
IN_HBM = pl.BlockSpec(memory_space=pltpu.HBM)


def call(body, name, micros, ins, outs, scratch, after=(), aliases={}):
    count = len(ins)

    def run(*refs):
        body(*refs[:count], *refs[count + len(after) :])

    return pl.pallas_call(
        run,
        in_specs=[spec for spec, _ in ins] + [pl.BlockSpec(memory_space=pl.ANY)] * len(after),
        out_specs=[spec for spec, _ in outs],
        out_shape=[out for _, out in outs],
        scratch_shapes=scratch,
        compiler_params=pltpu.CompilerParams(vmem_limit_bytes=24 * 1024 * 1024),
        cost_estimate=pl.CostEstimate(
            flops=0, bytes_accessed=int(micros * 3.5e6), transcendentals=0
        ),
        input_output_aliases=aliases,
        name=name,
    )(*[array for _, array in ins], *after)


def near(*arrays):
    return [(IN_VMEM, array) for array in arrays]


def far(*arrays):
    return [(IN_HBM, array) for array in arrays]


def pass_on(shard, by):
    length = lax.axis_size("tile")
    return lax.ppermute(shard, "tile", [(i, (i + by) % length) for i in range(length)])


def partners(array, masks):
    length = lax.axis_size("tile")
    return [
        lax.ppermute(array, "tile", [(i, i ^ mask) for i in range(length)]) for mask in masks
    ]


def swap(arrays, masks):
    length = lax.axis_size("tile")
    return [
        lax.ppermute(array, "tile", [(i, i ^ mask) for i in range(length)])
        for array, mask in zip(arrays, masks)
    ]


class Reduction:
    def __init__(self, devices):
        self.devices = devices
        self.rest = devices // 8
        self.near_masks = [2 * k for k in range(1, 4)]
        self.rest_masks = [8 * k for k in range(1, self.rest)]

    def start(self, keep, send):
        rows, channels = keep.shape
        (came,) = swap([send], [1])
        quarter = rows // 4
        parts = (4, quarter, channels)
        shape = jax.ShapeDtypeStruct((quarter, channels), BF16)
        pieces = call(
            share_near_kernel, "share_near", 0.7,
            near(keep.reshape(parts), came.reshape(parts)), near(*[shape] * 4), [],
        )
        return [pieces[0]] + swap(pieces[1:], self.near_masks)

    def finish(self, parts, after, small):
        quarter, channels = parts[0][0].shape
        dims = (self.rest, quarter // self.rest, channels)
        arrays = [part.reshape(dims) for layer in parts for part in layer]
        shape = jax.ShapeDtypeStruct((2,) + dims[1:], BF16)
        pieces = call(
            share_far_kernel, "share_far", 0.9,
            near(*arrays), near(*[shape] * self.rest), [], after,
        )
        arrived = swap(pieces[1:], self.rest_masks)
        small = small(pieces[0]).reshape((-1,) + dims[1:])
        shape = jax.ShapeDtypeStruct((2 + small.shape[0],) + dims[1:], BF16)
        (total,) = call(
            total_kernel, "total", 0.4, near(pieces[0], *arrived, small), near(shape), []
        )
        return total, small.shape[0]

    def gather(self, total, small_units, after):
        for level, masks, name in (
            (2, self.rest_masks, "order_far"),
            (1, self.near_masks, "order_near"),
        ):
            pieces = [total] + partners(total, masks)
            units = (total.shape[0] - small_units) * len(pieces) + small_units
            shape = jax.ShapeDtypeStruct((units,) + total.shape[1:], BF16)
            (total,) = call(
                functools.partial(order_kernel, level, small_units), name, 0.5,
                near(*pieces), near(shape), [], after,
            )
            after = ()
        return total, partners(total, [1])[0]


def on_device(
    inputs,
    out_grad,
    kernel,
    norm_gain,
    up_weight,
    down_weight,
    layer_scale,
    seam_table,
    corner_table,
):
    tiles, edge, _, channels = inputs.shape
    layers, _, hidden = up_weight.shape
    sz = Sizes(tiles, edge, channels, hidden)
    columns = lax.axis_size("tile")
    plan = [(IN_SMEM, table.transpose((1, 2, 0))) for table in (seam_table, corner_table)]
    kern = kernel.transpose((1, 2, 0, 3))
    gain, lscale, up, down = norm_gain, layer_scale, up_weight, down_weight
    reduction = Reduction(columns)

    shape = jax.ShapeDtypeStruct
    image = shape(inputs.shape, BF16)
    strips_shape = shape((sz.pieces, REACH, edge, channels), BF16)
    slabs = shape((sz.slabs, sz.cells, LANES), F32)
    padded = shape((sz.slabs, sz.outer * PITCH, LANES), F32)
    inverses = shape((tiles, sz.cells, LANES), F32)
    narrow_short = shape((sz.rows, channels), BF16)
    wide_short = shape((sz.rows, hidden), BF16)
    narrow = shape((sz.rows, channels), F32)
    wide = shape((sz.rows, hidden), F32)
    sums = shape((edge, channels), F32)
    grad_slabs = shape((sz.slabs, edge * GRAD_PITCH, LANES), F32)
    own_shape = shape((sz.pieces, REACH, sz.lanes, edge, LANES), F32)
    pool = shape((3 * sz.pieces, REACH, edge, channels), BF16)
    grad_pool = shape((3 * sz.pieces, REACH, sz.lanes, edge, LANES), F32)
    taps = shape((sz.lanes, TAPS * 8, LANES), F32)
    tap_sums = shape((sz.lanes, TAPS * TAPS, 8, LANES), F32)
    small = shape((SMALL_ROWS, channels), F32)
    half = shape((hidden, channels), BF16)
    two_halves = shape((2, hidden, channels), BF16)

    def vmem(*shapes):
        return [pltpu.VMEM(one.shape, one.dtype) for one in shapes]

    def sems(count):
        return [pltpu.SemaphoreType.DMA((count,))]

    strips, inputs = call(
        functools.partial(strips_kernel, sz),
        "strips", 0.3,
        near(inputs),
        near(strips_shape, image),
        vmem(slabs),
    )
    below, above = pass_on(strips, 1), pass_on(strips, -1)
    fetched = (kern, gain, lscale, up, down)
    kern, gain, lscale, up, down = call(
        fetch_kernel,
        "fetch", 2.0,
        far(*fetched),
        near(*[shape(one.shape, one.dtype) for one in fetched]),
        sems(len(fetched)),
        (strips,),
    )
    middle, strips, pad_zero, normal, inverse, normed, slope, active, branch = call(
        functools.partial(forward_kernel, sz, 0),
        "forward", 8.7,
        plan + near(inputs, strips, below, above, kern, gain, lscale, up, down),
        near(
            image, strips_shape, padded, slabs, inverses,
            narrow_short, wide_short, wide_short, narrow,
        ),
        vmem(pool, taps, slabs, wide, slabs),
    )
    below, above = pass_on(strips, 1), pass_on(strips, -1)
    result, base, grad_own, grad_below, grad_above, *for_weights = call(
        functools.partial(turn_kernel, sz, 1),
        "turn", 15.4,
        plan + near(middle, strips, below, above, kern, gain, lscale, up, down, out_grad),
        far(image)
        + near(
            slabs, own_shape, strips_shape, strips_shape,
            padded, grad_slabs, narrow_short, wide_short, narrow_short, wide_short, sums, sums,
        ),
        vmem(
            pool, taps, slabs, wide, image, slabs, inverses, wide_short, narrow, grad_pool, padded
        )
        + sems(1),
    )
    from_below, from_above = pass_on(grad_above, 1), pass_on(grad_below, -1)
    keep_one, send_one, small_one = call(
        functools.partial(weights_kernel, sz),
        "weights", 2.8,
        near(*for_weights),
        near(half, half, small),
        vmem(tap_sums, two_halves),
    )
    parts_one = reduction.start(keep_one, send_one)
    keep_zero, send_zero, flat, up_in, scale_sums = call(
        functools.partial(backward_kernel, sz, 0),
        "backward", 2.9,
        near(
            base, grad_own, from_below, from_above, lscale, down, normed, slope, active, branch
        ),
        near(half, half, slabs, wide_short, sums),
        vmem(wide, narrow_short, two_halves),
    )
    parts_zero = reduction.start(keep_zero, send_zero)
    base, grad_own, grad_below, grad_above, grad_conv, gain_sums = call(
        functools.partial(spread_kernel, sz, 0),
        "spread", 6.0,
        plan + near(kern, gain, up, flat, up_in, normal, inverse),
        near(slabs, own_shape, strips_shape, strips_shape, grad_slabs, sums),
        vmem(taps, narrow, grad_pool, padded),
        (parts_zero[0],),
    )
    from_below, from_above = pass_on(grad_above, 1), pass_on(grad_below, -1)

    def small_gradients(share):
        (both,) = call(
            functools.partial(taps_kernel, sz),
            "taps", 2.1,
            near(pad_zero, grad_conv, gain_sums, scale_sums, small_one),
            near(shape((2 * SMALL_ROWS, channels), BF16)),
            vmem(tap_sums, small),
            (share,),
        )
        return both

    total, small_units = reduction.finish(
        (parts_zero, parts_one), (gain_sums,), small_gradients
    )
    in_grad, token = call(
        functools.partial(last_kernel, sz),
        "last", 1.0,
        near(base, grad_own, from_below, from_above),
        far(image) + near(shape((8, LANES), F32)),
        vmem(slabs, image) + sems(1),
    )
    mine, theirs = reduction.gather(total, small_units, (token,))
    weight_shapes = [shape(up_weight.shape, F32), shape(down_weight.shape, F32)]
    copies = layers * hidden // channels
    scratch = vmem(shape(down_weight.shape, F32))
    grad_up, grad_down = call(
        functools.partial(unpack_mine_kernel, sz),
        "unpack_mine", 1.5,
        near(mine),
        far(*weight_shapes),
        scratch + [pltpu.SemaphoreType.DMA((2, copies))],
    )
    grad_up, grad_down, grad_kernel, grad_gain, grad_scale = call(
        functools.partial(unpack_theirs_kernel, sz),
        "unpack_theirs", 1.5,
        near(mine, theirs) + far(grad_up, grad_down),
        far(*weight_shapes)
        + near(
            shape(kern.shape, F32), shape(norm_gain.shape, F32), shape(norm_gain.shape, F32)
        ),
        scratch
        + vmem(shape((2 * SMALL_ROWS, channels), F32))
        + [pltpu.SemaphoreType.DMA((2, copies))],
        aliases={2: 0, 3: 1},
    )
    return (
        result, in_grad, grad_kernel.transpose((2, 0, 1, 3)),
        grad_gain, grad_up, grad_down, grad_scale,
    )


def solution(mesh):
    placed = (
        P(("groups", "tile"), None, None, None),
        P(("groups", "tile"), None, None, None),
        P(),
        P(),
        P(),
        P(),
        P(),
        P(),
        P(),
    )
    return jax.shard_map(
        on_device,
        mesh=mesh,
        in_specs=placed,
        out_specs=(
            P(("groups", "tile"), None, None, None),
            P(("groups", "tile"), None, None, None),
            P("groups", None, None, None),
            P("groups", None),
            P("groups", None, None),
            P("groups", None, None),
            P("groups", None),
        ),
        check_vma=False,
    )
```

```python
import functools

import jax
import jax.numpy as jnp
from jax import lax
from jax.experimental import pallas as pl
from jax.experimental.pallas import tpu as pltpu
from jax.sharding import PartitionSpec as P

epsilon = 1e-06
inverse_root_two = 0.7071067811865476
inverse_root_tau = 0.3989422804014327

LANES = 128
TAPS = 7
REACH = 3
PITCH = 24
GRAD_PITCH = 32
SMALL_ROWS = 64
F32 = jnp.float32
BF16 = jnp.bfloat16


def flip_rows(value):
    rows = value.shape[0]
    order = 7 - lax.broadcasted_iota(jnp.int32, (8, LANES), 0)
    parts = [
        jnp.take_along_axis(value[at : at + 8], order, axis=0, mode="promise_in_bounds")
        for at in range(0, rows, 8)
    ]
    return jnp.concatenate(parts[::-1], axis=0)


def halves(value):
    return [value[:, at : at + LANES] for at in range(0, value.shape[1], LANES)]


class Sizes:
    def __init__(self, tiles, edge, channels, hidden):
        self.tiles = tiles
        self.edge = edge
        self.channels = channels
        self.hidden = hidden
        self.lanes = channels // LANES
        self.cells = edge * edge
        self.rows = tiles * edge * edge
        self.pieces = tiles * 4
        self.outer = edge + 2 * REACH
        self.slabs = tiles * self.lanes

    def key(self):
        return (self.tiles, self.edge, self.channels, self.hidden)


def strip_window(edge, side, row):
    if side == 0:
        return pl.ds(row * edge, edge), False
    if side == 1:
        return pl.ds(edge - 1 - row, edge, stride=edge), False
    if side == 2:
        return pl.ds((edge - 1 - row) * edge, edge), True
    return pl.ds(row, edge, stride=edge), True


def margin_window(edge, side, row):
    last = edge + 2 * REACH - 1
    if side == 0:
        return pl.ds((2 - row) * PITCH + REACH, edge), True
    if side == 1:
        return pl.ds(REACH * PITCH + last - 2 + row, edge, stride=PITCH), True
    if side == 2:
        return pl.ds((last - 2 + row) * PITCH + REACH, edge), False
    return pl.ds(REACH * PITCH + 2 - row, edge, stride=PITCH), False


def corner_cell(edge, corner, row, column):
    last = edge + 2 * REACH - 1
    r, x = 2 - row, 2 - column
    if corner == 0:
        at = (r, x)
    elif corner == 1:
        at = (x, last - r)
    elif corner == 2:
        at = (last - r, last - x)
    else:
        at = (last - x, r)
    return at[0] * PITCH + at[1]


def read_plan(sz, table):
    columns = lax.axis_size("tile")
    device = lax.axis_index("tile")
    below = lax.rem(device + columns - 1, columns)
    plan = []
    for q in range(sz.tiles):
        for side in range(4):
            source = table[side, 0, device * sz.tiles + q]
            owner = lax.div(source, sz.tiles)
            local = (source - owner * sz.tiles) * 4 + table[side, 1, device * sz.tiles + q]
            shift = jnp.where(
                owner == device, 0, jnp.where(owner == below, sz.pieces, 2 * sz.pieces)
            )
            plan.append(shift + local)
    return plan


def digit_of(level):
    device = lax.axis_index("tile")
    if level == 0:
        return lax.rem(device, 2)
    if level == 1:
        return lax.rem(lax.div(device, 2), 4)
    return lax.div(device, 8)


def write_strips(sz, flat, strips_ref):
    for q in range(sz.tiles):
        for side in range(4):
            for row in range(REACH):
                window, turned = strip_window(sz.edge, side, row)
                parts = [flat[q * sz.lanes + h, window, :] for h in range(sz.lanes)]
                if turned:
                    parts = [flip_rows(part) for part in parts]
                strips_ref[q * 4 + side, row] = jnp.concatenate(parts, axis=1).astype(BF16)


def surround(sz, strip_at, corner_at, cur, own, below, above, pool, pad):
    pool[0 : sz.pieces] = own[...]
    pool[sz.pieces : 2 * sz.pieces] = below[...]
    pool[2 * sz.pieces : 3 * sz.pieces] = above[...]
    for q in range(sz.tiles):
        for i in range(sz.edge):
            for h, part in enumerate(halves(cur[q, i].astype(F32))):
                pad[q * sz.lanes + h, pl.ds((i + REACH) * PITCH + REACH, sz.edge), :] = part
    for q in range(sz.tiles):
        for side in range(4):
            piece = strip_at[q * 4 + side]
            for row in range(REACH):
                window, turned = margin_window(sz.edge, side, row)
                for h, part in enumerate(halves(pool[piece, row].astype(F32))):
                    pad[q * sz.lanes + h, window, :] = flip_rows(part) if turned else part
            piece = corner_at[q * 4 + side]
            for row in range(REACH):
                for h, part in enumerate(halves(pool[piece, row].astype(F32))):
                    for column in range(REACH):
                        at = corner_cell(sz.edge, side, row, column)
                        pad[q * sz.lanes + h, pl.ds(at, 1), :] = part[column : column + 1]


def hold_taps(sz, kern, layer, taps):
    for a in range(TAPS):
        for b in range(TAPS):
            for h, part in enumerate(halves(kern[a, b, layer : layer + 1])):
                taps[h, pl.ds(a * 8 + b, 1), :] = part


def tap(taps, h, a, b):
    return jnp.broadcast_to(taps[h, pl.ds(a * 8 + b, 1), :], (8, LANES))


def convolve(sz, pad, taps, conv):
    @pl.loop(0, sz.slabs)
    def _(slab):
        h = lax.rem(slab, sz.lanes)
        for g in range(sz.edge // 8):
            acc = [None] * sz.edge
            for b in range(TAPS):
                weights = [tap(taps, h, a, b) for a in range(TAPS)]
                for r in range(sz.outer):
                    x = pad[slab, pl.ds(r * PITCH + b + 8 * g, 8), :]
                    for a in range(TAPS):
                        i = r - a
                        if 0 <= i < sz.edge:
                            term = x * weights[a]
                            acc[i] = term if acc[i] is None else acc[i] + term
            for i in range(sz.edge):
                conv[slab, pl.ds(i * sz.edge + 8 * g, 8), :] = acc[i]


def normalise(sz, conv, gain, layer, normal, inverse, normed):
    scale = 1.0 / sz.channels
    for q in range(sz.tiles):

        @pl.loop(0, sz.edge, unroll=2)
        def _(i):
            at = pl.ds(pl.multiple_of(i * sz.edge, sz.edge), sz.edge)
            parts = [conv[q * sz.lanes + h, at, :] for h in range(sz.lanes)]
            mean = jnp.sum(sum(parts[1:], parts[0]), axis=-1, keepdims=True) * scale
            parts = [part - mean for part in parts]
            squares = [part * part for part in parts]
            variance = jnp.sum(sum(squares[1:], squares[0]), axis=-1, keepdims=True) * scale
            root = lax.rsqrt(variance + epsilon)
            inverse[q, at, :] = jnp.broadcast_to(root, (sz.edge, LANES))
            flat_at = pl.ds(pl.multiple_of(q * sz.cells + i * sz.edge, sz.edge), sz.edge)
            for h, part in enumerate(parts):
                part = part * root
                normal[q * sz.lanes + h, at, :] = part
                gains = gain[layer : layer + 1, h * LANES : (h + 1) * LANES]
                normed[flat_at, h * LANES : (h + 1) * LANES] = (part * gains).astype(BF16)


def activate(sz, upward, active, slope):
    width = 512

    @pl.loop(0, sz.rows // 16)
    def _(t):
        at = pl.ds(pl.multiple_of(t * 16, 16), 16)
        for start in range(0, sz.hidden, width):
            u = upward[at, start : start + width]
            chance = 0.5 * (1.0 + lax.erf(u * inverse_root_two))
            active[at, start : start + width] = (u * chance).astype(BF16)
            slope[at, start : start + width] = (
                chance + u * jnp.exp(-0.5 * u * u) * inverse_root_tau
            ).astype(slope.dtype)


def multiply(a, b, ca=1, cb=0):
    return lax.dot_general(a, b, (((ca,), (cb,)), ((), ())), preferred_element_type=F32)


def finish_forward(sz, cur, branch, lscale, layer, out, flat):
    for q in range(sz.tiles):

        @pl.loop(0, sz.edge, unroll=2)
        def _(i):
            at = pl.ds(pl.multiple_of(q * sz.cells + i * sz.edge, sz.edge), sz.edge)
            value = cur[q, i].astype(F32) + branch[at, :] * lscale[layer : layer + 1, :]
            value = value.astype(BF16)
            out[q, i] = value
            if flat is not None:
                local = pl.ds(pl.multiple_of(i * sz.edge, sz.edge), sz.edge)
                for h, part in enumerate(halves(value.astype(F32))):
                    flat[q * sz.lanes + h, local, :] = part


def scale_rows(sz, grad_row, branch, lscale, layer, down_in, sums):
    sums[...] = jnp.zeros_like(sums)
    for q in range(sz.tiles):

        @pl.loop(0, sz.edge, unroll=2)
        def _(i):
            at = pl.ds(pl.multiple_of(q * sz.cells + i * sz.edge, sz.edge), sz.edge)
            g = grad_row(q, i)
            down_in[at, :] = (g * lscale[layer : layer + 1, :]).astype(BF16)
            sums[...] += g * branch[at, :]


def slope_rows(sz, grad_active, slope, up_in):
    @pl.loop(0, sz.rows // 16, unroll=2)
    def _(t):
        at = pl.ds(pl.multiple_of(t * 16, 16), 16)
        up_in[at, :] = (grad_active[at, :] * slope[at, :].astype(F32)).astype(BF16)


def weight_gradients(sz, core, active, down_in, normed, up_in, both, keep, send):
    both[0] = multiply(active[...], down_in[...], 0, 0).astype(BF16)
    for k in range(sz.hidden // sz.channels):
        part = multiply(normed[...], up_in[:, k * sz.channels : (k + 1) * sz.channels], 0, 0)
        both[1, k * sz.channels : (k + 1) * sz.channels, :] = part.astype(BF16)
    keep[...] = both[core]
    send[...] = both[1 - core]


def norm_gradients(sz, grad_normed, normal, inverse, gain, layer, grad_conv, sums):
    scale = 1.0 / sz.channels
    sums[...] = jnp.zeros_like(sums)
    blank = jnp.zeros((8, LANES), F32)
    for q in range(sz.tiles):

        @pl.loop(0, sz.edge, unroll=2)
        def _(i):
            at = pl.ds(pl.multiple_of(q * sz.cells + i * sz.edge, sz.edge), sz.edge)
            local = pl.ds(pl.multiple_of(i * sz.edge, sz.edge), sz.edge)
            g = halves(grad_normed[at, :])
            n = [normal[q * sz.lanes + h, local, :] for h in range(sz.lanes)]
            sums[...] += jnp.concatenate([a * b for a, b in zip(g, n)], axis=1)
            s = [
                part * gain[layer : layer + 1, h * LANES : (h + 1) * LANES]
                for h, part in enumerate(g)
            ]
            products = [a * b for a, b in zip(s, n)]
            mean = jnp.sum(sum(s[1:], s[0]), axis=-1, keepdims=True) * scale
            slant = jnp.sum(sum(products[1:], products[0]), axis=-1, keepdims=True) * scale
            root = inverse[q, local, :]
            for h in range(sz.lanes):
                slab = q * sz.lanes + h
                base = pl.multiple_of(i * GRAD_PITCH, GRAD_PITCH)
                grad_conv[slab, pl.ds(base, 8), :] = blank
                grad_conv[slab, pl.ds(base + 8, sz.edge), :] = root * (s[h] - mean - n[h] * slant)
                grad_conv[slab, pl.ds(base + 8 + sz.edge, 8), :] = blank


def tap_gradients(sz, pad, grad_conv, tap_sums, small):
    tap_sums[...] = jnp.zeros_like(tap_sums)

    @pl.loop(0, sz.slabs)
    def _(slab):
        h = lax.rem(slab, sz.lanes)
        for b in range(TAPS):
            acc = [None] * TAPS
            for g in range(sz.edge // 8):
                grads = [
                    grad_conv[slab, pl.ds(i * GRAD_PITCH + 8 + 8 * g, 8), :]
                    for i in range(sz.edge)
                ]
                for r in range(sz.outer):
                    x = pad[slab, pl.ds(r * PITCH + b + 8 * g, 8), :]
                    for a in range(TAPS):
                        i = r - a
                        if 0 <= i < sz.edge:
                            term = x * grads[i]
                            acc[a] = term if acc[a] is None else acc[a] + term
            for a in range(TAPS):
                tap_sums[h, a * TAPS + b] += acc[a]

    for h in range(sz.lanes):
        for k in range(TAPS * TAPS):
            row = k // TAPS * 8 + k % TAPS
            small[row : row + 1, h * LANES : (h + 1) * LANES] = jnp.sum(
                tap_sums[h, k], axis=0, keepdims=True
            )


def spread_gradients(sz, grad_conv, taps, grad_pad):
    @pl.loop(0, sz.slabs)
    def _(slab):
        h = lax.rem(slab, sz.lanes)
        for g in range(PITCH // 8):
            acc = [None] * sz.outer
            for b in range(TAPS):
                start = 8 * g - b + 8
                if start >= 8 + sz.edge:
                    continue
                weights = [tap(taps, h, a, b) for a in range(TAPS)]
                for i in range(sz.edge):
                    x = grad_conv[slab, pl.ds(i * GRAD_PITCH + start, 8), :]
                    for a in range(TAPS):
                        term = x * weights[a]
                        acc[i + a] = term if acc[i + a] is None else acc[i + a] + term
            for p in range(sz.outer):
                grad_pad[slab, pl.ds(p * PITCH + 8 * g, 8), :] = acc[p]


def return_margins(sz, strip_at, corner_at, grad_pad, pool):
    pool[...] = jnp.zeros_like(pool)
    for q in range(sz.tiles):
        for side in range(4):
            piece = strip_at[q * 4 + side]
            for row in range(REACH):
                window, turned = margin_window(sz.edge, side, row)
                for h in range(sz.lanes):
                    part = grad_pad[q * sz.lanes + h, window, :]
                    pool[piece, row, h] = flip_rows(part) if turned else part
    for q in range(sz.tiles):
        for side in range(4):
            piece = corner_at[q * 4 + side]
            for row in range(REACH):
                for column in range(REACH):
                    at = corner_cell(sz.edge, side, row, column)
                    for h in range(sz.lanes):
                        pool[piece, row, h, pl.ds(column, 1), :] += grad_pad[
                            q * sz.lanes + h, pl.ds(at, 1), :
                        ]


def send_margins(sz, pool, own, below, above):
    own[...] = pool[0 : sz.pieces]
    for piece in range(sz.pieces):
        for row in range(REACH):
            for offset, ref in ((1, below), (2, above)):
                parts = [pool[offset * sz.pieces + piece, row, h] for h in range(sz.lanes)]
                ref[piece, row] = jnp.concatenate(parts, axis=1).astype(BF16)


def gather_inner(sz, grad_row, grad_pad, base):
    for q in range(sz.tiles):
        for i in range(sz.edge):
            for h, part in enumerate(halves(grad_row(q, i))):
                slab = q * sz.lanes + h
                base[slab, pl.ds(i * sz.edge, sz.edge), :] = (
                    part + grad_pad[slab, pl.ds((i + REACH) * PITCH + REACH, sz.edge), :]
                )


def add_strips(sz, base, own, first, second, flat):
    flat[...] = base[...]
    for q in range(sz.tiles):
        for side in range(4):
            piece = q * 4 + side
            for row in range(REACH):
                window, turned = strip_window(sz.edge, side, row)
                came = first[piece, row].astype(F32) + second[piece, row].astype(F32)
                for h, part in enumerate(halves(came)):
                    part = part + own[piece, row, h]
                    flat[q * sz.lanes + h, window, :] += flip_rows(part) if turned else part


def fill_small(small, gain_sums, scale_sums):
    small[TAPS * 8 : TAPS * 8 + 1, :] = jnp.sum(gain_sums[...], axis=0, keepdims=True)
    small[TAPS * 8 + 1 : TAPS * 8 + 2, :] = jnp.sum(scale_sums[...], axis=0, keepdims=True)


def flat_grad_row(sz, flat):
    def row(q, i):
        at = pl.ds(i * sz.edge, sz.edge)
        parts = [flat[q * sz.lanes + h, at, :] for h in range(sz.lanes)]
        return jnp.concatenate(parts, axis=1)

    return row


def fetch_kernel(*refs):
    count = (len(refs) - 1) // 2
    copies = [
        pltpu.make_async_copy(refs[k], refs[count + k], refs[-1].at[k]) for k in range(count)
    ]
    for copy in copies:
        copy.start()
    for copy in copies:
        copy.wait()


def strips_kernel(sz, cur, strips, held, flat):
    held[...] = cur[...]
    for q in range(sz.tiles):
        for i in range(sz.edge):
            for h, part in enumerate(halves(cur[q, i].astype(F32))):
                flat[q * sz.lanes + h, pl.ds(i * sz.edge, sz.edge), :] = part
    write_strips(sz, flat, strips)


def forward_kernel(
    sz, layer, seams, corners, cur, own, below, above, kern, gain, lscale, up, down,
    out, strips, pad, normal, inverse, normed, slope, active, branch,
    pool, taps, conv, upward, flat,
):
    strip_at, corner_at = read_plan(sz, seams), read_plan(sz, corners)
    surround(sz, strip_at, corner_at, cur, own, below, above, pool, pad)
    hold_taps(sz, kern, layer, taps)
    convolve(sz, pad, taps, conv)
    normalise(sz, conv, gain, layer, normal, inverse, normed)
    upward[...] = multiply(normed[...], up[layer])
    activate(sz, upward, active, slope)
    branch[...] = multiply(active[...], down[layer])
    finish_forward(sz, cur, branch, lscale, layer, out, flat)
    write_strips(sz, flat, strips)


def turn_kernel(
    sz, layer, seams, corners, cur, own, below, above, kern, gain, lscale, up, down, out_grad,
    out_hbm, base, grad_own, grad_below, grad_above,
    pad, grad_conv, normed, active, down_in, up_in, gain_sums, scale_sums,
    pool, taps, conv, upward, out, normal, inverse, slope, branch, grad_pool, grad_pad, out_sem,
):
    strip_at, corner_at = read_plan(sz, seams), read_plan(sz, corners)
    surround(sz, strip_at, corner_at, cur, own, below, above, pool, pad)
    hold_taps(sz, kern, layer, taps)
    convolve(sz, pad, taps, conv)
    normalise(sz, conv, gain, layer, normal, inverse, normed)
    upward[...] = multiply(normed[...], up[layer])
    activate(sz, upward, active, slope)
    branch[...] = multiply(active[...], down[layer])
    finish_forward(sz, cur, branch, lscale, layer, out, None)
    store = pltpu.make_async_copy(out, out_hbm, out_sem.at[0])
    store.start()

    def grad_row(q, i):
        return out_grad[q, i].astype(F32)

    scale_rows(sz, grad_row, branch, lscale, layer, down_in, scale_sums)
    upward[...] = multiply(down_in[...], down[layer], 1, 1)
    slope_rows(sz, upward, slope, up_in)
    branch[...] = multiply(up_in[...], up[layer], 1, 1)
    norm_gradients(sz, branch, normal, inverse, gain, layer, grad_conv, gain_sums)
    spread_gradients(sz, grad_conv, taps, grad_pad)
    return_margins(sz, strip_at, corner_at, grad_pad, grad_pool)
    send_margins(sz, grad_pool, grad_own, grad_below, grad_above)
    gather_inner(sz, grad_row, grad_pad, base)
    store.wait()


def weights_kernel(
    sz, pad, grad_conv, normed, active, down_in, up_in, gain_sums, scale_sums,
    keep, send, small, tap_sums, both,
):
    small[...] = jnp.zeros_like(small)
    weight_gradients(sz, digit_of(0), active, down_in, normed, up_in, both, keep, send)
    tap_gradients(sz, pad, grad_conv, tap_sums, small)
    fill_small(small, gain_sums, scale_sums)


def backward_kernel(
    sz, layer, base, own, first, second, lscale, down, normed, slope, active, branch,
    keep, send, flat, up_in, scale_sums,
    hidden, down_in, both,
):
    add_strips(sz, base, own, first, second, flat)
    for slab in range(sz.slabs):
        flat[slab] = flat[slab].astype(BF16).astype(F32)
    scale_rows(sz, flat_grad_row(sz, flat), branch, lscale, layer, down_in, scale_sums)
    hidden[...] = multiply(down_in[...], down[layer], 1, 1)
    slope_rows(sz, hidden, slope, up_in)
    weight_gradients(sz, digit_of(0), active, down_in, normed, up_in, both, keep, send)


def spread_kernel(
    sz, layer, seams, corners, kern, gain, up, flat, up_in, normal, inverse,
    base, grad_own, grad_below, grad_above, grad_conv, gain_sums,
    taps, branch, grad_pool, grad_pad,
):
    strip_at, corner_at = read_plan(sz, seams), read_plan(sz, corners)
    branch[...] = multiply(up_in[...], up[layer], 1, 1)
    norm_gradients(sz, branch, normal, inverse, gain, layer, grad_conv, gain_sums)
    hold_taps(sz, kern, layer, taps)
    spread_gradients(sz, grad_conv, taps, grad_pad)
    return_margins(sz, strip_at, corner_at, grad_pad, grad_pool)
    send_margins(sz, grad_pool, grad_own, grad_below, grad_above)
    gather_inner(sz, flat_grad_row(sz, flat), grad_pad, base)


def taps_kernel(sz, pad, grad_conv, gain_sums, scale_sums, other, both, tap_sums, small):
    small[...] = jnp.zeros_like(small)
    tap_gradients(sz, pad, grad_conv, tap_sums, small)
    fill_small(small, gain_sums, scale_sums)
    both[0:SMALL_ROWS] = small[...].astype(BF16)
    both[SMALL_ROWS : 2 * SMALL_ROWS] = other[...].astype(BF16)


def last_kernel(sz, base, own, first, second, out_hbm, token, flat, out, sems):
    token[...] = jnp.zeros_like(token)
    add_strips(sz, base, own, first, second, flat)
    row = flat_grad_row(sz, flat)
    for q in range(sz.tiles):
        for i in range(sz.edge):
            out[q, i] = row(q, i).astype(BF16)
    store = pltpu.make_async_copy(out, out_hbm, sems.at[0])
    store.start()
    store.wait()


def add_rows(out, parts):
    for start in range(0, out.shape[0], 16):
        rows = slice(start, start + 16)
        values = [part(rows).astype(F32) for part in parts]
        out[rows] = sum(values[1:], values[0]).astype(BF16)


def share_near_kernel(*refs):
    arrays, outs = refs[:4], refs[4:]
    for k, out in enumerate(outs):
        piece = digit_of(1) ^ k
        for layer in range(2):
            parts = arrays[2 * layer : 2 * layer + 2]
            add_rows(
                out.at[layer],
                [lambda rows, array=array: array[piece, rows] for array in parts],
            )


def share_far_kernel(*refs):
    arrays, outs = refs[:4], refs[4:]
    for k, out in enumerate(outs):
        piece = digit_of(2) ^ k
        for layer in range(2):
            add_rows(
                out.at[layer],
                [lambda rows, array=array: array[layer, piece, rows] for array in arrays],
            )


def total_kernel(*refs):
    out, small = refs[-1], refs[-2]
    for layer in range(2):
        add_rows(
            out.at[layer],
            [lambda rows, array=array: array[layer, rows] for array in refs[:-2]],
        )
    out[2:] = small[...]


def quarter_kernel(*refs):
    arrays, small, out = refs[:4], refs[4], refs[5]
    rest = arrays[0].shape[1]
    for piece in range(rest):
        for layer in range(2):
            add_rows(
                out.at[2 * piece + layer],
                [lambda rows, array=array: array[layer, piece, rows] for array in arrays],
            )
    out[2 * rest :] = small[...]


def pair_kernel(first, second, out):
    for j in range(out.shape[0]):
        add_rows(out.at[j], [lambda rows: first[j, rows], lambda rows: second[j, rows]])


def order_kernel(level, small_units, *refs):
    pieces, out, held = refs[:-2], refs[-2], refs[-1]
    units = pieces[0].shape[0] - small_units
    for k, piece in enumerate(pieces):
        place = digit_of(level) ^ k
        for j in range(units):
            out[place * units + j] = piece[j]
        held[place] = piece[units:]
    for j in range(small_units):
        add_rows(
            out.at[len(pieces) * units + j],
            [lambda rows, k=k: held[k, j, rows] for k in range(len(pieces))],
        )


def unpack_half(sz, half, source, staged, up_hbm, down_hbm, sems):
    share = source.shape[1]
    target = (down_hbm, up_hbm)[half]
    pieces = sz.hidden // share
    copies = []
    for layer in range(2):
        for j in range(pieces):
            value = source[2 * j + layer].astype(F32)
            if half == 0:
                staged[layer, j * share : (j + 1) * share] = value
            else:
                k, c = divmod(j * share, sz.channels)
                staged[layer, k * sz.channels + c : k * sz.channels + c + share] = value
        for k in range(sz.hidden // sz.channels):
            rows = pl.ds(k * sz.channels, sz.channels)
            place = target.at[layer, rows] if half == 0 else target.at[layer, :, rows]
            copy = pltpu.make_async_copy(
                staged.at[layer, rows], place, sems.at[half, len(copies)]
            )
            copy.start()
            copies.append(copy)
    for copy in copies:
        copy.wait()


def unpack_mine_kernel(sz, mine, up_hbm, down_hbm, staged, sems):
    for half in range(2):

        @pl.when(digit_of(0) == half)
        def _(half=half):
            unpack_half(sz, half, mine, staged, up_hbm, down_hbm, sems)


def unpack_theirs_kernel(
    sz, mine, theirs, _up, _down, up_hbm, down_hbm, kernel_out, gain_out, scale_out,
    staged, small, sems,
):
    for half in range(2):

        @pl.when(digit_of(0) == 1 - half)
        def _(half=half):
            unpack_half(sz, half, theirs, staged, up_hbm, down_hbm, sems)

    share = mine.shape[1]
    start = 2 * sz.hidden // share
    for j in range(start, mine.shape[0]):
        rows = pl.ds((j - start) * share, share)
        small[rows, :] = mine[j].astype(F32) + theirs[j].astype(F32)
    for layer in range(2):
        at = layer * SMALL_ROWS
        for a in range(TAPS):
            for b in range(TAPS):
                kernel_out[a, b, layer : layer + 1] = small[pl.ds(at + a * 8 + b, 1), :]
        at = at + TAPS * 8
        gain_out[layer : layer + 1] = small[pl.ds(at, 1), :]
        scale_out[layer : layer + 1] = small[pl.ds(at + 1, 1), :]


IN_VMEM = pl.BlockSpec(memory_space=pltpu.VMEM)
IN_SMEM = pl.BlockSpec(memory_space=pltpu.SMEM)
IN_HBM = pl.BlockSpec(memory_space=pltpu.HBM)


def call(body, name, micros, ins, outs, scratch, after=(), aliases={}):
    count = len(ins)

    def run(*refs):
        body(*refs[:count], *refs[count + len(after) :])

    return pl.pallas_call(
        run,
        in_specs=[spec for spec, _ in ins] + [pl.BlockSpec(memory_space=pl.ANY)] * len(after),
        out_specs=[spec for spec, _ in outs],
        out_shape=[out for _, out in outs],
        scratch_shapes=scratch,
        compiler_params=pltpu.CompilerParams(vmem_limit_bytes=24 * 1024 * 1024),
        cost_estimate=pl.CostEstimate(
            flops=0, bytes_accessed=int(micros * 3.5e6), transcendentals=0
        ),
        input_output_aliases=aliases,
        name=name,
    )(*[array for _, array in ins], *after)


def near(*arrays):
    return [(IN_VMEM, array) for array in arrays]


def far(*arrays):
    return [(IN_HBM, array) for array in arrays]


def pass_on(shard, by):
    length = lax.axis_size("tile")
    return lax.ppermute(shard, "tile", [(i, (i + by) % length) for i in range(length)])


def partners(array, masks):
    length = lax.axis_size("tile")
    return [
        lax.ppermute(array, "tile", [(i, i ^ mask) for i in range(length)]) for mask in masks
    ]


def swap(arrays, masks):
    length = lax.axis_size("tile")
    return [
        lax.ppermute(array, "tile", [(i, i ^ mask) for i in range(length)])
        for array, mask in zip(arrays, masks)
    ]


class Reduction:
    def __init__(self, devices):
        self.devices = devices
        self.rest = devices // 8
        self.near_masks = [2 * k for k in range(1, 4)]
        self.rest_masks = [8 * k for k in range(1, self.rest)]

    def start(self, halves_of_layers):
        arrays = []
        for keep, send in halves_of_layers:
            rows, channels = keep.shape
            dims = (4, rows // 4, channels)
            arrays += [keep.reshape(dims), swap([send], [1])[0].reshape(dims)]
        shape = jax.ShapeDtypeStruct((2,) + dims[1:], BF16)
        pieces = call(
            share_near_kernel, "share_near", 1.2, near(*arrays), near(*[shape] * 4), [],
        )
        return [pieces[0]] + swap(pieces[1:], self.near_masks)

    def finish(self, parts, after, small, beside):
        _, quarter, channels = parts[0].shape
        dims = (2, self.rest, quarter // self.rest, channels)
        arrays = [part.reshape(dims) for part in parts]
        if self.rest == 2:
            small = small(after).reshape((-1,) + dims[2:])
            shape = jax.ShapeDtypeStruct((2 * self.rest + small.shape[0],) + dims[2:], BF16)
            (total,) = call(
                quarter_kernel, "quarter", 0.9, near(*arrays, small), near(shape), []
            )
            (total,) = call(
                pair_kernel, "pair", 0.5, near(total, *partners(total, [8])), near(shape), [],
                beside,
            )
            return total, small.shape[0]
        shape = jax.ShapeDtypeStruct((2,) + dims[2:], BF16)
        pieces = call(
            share_far_kernel, "share_far", 0.9,
            near(*arrays), near(*[shape] * self.rest), [], (after,),
        )
        arrived = swap(pieces[1:], self.rest_masks)
        small = small(pieces[0]).reshape((-1,) + dims[2:])
        shape = jax.ShapeDtypeStruct((2 + small.shape[0],) + dims[2:], BF16)
        (total,) = call(
            total_kernel, "total", 0.4, near(pieces[0], *arrived, small), near(shape), [],
            beside,
        )
        return total, small.shape[0]

    def gather(self, total, small_units):
        levels = [(1, self.near_masks, "order_near")]
        if self.rest != 2:
            levels = [(2, self.rest_masks, "order_far")] + levels
        for level, masks, name in levels:
            pieces = [total] + partners(total, masks)
            units = (total.shape[0] - small_units) * len(pieces) + small_units
            shape = jax.ShapeDtypeStruct((units,) + total.shape[1:], BF16)
            (total,) = call(
                functools.partial(order_kernel, level, small_units), name, 0.5,
                near(*pieces), near(shape),
                [pltpu.VMEM((len(pieces), small_units) + total.shape[1:], BF16)],
            )
        return total, partners(total, [1])[0]


def on_device(
    inputs,
    out_grad,
    kernel,
    norm_gain,
    up_weight,
    down_weight,
    layer_scale,
    seam_table,
    corner_table,
):
    tiles, edge, _, channels = inputs.shape
    layers, _, hidden = up_weight.shape
    sz = Sizes(tiles, edge, channels, hidden)
    columns = lax.axis_size("tile")
    plan = [(IN_SMEM, table.transpose((1, 2, 0))) for table in (seam_table, corner_table)]
    kern = kernel.transpose((1, 2, 0, 3))
    gain, lscale, up, down = norm_gain, layer_scale, up_weight, down_weight
    reduction = Reduction(columns)

    shape = jax.ShapeDtypeStruct
    image = shape(inputs.shape, BF16)
    strips_shape = shape((sz.pieces, REACH, edge, channels), BF16)
    slabs = shape((sz.slabs, sz.cells, LANES), F32)
    padded = shape((sz.slabs, sz.outer * PITCH, LANES), F32)
    inverses = shape((tiles, sz.cells, LANES), F32)
    narrow_short = shape((sz.rows, channels), BF16)
    wide_short = shape((sz.rows, hidden), BF16)
    narrow = shape((sz.rows, channels), F32)
    wide = shape((sz.rows, hidden), F32)
    sums = shape((edge, channels), F32)
    grad_slabs = shape((sz.slabs, edge * GRAD_PITCH, LANES), F32)
    own_shape = shape((sz.pieces, REACH, sz.lanes, edge, LANES), F32)
    pool = shape((3 * sz.pieces, REACH, edge, channels), BF16)
    grad_pool = shape((3 * sz.pieces, REACH, sz.lanes, edge, LANES), F32)
    taps = shape((sz.lanes, TAPS * 8, LANES), F32)
    tap_sums = shape((sz.lanes, TAPS * TAPS, 8, LANES), F32)
    small = shape((SMALL_ROWS, channels), F32)
    half = shape((hidden, channels), BF16)
    two_halves = shape((2, hidden, channels), BF16)

    def vmem(*shapes):
        return [pltpu.VMEM(one.shape, one.dtype) for one in shapes]

    def sems(count):
        return [pltpu.SemaphoreType.DMA((count,))]

    strips, inputs = call(
        functools.partial(strips_kernel, sz),
        "strips", 0.3,
        near(inputs),
        near(strips_shape, image),
        vmem(slabs),
    )
    below, above = pass_on(strips, 1), pass_on(strips, -1)
    fetched = (kern, gain, lscale, up, down)
    kern, gain, lscale, up, down = call(
        fetch_kernel,
        "fetch", 2.0,
        far(*fetched),
        near(*[shape(one.shape, one.dtype) for one in fetched]),
        sems(len(fetched)),
        (strips,),
    )
    middle, strips, pad_zero, normal, inverse, normed, slope, active, branch = call(
        functools.partial(forward_kernel, sz, 0),
        "forward", 8.7,
        plan + near(inputs, strips, below, above, kern, gain, lscale, up, down),
        near(
            image, strips_shape, padded, slabs, inverses,
            narrow_short, wide_short, wide_short, narrow,
        ),
        vmem(pool, taps, slabs, wide, slabs),
    )
    below, above = pass_on(strips, 1), pass_on(strips, -1)
    result, base, grad_own, grad_below, grad_above, *for_weights = call(
        functools.partial(turn_kernel, sz, 1),
        "turn", 15.4,
        plan + near(middle, strips, below, above, kern, gain, lscale, up, down, out_grad),
        far(image)
        + near(
            slabs, own_shape, strips_shape, strips_shape,
            padded, grad_slabs, narrow_short, wide_short, narrow_short, wide_short, sums, sums,
        ),
        vmem(
            pool, taps, slabs, wide, image, slabs, inverses, wide_short, narrow, grad_pool, padded
        )
        + sems(1),
    )
    from_below, from_above = pass_on(grad_above, 1), pass_on(grad_below, -1)
    keep_one, send_one, small_one = call(
        functools.partial(weights_kernel, sz),
        "weights", 2.8,
        near(*for_weights),
        near(half, half, small),
        vmem(tap_sums, two_halves),
    )
    keep_zero, send_zero, flat, up_in, scale_sums = call(
        functools.partial(backward_kernel, sz, 0),
        "backward", 2.9,
        near(
            base, grad_own, from_below, from_above, lscale, down, normed, slope, active, branch
        ),
        near(half, half, slabs, wide_short, sums),
        vmem(wide, narrow_short, two_halves),
    )
    parts = reduction.start(((keep_zero, send_zero), (keep_one, send_one)))
    base, grad_own, grad_below, grad_above, grad_conv, gain_sums = call(
        functools.partial(spread_kernel, sz, 0),
        "spread", 6.0,
        plan + near(kern, gain, up, flat, up_in, normal, inverse),
        near(slabs, own_shape, strips_shape, strips_shape, grad_slabs, sums),
        vmem(taps, narrow, grad_pool, padded),
        (parts[0],),
    )
    from_below, from_above = pass_on(grad_above, 1), pass_on(grad_below, -1)

    def small_gradients(share):
        (both,) = call(
            functools.partial(taps_kernel, sz),
            "taps", 2.1,
            near(pad_zero, grad_conv, gain_sums, scale_sums, small_one),
            near(shape((2 * SMALL_ROWS, channels), BF16)),
            vmem(tap_sums, small),
            (share,),
        )
        return both

    in_grad, token = call(
        functools.partial(last_kernel, sz),
        "last", 1.0,
        near(base, grad_own, from_below, from_above),
        far(image) + near(shape((8, LANES), F32)),
        vmem(slabs, image) + sems(1),
    )
    total, small_units = reduction.finish(
        parts, gain_sums, small_gradients, (token,)
    )
    mine, theirs = reduction.gather(total, small_units)
    weight_shapes = [shape(up_weight.shape, F32), shape(down_weight.shape, F32)]
    copies = layers * hidden // channels
    scratch = vmem(shape(down_weight.shape, F32))
    grad_up, grad_down = call(
        functools.partial(unpack_mine_kernel, sz),
        "unpack_mine", 1.5,
        near(mine),
        far(*weight_shapes),
        scratch + [pltpu.SemaphoreType.DMA((2, copies))],
    )
    grad_up, grad_down, grad_kernel, grad_gain, grad_scale = call(
        functools.partial(unpack_theirs_kernel, sz),
        "unpack_theirs", 1.5,
        near(mine, theirs) + far(grad_up, grad_down),
        far(*weight_shapes)
        + near(
            shape(kern.shape, F32), shape(norm_gain.shape, F32), shape(norm_gain.shape, F32)
        ),
        scratch
        + vmem(shape((2 * SMALL_ROWS, channels), F32))
        + [pltpu.SemaphoreType.DMA((2, copies))],
        aliases={2: 0, 3: 1},
    )
    return (
        result, in_grad, grad_kernel.transpose((2, 0, 1, 3)),
        grad_gain, grad_up, grad_down, grad_scale,
    )


def solution(mesh):
    placed = (
        P(("groups", "tile"), None, None, None),
        P(("groups", "tile"), None, None, None),
        P(),
        P(),
        P(),
        P(),
        P(),
        P(),
        P(),
    )
    return jax.shard_map(
        on_device,
        mesh=mesh,
        in_specs=placed,
        out_specs=(
            P(("groups", "tile"), None, None, None),
            P(("groups", "tile"), None, None, None),
            P("groups", None, None, None),
            P("groups", None),
            P("groups", None, None),
            P("groups", None, None),
            P("groups", None),
        ),
        check_vma=False,
    )
```

```python
import functools

import jax
import jax.numpy as jnp
from jax import lax
from jax.experimental import pallas as pl
from jax.experimental.pallas import tpu as pltpu
from jax.sharding import PartitionSpec as P

epsilon = 1e-06
inverse_root_two = 0.7071067811865476
inverse_root_tau = 0.3989422804014327

LANES = 128
TAPS = 7
REACH = 3
PITCH = 24
GRAD_PITCH = 32
SMALL_ROWS = 64
F32 = jnp.float32
BF16 = jnp.bfloat16


def flip_rows(value):
    rows = value.shape[0]
    order = 7 - lax.broadcasted_iota(jnp.int32, (8, LANES), 0)
    parts = [
        jnp.take_along_axis(value[at : at + 8], order, axis=0, mode="promise_in_bounds")
        for at in range(0, rows, 8)
    ]
    return jnp.concatenate(parts[::-1], axis=0)


def halves(value):
    return [value[:, at : at + LANES] for at in range(0, value.shape[1], LANES)]


class Sizes:
    def __init__(self, tiles, edge, channels, hidden):
        self.tiles = tiles
        self.edge = edge
        self.channels = channels
        self.hidden = hidden
        self.lanes = channels // LANES
        self.cells = edge * edge
        self.rows = tiles * edge * edge
        self.pieces = tiles * 4
        self.outer = edge + 2 * REACH
        self.slabs = tiles * self.lanes

    def key(self):
        return (self.tiles, self.edge, self.channels, self.hidden)


def strip_window(edge, side, row):
    if side == 0:
        return pl.ds(row * edge, edge), False
    if side == 1:
        return pl.ds(edge - 1 - row, edge, stride=edge), False
    if side == 2:
        return pl.ds((edge - 1 - row) * edge, edge), True
    return pl.ds(row, edge, stride=edge), True


def margin_window(edge, side, row):
    last = edge + 2 * REACH - 1
    if side == 0:
        return pl.ds((2 - row) * PITCH + REACH, edge), True
    if side == 1:
        return pl.ds(REACH * PITCH + last - 2 + row, edge, stride=PITCH), True
    if side == 2:
        return pl.ds((last - 2 + row) * PITCH + REACH, edge), False
    return pl.ds(REACH * PITCH + 2 - row, edge, stride=PITCH), False


def corner_cell(edge, corner, row, column):
    last = edge + 2 * REACH - 1
    r, x = 2 - row, 2 - column
    if corner == 0:
        at = (r, x)
    elif corner == 1:
        at = (x, last - r)
    elif corner == 2:
        at = (last - r, last - x)
    else:
        at = (last - x, r)
    return at[0] * PITCH + at[1]


def read_plan(sz, table):
    columns = lax.axis_size("tile")
    device = lax.axis_index("tile")
    below = lax.rem(device + columns - 1, columns)
    plan = []
    for q in range(sz.tiles):
        for side in range(4):
            source = table[side, 0, device * sz.tiles + q]
            owner = lax.div(source, sz.tiles)
            local = (source - owner * sz.tiles) * 4 + table[side, 1, device * sz.tiles + q]
            shift = jnp.where(
                owner == device, 0, jnp.where(owner == below, sz.pieces, 2 * sz.pieces)
            )
            plan.append(shift + local)
    return plan


def digit_of(level):
    device = lax.axis_index("tile")
    if level == 0:
        return lax.rem(device, 2)
    if level == 1:
        return lax.rem(lax.div(device, 2), 4)
    return lax.div(device, 8)


def write_strips(sz, flat, strips_ref):
    for q in range(sz.tiles):
        for side in range(4):
            for row in range(REACH):
                window, turned = strip_window(sz.edge, side, row)
                parts = [flat[q * sz.lanes + h, window, :] for h in range(sz.lanes)]
                if turned:
                    parts = [flip_rows(part) for part in parts]
                strips_ref[q * 4 + side, row] = jnp.concatenate(parts, axis=1).astype(BF16)


def surround(sz, strip_at, corner_at, cur, own, below, above, pool, pad):
    pool[0 : sz.pieces] = own[...]
    pool[sz.pieces : 2 * sz.pieces] = below[...]
    pool[2 * sz.pieces : 3 * sz.pieces] = above[...]
    for q in range(sz.tiles):
        for i in range(sz.edge):
            for h, part in enumerate(halves(cur[q, i].astype(F32))):
                pad[q * sz.lanes + h, pl.ds((i + REACH) * PITCH + REACH, sz.edge), :] = part
    for q in range(sz.tiles):
        for side in range(4):
            piece = strip_at[q * 4 + side]
            for row in range(REACH):
                window, turned = margin_window(sz.edge, side, row)
                for h, part in enumerate(halves(pool[piece, row].astype(F32))):
                    pad[q * sz.lanes + h, window, :] = flip_rows(part) if turned else part
            piece = corner_at[q * 4 + side]
            for row in range(REACH):
                for h, part in enumerate(halves(pool[piece, row].astype(F32))):
                    for column in range(REACH):
                        at = corner_cell(sz.edge, side, row, column)
                        pad[q * sz.lanes + h, pl.ds(at, 1), :] = part[column : column + 1]


def hold_taps(sz, kern, layer, taps):
    for a in range(TAPS):
        for b in range(TAPS):
            for h, part in enumerate(halves(kern[a, b, layer : layer + 1])):
                taps[h, pl.ds(a * 8 + b, 1), :] = part


def tap(taps, h, a, b):
    return jnp.broadcast_to(taps[h, pl.ds(a * 8 + b, 1), :], (8, LANES))


def convolve(sz, pad, taps, conv):
    @pl.loop(0, sz.slabs)
    def _(slab):
        h = lax.rem(slab, sz.lanes)
        for g in range(sz.edge // 8):
            acc = [None] * sz.edge
            for b in range(TAPS):
                weights = [tap(taps, h, a, b) for a in range(TAPS)]
                for r in range(sz.outer):
                    x = pad[slab, pl.ds(r * PITCH + b + 8 * g, 8), :]
                    for a in range(TAPS):
                        i = r - a
                        if 0 <= i < sz.edge:
                            term = x * weights[a]
                            acc[i] = term if acc[i] is None else acc[i] + term
            for i in range(sz.edge):
                conv[slab, pl.ds(i * sz.edge + 8 * g, 8), :] = acc[i]


def normalise(sz, conv, gain, layer, normal, inverse, normed):
    scale = 1.0 / sz.channels
    for q in range(sz.tiles):

        @pl.loop(0, sz.edge, unroll=2)
        def _(i):
            at = pl.ds(pl.multiple_of(i * sz.edge, sz.edge), sz.edge)
            parts = [conv[q * sz.lanes + h, at, :] for h in range(sz.lanes)]
            mean = jnp.sum(sum(parts[1:], parts[0]), axis=-1, keepdims=True) * scale
            parts = [part - mean for part in parts]
            squares = [part * part for part in parts]
            variance = jnp.sum(sum(squares[1:], squares[0]), axis=-1, keepdims=True) * scale
            root = lax.rsqrt(variance + epsilon)
            inverse[q, at, :] = jnp.broadcast_to(root, (sz.edge, LANES))
            flat_at = pl.ds(pl.multiple_of(q * sz.cells + i * sz.edge, sz.edge), sz.edge)
            for h, part in enumerate(parts):
                part = part * root
                normal[q * sz.lanes + h, at, :] = part
                gains = gain[layer : layer + 1, h * LANES : (h + 1) * LANES]
                normed[flat_at, h * LANES : (h + 1) * LANES] = (part * gains).astype(BF16)


def activate(sz, upward, active, slope):
    width = 512

    @pl.loop(0, sz.rows // 16)
    def _(t):
        at = pl.ds(pl.multiple_of(t * 16, 16), 16)
        for start in range(0, sz.hidden, width):
            u = upward[at, start : start + width]
            chance = 0.5 * (1.0 + lax.erf(u * inverse_root_two))
            active[at, start : start + width] = (u * chance).astype(BF16)
            slope[at, start : start + width] = (
                chance + u * jnp.exp(-0.5 * u * u) * inverse_root_tau
            ).astype(slope.dtype)


def multiply(a, b, ca=1, cb=0):
    return lax.dot_general(a, b, (((ca,), (cb,)), ((), ())), preferred_element_type=F32)


def finish_forward(sz, cur, branch, lscale, layer, out, flat):
    for q in range(sz.tiles):

        @pl.loop(0, sz.edge, unroll=2)
        def _(i):
            at = pl.ds(pl.multiple_of(q * sz.cells + i * sz.edge, sz.edge), sz.edge)
            value = cur[q, i].astype(F32) + branch[at, :] * lscale[layer : layer + 1, :]
            value = value.astype(BF16)
            out[q, i] = value
            if flat is not None:
                local = pl.ds(pl.multiple_of(i * sz.edge, sz.edge), sz.edge)
                for h, part in enumerate(halves(value.astype(F32))):
                    flat[q * sz.lanes + h, local, :] = part


def scale_rows(sz, grad_row, branch, lscale, layer, down_in, sums):
    sums[...] = jnp.zeros_like(sums)
    for q in range(sz.tiles):

        @pl.loop(0, sz.edge, unroll=2)
        def _(i):
            at = pl.ds(pl.multiple_of(q * sz.cells + i * sz.edge, sz.edge), sz.edge)
            g = grad_row(q, i)
            down_in[at, :] = (g * lscale[layer : layer + 1, :]).astype(BF16)
            sums[...] += g * branch[at, :]


def slope_rows(sz, grad_active, slope, up_in):
    @pl.loop(0, sz.rows // 16, unroll=2)
    def _(t):
        at = pl.ds(pl.multiple_of(t * 16, 16), 16)
        up_in[at, :] = (grad_active[at, :] * slope[at, :].astype(F32)).astype(BF16)


def weight_gradients(sz, core, active, down_in, normed, up_in, both, keep, send):
    both[0] = multiply(active[...], down_in[...], 0, 0).astype(BF16)
    for k in range(sz.hidden // sz.channels):
        part = multiply(normed[...], up_in[:, k * sz.channels : (k + 1) * sz.channels], 0, 0)
        both[1, k * sz.channels : (k + 1) * sz.channels, :] = part.astype(BF16)
    keep[...] = both[core]
    send[...] = both[1 - core]


def norm_gradients(sz, grad_normed, normal, inverse, gain, layer, grad_conv, sums):
    scale = 1.0 / sz.channels
    sums[...] = jnp.zeros_like(sums)
    blank = jnp.zeros((8, LANES), F32)
    for q in range(sz.tiles):

        @pl.loop(0, sz.edge, unroll=2)
        def _(i):
            at = pl.ds(pl.multiple_of(q * sz.cells + i * sz.edge, sz.edge), sz.edge)
            local = pl.ds(pl.multiple_of(i * sz.edge, sz.edge), sz.edge)
            g = halves(grad_normed[at, :])
            n = [normal[q * sz.lanes + h, local, :] for h in range(sz.lanes)]
            sums[...] += jnp.concatenate([a * b for a, b in zip(g, n)], axis=1)
            s = [
                part * gain[layer : layer + 1, h * LANES : (h + 1) * LANES]
                for h, part in enumerate(g)
            ]
            products = [a * b for a, b in zip(s, n)]
            mean = jnp.sum(sum(s[1:], s[0]), axis=-1, keepdims=True) * scale
            slant = jnp.sum(sum(products[1:], products[0]), axis=-1, keepdims=True) * scale
            root = inverse[q, local, :]
            for h in range(sz.lanes):
                slab = q * sz.lanes + h
                base = pl.multiple_of(i * GRAD_PITCH, GRAD_PITCH)
                grad_conv[slab, pl.ds(base, 8), :] = blank
                grad_conv[slab, pl.ds(base + 8, sz.edge), :] = root * (s[h] - mean - n[h] * slant)
                grad_conv[slab, pl.ds(base + 8 + sz.edge, 8), :] = blank


def tap_gradients(sz, pad, grad_conv, tap_sums, small):
    tap_sums[...] = jnp.zeros_like(tap_sums)

    @pl.loop(0, sz.slabs)
    def _(slab):
        h = lax.rem(slab, sz.lanes)
        for b in range(TAPS):
            acc = [None] * TAPS
            for g in range(sz.edge // 8):
                grads = [
                    grad_conv[slab, pl.ds(i * GRAD_PITCH + 8 + 8 * g, 8), :]
                    for i in range(sz.edge)
                ]
                for r in range(sz.outer):
                    x = pad[slab, pl.ds(r * PITCH + b + 8 * g, 8), :]
                    for a in range(TAPS):
                        i = r - a
                        if 0 <= i < sz.edge:
                            term = x * grads[i]
                            acc[a] = term if acc[a] is None else acc[a] + term
            for a in range(TAPS):
                tap_sums[h, a * TAPS + b] += acc[a]

    for h in range(sz.lanes):
        for k in range(TAPS * TAPS):
            row = k // TAPS * 8 + k % TAPS
            small[row : row + 1, h * LANES : (h + 1) * LANES] = jnp.sum(
                tap_sums[h, k], axis=0, keepdims=True
            )


def spread_gradients(sz, grad_conv, taps, grad_pad):
    @pl.loop(0, sz.slabs)
    def _(slab):
        h = lax.rem(slab, sz.lanes)
        for g in range(PITCH // 8):
            acc = [None] * sz.outer
            for b in range(TAPS):
                start = 8 * g - b + 8
                if start >= 8 + sz.edge:
                    continue
                weights = [tap(taps, h, a, b) for a in range(TAPS)]
                for i in range(sz.edge):
                    x = grad_conv[slab, pl.ds(i * GRAD_PITCH + start, 8), :]
                    for a in range(TAPS):
                        term = x * weights[a]
                        acc[i + a] = term if acc[i + a] is None else acc[i + a] + term
            for p in range(sz.outer):
                grad_pad[slab, pl.ds(p * PITCH + 8 * g, 8), :] = acc[p]


def return_margins(sz, strip_at, corner_at, grad_pad, pool):
    pool[...] = jnp.zeros_like(pool)
    for q in range(sz.tiles):
        for side in range(4):
            piece = strip_at[q * 4 + side]
            for row in range(REACH):
                window, turned = margin_window(sz.edge, side, row)
                for h in range(sz.lanes):
                    part = grad_pad[q * sz.lanes + h, window, :]
                    pool[piece, row, h] = flip_rows(part) if turned else part
    for q in range(sz.tiles):
        for side in range(4):
            piece = corner_at[q * 4 + side]
            for row in range(REACH):
                for column in range(REACH):
                    at = corner_cell(sz.edge, side, row, column)
                    for h in range(sz.lanes):
                        pool[piece, row, h, pl.ds(column, 1), :] += grad_pad[
                            q * sz.lanes + h, pl.ds(at, 1), :
                        ]


def send_margins(sz, pool, own, below, above):
    own[...] = pool[0 : sz.pieces]
    for piece in range(sz.pieces):
        for row in range(REACH):
            for offset, ref in ((1, below), (2, above)):
                parts = [pool[offset * sz.pieces + piece, row, h] for h in range(sz.lanes)]
                ref[piece, row] = jnp.concatenate(parts, axis=1).astype(BF16)


def gather_inner(sz, grad_row, grad_pad, base):
    for q in range(sz.tiles):
        for i in range(sz.edge):
            for h, part in enumerate(halves(grad_row(q, i))):
                slab = q * sz.lanes + h
                base[slab, pl.ds(i * sz.edge, sz.edge), :] = (
                    part + grad_pad[slab, pl.ds((i + REACH) * PITCH + REACH, sz.edge), :]
                )


def add_strips(sz, base, own, first, second, flat):
    flat[...] = base[...]
    for q in range(sz.tiles):
        for side in range(4):
            piece = q * 4 + side
            for row in range(REACH):
                window, turned = strip_window(sz.edge, side, row)
                came = first[piece, row].astype(F32) + second[piece, row].astype(F32)
                for h, part in enumerate(halves(came)):
                    part = part + own[piece, row, h]
                    flat[q * sz.lanes + h, window, :] += flip_rows(part) if turned else part


def fill_small(small, gain_sums, scale_sums):
    small[TAPS * 8 : TAPS * 8 + 1, :] = jnp.sum(gain_sums[...], axis=0, keepdims=True)
    small[TAPS * 8 + 1 : TAPS * 8 + 2, :] = jnp.sum(scale_sums[...], axis=0, keepdims=True)


def flat_grad_row(sz, flat):
    def row(q, i):
        at = pl.ds(i * sz.edge, sz.edge)
        parts = [flat[q * sz.lanes + h, at, :] for h in range(sz.lanes)]
        return jnp.concatenate(parts, axis=1)

    return row


def fetch_kernel(*refs):
    count = (len(refs) - 1) // 2
    copies = [
        pltpu.make_async_copy(refs[k], refs[count + k], refs[-1].at[k]) for k in range(count)
    ]
    for copy in copies:
        copy.start()
    for copy in copies:
        copy.wait()


def strips_kernel(sz, cur, strips, held, flat):
    held[...] = cur[...]
    for q in range(sz.tiles):
        for i in range(sz.edge):
            for h, part in enumerate(halves(cur[q, i].astype(F32))):
                flat[q * sz.lanes + h, pl.ds(i * sz.edge, sz.edge), :] = part
    write_strips(sz, flat, strips)


def forward_kernel(
    sz, layer, seams, corners, cur, own, below, above, kern, gain, lscale, up, down,
    out, strips, pad, normal, inverse, normed, slope, active, branch,
    pool, taps, conv, upward, flat,
):
    strip_at, corner_at = read_plan(sz, seams), read_plan(sz, corners)
    surround(sz, strip_at, corner_at, cur, own, below, above, pool, pad)
    hold_taps(sz, kern, layer, taps)
    convolve(sz, pad, taps, conv)
    normalise(sz, conv, gain, layer, normal, inverse, normed)
    upward[...] = multiply(normed[...], up[layer])
    activate(sz, upward, active, slope)
    branch[...] = multiply(active[...], down[layer])
    finish_forward(sz, cur, branch, lscale, layer, out, flat)
    write_strips(sz, flat, strips)


def turn_kernel(
    sz, layer, seams, corners, cur, own, below, above, kern, gain, lscale, up, down, out_grad,
    out_hbm, base, grad_own, grad_below, grad_above,
    pad, grad_conv, normed, active, down_in, up_in, gain_sums, scale_sums,
    pool, taps, conv, upward, out, normal, inverse, slope, branch, grad_pool, grad_pad, out_sem,
):
    strip_at, corner_at = read_plan(sz, seams), read_plan(sz, corners)
    surround(sz, strip_at, corner_at, cur, own, below, above, pool, pad)
    hold_taps(sz, kern, layer, taps)
    convolve(sz, pad, taps, conv)
    normalise(sz, conv, gain, layer, normal, inverse, normed)
    upward[...] = multiply(normed[...], up[layer])
    activate(sz, upward, active, slope)
    branch[...] = multiply(active[...], down[layer])
    finish_forward(sz, cur, branch, lscale, layer, out, None)
    store = pltpu.make_async_copy(out, out_hbm, out_sem.at[0])
    store.start()

    def grad_row(q, i):
        return out_grad[q, i].astype(F32)

    scale_rows(sz, grad_row, branch, lscale, layer, down_in, scale_sums)
    upward[...] = multiply(down_in[...], down[layer], 1, 1)
    slope_rows(sz, upward, slope, up_in)
    branch[...] = multiply(up_in[...], up[layer], 1, 1)
    norm_gradients(sz, branch, normal, inverse, gain, layer, grad_conv, gain_sums)
    spread_gradients(sz, grad_conv, taps, grad_pad)
    return_margins(sz, strip_at, corner_at, grad_pad, grad_pool)
    send_margins(sz, grad_pool, grad_own, grad_below, grad_above)
    gather_inner(sz, grad_row, grad_pad, base)
    store.wait()


def weights_kernel(
    sz, pad, grad_conv, normed, active, down_in, up_in, gain_sums, scale_sums,
    keep, send, small, tap_sums, both,
):
    small[...] = jnp.zeros_like(small)
    weight_gradients(sz, digit_of(0), active, down_in, normed, up_in, both, keep, send)
    tap_gradients(sz, pad, grad_conv, tap_sums, small)
    fill_small(small, gain_sums, scale_sums)


def backward_kernel(
    sz, layer, base, own, first, second, lscale, down, normed, slope, active, branch,
    keep, send, flat, up_in, scale_sums,
    hidden, down_in, both,
):
    add_strips(sz, base, own, first, second, flat)
    for slab in range(sz.slabs):
        flat[slab] = flat[slab].astype(BF16).astype(F32)
    scale_rows(sz, flat_grad_row(sz, flat), branch, lscale, layer, down_in, scale_sums)
    hidden[...] = multiply(down_in[...], down[layer], 1, 1)
    slope_rows(sz, hidden, slope, up_in)
    weight_gradients(sz, digit_of(0), active, down_in, normed, up_in, both, keep, send)


def spread_kernel(
    sz, layer, seams, corners, kern, gain, up, flat, up_in, normal, inverse,
    base, grad_own, grad_below, grad_above, grad_conv, gain_sums,
    taps, branch, grad_pool, grad_pad,
):
    strip_at, corner_at = read_plan(sz, seams), read_plan(sz, corners)
    branch[...] = multiply(up_in[...], up[layer], 1, 1)
    norm_gradients(sz, branch, normal, inverse, gain, layer, grad_conv, gain_sums)
    hold_taps(sz, kern, layer, taps)
    spread_gradients(sz, grad_conv, taps, grad_pad)
    return_margins(sz, strip_at, corner_at, grad_pad, grad_pool)
    send_margins(sz, grad_pool, grad_own, grad_below, grad_above)
    gather_inner(sz, flat_grad_row(sz, flat), grad_pad, base)


def taps_kernel(
    sz, pad, grad_conv, gain_sums, scale_sums, other, keep, send, tap_sums, small, both
):
    small[...] = jnp.zeros_like(small)
    tap_gradients(sz, pad, grad_conv, tap_sums, small)
    fill_small(small, gain_sums, scale_sums)
    both[0] = small[...]
    both[1] = other[...]
    keep[...] = both[digit_of(0)].astype(BF16)
    send[...] = both[1 - digit_of(0)].astype(BF16)


def last_kernel(sz, base, own, first, second, out_hbm, token, flat, out, sems):
    token[...] = jnp.zeros_like(token)
    add_strips(sz, base, own, first, second, flat)
    row = flat_grad_row(sz, flat)
    for q in range(sz.tiles):
        for i in range(sz.edge):
            out[q, i] = row(q, i).astype(BF16)
    store = pltpu.make_async_copy(out, out_hbm, sems.at[0])
    store.start()
    store.wait()


def add_rows(out, parts):
    for start in range(0, out.shape[0], 16):
        rows = slice(start, start + 16)
        values = [part(rows).astype(F32) for part in parts]
        out[rows] = sum(values[1:], values[0]).astype(BF16)


def share_near_kernel(*refs):
    arrays, outs = refs[:4], refs[4:]
    for k, out in enumerate(outs):
        piece = digit_of(1) ^ k
        for layer in range(2):
            parts = arrays[2 * layer : 2 * layer + 2]
            add_rows(
                out.at[layer],
                [lambda rows, array=array: array[piece, rows] for array in parts],
            )


def quarter_kernel(*refs):
    arrays, keep, came, out = refs[:4], refs[4], refs[5], refs[6]
    quarter = arrays[0].shape[1]
    for layer in range(2):
        add_rows(
            out.at[layer * quarter : (layer + 1) * quarter],
            [lambda rows, array=array: array[layer, rows] for array in arrays],
        )
    add_rows(out.at[2 * quarter :], [lambda rows: keep[rows], lambda rows: came[rows]])


def far_kernel(*refs):
    pieces, out, held = refs[:-2], refs[-2], refs[-1]
    if len(pieces) == 2:
        add_rows(out, [lambda rows: pieces[0][rows], lambda rows: pieces[1][rows]])
        return
    for k, piece in enumerate(pieces):
        held[digit_of(2) ^ k] = piece[...]
    add_rows(out, [lambda rows, k=k: held[k, rows] for k in range(len(pieces))])


def order_kernel(quarter, *refs):
    pieces, out, held = refs[:4], refs[4], refs[5]
    for k, piece in enumerate(pieces):
        place = digit_of(1) ^ k
        out[pl.ds(pl.multiple_of(place * quarter, quarter), quarter), :] = piece[0:quarter]
        if quarter < piece.shape[0]:
            held[place] = piece[quarter:]
    if out.shape[0] > 4 * quarter:
        add_rows(out.at[4 * quarter :], [lambda rows, k=k: held[k, rows] for k in range(4)])


def unpack_half(sz, half, source, staged, up_hbm, down_hbm, sems):
    copies = []
    size = sz.hidden // 4
    for layer in range(2):
        for k in range(4):
            start = (2 * k + layer) * size
            rows = slice(k * size, (k + 1) * size)
            staged[layer, rows] = source[start : start + size].astype(F32)
            if half == 0:
                pairs = [(rows, down_hbm.at[layer, rows])]
            else:
                pairs = []
                for at in range(k * size, (k + 1) * size, sz.channels):
                    columns = slice(at, at + sz.channels)
                    pairs.append((columns, up_hbm.at[layer, :, columns]))
            for part, place in pairs:
                copy = pltpu.make_async_copy(
                    staged.at[layer, part], place, sems.at[half, len(copies)]
                )
                copy.start()
                copies.append(copy)
    for copy in copies:
        copy.wait()


def unpack_mine_kernel(sz, mine, up_hbm, down_hbm, staged, sems):
    for half in range(2):

        @pl.when(digit_of(0) == half)
        def _(half=half):
            unpack_half(sz, half, mine, staged, up_hbm, down_hbm, sems)


def unpack_theirs_kernel(
    sz, mine, theirs, _up, _down, up_hbm, down_hbm, kernel_out, gain_out, scale_out,
    staged, small, sems,
):
    start = 2 * sz.hidden
    small[digit_of(0)] = mine[start:].astype(F32)
    small[1 - digit_of(0)] = theirs[start:].astype(F32)
    for layer in range(2):
        for a in range(TAPS):
            for b in range(TAPS):
                kernel_out[a, b, layer : layer + 1] = small[layer, pl.ds(a * 8 + b, 1), :]
        gain_out[layer : layer + 1] = small[layer, pl.ds(TAPS * 8, 1), :]
        scale_out[layer : layer + 1] = small[layer, pl.ds(TAPS * 8 + 1, 1), :]
    for half in range(2):

        @pl.when(digit_of(0) == 1 - half)
        def _(half=half):
            unpack_half(sz, half, theirs, staged, up_hbm, down_hbm, sems)


IN_VMEM = pl.BlockSpec(memory_space=pltpu.VMEM)
IN_SMEM = pl.BlockSpec(memory_space=pltpu.SMEM)
IN_HBM = pl.BlockSpec(memory_space=pltpu.HBM)


def call(body, name, micros, ins, outs, scratch, after=(), aliases={}):
    count = len(ins)

    def run(*refs):
        body(*refs[:count], *refs[count + len(after) :])

    return pl.pallas_call(
        run,
        in_specs=[spec for spec, _ in ins] + [pl.BlockSpec(memory_space=pl.ANY)] * len(after),
        out_specs=[spec for spec, _ in outs],
        out_shape=[out for _, out in outs],
        scratch_shapes=scratch,
        compiler_params=pltpu.CompilerParams(vmem_limit_bytes=24 * 1024 * 1024),
        cost_estimate=pl.CostEstimate(
            flops=0, bytes_accessed=int(micros * 3.5e6), transcendentals=0
        ),
        input_output_aliases=aliases,
        name=name,
    )(*[array for _, array in ins], *after)


def near(*arrays):
    return [(IN_VMEM, array) for array in arrays]


def far(*arrays):
    return [(IN_HBM, array) for array in arrays]


def pass_on(shard, by):
    length = lax.axis_size("tile")
    return lax.ppermute(shard, "tile", [(i, (i + by) % length) for i in range(length)])


def partners(array, masks):
    length = lax.axis_size("tile")
    return [
        lax.ppermute(array, "tile", [(i, i ^ mask) for i in range(length)]) for mask in masks
    ]


def swap(arrays, masks):
    length = lax.axis_size("tile")
    return [
        lax.ppermute(array, "tile", [(i, i ^ mask) for i in range(length)])
        for array, mask in zip(arrays, masks)
    ]


class Reduction:
    def __init__(self, devices):
        self.near_masks = [2 * k for k in range(1, 4)]
        self.far_masks = [8 * k for k in range(1, devices // 8)]

    def share(self, *halves_of_layers):
        arrays = []
        for keep, send in halves_of_layers:
            rows, channels = keep.shape
            dims = (4, rows // 4, channels)
            arrays += [keep.reshape(dims), swap([send], [1])[0].reshape(dims)]
        shape = jax.ShapeDtypeStruct((2,) + dims[1:], BF16)
        pieces = call(
            share_near_kernel, "share_near", 0.3, near(*arrays), near(*[shape] * 4), [],
        )
        return [pieces[0]] + swap(pieces[1:], self.near_masks)

    def quarters(self, parts, keep, send):
        _, rows, channels = parts[0].shape
        shape = jax.ShapeDtypeStruct((2 * rows + keep.shape[0], channels), BF16)
        (total,) = call(
            quarter_kernel, "quarter", 0.4,
            near(*parts, keep, *swap([send], [1])), near(shape), [],
        )
        return total

    def exchange(self, total, after=()):
        shape = jax.ShapeDtypeStruct(total.shape, BF16)
        pieces = [total] + partners(total, self.far_masks)
        held = (len(pieces),) + total.shape if len(pieces) > 2 else (1, 16, LANES)
        (total,) = call(
            far_kernel, "far", 0.3, near(*pieces), near(shape), [pltpu.VMEM(held, BF16)], after
        )
        return total

    def gather(self, total, quarter, after=()):
        rows, channels = total.shape
        shape = jax.ShapeDtypeStruct((3 * quarter + rows, channels), BF16)
        (whole,) = call(
            functools.partial(order_kernel, quarter), "order", 0.4,
            near(total, *partners(total, self.near_masks)), near(shape),
            [pltpu.VMEM((4, max(rows - quarter, 16), channels), BF16)], after,
        )
        return whole


def on_device(
    inputs,
    out_grad,
    kernel,
    norm_gain,
    up_weight,
    down_weight,
    layer_scale,
    seam_table,
    corner_table,
):
    tiles, edge, _, channels = inputs.shape
    layers, _, hidden = up_weight.shape
    sz = Sizes(tiles, edge, channels, hidden)
    columns = lax.axis_size("tile")
    plan = [(IN_SMEM, table.transpose((1, 2, 0))) for table in (seam_table, corner_table)]
    kern = kernel.transpose((1, 2, 0, 3))
    gain, lscale, up, down = norm_gain, layer_scale, up_weight, down_weight
    reduction = Reduction(columns)

    shape = jax.ShapeDtypeStruct
    image = shape(inputs.shape, BF16)
    strips_shape = shape((sz.pieces, REACH, edge, channels), BF16)
    slabs = shape((sz.slabs, sz.cells, LANES), F32)
    padded = shape((sz.slabs, sz.outer * PITCH, LANES), F32)
    inverses = shape((tiles, sz.cells, LANES), F32)
    narrow_short = shape((sz.rows, channels), BF16)
    wide_short = shape((sz.rows, hidden), BF16)
    narrow = shape((sz.rows, channels), F32)
    wide = shape((sz.rows, hidden), F32)
    sums = shape((edge, channels), F32)
    grad_slabs = shape((sz.slabs, edge * GRAD_PITCH, LANES), F32)
    own_shape = shape((sz.pieces, REACH, sz.lanes, edge, LANES), F32)
    pool = shape((3 * sz.pieces, REACH, edge, channels), BF16)
    grad_pool = shape((3 * sz.pieces, REACH, sz.lanes, edge, LANES), F32)
    taps = shape((sz.lanes, TAPS * 8, LANES), F32)
    tap_sums = shape((sz.lanes, TAPS * TAPS, 8, LANES), F32)
    small = shape((SMALL_ROWS, channels), F32)
    half = shape((hidden, channels), BF16)
    two_halves = shape((2, hidden, channels), BF16)

    def vmem(*shapes):
        return [pltpu.VMEM(one.shape, one.dtype) for one in shapes]

    def sems(count):
        return [pltpu.SemaphoreType.DMA((count,))]

    strips, inputs = call(
        functools.partial(strips_kernel, sz),
        "strips", 0.3,
        near(inputs),
        near(strips_shape, image),
        vmem(slabs),
    )
    below, above = pass_on(strips, 1), pass_on(strips, -1)
    fetched = (kern, gain, lscale, up, down)
    kern, gain, lscale, up, down = call(
        fetch_kernel,
        "fetch", 2.0,
        far(*fetched),
        near(*[shape(one.shape, one.dtype) for one in fetched]),
        sems(len(fetched)),
        (strips,),
    )
    middle, strips, pad_zero, normal, inverse, normed, slope, active, branch = call(
        functools.partial(forward_kernel, sz, 0),
        "forward", 8.7,
        plan + near(inputs, strips, below, above, kern, gain, lscale, up, down),
        near(
            image, strips_shape, padded, slabs, inverses,
            narrow_short, wide_short, wide_short, narrow,
        ),
        vmem(pool, taps, slabs, wide, slabs),
    )
    below, above = pass_on(strips, 1), pass_on(strips, -1)
    result, base, grad_own, grad_below, grad_above, *for_weights = call(
        functools.partial(turn_kernel, sz, 1),
        "turn", 15.4,
        plan + near(middle, strips, below, above, kern, gain, lscale, up, down, out_grad),
        far(image)
        + near(
            slabs, own_shape, strips_shape, strips_shape,
            padded, grad_slabs, narrow_short, wide_short, narrow_short, wide_short, sums, sums,
        ),
        vmem(
            pool, taps, slabs, wide, image, slabs, inverses, wide_short, narrow, grad_pool, padded
        )
        + sems(1),
    )
    from_below, from_above = pass_on(grad_above, 1), pass_on(grad_below, -1)
    keep_one, send_one, small_one = call(
        functools.partial(weights_kernel, sz),
        "weights", 2.8,
        near(*for_weights),
        near(half, half, small),
        vmem(tap_sums, two_halves),
    )
    keep_zero, send_zero, flat, up_in, scale_sums = call(
        functools.partial(backward_kernel, sz, 0),
        "backward", 2.9,
        near(
            base, grad_own, from_below, from_above, lscale, down, normed, slope, active, branch
        ),
        near(half, half, slabs, wide_short, sums),
        vmem(wide, narrow_short, two_halves),
    )
    parts = reduction.share((keep_zero, send_zero), (keep_one, send_one))
    base, grad_own, grad_below, grad_above, grad_conv, gain_sums = call(
        functools.partial(spread_kernel, sz, 0),
        "spread", 6.0,
        plan + near(kern, gain, up, flat, up_in, normal, inverse),
        near(slabs, own_shape, strips_shape, strips_shape, grad_slabs, sums),
        vmem(taps, narrow, grad_pool, padded),
        (parts[0],),
    )
    from_below, from_above = pass_on(grad_above, 1), pass_on(grad_below, -1)
    small_keep, small_send = call(
        functools.partial(taps_kernel, sz),
        "taps", 2.1,
        near(pad_zero, grad_conv, gain_sums, scale_sums, small_one),
        near(*[shape(small.shape, BF16)] * 2),
        vmem(tap_sums, small, shape((2,) + small.shape, F32)),
    )
    in_grad, token = call(
        functools.partial(last_kernel, sz),
        "last", 1.0,
        near(base, grad_own, from_below, from_above),
        far(image) + near(shape((8, LANES), F32)),
        vmem(slabs, image) + sems(1),
    )
    total = reduction.quarters(parts, small_keep, small_send)
    total = reduction.exchange(total, (token,))
    mine = reduction.gather(total, hidden // 2)
    theirs = partners(mine, [1])[0]
    weight_shapes = [shape(up_weight.shape, F32), shape(down_weight.shape, F32)]
    staged = shape((layers, hidden, channels), F32)
    copies = [pltpu.SemaphoreType.DMA((2, layers * hidden // channels))]
    grad_up, grad_down = call(
        functools.partial(unpack_mine_kernel, sz),
        "unpack_mine", 1.0,
        near(mine),
        far(*weight_shapes),
        vmem(staged) + copies,
    )
    grad_up, grad_down, grad_kernel, grad_gain, grad_scale = call(
        functools.partial(unpack_theirs_kernel, sz),
        "unpack_theirs", 1.3,
        near(mine, theirs) + far(grad_up, grad_down),
        far(*weight_shapes)
        + near(
            shape(kern.shape, F32), shape(norm_gain.shape, F32), shape(norm_gain.shape, F32)
        ),
        vmem(staged, shape((2,) + small.shape, F32)) + copies,
        aliases={2: 0, 3: 1},
    )
    return (
        result, in_grad, grad_kernel.transpose((2, 0, 1, 3)),
        grad_gain, grad_up, grad_down, grad_scale,
    )


def solution(mesh):
    placed = (
        P(("groups", "tile"), None, None, None),
        P(("groups", "tile"), None, None, None),
        P(),
        P(),
        P(),
        P(),
        P(),
        P(),
        P(),
    )
    return jax.shard_map(
        on_device,
        mesh=mesh,
        in_specs=placed,
        out_specs=(
            P(("groups", "tile"), None, None, None),
            P(("groups", "tile"), None, None, None),
            P("groups", None, None, None),
            P("groups", None),
            P("groups", None, None),
            P("groups", None, None),
            P("groups", None),
        ),
        check_vma=False,
    )
```

```python
import functools

import jax
import jax.numpy as jnp
from jax import lax
from jax.experimental import pallas as pl
from jax.experimental.pallas import tpu as pltpu
from jax.sharding import PartitionSpec as P

epsilon = 1e-06
inverse_root_two = 0.7071067811865476
inverse_root_tau = 0.3989422804014327

LANES = 128
TAPS = 7
REACH = 3
PITCH = 24
GRAD_PITCH = 32
SMALL_ROWS = 64
F32 = jnp.float32
BF16 = jnp.bfloat16


def flip_rows(value):
    rows = value.shape[0]
    order = 7 - lax.broadcasted_iota(jnp.int32, (8, LANES), 0)
    parts = [
        jnp.take_along_axis(value[at : at + 8], order, axis=0, mode="promise_in_bounds")
        for at in range(0, rows, 8)
    ]
    return jnp.concatenate(parts[::-1], axis=0)


def halves(value):
    return [value[:, at : at + LANES] for at in range(0, value.shape[1], LANES)]


class Sizes:
    def __init__(self, tiles, edge, channels, hidden):
        self.tiles = tiles
        self.edge = edge
        self.channels = channels
        self.hidden = hidden
        self.lanes = channels // LANES
        self.cells = edge * edge
        self.rows = tiles * edge * edge
        self.pieces = tiles * 4
        self.outer = edge + 2 * REACH
        self.slabs = tiles * self.lanes

    def key(self):
        return (self.tiles, self.edge, self.channels, self.hidden)


def strip_window(edge, side, row):
    if side == 0:
        return pl.ds(row * edge, edge), False
    if side == 1:
        return pl.ds(edge - 1 - row, edge, stride=edge), False
    if side == 2:
        return pl.ds((edge - 1 - row) * edge, edge), True
    return pl.ds(row, edge, stride=edge), True


def margin_window(edge, side, row):
    last = edge + 2 * REACH - 1
    if side == 0:
        return pl.ds((2 - row) * PITCH + REACH, edge), True
    if side == 1:
        return pl.ds(REACH * PITCH + last - 2 + row, edge, stride=PITCH), True
    if side == 2:
        return pl.ds((last - 2 + row) * PITCH + REACH, edge), False
    return pl.ds(REACH * PITCH + 2 - row, edge, stride=PITCH), False


def corner_cell(edge, corner, row, column):
    last = edge + 2 * REACH - 1
    r, x = 2 - row, 2 - column
    if corner == 0:
        at = (r, x)
    elif corner == 1:
        at = (x, last - r)
    elif corner == 2:
        at = (last - r, last - x)
    else:
        at = (last - x, r)
    return at[0] * PITCH + at[1]


def read_plan(sz, table):
    columns = lax.axis_size("tile")
    device = lax.axis_index("tile")
    below = lax.rem(device + columns - 1, columns)
    plan = []
    for q in range(sz.tiles):
        for side in range(4):
            source = table[side, 0, device * sz.tiles + q]
            owner = lax.div(source, sz.tiles)
            local = (source - owner * sz.tiles) * 4 + table[side, 1, device * sz.tiles + q]
            shift = jnp.where(
                owner == device, 0, jnp.where(owner == below, sz.pieces, 2 * sz.pieces)
            )
            plan.append(shift + local)
    return plan


def digit_of(level):
    device = lax.axis_index("tile")
    if level == 0:
        return lax.rem(device, 2)
    if level == 1:
        return lax.rem(lax.div(device, 2), 4)
    return lax.div(device, 8)


def write_strips(sz, flat, strips_ref):
    for q in range(sz.tiles):
        for side in range(4):
            for row in range(REACH):
                window, turned = strip_window(sz.edge, side, row)
                parts = [flat[q * sz.lanes + h, window, :] for h in range(sz.lanes)]
                if turned:
                    parts = [flip_rows(part) for part in parts]
                strips_ref[q * 4 + side, row] = jnp.concatenate(parts, axis=1).astype(BF16)


def surround(sz, strip_at, corner_at, cur, own, below, above, pool, pad):
    pool[0 : sz.pieces] = own[...]
    pool[sz.pieces : 2 * sz.pieces] = below[...]
    pool[2 * sz.pieces : 3 * sz.pieces] = above[...]
    for q in range(sz.tiles):
        for i in range(sz.edge):
            for h, part in enumerate(halves(cur[q, i].astype(F32))):
                pad[q * sz.lanes + h, pl.ds((i + REACH) * PITCH + REACH, sz.edge), :] = part
    for q in range(sz.tiles):
        for side in range(4):
            piece = strip_at[q * 4 + side]
            for row in range(REACH):
                window, turned = margin_window(sz.edge, side, row)
                for h, part in enumerate(halves(pool[piece, row].astype(F32))):
                    pad[q * sz.lanes + h, window, :] = flip_rows(part) if turned else part
            piece = corner_at[q * 4 + side]
            for row in range(REACH):
                for h, part in enumerate(halves(pool[piece, row].astype(F32))):
                    for column in range(REACH):
                        at = corner_cell(sz.edge, side, row, column)
                        pad[q * sz.lanes + h, pl.ds(at, 1), :] = part[column : column + 1]


def hold_taps(sz, kern, layer, taps):
    for a in range(TAPS):
        for b in range(TAPS):
            for h, part in enumerate(halves(kern[a, b, layer : layer + 1])):
                taps[h, pl.ds(a * 8 + b, 1), :] = part


def tap(taps, h, a, b):
    return jnp.broadcast_to(taps[h, pl.ds(a * 8 + b, 1), :], (8, LANES))


def convolve(sz, pad, taps, conv):
    @pl.loop(0, sz.slabs)
    def _(slab):
        h = lax.rem(slab, sz.lanes)
        for g in range(sz.edge // 8):
            acc = [None] * sz.edge
            for b in range(TAPS):
                weights = [tap(taps, h, a, b) for a in range(TAPS)]
                for r in range(sz.outer):
                    x = pad[slab, pl.ds(r * PITCH + b + 8 * g, 8), :]
                    for a in range(TAPS):
                        i = r - a
                        if 0 <= i < sz.edge:
                            term = x * weights[a]
                            acc[i] = term if acc[i] is None else acc[i] + term
            for i in range(sz.edge):
                conv[slab, pl.ds(i * sz.edge + 8 * g, 8), :] = acc[i]


def normalise(sz, conv, gain, layer, normal, inverse, normed):
    scale = 1.0 / sz.channels
    for q in range(sz.tiles):

        @pl.loop(0, sz.edge, unroll=2)
        def _(i):
            at = pl.ds(pl.multiple_of(i * sz.edge, sz.edge), sz.edge)
            parts = [conv[q * sz.lanes + h, at, :] for h in range(sz.lanes)]
            mean = jnp.sum(sum(parts[1:], parts[0]), axis=-1, keepdims=True) * scale
            parts = [part - mean for part in parts]
            squares = [part * part for part in parts]
            variance = jnp.sum(sum(squares[1:], squares[0]), axis=-1, keepdims=True) * scale
            root = lax.rsqrt(variance + epsilon)
            inverse[q, at, :] = jnp.broadcast_to(root, (sz.edge, LANES))
            flat_at = pl.ds(pl.multiple_of(q * sz.cells + i * sz.edge, sz.edge), sz.edge)
            for h, part in enumerate(parts):
                part = part * root
                normal[q * sz.lanes + h, at, :] = part
                gains = gain[layer : layer + 1, h * LANES : (h + 1) * LANES]
                normed[flat_at, h * LANES : (h + 1) * LANES] = (part * gains).astype(BF16)


def activate(sz, upward, active, slope):
    width = 512

    @pl.loop(0, sz.rows // 16)
    def _(t):
        at = pl.ds(pl.multiple_of(t * 16, 16), 16)
        for start in range(0, sz.hidden, width):
            u = upward[at, start : start + width]
            chance = 0.5 * (1.0 + lax.erf(u * inverse_root_two))
            active[at, start : start + width] = (u * chance).astype(BF16)
            slope[at, start : start + width] = (
                chance + u * jnp.exp(-0.5 * u * u) * inverse_root_tau
            ).astype(slope.dtype)


def multiply(a, b, ca=1, cb=0):
    return lax.dot_general(a, b, (((ca,), (cb,)), ((), ())), preferred_element_type=F32)


def finish_forward(sz, cur, branch, lscale, layer, out, flat):
    for q in range(sz.tiles):

        @pl.loop(0, sz.edge, unroll=2)
        def _(i):
            at = pl.ds(pl.multiple_of(q * sz.cells + i * sz.edge, sz.edge), sz.edge)
            value = cur[q, i].astype(F32) + branch[at, :] * lscale[layer : layer + 1, :]
            value = value.astype(BF16)
            out[q, i] = value
            if flat is not None:
                local = pl.ds(pl.multiple_of(i * sz.edge, sz.edge), sz.edge)
                for h, part in enumerate(halves(value.astype(F32))):
                    flat[q * sz.lanes + h, local, :] = part


def scale_rows(sz, grad_row, branch, lscale, layer, down_in, sums):
    sums[...] = jnp.zeros_like(sums)
    for q in range(sz.tiles):

        @pl.loop(0, sz.edge, unroll=2)
        def _(i):
            at = pl.ds(pl.multiple_of(q * sz.cells + i * sz.edge, sz.edge), sz.edge)
            g = grad_row(q, i)
            down_in[at, :] = (g * lscale[layer : layer + 1, :]).astype(BF16)
            sums[...] += g * branch[at, :]


def slope_rows(sz, grad_active, slope, up_in):
    @pl.loop(0, sz.rows // 16, unroll=2)
    def _(t):
        at = pl.ds(pl.multiple_of(t * 16, 16), 16)
        up_in[at, :] = (grad_active[at, :] * slope[at, :].astype(F32)).astype(BF16)


def weight_gradients(sz, core, active, down_in, normed, up_in, both, keep, send):
    both[0] = multiply(active[...], down_in[...], 0, 0).astype(BF16)
    for k in range(sz.hidden // sz.channels):
        part = multiply(normed[...], up_in[:, k * sz.channels : (k + 1) * sz.channels], 0, 0)
        both[1, k * sz.channels : (k + 1) * sz.channels, :] = part.astype(BF16)
    keep[...] = both[core]
    send[...] = both[1 - core]


def norm_gradients(sz, grad_normed, normal, inverse, gain, layer, grad_conv, sums):
    scale = 1.0 / sz.channels
    sums[...] = jnp.zeros_like(sums)
    blank = jnp.zeros((8, LANES), F32)
    for q in range(sz.tiles):

        @pl.loop(0, sz.edge, unroll=2)
        def _(i):
            at = pl.ds(pl.multiple_of(q * sz.cells + i * sz.edge, sz.edge), sz.edge)
            local = pl.ds(pl.multiple_of(i * sz.edge, sz.edge), sz.edge)
            g = halves(grad_normed[at, :])
            n = [normal[q * sz.lanes + h, local, :] for h in range(sz.lanes)]
            sums[...] += jnp.concatenate([a * b for a, b in zip(g, n)], axis=1)
            s = [
                part * gain[layer : layer + 1, h * LANES : (h + 1) * LANES]
                for h, part in enumerate(g)
            ]
            products = [a * b for a, b in zip(s, n)]
            mean = jnp.sum(sum(s[1:], s[0]), axis=-1, keepdims=True) * scale
            slant = jnp.sum(sum(products[1:], products[0]), axis=-1, keepdims=True) * scale
            root = inverse[q, local, :]
            for h in range(sz.lanes):
                slab = q * sz.lanes + h
                base = pl.multiple_of(i * GRAD_PITCH, GRAD_PITCH)
                grad_conv[slab, pl.ds(base, 8), :] = blank
                grad_conv[slab, pl.ds(base + 8, sz.edge), :] = root * (s[h] - mean - n[h] * slant)
                grad_conv[slab, pl.ds(base + 8 + sz.edge, 8), :] = blank


def tap_gradients(sz, pad, grad_conv, tap_sums, small):
    tap_sums[...] = jnp.zeros_like(tap_sums)

    @pl.loop(0, sz.slabs)
    def _(slab):
        h = lax.rem(slab, sz.lanes)
        for b in range(TAPS):
            acc = [None] * TAPS
            for g in range(sz.edge // 8):
                grads = [
                    grad_conv[slab, pl.ds(i * GRAD_PITCH + 8 + 8 * g, 8), :]
                    for i in range(sz.edge)
                ]
                for r in range(sz.outer):
                    x = pad[slab, pl.ds(r * PITCH + b + 8 * g, 8), :]
                    for a in range(TAPS):
                        i = r - a
                        if 0 <= i < sz.edge:
                            term = x * grads[i]
                            acc[a] = term if acc[a] is None else acc[a] + term
            for a in range(TAPS):
                tap_sums[h, a * TAPS + b] += acc[a]

    for h in range(sz.lanes):
        for k in range(TAPS * TAPS):
            row = k // TAPS * 8 + k % TAPS
            small[row : row + 1, h * LANES : (h + 1) * LANES] = jnp.sum(
                tap_sums[h, k], axis=0, keepdims=True
            )


def spread_gradients(sz, grad_conv, taps, grad_pad):
    @pl.loop(0, sz.slabs)
    def _(slab):
        h = lax.rem(slab, sz.lanes)
        for g in range(PITCH // 8):
            acc = [None] * sz.outer
            for b in range(TAPS):
                start = 8 * g - b + 8
                if start >= 8 + sz.edge:
                    continue
                weights = [tap(taps, h, a, b) for a in range(TAPS)]
                for i in range(sz.edge):
                    x = grad_conv[slab, pl.ds(i * GRAD_PITCH + start, 8), :]
                    for a in range(TAPS):
                        term = x * weights[a]
                        acc[i + a] = term if acc[i + a] is None else acc[i + a] + term
            for p in range(sz.outer):
                grad_pad[slab, pl.ds(p * PITCH + 8 * g, 8), :] = acc[p]


def return_margins(sz, strip_at, corner_at, grad_pad, pool):
    pool[...] = jnp.zeros_like(pool)
    for q in range(sz.tiles):
        for side in range(4):
            piece = strip_at[q * 4 + side]
            for row in range(REACH):
                window, turned = margin_window(sz.edge, side, row)
                for h in range(sz.lanes):
                    part = grad_pad[q * sz.lanes + h, window, :]
                    pool[piece, row, h] = flip_rows(part) if turned else part
    for q in range(sz.tiles):
        for side in range(4):
            piece = corner_at[q * 4 + side]
            for row in range(REACH):
                for column in range(REACH):
                    at = corner_cell(sz.edge, side, row, column)
                    for h in range(sz.lanes):
                        pool[piece, row, h, pl.ds(column, 1), :] += grad_pad[
                            q * sz.lanes + h, pl.ds(at, 1), :
                        ]


def send_margins(sz, pool, own, below, above):
    own[...] = pool[0 : sz.pieces]
    for piece in range(sz.pieces):
        for row in range(REACH):
            for offset, ref in ((1, below), (2, above)):
                parts = [pool[offset * sz.pieces + piece, row, h] for h in range(sz.lanes)]
                ref[piece, row] = jnp.concatenate(parts, axis=1).astype(BF16)


def gather_inner(sz, grad_row, grad_pad, base):
    for q in range(sz.tiles):
        for i in range(sz.edge):
            for h, part in enumerate(halves(grad_row(q, i))):
                slab = q * sz.lanes + h
                base[slab, pl.ds(i * sz.edge, sz.edge), :] = (
                    part + grad_pad[slab, pl.ds((i + REACH) * PITCH + REACH, sz.edge), :]
                )


def add_strips(sz, base, own, first, second, flat):
    flat[...] = base[...]
    for q in range(sz.tiles):
        for side in range(4):
            piece = q * 4 + side
            for row in range(REACH):
                window, turned = strip_window(sz.edge, side, row)
                came = first[piece, row].astype(F32) + second[piece, row].astype(F32)
                for h, part in enumerate(halves(came)):
                    part = part + own[piece, row, h]
                    flat[q * sz.lanes + h, window, :] += flip_rows(part) if turned else part


def fill_small(small, gain_sums, scale_sums):
    small[TAPS * 8 : TAPS * 8 + 1, :] = jnp.sum(gain_sums[...], axis=0, keepdims=True)
    small[TAPS * 8 + 1 : TAPS * 8 + 2, :] = jnp.sum(scale_sums[...], axis=0, keepdims=True)


def flat_grad_row(sz, flat):
    def row(q, i):
        at = pl.ds(i * sz.edge, sz.edge)
        parts = [flat[q * sz.lanes + h, at, :] for h in range(sz.lanes)]
        return jnp.concatenate(parts, axis=1)

    return row


def fetch_kernel(*refs):
    count = (len(refs) - 1) // 2
    copies = [
        pltpu.make_async_copy(refs[k], refs[count + k], refs[-1].at[k]) for k in range(count)
    ]
    for copy in copies:
        copy.start()
    for copy in copies:
        copy.wait()


def strips_kernel(sz, cur, strips, held, flat):
    held[...] = cur[...]
    for q in range(sz.tiles):
        for i in range(sz.edge):
            for h, part in enumerate(halves(cur[q, i].astype(F32))):
                flat[q * sz.lanes + h, pl.ds(i * sz.edge, sz.edge), :] = part
    write_strips(sz, flat, strips)


def forward_kernel(
    sz, layer, seams, corners, cur, own, below, above, kern, gain, lscale, up, down,
    out, strips, pad, normal, inverse, normed, slope, active, branch,
    pool, taps, conv, upward, flat,
):
    strip_at, corner_at = read_plan(sz, seams), read_plan(sz, corners)
    surround(sz, strip_at, corner_at, cur, own, below, above, pool, pad)
    hold_taps(sz, kern, layer, taps)
    convolve(sz, pad, taps, conv)
    normalise(sz, conv, gain, layer, normal, inverse, normed)
    upward[...] = multiply(normed[...], up[layer])
    activate(sz, upward, active, slope)
    branch[...] = multiply(active[...], down[layer])
    finish_forward(sz, cur, branch, lscale, layer, out, flat)
    write_strips(sz, flat, strips)


def turn_kernel(
    sz, layer, seams, corners, cur, own, below, above, kern, gain, lscale, up, down, out_grad,
    out_hbm, base, grad_own, grad_below, grad_above,
    pad, grad_conv, normed, active, down_in, up_in, gain_sums, scale_sums,
    pool, taps, conv, upward, out, normal, inverse, slope, branch, grad_pool, grad_pad, out_sem,
):
    strip_at, corner_at = read_plan(sz, seams), read_plan(sz, corners)
    surround(sz, strip_at, corner_at, cur, own, below, above, pool, pad)
    hold_taps(sz, kern, layer, taps)
    convolve(sz, pad, taps, conv)
    normalise(sz, conv, gain, layer, normal, inverse, normed)
    upward[...] = multiply(normed[...], up[layer])
    activate(sz, upward, active, slope)
    branch[...] = multiply(active[...], down[layer])
    finish_forward(sz, cur, branch, lscale, layer, out, None)
    store = pltpu.make_async_copy(out, out_hbm, out_sem.at[0])
    store.start()

    def grad_row(q, i):
        return out_grad[q, i].astype(F32)

    scale_rows(sz, grad_row, branch, lscale, layer, down_in, scale_sums)
    upward[...] = multiply(down_in[...], down[layer], 1, 1)
    slope_rows(sz, upward, slope, up_in)
    branch[...] = multiply(up_in[...], up[layer], 1, 1)
    norm_gradients(sz, branch, normal, inverse, gain, layer, grad_conv, gain_sums)
    spread_gradients(sz, grad_conv, taps, grad_pad)
    return_margins(sz, strip_at, corner_at, grad_pad, grad_pool)
    send_margins(sz, grad_pool, grad_own, grad_below, grad_above)
    gather_inner(sz, grad_row, grad_pad, base)
    store.wait()


def weights_kernel(
    sz, pad, grad_conv, normed, active, down_in, up_in, gain_sums, scale_sums,
    keep, send, small, tap_sums, both,
):
    small[...] = jnp.zeros_like(small)
    weight_gradients(sz, digit_of(0), active, down_in, normed, up_in, both, keep, send)
    tap_gradients(sz, pad, grad_conv, tap_sums, small)
    fill_small(small, gain_sums, scale_sums)


def backward_kernel(
    sz, layer, base, own, first, second, lscale, down, normed, slope, active, branch,
    keep, send, flat, up_in, scale_sums,
    hidden, down_in, both,
):
    add_strips(sz, base, own, first, second, flat)
    for slab in range(sz.slabs):
        flat[slab] = flat[slab].astype(BF16).astype(F32)
    scale_rows(sz, flat_grad_row(sz, flat), branch, lscale, layer, down_in, scale_sums)
    hidden[...] = multiply(down_in[...], down[layer], 1, 1)
    slope_rows(sz, hidden, slope, up_in)
    weight_gradients(sz, digit_of(0), active, down_in, normed, up_in, both, keep, send)


def spread_kernel(
    sz, layer, seams, corners, kern, gain, up, flat, up_in, normal, inverse,
    base, grad_own, grad_below, grad_above, grad_conv, gain_sums,
    taps, branch, grad_pool, grad_pad,
):
    strip_at, corner_at = read_plan(sz, seams), read_plan(sz, corners)
    branch[...] = multiply(up_in[...], up[layer], 1, 1)
    norm_gradients(sz, branch, normal, inverse, gain, layer, grad_conv, gain_sums)
    hold_taps(sz, kern, layer, taps)
    spread_gradients(sz, grad_conv, taps, grad_pad)
    return_margins(sz, strip_at, corner_at, grad_pad, grad_pool)
    send_margins(sz, grad_pool, grad_own, grad_below, grad_above)
    gather_inner(sz, flat_grad_row(sz, flat), grad_pad, base)


def taps_kernel(
    sz, pad, grad_conv, gain_sums, scale_sums, other, keep, send, tap_sums, small, both
):
    small[...] = jnp.zeros_like(small)
    tap_gradients(sz, pad, grad_conv, tap_sums, small)
    fill_small(small, gain_sums, scale_sums)
    both[0] = small[...]
    both[1] = other[...]
    keep[...] = both[digit_of(0)].astype(BF16)
    send[...] = both[1 - digit_of(0)].astype(BF16)


def last_kernel(sz, base, own, first, second, out_hbm, token, flat, out, sems):
    token[...] = jnp.zeros_like(token)
    add_strips(sz, base, own, first, second, flat)
    row = flat_grad_row(sz, flat)
    for q in range(sz.tiles):
        for i in range(sz.edge):
            out[q, i] = row(q, i).astype(BF16)
    store = pltpu.make_async_copy(out, out_hbm, sems.at[0])
    store.start()
    store.wait()


def add_rows(out, parts):
    for start in range(0, out.shape[0], 16):
        rows = slice(start, start + 16)
        values = [part(rows).astype(F32) for part in parts]
        out[rows] = sum(values[1:], values[0]).astype(BF16)


def share_near_kernel(keep, came, *outs):
    for k, out in enumerate(outs):
        piece = digit_of(1) ^ k
        add_rows(out, [lambda rows: keep[piece, rows], lambda rows: came[piece, rows]])


def quarter_kernel(*refs):
    add_rows(refs[4], [lambda rows, array=array: array[rows] for array in refs[:4]])


def far_kernel(*refs):
    pieces, out, held = refs[:-2], refs[-2], refs[-1]
    if len(pieces) == 2:
        add_rows(out, [lambda rows: pieces[0][rows], lambda rows: pieces[1][rows]])
        return
    for k, piece in enumerate(pieces):
        held[digit_of(2) ^ k] = piece[...]
    add_rows(out, [lambda rows, k=k: held[k, rows] for k in range(len(pieces))])


def middle_kernel(*refs):
    total, payload, held = refs[-3:]
    pieces, (parts, small) = refs[:-9], (refs[-9:-5], refs[-5:-3])
    far_kernel(*pieces, total, held)
    quarter = parts[0].shape[0]
    add_rows(
        payload.at[0:quarter], [lambda rows, array=array: array[rows] for array in parts]
    )
    add_rows(payload.at[quarter:], [lambda rows, array=array: array[rows] for array in small])


def order_kernel(quarter, *refs):
    pieces, out, held = refs[:4], refs[4], refs[5]
    for k, piece in enumerate(pieces):
        place = digit_of(1) ^ k
        out[pl.ds(pl.multiple_of(place * quarter, quarter), quarter), :] = piece[0:quarter]
        if quarter < piece.shape[0]:
            held[place] = piece[quarter:]
    if out.shape[0] > 4 * quarter:
        add_rows(out.at[4 * quarter :], [lambda rows, k=k: held[k, rows] for k in range(4)])


def unpack_half(sz, half, layer, source, staged, up_hbm, down_hbm, sems):
    copies = []
    for k in range(sz.hidden // sz.channels):
        rows = slice(k * sz.channels, (k + 1) * sz.channels)
        staged[rows, :] = source[rows, :].astype(F32)
        place = down_hbm.at[layer, rows] if half == 0 else up_hbm.at[layer, :, rows]
        copy = pltpu.make_async_copy(staged.at[rows], place, sems.at[half, k])
        copy.start()
        copies.append(copy)
    return copies


def unpack_layer_kernel(sz, layer, mine, theirs, up_hbm, down_hbm, token, first, second, sems):
    token[...] = jnp.zeros_like(token)
    for half in range(2):

        @pl.when(digit_of(0) == half)
        def _(half=half):
            copies = unpack_half(sz, half, layer, mine, first, up_hbm, down_hbm, sems)
            copies += unpack_half(sz, 1 - half, layer, theirs, second, up_hbm, down_hbm, sems)
            for copy in copies:
                copy.wait()


def unpack_mine_kernel(sz, layer, mine, _up, _down, up_hbm, down_hbm, staged, sems):
    for half in range(2):

        @pl.when(digit_of(0) == half)
        def _(half=half):
            for copy in unpack_half(sz, half, layer, mine, staged, up_hbm, down_hbm, sems):
                copy.wait()


def unpack_theirs_kernel(
    sz, layer, mine, theirs, _up, _down, up_hbm, down_hbm, kernel_out, gain_out, scale_out,
    staged, small, sems,
):
    for half in range(2):

        @pl.when(digit_of(0) == 1 - half)
        def _(half=half):
            for copy in unpack_half(sz, half, layer, theirs, staged, up_hbm, down_hbm, sems):
                copy.wait()

    small[digit_of(0)] = mine[sz.hidden :].astype(F32)
    small[1 - digit_of(0)] = theirs[sz.hidden :].astype(F32)
    for layer in range(2):
        for a in range(TAPS):
            for b in range(TAPS):
                kernel_out[a, b, layer : layer + 1] = small[layer, pl.ds(a * 8 + b, 1), :]
        gain_out[layer : layer + 1] = small[layer, pl.ds(TAPS * 8, 1), :]
        scale_out[layer : layer + 1] = small[layer, pl.ds(TAPS * 8 + 1, 1), :]


IN_VMEM = pl.BlockSpec(memory_space=pltpu.VMEM)
IN_SMEM = pl.BlockSpec(memory_space=pltpu.SMEM)
IN_HBM = pl.BlockSpec(memory_space=pltpu.HBM)


def call(body, name, micros, ins, outs, scratch, after=(), aliases={}):
    count = len(ins)

    def run(*refs):
        body(*refs[:count], *refs[count + len(after) :])

    return pl.pallas_call(
        run,
        in_specs=[spec for spec, _ in ins] + [pl.BlockSpec(memory_space=pl.ANY)] * len(after),
        out_specs=[spec for spec, _ in outs],
        out_shape=[out for _, out in outs],
        scratch_shapes=scratch,
        compiler_params=pltpu.CompilerParams(vmem_limit_bytes=24 * 1024 * 1024),
        cost_estimate=pl.CostEstimate(
            flops=0, bytes_accessed=int(micros * 3.5e6), transcendentals=0
        ),
        input_output_aliases=aliases,
        name=name,
    )(*[array for _, array in ins], *after)


def near(*arrays):
    return [(IN_VMEM, array) for array in arrays]


def far(*arrays):
    return [(IN_HBM, array) for array in arrays]


def pass_on(shard, by):
    length = lax.axis_size("tile")
    return lax.ppermute(shard, "tile", [(i, (i + by) % length) for i in range(length)])


def partners(array, masks):
    length = lax.axis_size("tile")
    return [
        lax.ppermute(array, "tile", [(i, i ^ mask) for i in range(length)]) for mask in masks
    ]


def swap(arrays, masks):
    length = lax.axis_size("tile")
    return [
        lax.ppermute(array, "tile", [(i, i ^ mask) for i in range(length)])
        for array, mask in zip(arrays, masks)
    ]


class Reduction:
    def __init__(self, devices):
        self.near_masks = [2 * k for k in range(1, 4)]
        self.far_masks = [8 * k for k in range(1, devices // 8)]

    def share(self, keep, send, after=()):
        rows, channels = keep.shape
        dims = (4, rows // 4, channels)
        shape = jax.ShapeDtypeStruct(dims[1:], BF16)
        pieces = call(
            share_near_kernel, "share_near", 0.3,
            near(keep.reshape(dims), swap([send], [1])[0].reshape(dims)),
            near(*[shape] * 4), [], after,
        )
        return [pieces[0]] + swap(pieces[1:], self.near_masks)

    def quarter(self, parts):
        shape = jax.ShapeDtypeStruct(parts[0].shape, BF16)
        (total,) = call(quarter_kernel, "quarter", 0.3, near(*parts), near(shape), [])
        return total

    def far(self, total):
        pieces = [total] + partners(total, self.far_masks)
        held = (len(pieces),) + total.shape if len(pieces) > 2 else (1, 16, LANES)
        return pieces, [pltpu.VMEM(held, BF16)]

    def middle(self, quarter, parts, keep, send):
        pieces, scratch = self.far(quarter)
        rows, channels = quarter.shape
        shapes = [
            jax.ShapeDtypeStruct((rows + more, channels), BF16) for more in (0, keep.shape[0])
        ]
        return call(
            middle_kernel, "middle", 0.5,
            near(*pieces, *parts, keep, *swap([send], [1])), near(*shapes), scratch,
        )

    def exchange(self, total, after=()):
        pieces, scratch = self.far(total)
        shape = jax.ShapeDtypeStruct(total.shape, BF16)
        (total,) = call(far_kernel, "far", 0.3, near(*pieces), near(shape), scratch, after)
        return total

    def gather(self, total, quarter, after=()):
        rows, channels = total.shape
        shape = jax.ShapeDtypeStruct((3 * quarter + rows, channels), BF16)
        (whole,) = call(
            functools.partial(order_kernel, quarter), "order", 0.4,
            near(total, *partners(total, self.near_masks)), near(shape),
            [pltpu.VMEM((4, max(rows - quarter, 16), channels), BF16)], after,
        )
        return whole


def on_device(
    inputs,
    out_grad,
    kernel,
    norm_gain,
    up_weight,
    down_weight,
    layer_scale,
    seam_table,
    corner_table,
):
    tiles, edge, _, channels = inputs.shape
    layers, _, hidden = up_weight.shape
    sz = Sizes(tiles, edge, channels, hidden)
    columns = lax.axis_size("tile")
    plan = [(IN_SMEM, table.transpose((1, 2, 0))) for table in (seam_table, corner_table)]
    kern = kernel.transpose((1, 2, 0, 3))
    gain, lscale, up, down = norm_gain, layer_scale, up_weight, down_weight
    reduction = Reduction(columns)

    shape = jax.ShapeDtypeStruct
    image = shape(inputs.shape, BF16)
    strips_shape = shape((sz.pieces, REACH, edge, channels), BF16)
    slabs = shape((sz.slabs, sz.cells, LANES), F32)
    padded = shape((sz.slabs, sz.outer * PITCH, LANES), F32)
    inverses = shape((tiles, sz.cells, LANES), F32)
    narrow_short = shape((sz.rows, channels), BF16)
    wide_short = shape((sz.rows, hidden), BF16)
    narrow = shape((sz.rows, channels), F32)
    wide = shape((sz.rows, hidden), F32)
    sums = shape((edge, channels), F32)
    grad_slabs = shape((sz.slabs, edge * GRAD_PITCH, LANES), F32)
    own_shape = shape((sz.pieces, REACH, sz.lanes, edge, LANES), F32)
    pool = shape((3 * sz.pieces, REACH, edge, channels), BF16)
    grad_pool = shape((3 * sz.pieces, REACH, sz.lanes, edge, LANES), F32)
    taps = shape((sz.lanes, TAPS * 8, LANES), F32)
    tap_sums = shape((sz.lanes, TAPS * TAPS, 8, LANES), F32)
    small = shape((SMALL_ROWS, channels), F32)
    half = shape((hidden, channels), BF16)
    two_halves = shape((2, hidden, channels), BF16)

    def vmem(*shapes):
        return [pltpu.VMEM(one.shape, one.dtype) for one in shapes]

    def sems(count):
        return [pltpu.SemaphoreType.DMA((count,))]

    strips, inputs = call(
        functools.partial(strips_kernel, sz),
        "strips", 0.3,
        near(inputs),
        near(strips_shape, image),
        vmem(slabs),
    )
    below, above = pass_on(strips, 1), pass_on(strips, -1)
    fetched = (kern, gain, lscale, up, down)
    kern, gain, lscale, up, down = call(
        fetch_kernel,
        "fetch", 2.0,
        far(*fetched),
        near(*[shape(one.shape, one.dtype) for one in fetched]),
        sems(len(fetched)),
        (strips,),
    )
    middle, strips, pad_zero, normal, inverse, normed, slope, active, branch = call(
        functools.partial(forward_kernel, sz, 0),
        "forward", 8.7,
        plan + near(inputs, strips, below, above, kern, gain, lscale, up, down),
        near(
            image, strips_shape, padded, slabs, inverses,
            narrow_short, wide_short, wide_short, narrow,
        ),
        vmem(pool, taps, slabs, wide, slabs),
    )
    below, above = pass_on(strips, 1), pass_on(strips, -1)
    result, base, grad_own, grad_below, grad_above, *for_weights = call(
        functools.partial(turn_kernel, sz, 1),
        "turn", 15.4,
        plan + near(middle, strips, below, above, kern, gain, lscale, up, down, out_grad),
        far(image)
        + near(
            slabs, own_shape, strips_shape, strips_shape,
            padded, grad_slabs, narrow_short, wide_short, narrow_short, wide_short, sums, sums,
        ),
        vmem(
            pool, taps, slabs, wide, image, slabs, inverses, wide_short, narrow, grad_pool, padded
        )
        + sems(1),
    )
    from_below, from_above = pass_on(grad_above, 1), pass_on(grad_below, -1)
    keep_one, send_one, small_one = call(
        functools.partial(weights_kernel, sz),
        "weights", 2.8,
        near(*for_weights),
        near(half, half, small),
        vmem(tap_sums, two_halves),
    )
    keep_zero, send_zero, flat, up_in, scale_sums = call(
        functools.partial(backward_kernel, sz, 0),
        "backward", 2.9,
        near(
            base, grad_own, from_below, from_above, lscale, down, normed, slope, active, branch
        ),
        near(half, half, slabs, wide_short, sums),
        vmem(wide, narrow_short, two_halves),
    )
    parts_one = reduction.share(keep_one, send_one, (scale_sums,))
    quarter_one = reduction.quarter(parts_one)
    parts_zero = reduction.share(keep_zero, send_zero)
    base, grad_own, grad_below, grad_above, grad_conv, gain_sums = call(
        functools.partial(spread_kernel, sz, 0),
        "spread", 6.0,
        plan + near(kern, gain, up, flat, up_in, normal, inverse),
        near(slabs, own_shape, strips_shape, strips_shape, grad_slabs, sums),
        vmem(taps, narrow, grad_pool, padded),
        (parts_zero[0], quarter_one),
    )
    from_below, from_above = pass_on(grad_above, 1), pass_on(grad_below, -1)
    small_keep, small_send = call(
        functools.partial(taps_kernel, sz),
        "taps", 2.1,
        near(pad_zero, grad_conv, gain_sums, scale_sums, small_one),
        near(*[shape(small.shape, BF16)] * 2),
        vmem(tap_sums, small, shape((2,) + small.shape, F32)),
    )
    in_grad, token = call(
        functools.partial(last_kernel, sz),
        "last", 1.0,
        near(base, grad_own, from_below, from_above),
        far(image) + near(shape((8, LANES), F32)),
        vmem(slabs, image) + sems(1),
    )
    rows = hidden // 4
    total_one, total_zero = reduction.middle(quarter_one, parts_zero, small_keep, small_send)
    total_zero = reduction.exchange(total_zero, (token,))
    mine_one = reduction.gather(total_one, rows, (total_zero,))
    theirs_one = partners(mine_one, [1])[0]
    weight_shapes = [shape(up_weight.shape, F32), shape(down_weight.shape, F32)]
    staged = shape((hidden, channels), F32)
    copies = [pltpu.SemaphoreType.DMA((2, hidden // channels))]
    grad_up, grad_down, token = call(
        functools.partial(unpack_layer_kernel, sz, 1),
        "unpack_one", 1.8,
        near(mine_one, theirs_one),
        far(*weight_shapes) + near(shape((8, LANES), F32)),
        vmem(staged, staged) + copies,
    )
    mine = reduction.gather(total_zero, rows, (token,))
    theirs = partners(mine, [1])[0]
    grad_up, grad_down = call(
        functools.partial(unpack_mine_kernel, sz, 0),
        "unpack_mine", 1.0,
        near(mine) + far(grad_up, grad_down),
        far(*weight_shapes),
        vmem(staged) + copies,
        aliases={1: 0, 2: 1},
    )
    grad_up, grad_down, grad_kernel, grad_gain, grad_scale = call(
        functools.partial(unpack_theirs_kernel, sz, 0),
        "unpack_theirs", 1.3,
        near(mine, theirs) + far(grad_up, grad_down),
        far(*weight_shapes)
        + near(
            shape(kern.shape, F32), shape(norm_gain.shape, F32), shape(norm_gain.shape, F32)
        ),
        vmem(staged, shape((2,) + small.shape, F32)) + copies,
        aliases={2: 0, 3: 1},
    )
    return (
        result, in_grad, grad_kernel.transpose((2, 0, 1, 3)),
        grad_gain, grad_up, grad_down, grad_scale,
    )


def solution(mesh):
    placed = (
        P(("groups", "tile"), None, None, None),
        P(("groups", "tile"), None, None, None),
        P(),
        P(),
        P(),
        P(),
        P(),
        P(),
        P(),
    )
    return jax.shard_map(
        on_device,
        mesh=mesh,
        in_specs=placed,
        out_specs=(
            P(("groups", "tile"), None, None, None),
            P(("groups", "tile"), None, None, None),
            P("groups", None, None, None),
            P("groups", None),
            P("groups", None, None),
            P("groups", None, None),
            P("groups", None),
        ),
        check_vma=False,
    )
```

```python
import functools

import jax
import jax.numpy as jnp
from jax import lax
from jax.experimental import pallas as pl
from jax.experimental.pallas import tpu as pltpu
from jax.sharding import PartitionSpec as P

epsilon = 1e-06
inverse_root_two = 0.7071067811865476
inverse_root_tau = 0.3989422804014327

LANES = 128
TAPS = 7
REACH = 3
PITCH = 24
GRAD_PITCH = 32
SMALL_ROWS = 64
F32 = jnp.float32
BF16 = jnp.bfloat16


def flip_rows(value):
    rows = value.shape[0]
    order = 7 - lax.broadcasted_iota(jnp.int32, (8, LANES), 0)
    parts = [
        jnp.take_along_axis(value[at : at + 8], order, axis=0, mode="promise_in_bounds")
        for at in range(0, rows, 8)
    ]
    return jnp.concatenate(parts[::-1], axis=0)


def halves(value):
    return [value[:, at : at + LANES] for at in range(0, value.shape[1], LANES)]


class Sizes:
    def __init__(self, tiles, edge, channels, hidden):
        self.tiles = tiles
        self.edge = edge
        self.channels = channels
        self.hidden = hidden
        self.lanes = channels // LANES
        self.cells = edge * edge
        self.rows = tiles * edge * edge
        self.pieces = tiles * 4
        self.outer = edge + 2 * REACH
        self.slabs = tiles * self.lanes

    def key(self):
        return (self.tiles, self.edge, self.channels, self.hidden)


def strip_window(edge, side, row):
    if side == 0:
        return pl.ds(row * edge, edge), False
    if side == 1:
        return pl.ds(edge - 1 - row, edge, stride=edge), False
    if side == 2:
        return pl.ds((edge - 1 - row) * edge, edge), True
    return pl.ds(row, edge, stride=edge), True


def margin_window(edge, side, row):
    last = edge + 2 * REACH - 1
    if side == 0:
        return pl.ds((2 - row) * PITCH + REACH, edge), True
    if side == 1:
        return pl.ds(REACH * PITCH + last - 2 + row, edge, stride=PITCH), True
    if side == 2:
        return pl.ds((last - 2 + row) * PITCH + REACH, edge), False
    return pl.ds(REACH * PITCH + 2 - row, edge, stride=PITCH), False


def corner_cell(edge, corner, row, column):
    last = edge + 2 * REACH - 1
    r, x = 2 - row, 2 - column
    if corner == 0:
        at = (r, x)
    elif corner == 1:
        at = (x, last - r)
    elif corner == 2:
        at = (last - r, last - x)
    else:
        at = (last - x, r)
    return at[0] * PITCH + at[1]


def read_plan(sz, table):
    columns = lax.axis_size("tile")
    device = lax.axis_index("tile")
    below = lax.rem(device + columns - 1, columns)
    plan = []
    for q in range(sz.tiles):
        for side in range(4):
            source = table[side, 0, device * sz.tiles + q]
            owner = lax.div(source, sz.tiles)
            local = (source - owner * sz.tiles) * 4 + table[side, 1, device * sz.tiles + q]
            shift = jnp.where(
                owner == device, 0, jnp.where(owner == below, sz.pieces, 2 * sz.pieces)
            )
            plan.append(shift + local)
    return plan


def digit_of(level):
    device = lax.axis_index("tile")
    if level == 0:
        return lax.rem(device, 2)
    if level == 1:
        return lax.rem(lax.div(device, 2), 4)
    return lax.div(device, 8)


def write_strips(sz, flat, strips_ref):
    for q in range(sz.tiles):
        for side in range(4):
            for row in range(REACH):
                window, turned = strip_window(sz.edge, side, row)
                parts = [flat[q * sz.lanes + h, window, :] for h in range(sz.lanes)]
                if turned:
                    parts = [flip_rows(part) for part in parts]
                strips_ref[q * 4 + side, row] = jnp.concatenate(parts, axis=1).astype(BF16)


def surround(sz, strip_at, corner_at, cur, own, below, above, pool, pad):
    pool[0 : sz.pieces] = own[...]
    pool[sz.pieces : 2 * sz.pieces] = below[...]
    pool[2 * sz.pieces : 3 * sz.pieces] = above[...]
    for q in range(sz.tiles):
        for i in range(sz.edge):
            for h, part in enumerate(halves(cur[q, i].astype(F32))):
                pad[q * sz.lanes + h, pl.ds((i + REACH) * PITCH + REACH, sz.edge), :] = part
    for q in range(sz.tiles):
        for side in range(4):
            piece = strip_at[q * 4 + side]
            for row in range(REACH):
                window, turned = margin_window(sz.edge, side, row)
                for h, part in enumerate(halves(pool[piece, row].astype(F32))):
                    pad[q * sz.lanes + h, window, :] = flip_rows(part) if turned else part
            piece = corner_at[q * 4 + side]
            for row in range(REACH):
                for h, part in enumerate(halves(pool[piece, row].astype(F32))):
                    for column in range(REACH):
                        at = corner_cell(sz.edge, side, row, column)
                        pad[q * sz.lanes + h, pl.ds(at, 1), :] = part[column : column + 1]


def hold_taps(sz, kern, layer, taps):
    for a in range(TAPS):
        for b in range(TAPS):
            for h, part in enumerate(halves(kern[a, b, layer : layer + 1])):
                taps[h, pl.ds(a * 8 + b, 1), :] = part


def tap(taps, h, a, b):
    return jnp.broadcast_to(taps[h, pl.ds(a * 8 + b, 1), :], (8, LANES))


def convolve(sz, pad, taps, conv):
    @pl.loop(0, sz.slabs)
    def _(slab):
        h = lax.rem(slab, sz.lanes)
        for g in range(sz.edge // 8):
            acc = [None] * sz.edge
            for b in range(TAPS):
                weights = [tap(taps, h, a, b) for a in range(TAPS)]
                for r in range(sz.outer):
                    x = pad[slab, pl.ds(r * PITCH + b + 8 * g, 8), :]
                    for a in range(TAPS):
                        i = r - a
                        if 0 <= i < sz.edge:
                            term = x * weights[a]
                            acc[i] = term if acc[i] is None else acc[i] + term
            for i in range(sz.edge):
                conv[slab, pl.ds(i * sz.edge + 8 * g, 8), :] = acc[i]


def normalise(sz, conv, gain, layer, normal, inverse, normed):
    scale = 1.0 / sz.channels
    for q in range(sz.tiles):

        @pl.loop(0, sz.edge, unroll=2)
        def _(i):
            at = pl.ds(pl.multiple_of(i * sz.edge, sz.edge), sz.edge)
            parts = [conv[q * sz.lanes + h, at, :] for h in range(sz.lanes)]
            mean = jnp.sum(sum(parts[1:], parts[0]), axis=-1, keepdims=True) * scale
            parts = [part - mean for part in parts]
            squares = [part * part for part in parts]
            variance = jnp.sum(sum(squares[1:], squares[0]), axis=-1, keepdims=True) * scale
            root = lax.rsqrt(variance + epsilon)
            inverse[q, at, :] = jnp.broadcast_to(root, (sz.edge, LANES))
            flat_at = pl.ds(pl.multiple_of(q * sz.cells + i * sz.edge, sz.edge), sz.edge)
            for h, part in enumerate(parts):
                part = part * root
                normal[q * sz.lanes + h, at, :] = part
                gains = gain[layer : layer + 1, h * LANES : (h + 1) * LANES]
                normed[flat_at, h * LANES : (h + 1) * LANES] = (part * gains).astype(BF16)


def activate(sz, upward, active, slope):
    width = 512

    @pl.loop(0, sz.rows // 16)
    def _(t):
        at = pl.ds(pl.multiple_of(t * 16, 16), 16)
        for start in range(0, sz.hidden, width):
            u = upward[at, start : start + width]
            chance = 0.5 * (1.0 + lax.erf(u * inverse_root_two))
            active[at, start : start + width] = (u * chance).astype(BF16)
            slope[at, start : start + width] = (
                chance + u * jnp.exp(-0.5 * u * u) * inverse_root_tau
            ).astype(slope.dtype)


def multiply(a, b, ca=1, cb=0):
    return lax.dot_general(a, b, (((ca,), (cb,)), ((), ())), preferred_element_type=F32)


def finish_forward(sz, cur, branch, lscale, layer, out, flat):
    for q in range(sz.tiles):

        @pl.loop(0, sz.edge, unroll=2)
        def _(i):
            at = pl.ds(pl.multiple_of(q * sz.cells + i * sz.edge, sz.edge), sz.edge)
            value = cur[q, i].astype(F32) + branch[at, :] * lscale[layer : layer + 1, :]
            value = value.astype(BF16)
            out[q, i] = value
            if flat is not None:
                local = pl.ds(pl.multiple_of(i * sz.edge, sz.edge), sz.edge)
                for h, part in enumerate(halves(value.astype(F32))):
                    flat[q * sz.lanes + h, local, :] = part


def scale_rows(sz, grad_row, branch, lscale, layer, down_in, sums):
    sums[...] = jnp.zeros_like(sums)
    for q in range(sz.tiles):

        @pl.loop(0, sz.edge, unroll=2)
        def _(i):
            at = pl.ds(pl.multiple_of(q * sz.cells + i * sz.edge, sz.edge), sz.edge)
            g = grad_row(q, i)
            down_in[at, :] = (g * lscale[layer : layer + 1, :]).astype(BF16)
            sums[...] += g * branch[at, :]


def slope_rows(sz, grad_active, slope, up_in):
    @pl.loop(0, sz.rows // 16, unroll=2)
    def _(t):
        at = pl.ds(pl.multiple_of(t * 16, 16), 16)
        up_in[at, :] = (grad_active[at, :] * slope[at, :].astype(F32)).astype(BF16)


def weight_gradients(sz, core, active, down_in, normed, up_in, both, keep, send):
    both[0] = multiply(active[...], down_in[...], 0, 0).astype(BF16)
    for k in range(sz.hidden // sz.channels):
        part = multiply(normed[...], up_in[:, k * sz.channels : (k + 1) * sz.channels], 0, 0)
        both[1, k * sz.channels : (k + 1) * sz.channels, :] = part.astype(BF16)
    keep[...] = both[core]
    send[...] = both[1 - core]


def norm_gradients(sz, grad_normed, normal, inverse, gain, layer, grad_conv, sums):
    scale = 1.0 / sz.channels
    sums[...] = jnp.zeros_like(sums)
    blank = jnp.zeros((8, LANES), F32)
    for q in range(sz.tiles):

        @pl.loop(0, sz.edge, unroll=2)
        def _(i):
            at = pl.ds(pl.multiple_of(q * sz.cells + i * sz.edge, sz.edge), sz.edge)
            local = pl.ds(pl.multiple_of(i * sz.edge, sz.edge), sz.edge)
            g = halves(grad_normed[at, :])
            n = [normal[q * sz.lanes + h, local, :] for h in range(sz.lanes)]
            sums[...] += jnp.concatenate([a * b for a, b in zip(g, n)], axis=1)
            s = [
                part * gain[layer : layer + 1, h * LANES : (h + 1) * LANES]
                for h, part in enumerate(g)
            ]
            products = [a * b for a, b in zip(s, n)]
            mean = jnp.sum(sum(s[1:], s[0]), axis=-1, keepdims=True) * scale
            slant = jnp.sum(sum(products[1:], products[0]), axis=-1, keepdims=True) * scale
            root = inverse[q, local, :]
            for h in range(sz.lanes):
                slab = q * sz.lanes + h
                base = pl.multiple_of(i * GRAD_PITCH, GRAD_PITCH)
                grad_conv[slab, pl.ds(base, 8), :] = blank
                grad_conv[slab, pl.ds(base + 8, sz.edge), :] = root * (s[h] - mean - n[h] * slant)
                grad_conv[slab, pl.ds(base + 8 + sz.edge, 8), :] = blank


def tap_gradients(sz, pad, grad_conv, tap_sums, small):
    tap_sums[...] = jnp.zeros_like(tap_sums)

    @pl.loop(0, sz.slabs)
    def _(slab):
        h = lax.rem(slab, sz.lanes)
        for b in range(TAPS):
            acc = [None] * TAPS
            for g in range(sz.edge // 8):
                grads = [
                    grad_conv[slab, pl.ds(i * GRAD_PITCH + 8 + 8 * g, 8), :]
                    for i in range(sz.edge)
                ]
                for r in range(sz.outer):
                    x = pad[slab, pl.ds(r * PITCH + b + 8 * g, 8), :]
                    for a in range(TAPS):
                        i = r - a
                        if 0 <= i < sz.edge:
                            term = x * grads[i]
                            acc[a] = term if acc[a] is None else acc[a] + term
            for a in range(TAPS):
                tap_sums[h, a * TAPS + b] += acc[a]

    for h in range(sz.lanes):
        for k in range(TAPS * TAPS):
            row = k // TAPS * 8 + k % TAPS
            small[row : row + 1, h * LANES : (h + 1) * LANES] = jnp.sum(
                tap_sums[h, k], axis=0, keepdims=True
            )


def spread_gradients(sz, grad_conv, taps, grad_pad):
    @pl.loop(0, sz.slabs)
    def _(slab):
        h = lax.rem(slab, sz.lanes)
        for g in range(PITCH // 8):
            acc = [None] * sz.outer
            for b in range(TAPS):
                start = 8 * g - b + 8
                if start >= 8 + sz.edge:
                    continue
                weights = [tap(taps, h, a, b) for a in range(TAPS)]
                for i in range(sz.edge):
                    x = grad_conv[slab, pl.ds(i * GRAD_PITCH + start, 8), :]
                    for a in range(TAPS):
                        term = x * weights[a]
                        acc[i + a] = term if acc[i + a] is None else acc[i + a] + term
            for p in range(sz.outer):
                grad_pad[slab, pl.ds(p * PITCH + 8 * g, 8), :] = acc[p]


def return_margins(sz, strip_at, corner_at, grad_pad, pool):
    pool[...] = jnp.zeros_like(pool)
    for q in range(sz.tiles):
        for side in range(4):
            piece = strip_at[q * 4 + side]
            for row in range(REACH):
                window, turned = margin_window(sz.edge, side, row)
                for h in range(sz.lanes):
                    part = grad_pad[q * sz.lanes + h, window, :]
                    pool[piece, row, h] = flip_rows(part) if turned else part
    for q in range(sz.tiles):
        for side in range(4):
            piece = corner_at[q * 4 + side]
            for row in range(REACH):
                for column in range(REACH):
                    at = corner_cell(sz.edge, side, row, column)
                    for h in range(sz.lanes):
                        pool[piece, row, h, pl.ds(column, 1), :] += grad_pad[
                            q * sz.lanes + h, pl.ds(at, 1), :
                        ]


def send_margins(sz, pool, own, below, above):
    own[...] = pool[0 : sz.pieces]
    for piece in range(sz.pieces):
        for row in range(REACH):
            for offset, ref in ((1, below), (2, above)):
                parts = [pool[offset * sz.pieces + piece, row, h] for h in range(sz.lanes)]
                ref[piece, row] = jnp.concatenate(parts, axis=1).astype(BF16)


def gather_inner(sz, grad_row, grad_pad, base):
    for q in range(sz.tiles):
        for i in range(sz.edge):
            for h, part in enumerate(halves(grad_row(q, i))):
                slab = q * sz.lanes + h
                base[slab, pl.ds(i * sz.edge, sz.edge), :] = (
                    part + grad_pad[slab, pl.ds((i + REACH) * PITCH + REACH, sz.edge), :]
                )


def add_strips(sz, base, own, first, second, flat):
    flat[...] = base[...]
    for q in range(sz.tiles):
        for side in range(4):
            piece = q * 4 + side
            for row in range(REACH):
                window, turned = strip_window(sz.edge, side, row)
                came = first[piece, row].astype(F32) + second[piece, row].astype(F32)
                for h, part in enumerate(halves(came)):
                    part = part + own[piece, row, h]
                    flat[q * sz.lanes + h, window, :] += flip_rows(part) if turned else part


def fill_small(small, gain_sums, scale_sums):
    small[TAPS * 8 : TAPS * 8 + 1, :] = jnp.sum(gain_sums[...], axis=0, keepdims=True)
    small[TAPS * 8 + 1 : TAPS * 8 + 2, :] = jnp.sum(scale_sums[...], axis=0, keepdims=True)


def flat_grad_row(sz, flat):
    def row(q, i):
        at = pl.ds(i * sz.edge, sz.edge)
        parts = [flat[q * sz.lanes + h, at, :] for h in range(sz.lanes)]
        return jnp.concatenate(parts, axis=1)

    return row


def fetch_kernel(*refs):
    count = (len(refs) - 1) // 2
    copies = [
        pltpu.make_async_copy(refs[k], refs[count + k], refs[-1].at[k]) for k in range(count)
    ]
    for copy in copies:
        copy.start()
    for copy in copies:
        copy.wait()


def strips_kernel(sz, cur, strips, held, flat):
    held[...] = cur[...]
    for q in range(sz.tiles):
        for i in range(sz.edge):
            for h, part in enumerate(halves(cur[q, i].astype(F32))):
                flat[q * sz.lanes + h, pl.ds(i * sz.edge, sz.edge), :] = part
    write_strips(sz, flat, strips)


def forward_kernel(
    sz, layer, seams, corners, cur, own, below, above, kern, gain, lscale, up, down,
    out, strips, pad, normal, inverse, normed, slope, active, branch,
    pool, taps, conv, upward, flat,
):
    strip_at, corner_at = read_plan(sz, seams), read_plan(sz, corners)
    surround(sz, strip_at, corner_at, cur, own, below, above, pool, pad)
    hold_taps(sz, kern, layer, taps)
    convolve(sz, pad, taps, conv)
    normalise(sz, conv, gain, layer, normal, inverse, normed)
    upward[...] = multiply(normed[...], up[layer])
    activate(sz, upward, active, slope)
    branch[...] = multiply(active[...], down[layer])
    finish_forward(sz, cur, branch, lscale, layer, out, flat)
    write_strips(sz, flat, strips)


def turn_kernel(
    sz, layer, seams, corners, cur, own, below, above, kern, gain, lscale, up, down, out_grad,
    out_hbm, base, grad_own, grad_below, grad_above,
    pad, grad_conv, normed, active, down_in, up_in, gain_sums, scale_sums,
    pool, taps, conv, upward, out, normal, inverse, slope, branch, grad_pool, grad_pad, out_sem,
):
    strip_at, corner_at = read_plan(sz, seams), read_plan(sz, corners)
    surround(sz, strip_at, corner_at, cur, own, below, above, pool, pad)
    hold_taps(sz, kern, layer, taps)
    convolve(sz, pad, taps, conv)
    normalise(sz, conv, gain, layer, normal, inverse, normed)
    upward[...] = multiply(normed[...], up[layer])
    activate(sz, upward, active, slope)
    branch[...] = multiply(active[...], down[layer])
    finish_forward(sz, cur, branch, lscale, layer, out, None)
    store = pltpu.make_async_copy(out, out_hbm, out_sem.at[0])
    store.start()

    def grad_row(q, i):
        return out_grad[q, i].astype(F32)

    scale_rows(sz, grad_row, branch, lscale, layer, down_in, scale_sums)
    upward[...] = multiply(down_in[...], down[layer], 1, 1)
    slope_rows(sz, upward, slope, up_in)
    branch[...] = multiply(up_in[...], up[layer], 1, 1)
    norm_gradients(sz, branch, normal, inverse, gain, layer, grad_conv, gain_sums)
    spread_gradients(sz, grad_conv, taps, grad_pad)
    return_margins(sz, strip_at, corner_at, grad_pad, grad_pool)
    send_margins(sz, grad_pool, grad_own, grad_below, grad_above)
    gather_inner(sz, grad_row, grad_pad, base)
    store.wait()


def weights_kernel(
    sz, pad, grad_conv, normed, active, down_in, up_in, gain_sums, scale_sums,
    keep, send, small, tap_sums, both,
):
    small[...] = jnp.zeros_like(small)
    weight_gradients(sz, digit_of(0), active, down_in, normed, up_in, both, keep, send)
    tap_gradients(sz, pad, grad_conv, tap_sums, small)
    fill_small(small, gain_sums, scale_sums)


def backward_kernel(
    sz, layer, base, own, first, second, lscale, down, normed, slope, active, branch,
    keep, send, flat, up_in, scale_sums,
    hidden, down_in, both,
):
    add_strips(sz, base, own, first, second, flat)
    for slab in range(sz.slabs):
        flat[slab] = flat[slab].astype(BF16).astype(F32)
    scale_rows(sz, flat_grad_row(sz, flat), branch, lscale, layer, down_in, scale_sums)
    hidden[...] = multiply(down_in[...], down[layer], 1, 1)
    slope_rows(sz, hidden, slope, up_in)
    weight_gradients(sz, digit_of(0), active, down_in, normed, up_in, both, keep, send)


def spread_kernel(
    sz, layer, seams, corners, kern, gain, up, flat, up_in, normal, inverse,
    base, grad_own, grad_below, grad_above, grad_conv, gain_sums,
    taps, branch, grad_pool, grad_pad,
):
    strip_at, corner_at = read_plan(sz, seams), read_plan(sz, corners)
    branch[...] = multiply(up_in[...], up[layer], 1, 1)
    norm_gradients(sz, branch, normal, inverse, gain, layer, grad_conv, gain_sums)
    hold_taps(sz, kern, layer, taps)
    spread_gradients(sz, grad_conv, taps, grad_pad)
    return_margins(sz, strip_at, corner_at, grad_pad, grad_pool)
    send_margins(sz, grad_pool, grad_own, grad_below, grad_above)
    gather_inner(sz, flat_grad_row(sz, flat), grad_pad, base)


def taps_kernel(
    sz, pad, grad_conv, gain_sums, scale_sums, other, keep, send, tap_sums, small, both
):
    small[...] = jnp.zeros_like(small)
    tap_gradients(sz, pad, grad_conv, tap_sums, small)
    fill_small(small, gain_sums, scale_sums)
    both[0] = small[...]
    both[1] = other[...]
    keep[...] = both[digit_of(0)].astype(BF16)
    send[...] = both[1 - digit_of(0)].astype(BF16)


def last_kernel(sz, base, own, first, second, out_hbm, token, flat, out, sems):
    token[...] = jnp.zeros_like(token)
    add_strips(sz, base, own, first, second, flat)
    row = flat_grad_row(sz, flat)
    for q in range(sz.tiles):
        for i in range(sz.edge):
            out[q, i] = row(q, i).astype(BF16)
    store = pltpu.make_async_copy(out, out_hbm, sems.at[0])
    store.start()
    store.wait()


def add_rows(out, parts):
    for start in range(0, out.shape[0], 16):
        rows = slice(start, start + 16)
        values = [part(rows).astype(F32) for part in parts]
        out[rows] = sum(values[1:], values[0]).astype(BF16)


def share_near_kernel(keep, came, *outs):
    for k, out in enumerate(outs):
        piece = digit_of(1) ^ k
        add_rows(out, [lambda rows: keep[piece, rows], lambda rows: came[piece, rows]])


def quarter_kernel(*refs):
    add_rows(refs[4], [lambda rows, array=array: array[rows] for array in refs[:4]])


def far_kernel(*refs):
    pieces, out, held = refs[:-2], refs[-2], refs[-1]
    if len(pieces) == 2:
        add_rows(out, [lambda rows: pieces[0][rows], lambda rows: pieces[1][rows]])
        return
    for k, piece in enumerate(pieces):
        held[digit_of(2) ^ k] = piece[...]
    add_rows(out, [lambda rows, k=k: held[k, rows] for k in range(len(pieces))])


def middle_kernel(*refs):
    total, payload, held = refs[-3:]
    pieces, quarter, small = refs[:-6], refs[-6], refs[-5:-3]
    far_kernel(*pieces, total, held)
    rows = quarter.shape[0]
    payload[0:rows] = quarter[...]
    add_rows(payload.at[rows:], [lambda rows, array=array: array[rows] for array in small])


def order_kernel(quarter, *refs):
    pieces, out, held = refs[:4], refs[4], refs[5]
    for k, piece in enumerate(pieces):
        place = digit_of(1) ^ k
        out[pl.ds(pl.multiple_of(place * quarter, quarter), quarter), :] = piece[0:quarter]
        if quarter < piece.shape[0]:
            held[place] = piece[quarter:]
    if out.shape[0] > 4 * quarter:
        add_rows(out.at[4 * quarter :], [lambda rows, k=k: held[k, rows] for k in range(4)])


def unpack_half(sz, half, layer, source, staged, up_hbm, down_hbm, sems):
    copies = []
    for k in range(sz.hidden // sz.channels):
        rows = slice(k * sz.channels, (k + 1) * sz.channels)
        staged[rows, :] = source[rows, :].astype(F32)
        place = down_hbm.at[layer, rows] if half == 0 else up_hbm.at[layer, :, rows]
        copy = pltpu.make_async_copy(staged.at[rows], place, sems.at[half, k])
        copy.start()
        copies.append(copy)
    return copies


def unpack_layer_kernel(sz, layer, mine, theirs, up_hbm, down_hbm, token, first, second, sems):
    token[...] = jnp.zeros_like(token)
    for half in range(2):

        @pl.when(digit_of(0) == half)
        def _(half=half):
            copies = unpack_half(sz, half, layer, mine, first, up_hbm, down_hbm, sems)
            copies += unpack_half(sz, 1 - half, layer, theirs, second, up_hbm, down_hbm, sems)
            for copy in copies:
                copy.wait()


def unpack_mine_kernel(sz, layer, mine, _up, _down, up_hbm, down_hbm, staged, sems):
    for half in range(2):

        @pl.when(digit_of(0) == half)
        def _(half=half):
            for copy in unpack_half(sz, half, layer, mine, staged, up_hbm, down_hbm, sems):
                copy.wait()


def unpack_theirs_kernel(
    sz, layer, mine, theirs, _up, _down, up_hbm, down_hbm, kernel_out, gain_out, scale_out,
    staged, small, sems,
):
    for half in range(2):

        @pl.when(digit_of(0) == 1 - half)
        def _(half=half):
            for copy in unpack_half(sz, half, layer, theirs, staged, up_hbm, down_hbm, sems):
                copy.wait()

    small[digit_of(0)] = mine[sz.hidden :].astype(F32)
    small[1 - digit_of(0)] = theirs[sz.hidden :].astype(F32)
    for layer in range(2):
        for a in range(TAPS):
            for b in range(TAPS):
                kernel_out[a, b, layer : layer + 1] = small[layer, pl.ds(a * 8 + b, 1), :]
        gain_out[layer : layer + 1] = small[layer, pl.ds(TAPS * 8, 1), :]
        scale_out[layer : layer + 1] = small[layer, pl.ds(TAPS * 8 + 1, 1), :]


IN_VMEM = pl.BlockSpec(memory_space=pltpu.VMEM)
IN_SMEM = pl.BlockSpec(memory_space=pltpu.SMEM)
IN_HBM = pl.BlockSpec(memory_space=pltpu.HBM)


def call(body, name, micros, ins, outs, scratch, after=(), aliases={}):
    count = len(ins)

    def run(*refs):
        body(*refs[:count], *refs[count + len(after) :])

    return pl.pallas_call(
        run,
        in_specs=[spec for spec, _ in ins] + [pl.BlockSpec(memory_space=pl.ANY)] * len(after),
        out_specs=[spec for spec, _ in outs],
        out_shape=[out for _, out in outs],
        scratch_shapes=scratch,
        compiler_params=pltpu.CompilerParams(vmem_limit_bytes=24 * 1024 * 1024),
        cost_estimate=pl.CostEstimate(
            flops=0, bytes_accessed=int(micros * 3.5e6), transcendentals=0
        ),
        input_output_aliases=aliases,
        name=name,
    )(*[array for _, array in ins], *after)


def near(*arrays):
    return [(IN_VMEM, array) for array in arrays]


def far(*arrays):
    return [(IN_HBM, array) for array in arrays]


def pass_on(shard, by):
    length = lax.axis_size("tile")
    return lax.ppermute(shard, "tile", [(i, (i + by) % length) for i in range(length)])


def partners(array, masks):
    length = lax.axis_size("tile")
    return [
        lax.ppermute(array, "tile", [(i, i ^ mask) for i in range(length)]) for mask in masks
    ]


def swap(arrays, masks):
    length = lax.axis_size("tile")
    return [
        lax.ppermute(array, "tile", [(i, i ^ mask) for i in range(length)])
        for array, mask in zip(arrays, masks)
    ]


class Reduction:
    def __init__(self, devices):
        self.near_masks = [2 * k for k in range(1, 4)]
        self.far_masks = [8 * k for k in range(1, devices // 8)]

    def share(self, keep, send, after=()):
        rows, channels = keep.shape
        dims = (4, rows // 4, channels)
        shape = jax.ShapeDtypeStruct(dims[1:], BF16)
        pieces = call(
            share_near_kernel, "share_near", 0.3,
            near(keep.reshape(dims), swap([send], [1])[0].reshape(dims)),
            near(*[shape] * 4), [], after,
        )
        return [pieces[0]] + swap(pieces[1:], self.near_masks)

    def quarter(self, parts, after):
        shape = jax.ShapeDtypeStruct(parts[0].shape, BF16)
        (total,) = call(quarter_kernel, "quarter", 0.3, near(*parts), near(shape), [], after)
        return total

    def far(self, total):
        pieces = [total] + partners(total, self.far_masks)
        held = (len(pieces),) + total.shape if len(pieces) > 2 else (1, 16, LANES)
        return pieces, [pltpu.VMEM(held, BF16)]

    def middle(self, quarter, other, keep, send):
        pieces, scratch = self.far(quarter)
        rows, channels = quarter.shape
        shapes = [
            jax.ShapeDtypeStruct((rows + more, channels), BF16) for more in (0, keep.shape[0])
        ]
        return call(
            middle_kernel, "middle", 0.5,
            near(*pieces, other, keep, *swap([send], [1])), near(*shapes), scratch,
        )

    def exchange(self, total, after=()):
        pieces, scratch = self.far(total)
        shape = jax.ShapeDtypeStruct(total.shape, BF16)
        (total,) = call(far_kernel, "far", 0.3, near(*pieces), near(shape), scratch, after)
        return total

    def gather(self, total, quarter, after=()):
        rows, channels = total.shape
        shape = jax.ShapeDtypeStruct((3 * quarter + rows, channels), BF16)
        (whole,) = call(
            functools.partial(order_kernel, quarter), "order", 0.4,
            near(total, *partners(total, self.near_masks)), near(shape),
            [pltpu.VMEM((4, max(rows - quarter, 16), channels), BF16)], after,
        )
        return whole


def on_device(
    inputs,
    out_grad,
    kernel,
    norm_gain,
    up_weight,
    down_weight,
    layer_scale,
    seam_table,
    corner_table,
):
    tiles, edge, _, channels = inputs.shape
    layers, _, hidden = up_weight.shape
    sz = Sizes(tiles, edge, channels, hidden)
    columns = lax.axis_size("tile")
    plan = [(IN_SMEM, table.transpose((1, 2, 0))) for table in (seam_table, corner_table)]
    kern = kernel.transpose((1, 2, 0, 3))
    gain, lscale, up, down = norm_gain, layer_scale, up_weight, down_weight
    reduction = Reduction(columns)

    shape = jax.ShapeDtypeStruct
    image = shape(inputs.shape, BF16)
    strips_shape = shape((sz.pieces, REACH, edge, channels), BF16)
    slabs = shape((sz.slabs, sz.cells, LANES), F32)
    padded = shape((sz.slabs, sz.outer * PITCH, LANES), F32)
    inverses = shape((tiles, sz.cells, LANES), F32)
    narrow_short = shape((sz.rows, channels), BF16)
    wide_short = shape((sz.rows, hidden), BF16)
    narrow = shape((sz.rows, channels), F32)
    wide = shape((sz.rows, hidden), F32)
    sums = shape((edge, channels), F32)
    grad_slabs = shape((sz.slabs, edge * GRAD_PITCH, LANES), F32)
    own_shape = shape((sz.pieces, REACH, sz.lanes, edge, LANES), F32)
    pool = shape((3 * sz.pieces, REACH, edge, channels), BF16)
    grad_pool = shape((3 * sz.pieces, REACH, sz.lanes, edge, LANES), F32)
    taps = shape((sz.lanes, TAPS * 8, LANES), F32)
    tap_sums = shape((sz.lanes, TAPS * TAPS, 8, LANES), F32)
    small = shape((SMALL_ROWS, channels), F32)
    half = shape((hidden, channels), BF16)
    two_halves = shape((2, hidden, channels), BF16)

    def vmem(*shapes):
        return [pltpu.VMEM(one.shape, one.dtype) for one in shapes]

    def sems(count):
        return [pltpu.SemaphoreType.DMA((count,))]

    strips, inputs = call(
        functools.partial(strips_kernel, sz),
        "strips", 0.3,
        near(inputs),
        near(strips_shape, image),
        vmem(slabs),
    )
    below, above = pass_on(strips, 1), pass_on(strips, -1)
    fetched = (kern, gain, lscale, up, down)
    kern, gain, lscale, up, down = call(
        fetch_kernel,
        "fetch", 2.0,
        far(*fetched),
        near(*[shape(one.shape, one.dtype) for one in fetched]),
        sems(len(fetched)),
        (strips,),
    )
    middle, strips, pad_zero, normal, inverse, normed, slope, active, branch = call(
        functools.partial(forward_kernel, sz, 0),
        "forward", 8.7,
        plan + near(inputs, strips, below, above, kern, gain, lscale, up, down),
        near(
            image, strips_shape, padded, slabs, inverses,
            narrow_short, wide_short, wide_short, narrow,
        ),
        vmem(pool, taps, slabs, wide, slabs),
    )
    below, above = pass_on(strips, 1), pass_on(strips, -1)
    result, base, grad_own, grad_below, grad_above, *for_weights = call(
        functools.partial(turn_kernel, sz, 1),
        "turn", 15.4,
        plan + near(middle, strips, below, above, kern, gain, lscale, up, down, out_grad),
        far(image)
        + near(
            slabs, own_shape, strips_shape, strips_shape,
            padded, grad_slabs, narrow_short, wide_short, narrow_short, wide_short, sums, sums,
        ),
        vmem(
            pool, taps, slabs, wide, image, slabs, inverses, wide_short, narrow, grad_pool, padded
        )
        + sems(1),
    )
    from_below, from_above = pass_on(grad_above, 1), pass_on(grad_below, -1)
    keep_one, send_one, small_one = call(
        functools.partial(weights_kernel, sz),
        "weights", 2.8,
        near(*for_weights),
        near(half, half, small),
        vmem(tap_sums, two_halves),
    )
    keep_zero, send_zero, flat, up_in, scale_sums = call(
        functools.partial(backward_kernel, sz, 0),
        "backward", 2.9,
        near(
            base, grad_own, from_below, from_above, lscale, down, normed, slope, active, branch
        ),
        near(half, half, slabs, wide_short, sums),
        vmem(wide, narrow_short, two_halves),
    )
    parts_one = reduction.share(keep_one, send_one, (scale_sums,))
    parts_zero = reduction.share(keep_zero, send_zero)
    base, grad_own, grad_below, grad_above, grad_conv, gain_sums = call(
        functools.partial(spread_kernel, sz, 0),
        "spread", 6.0,
        plan + near(kern, gain, up, flat, up_in, normal, inverse),
        near(slabs, own_shape, strips_shape, strips_shape, grad_slabs, sums),
        vmem(taps, narrow, grad_pool, padded),
        (parts_zero[0], parts_one[0]),
    )
    quarter_one = reduction.quarter(parts_one, (gain_sums,))
    quarter_zero = reduction.quarter(parts_zero, (quarter_one,))
    from_below, from_above = pass_on(grad_above, 1), pass_on(grad_below, -1)
    small_keep, small_send = call(
        functools.partial(taps_kernel, sz),
        "taps", 2.1,
        near(pad_zero, grad_conv, gain_sums, scale_sums, small_one),
        near(*[shape(small.shape, BF16)] * 2),
        vmem(tap_sums, small, shape((2,) + small.shape, F32)),
        (quarter_zero,),
    )
    in_grad, token = call(
        functools.partial(last_kernel, sz),
        "last", 1.0,
        near(base, grad_own, from_below, from_above),
        far(image) + near(shape((8, LANES), F32)),
        vmem(slabs, image) + sems(1),
    )
    rows = hidden // 4
    total_one, total_zero = reduction.middle(quarter_one, quarter_zero, small_keep, small_send)
    total_zero = reduction.exchange(total_zero, (token,))
    mine_one = reduction.gather(total_one, rows, (total_zero,))
    theirs_one = partners(mine_one, [1])[0]
    weight_shapes = [shape(up_weight.shape, F32), shape(down_weight.shape, F32)]
    staged = shape((hidden, channels), F32)
    copies = [pltpu.SemaphoreType.DMA((2, hidden // channels))]
    grad_up, grad_down, token = call(
        functools.partial(unpack_layer_kernel, sz, 1),
        "unpack_one", 1.8,
        near(mine_one, theirs_one),
        far(*weight_shapes) + near(shape((8, LANES), F32)),
        vmem(staged, staged) + copies,
    )
    mine = reduction.gather(total_zero, rows, (token,))
    theirs = partners(mine, [1])[0]
    grad_up, grad_down = call(
        functools.partial(unpack_mine_kernel, sz, 0),
        "unpack_mine", 1.0,
        near(mine) + far(grad_up, grad_down),
        far(*weight_shapes),
        vmem(staged) + copies,
        aliases={1: 0, 2: 1},
    )
    grad_up, grad_down, grad_kernel, grad_gain, grad_scale = call(
        functools.partial(unpack_theirs_kernel, sz, 0),
        "unpack_theirs", 1.3,
        near(mine, theirs) + far(grad_up, grad_down),
        far(*weight_shapes)
        + near(
            shape(kern.shape, F32), shape(norm_gain.shape, F32), shape(norm_gain.shape, F32)
        ),
        vmem(staged, shape((2,) + small.shape, F32)) + copies,
        aliases={2: 0, 3: 1},
    )
    return (
        result, in_grad, grad_kernel.transpose((2, 0, 1, 3)),
        grad_gain, grad_up, grad_down, grad_scale,
    )


def solution(mesh):
    placed = (
        P(("groups", "tile"), None, None, None),
        P(("groups", "tile"), None, None, None),
        P(),
        P(),
        P(),
        P(),
        P(),
        P(),
        P(),
    )
    return jax.shard_map(
        on_device,
        mesh=mesh,
        in_specs=placed,
        out_specs=(
            P(("groups", "tile"), None, None, None),
            P(("groups", "tile"), None, None, None),
            P("groups", None, None, None),
            P("groups", None),
            P("groups", None, None),
            P("groups", None, None),
            P("groups", None),
        ),
        check_vma=False,
    )
```

```python
import functools

import jax
import jax.numpy as jnp
from jax import lax
from jax.experimental import pallas as pl
from jax.experimental.pallas import tpu as pltpu
from jax.sharding import PartitionSpec as P

epsilon = 1e-06
inverse_root_two = 0.7071067811865476
inverse_root_tau = 0.3989422804014327

LANES = 128
TAPS = 7
REACH = 3
PITCH = 24
GRAD_PITCH = 32
SMALL_ROWS = 64
F32 = jnp.float32
BF16 = jnp.bfloat16


def flip_rows(value):
    rows = value.shape[0]
    order = 7 - lax.broadcasted_iota(jnp.int32, (8, LANES), 0)
    parts = [
        jnp.take_along_axis(value[at : at + 8], order, axis=0, mode="promise_in_bounds")
        for at in range(0, rows, 8)
    ]
    return jnp.concatenate(parts[::-1], axis=0)


def halves(value):
    return [value[:, at : at + LANES] for at in range(0, value.shape[1], LANES)]


class Sizes:
    def __init__(self, tiles, edge, channels, hidden):
        self.tiles = tiles
        self.edge = edge
        self.channels = channels
        self.hidden = hidden
        self.lanes = channels // LANES
        self.cells = edge * edge
        self.rows = tiles * edge * edge
        self.pieces = tiles * 4
        self.outer = edge + 2 * REACH
        self.slabs = tiles * self.lanes

    def key(self):
        return (self.tiles, self.edge, self.channels, self.hidden)


def strip_window(edge, side, row):
    if side == 0:
        return pl.ds(row * edge, edge), False
    if side == 1:
        return pl.ds(edge - 1 - row, edge, stride=edge), False
    if side == 2:
        return pl.ds((edge - 1 - row) * edge, edge), True
    return pl.ds(row, edge, stride=edge), True


def margin_window(edge, side, row):
    last = edge + 2 * REACH - 1
    if side == 0:
        return pl.ds((2 - row) * PITCH + REACH, edge), True
    if side == 1:
        return pl.ds(REACH * PITCH + last - 2 + row, edge, stride=PITCH), True
    if side == 2:
        return pl.ds((last - 2 + row) * PITCH + REACH, edge), False
    return pl.ds(REACH * PITCH + 2 - row, edge, stride=PITCH), False


def corner_cell(edge, corner, row, column):
    last = edge + 2 * REACH - 1
    r, x = 2 - row, 2 - column
    if corner == 0:
        at = (r, x)
    elif corner == 1:
        at = (x, last - r)
    elif corner == 2:
        at = (last - r, last - x)
    else:
        at = (last - x, r)
    return at[0] * PITCH + at[1]


def read_plan(sz, table):
    columns = lax.axis_size("tile")
    device = lax.axis_index("tile")
    below = lax.rem(device + columns - 1, columns)
    plan = []
    for q in range(sz.tiles):
        for side in range(4):
            source = table[side, 0, device * sz.tiles + q]
            owner = lax.div(source, sz.tiles)
            local = (source - owner * sz.tiles) * 4 + table[side, 1, device * sz.tiles + q]
            shift = jnp.where(
                owner == device, 0, jnp.where(owner == below, sz.pieces, 2 * sz.pieces)
            )
            plan.append(shift + local)
    return plan


def digit_of(level):
    device = lax.axis_index("tile")
    if level == 0:
        return lax.rem(device, 2)
    if level == 1:
        return lax.rem(lax.div(device, 2), 4)
    return lax.div(device, 8)


def write_strips(sz, flat, strips_ref):
    for q in range(sz.tiles):
        for side in range(4):
            for row in range(REACH):
                window, turned = strip_window(sz.edge, side, row)
                parts = [flat[q * sz.lanes + h, window, :] for h in range(sz.lanes)]
                if turned:
                    parts = [flip_rows(part) for part in parts]
                strips_ref[q * 4 + side, row] = jnp.concatenate(parts, axis=1).astype(BF16)


def surround(sz, strip_at, corner_at, cur, own, below, above, pool, pad):
    pool[0 : sz.pieces] = own[...]
    pool[sz.pieces : 2 * sz.pieces] = below[...]
    pool[2 * sz.pieces : 3 * sz.pieces] = above[...]
    for q in range(sz.tiles):
        for i in range(sz.edge):
            for h, part in enumerate(halves(cur[q, i].astype(F32))):
                pad[q * sz.lanes + h, pl.ds((i + REACH) * PITCH + REACH, sz.edge), :] = part
    for q in range(sz.tiles):
        for side in range(4):
            piece = strip_at[q * 4 + side]
            for row in range(REACH):
                window, turned = margin_window(sz.edge, side, row)
                for h, part in enumerate(halves(pool[piece, row].astype(F32))):
                    pad[q * sz.lanes + h, window, :] = flip_rows(part) if turned else part
            piece = corner_at[q * 4 + side]
            for row in range(REACH):
                for h, part in enumerate(halves(pool[piece, row].astype(F32))):
                    for column in range(REACH):
                        at = corner_cell(sz.edge, side, row, column)
                        pad[q * sz.lanes + h, pl.ds(at, 1), :] = part[column : column + 1]


def hold_taps(sz, kern, layer, taps):
    for a in range(TAPS):
        for b in range(TAPS):
            for h, part in enumerate(halves(kern[a, b, layer : layer + 1])):
                taps[h, pl.ds(a * 8 + b, 1), :] = part


def tap(taps, h, a, b):
    return jnp.broadcast_to(taps[h, pl.ds(a * 8 + b, 1), :], (8, LANES))


def convolve(sz, pad, taps, conv):
    @pl.loop(0, sz.slabs)
    def _(slab):
        h = lax.rem(slab, sz.lanes)
        for g in range(sz.edge // 8):
            acc = [None] * sz.edge
            for b in range(TAPS):
                weights = [tap(taps, h, a, b) for a in range(TAPS)]
                for r in range(sz.outer):
                    x = pad[slab, pl.ds(r * PITCH + b + 8 * g, 8), :]
                    for a in range(TAPS):
                        i = r - a
                        if 0 <= i < sz.edge:
                            term = x * weights[a]
                            acc[i] = term if acc[i] is None else acc[i] + term
            for i in range(sz.edge):
                conv[slab, pl.ds(i * sz.edge + 8 * g, 8), :] = acc[i]


def normalise(sz, conv, gain, layer, normal, inverse, normed):
    scale = 1.0 / sz.channels
    for q in range(sz.tiles):

        @pl.loop(0, sz.edge, unroll=2)
        def _(i):
            at = pl.ds(pl.multiple_of(i * sz.edge, sz.edge), sz.edge)
            parts = [conv[q * sz.lanes + h, at, :] for h in range(sz.lanes)]
            mean = jnp.sum(sum(parts[1:], parts[0]), axis=-1, keepdims=True) * scale
            parts = [part - mean for part in parts]
            squares = [part * part for part in parts]
            variance = jnp.sum(sum(squares[1:], squares[0]), axis=-1, keepdims=True) * scale
            root = lax.rsqrt(variance + epsilon)
            inverse[q, at, :] = jnp.broadcast_to(root, (sz.edge, LANES))
            flat_at = pl.ds(pl.multiple_of(q * sz.cells + i * sz.edge, sz.edge), sz.edge)
            for h, part in enumerate(parts):
                part = part * root
                normal[q * sz.lanes + h, at, :] = part
                gains = gain[layer : layer + 1, h * LANES : (h + 1) * LANES]
                normed[flat_at, h * LANES : (h + 1) * LANES] = (part * gains).astype(BF16)


def activate(sz, upward, active, slope):
    width = 512

    @pl.loop(0, sz.rows // 16, unroll=2)
    def _(t):
        at = pl.ds(pl.multiple_of(t * 16, 16), 16)
        for start in range(0, sz.hidden, width):
            u = upward[at, start : start + width]
            chance = 0.5 * (1.0 + lax.erf(u * inverse_root_two))
            active[at, start : start + width] = (u * chance).astype(BF16)
            slope[at, start : start + width] = (
                chance + u * jnp.exp(-0.5 * u * u) * inverse_root_tau
            ).astype(slope.dtype)


def multiply(a, b, ca=1, cb=0):
    return lax.dot_general(a, b, (((ca,), (cb,)), ((), ())), preferred_element_type=F32)


def finish_forward(sz, cur, branch, lscale, layer, out, flat):
    for q in range(sz.tiles):

        @pl.loop(0, sz.edge, unroll=2)
        def _(i):
            at = pl.ds(pl.multiple_of(q * sz.cells + i * sz.edge, sz.edge), sz.edge)
            value = cur[q, i].astype(F32) + branch[at, :] * lscale[layer : layer + 1, :]
            value = value.astype(BF16)
            out[q, i] = value
            if flat is not None:
                local = pl.ds(pl.multiple_of(i * sz.edge, sz.edge), sz.edge)
                for h, part in enumerate(halves(value.astype(F32))):
                    flat[q * sz.lanes + h, local, :] = part


def scale_rows(sz, grad_row, branch, lscale, layer, down_in, sums):
    sums[...] = jnp.zeros_like(sums)
    for q in range(sz.tiles):

        @pl.loop(0, sz.edge, unroll=2)
        def _(i):
            at = pl.ds(pl.multiple_of(q * sz.cells + i * sz.edge, sz.edge), sz.edge)
            g = grad_row(q, i)
            down_in[at, :] = (g * lscale[layer : layer + 1, :]).astype(BF16)
            sums[...] += g * branch[at, :]


def slope_rows(sz, grad_active, slope, up_in):
    @pl.loop(0, sz.rows // 16, unroll=2)
    def _(t):
        at = pl.ds(pl.multiple_of(t * 16, 16), 16)
        up_in[at, :] = (grad_active[at, :] * slope[at, :].astype(F32)).astype(BF16)


def weight_gradients(sz, core, active, down_in, normed, up_in, both, keep, send):
    both[0] = multiply(active[...], down_in[...], 0, 0).astype(BF16)
    for k in range(sz.hidden // sz.channels):
        part = multiply(normed[...], up_in[:, k * sz.channels : (k + 1) * sz.channels], 0, 0)
        both[1, k * sz.channels : (k + 1) * sz.channels, :] = part.astype(BF16)
    keep[...] = both[core]
    send[...] = both[1 - core]


def norm_gradients(sz, grad_normed, normal, inverse, gain, layer, grad_conv, sums):
    scale = 1.0 / sz.channels
    sums[...] = jnp.zeros_like(sums)
    blank = jnp.zeros((8, LANES), F32)
    for q in range(sz.tiles):

        @pl.loop(0, sz.edge, unroll=2)
        def _(i):
            at = pl.ds(pl.multiple_of(q * sz.cells + i * sz.edge, sz.edge), sz.edge)
            local = pl.ds(pl.multiple_of(i * sz.edge, sz.edge), sz.edge)
            g = halves(grad_normed[at, :])
            n = [normal[q * sz.lanes + h, local, :] for h in range(sz.lanes)]
            sums[...] += jnp.concatenate([a * b for a, b in zip(g, n)], axis=1)
            s = [
                part * gain[layer : layer + 1, h * LANES : (h + 1) * LANES]
                for h, part in enumerate(g)
            ]
            products = [a * b for a, b in zip(s, n)]
            mean = jnp.sum(sum(s[1:], s[0]), axis=-1, keepdims=True) * scale
            slant = jnp.sum(sum(products[1:], products[0]), axis=-1, keepdims=True) * scale
            root = inverse[q, local, :]
            for h in range(sz.lanes):
                slab = q * sz.lanes + h
                base = pl.multiple_of(i * GRAD_PITCH, GRAD_PITCH)
                grad_conv[slab, pl.ds(base, 8), :] = blank
                grad_conv[slab, pl.ds(base + 8, sz.edge), :] = root * (s[h] - mean - n[h] * slant)
                grad_conv[slab, pl.ds(base + 8 + sz.edge, 8), :] = blank


def tap_gradients(sz, pad, grad_conv, tap_sums, small):
    tap_sums[...] = jnp.zeros_like(tap_sums)

    @pl.loop(0, sz.slabs)
    def _(slab):
        h = lax.rem(slab, sz.lanes)
        for b in range(TAPS):
            acc = [None] * TAPS
            for g in range(sz.edge // 8):
                grads = [
                    grad_conv[slab, pl.ds(i * GRAD_PITCH + 8 + 8 * g, 8), :]
                    for i in range(sz.edge)
                ]
                for r in range(sz.outer):
                    x = pad[slab, pl.ds(r * PITCH + b + 8 * g, 8), :]
                    for a in range(TAPS):
                        i = r - a
                        if 0 <= i < sz.edge:
                            term = x * grads[i]
                            acc[a] = term if acc[a] is None else acc[a] + term
            for a in range(TAPS):
                tap_sums[h, a * TAPS + b] += acc[a]

    for h in range(sz.lanes):
        for k in range(TAPS * TAPS):
            row = k // TAPS * 8 + k % TAPS
            small[row : row + 1, h * LANES : (h + 1) * LANES] = jnp.sum(
                tap_sums[h, k], axis=0, keepdims=True
            )


def spread_gradients(sz, grad_conv, taps, grad_pad):
    @pl.loop(0, sz.slabs)
    def _(slab):
        h = lax.rem(slab, sz.lanes)
        for g in range(PITCH // 8):
            acc = [None] * sz.outer
            for b in range(TAPS):
                start = 8 * g - b + 8
                if start >= 8 + sz.edge:
                    continue
                weights = [tap(taps, h, a, b) for a in range(TAPS)]
                for i in range(sz.edge):
                    x = grad_conv[slab, pl.ds(i * GRAD_PITCH + start, 8), :]
                    for a in range(TAPS):
                        term = x * weights[a]
                        acc[i + a] = term if acc[i + a] is None else acc[i + a] + term
            for p in range(sz.outer):
                grad_pad[slab, pl.ds(p * PITCH + 8 * g, 8), :] = acc[p]


def return_margins(sz, strip_at, corner_at, grad_pad, pool):
    pool[...] = jnp.zeros_like(pool)
    for q in range(sz.tiles):
        for side in range(4):
            piece = strip_at[q * 4 + side]
            for row in range(REACH):
                window, turned = margin_window(sz.edge, side, row)
                for h in range(sz.lanes):
                    part = grad_pad[q * sz.lanes + h, window, :]
                    pool[piece, row, h] = flip_rows(part) if turned else part
    for q in range(sz.tiles):
        for side in range(4):
            piece = corner_at[q * 4 + side]
            for row in range(REACH):
                for column in range(REACH):
                    at = corner_cell(sz.edge, side, row, column)
                    for h in range(sz.lanes):
                        pool[piece, row, h, pl.ds(column, 1), :] += grad_pad[
                            q * sz.lanes + h, pl.ds(at, 1), :
                        ]


def send_margins(sz, pool, own, below, above):
    own[...] = pool[0 : sz.pieces]
    for piece in range(sz.pieces):
        for row in range(REACH):
            for offset, ref in ((1, below), (2, above)):
                parts = [pool[offset * sz.pieces + piece, row, h] for h in range(sz.lanes)]
                ref[piece, row] = jnp.concatenate(parts, axis=1).astype(BF16)


def gather_inner(sz, grad_row, grad_pad, base):
    for q in range(sz.tiles):
        for i in range(sz.edge):
            for h, part in enumerate(halves(grad_row(q, i))):
                slab = q * sz.lanes + h
                base[slab, pl.ds(i * sz.edge, sz.edge), :] = (
                    part + grad_pad[slab, pl.ds((i + REACH) * PITCH + REACH, sz.edge), :]
                )


def add_strips(sz, base, own, first, second, flat):
    flat[...] = base[...]
    for q in range(sz.tiles):
        for side in range(4):
            piece = q * 4 + side
            for row in range(REACH):
                window, turned = strip_window(sz.edge, side, row)
                came = first[piece, row].astype(F32) + second[piece, row].astype(F32)
                for h, part in enumerate(halves(came)):
                    part = part + own[piece, row, h]
                    flat[q * sz.lanes + h, window, :] += flip_rows(part) if turned else part


def fill_small(small, gain_sums, scale_sums):
    small[TAPS * 8 : TAPS * 8 + 1, :] = jnp.sum(gain_sums[...], axis=0, keepdims=True)
    small[TAPS * 8 + 1 : TAPS * 8 + 2, :] = jnp.sum(scale_sums[...], axis=0, keepdims=True)


def flat_grad_row(sz, flat):
    def row(q, i):
        at = pl.ds(i * sz.edge, sz.edge)
        parts = [flat[q * sz.lanes + h, at, :] for h in range(sz.lanes)]
        return jnp.concatenate(parts, axis=1)

    return row


def fetch_kernel(*refs):
    count = (len(refs) - 1) // 2
    copies = [
        pltpu.make_async_copy(refs[k], refs[count + k], refs[-1].at[k]) for k in range(count)
    ]
    for copy in copies:
        copy.start()
    for copy in copies:
        copy.wait()


def strips_kernel(sz, cur, strips, held, flat):
    held[...] = cur[...]
    for q in range(sz.tiles):
        for i in range(sz.edge):
            for h, part in enumerate(halves(cur[q, i].astype(F32))):
                flat[q * sz.lanes + h, pl.ds(i * sz.edge, sz.edge), :] = part
    write_strips(sz, flat, strips)


def forward_kernel(
    sz, layer, seams, corners, cur, own, below, above, kern, gain, lscale, up, down,
    out, strips, pad, normal, inverse, normed, slope, active, branch,
    pool, taps, conv, upward, flat,
):
    strip_at, corner_at = read_plan(sz, seams), read_plan(sz, corners)
    surround(sz, strip_at, corner_at, cur, own, below, above, pool, pad)
    hold_taps(sz, kern, layer, taps)
    convolve(sz, pad, taps, conv)
    normalise(sz, conv, gain, layer, normal, inverse, normed)
    upward[...] = multiply(normed[...], up[layer])
    activate(sz, upward, active, slope)
    branch[...] = multiply(active[...], down[layer])
    finish_forward(sz, cur, branch, lscale, layer, out, flat)
    write_strips(sz, flat, strips)


def turn_kernel(
    sz, layer, seams, corners, cur, own, below, above, kern, gain, lscale, up, down, out_grad,
    out_hbm, base, grad_own, grad_below, grad_above,
    pad, grad_conv, normed, active, down_in, up_in, gain_sums, scale_sums,
    pool, taps, conv, upward, out, normal, inverse, slope, branch, grad_pool, grad_pad, out_sem,
):
    strip_at, corner_at = read_plan(sz, seams), read_plan(sz, corners)
    surround(sz, strip_at, corner_at, cur, own, below, above, pool, pad)
    hold_taps(sz, kern, layer, taps)
    convolve(sz, pad, taps, conv)
    normalise(sz, conv, gain, layer, normal, inverse, normed)
    upward[...] = multiply(normed[...], up[layer])
    activate(sz, upward, active, slope)
    branch[...] = multiply(active[...], down[layer])
    finish_forward(sz, cur, branch, lscale, layer, out, None)
    store = pltpu.make_async_copy(out, out_hbm, out_sem.at[0])
    store.start()

    def grad_row(q, i):
        return out_grad[q, i].astype(F32)

    scale_rows(sz, grad_row, branch, lscale, layer, down_in, scale_sums)
    upward[...] = multiply(down_in[...], down[layer], 1, 1)
    slope_rows(sz, upward, slope, up_in)
    branch[...] = multiply(up_in[...], up[layer], 1, 1)
    norm_gradients(sz, branch, normal, inverse, gain, layer, grad_conv, gain_sums)
    spread_gradients(sz, grad_conv, taps, grad_pad)
    return_margins(sz, strip_at, corner_at, grad_pad, grad_pool)
    send_margins(sz, grad_pool, grad_own, grad_below, grad_above)
    gather_inner(sz, grad_row, grad_pad, base)
    store.wait()


def weights_kernel(
    sz, pad, grad_conv, normed, active, down_in, up_in, gain_sums, scale_sums,
    keep, send, small, tap_sums, both,
):
    small[...] = jnp.zeros_like(small)
    weight_gradients(sz, digit_of(0), active, down_in, normed, up_in, both, keep, send)
    tap_gradients(sz, pad, grad_conv, tap_sums, small)
    fill_small(small, gain_sums, scale_sums)


def backward_kernel(
    sz, layer, base, own, first, second, lscale, down, normed, slope, active, branch,
    keep, send, flat, up_in, scale_sums,
    hidden, down_in, both,
):
    add_strips(sz, base, own, first, second, flat)
    for slab in range(sz.slabs):
        flat[slab] = flat[slab].astype(BF16).astype(F32)
    scale_rows(sz, flat_grad_row(sz, flat), branch, lscale, layer, down_in, scale_sums)
    hidden[...] = multiply(down_in[...], down[layer], 1, 1)
    slope_rows(sz, hidden, slope, up_in)
    weight_gradients(sz, digit_of(0), active, down_in, normed, up_in, both, keep, send)


def spread_kernel(
    sz, layer, seams, corners, kern, gain, up, flat, up_in, normal, inverse,
    base, grad_own, grad_below, grad_above, grad_conv, gain_sums,
    taps, branch, grad_pool, grad_pad,
):
    strip_at, corner_at = read_plan(sz, seams), read_plan(sz, corners)
    branch[...] = multiply(up_in[...], up[layer], 1, 1)
    norm_gradients(sz, branch, normal, inverse, gain, layer, grad_conv, gain_sums)
    hold_taps(sz, kern, layer, taps)
    spread_gradients(sz, grad_conv, taps, grad_pad)
    return_margins(sz, strip_at, corner_at, grad_pad, grad_pool)
    send_margins(sz, grad_pool, grad_own, grad_below, grad_above)
    gather_inner(sz, flat_grad_row(sz, flat), grad_pad, base)


def taps_kernel(
    sz, pad, grad_conv, gain_sums, scale_sums, other, keep, send, tap_sums, small, both
):
    small[...] = jnp.zeros_like(small)
    tap_gradients(sz, pad, grad_conv, tap_sums, small)
    fill_small(small, gain_sums, scale_sums)
    both[0] = small[...]
    both[1] = other[...]
    keep[...] = both[digit_of(0)].astype(BF16)
    send[...] = both[1 - digit_of(0)].astype(BF16)


def last_kernel(sz, base, own, first, second, out_hbm, token, flat, out, sems):
    token[...] = jnp.zeros_like(token)
    add_strips(sz, base, own, first, second, flat)
    row = flat_grad_row(sz, flat)
    for q in range(sz.tiles):
        for i in range(sz.edge):
            out[q, i] = row(q, i).astype(BF16)
    store = pltpu.make_async_copy(out, out_hbm, sems.at[0])
    store.start()
    store.wait()


def add_rows(out, parts):
    for start in range(0, out.shape[0], 16):
        rows = slice(start, start + 16)
        values = [part(rows).astype(F32) for part in parts]
        out[rows] = sum(values[1:], values[0]).astype(BF16)


def share_near_kernel(keep, came, *outs):
    for k, out in enumerate(outs):
        piece = digit_of(1) ^ k
        add_rows(out, [lambda rows: keep[piece, rows], lambda rows: came[piece, rows]])


def quarter_kernel(*refs):
    add_rows(refs[4], [lambda rows, array=array: array[rows] for array in refs[:4]])


def far_kernel(*refs):
    pieces, out, held = refs[:-2], refs[-2], refs[-1]
    if len(pieces) == 2:
        add_rows(out, [lambda rows: pieces[0][rows], lambda rows: pieces[1][rows]])
        return
    for k, piece in enumerate(pieces):
        held[digit_of(2) ^ k] = piece[...]
    add_rows(out, [lambda rows, k=k: held[k, rows] for k in range(len(pieces))])


def middle_kernel(*refs):
    total, payload, held = refs[-3:]
    pieces, quarter, small = refs[:-6], refs[-6], refs[-5:-3]
    far_kernel(*pieces, total, held)
    rows = quarter.shape[0]
    payload[0:rows] = quarter[...]
    add_rows(payload.at[rows:], [lambda rows, array=array: array[rows] for array in small])


def order_kernel(quarter, *refs):
    pieces, out, held = refs[:4], refs[4], refs[5]
    for k, piece in enumerate(pieces):
        place = digit_of(1) ^ k
        out[pl.ds(pl.multiple_of(place * quarter, quarter), quarter), :] = piece[0:quarter]
        if quarter < piece.shape[0]:
            held[place] = piece[quarter:]
    if out.shape[0] > 4 * quarter:
        add_rows(out.at[4 * quarter :], [lambda rows, k=k: held[k, rows] for k in range(4)])


def unpack_half(sz, half, layer, source, staged, up_hbm, down_hbm, sems):
    copies = []
    for k in range(sz.hidden // sz.channels):
        rows = slice(k * sz.channels, (k + 1) * sz.channels)
        staged[rows, :] = source[rows, :].astype(F32)
        place = down_hbm.at[layer, rows] if half == 0 else up_hbm.at[layer, :, rows]
        copy = pltpu.make_async_copy(staged.at[rows], place, sems.at[half, k])
        copy.start()
        copies.append(copy)
    return copies


def unpack_layer_kernel(sz, layer, mine, theirs, up_hbm, down_hbm, token, first, second, sems):
    token[...] = jnp.zeros_like(token)
    for half in range(2):

        @pl.when(digit_of(0) == half)
        def _(half=half):
            copies = unpack_half(sz, half, layer, mine, first, up_hbm, down_hbm, sems)
            copies += unpack_half(sz, 1 - half, layer, theirs, second, up_hbm, down_hbm, sems)
            for copy in copies:
                copy.wait()


def unpack_mine_kernel(sz, layer, mine, _up, _down, up_hbm, down_hbm, staged, sems):
    for half in range(2):

        @pl.when(digit_of(0) == half)
        def _(half=half):
            for copy in unpack_half(sz, half, layer, mine, staged, up_hbm, down_hbm, sems):
                copy.wait()


def unpack_theirs_kernel(
    sz, layer, mine, theirs, _up, _down, up_hbm, down_hbm, kernel_out, gain_out, scale_out,
    staged, small, sems,
):
    for half in range(2):

        @pl.when(digit_of(0) == 1 - half)
        def _(half=half):
            for copy in unpack_half(sz, half, layer, theirs, staged, up_hbm, down_hbm, sems):
                copy.wait()

    small[digit_of(0)] = mine[sz.hidden :].astype(F32)
    small[1 - digit_of(0)] = theirs[sz.hidden :].astype(F32)
    for layer in range(2):
        for a in range(TAPS):
            for b in range(TAPS):
                kernel_out[a, b, layer : layer + 1] = small[layer, pl.ds(a * 8 + b, 1), :]
        gain_out[layer : layer + 1] = small[layer, pl.ds(TAPS * 8, 1), :]
        scale_out[layer : layer + 1] = small[layer, pl.ds(TAPS * 8 + 1, 1), :]


IN_VMEM = pl.BlockSpec(memory_space=pltpu.VMEM)
IN_SMEM = pl.BlockSpec(memory_space=pltpu.SMEM)
IN_HBM = pl.BlockSpec(memory_space=pltpu.HBM)


def call(body, name, micros, ins, outs, scratch, after=(), aliases={}):
    count = len(ins)

    def run(*refs):
        body(*refs[:count], *refs[count + len(after) :])

    return pl.pallas_call(
        run,
        in_specs=[spec for spec, _ in ins] + [pl.BlockSpec(memory_space=pl.ANY)] * len(after),
        out_specs=[spec for spec, _ in outs],
        out_shape=[out for _, out in outs],
        scratch_shapes=scratch,
        compiler_params=pltpu.CompilerParams(vmem_limit_bytes=24 * 1024 * 1024),
        cost_estimate=pl.CostEstimate(
            flops=0, bytes_accessed=int(micros * 3.5e6), transcendentals=0
        ),
        input_output_aliases=aliases,
        name=name,
    )(*[array for _, array in ins], *after)


def near(*arrays):
    return [(IN_VMEM, array) for array in arrays]


def far(*arrays):
    return [(IN_HBM, array) for array in arrays]


def pass_on(shard, by):
    length = lax.axis_size("tile")
    return lax.ppermute(shard, "tile", [(i, (i + by) % length) for i in range(length)])


def partners(array, masks):
    length = lax.axis_size("tile")
    return [
        lax.ppermute(array, "tile", [(i, i ^ mask) for i in range(length)]) for mask in masks
    ]


def swap(arrays, masks):
    length = lax.axis_size("tile")
    return [
        lax.ppermute(array, "tile", [(i, i ^ mask) for i in range(length)])
        for array, mask in zip(arrays, masks)
    ]


class Reduction:
    def __init__(self, devices):
        self.near_masks = [2 * k for k in range(1, 4)]
        self.far_masks = [8 * k for k in range(1, devices // 8)]

    def share(self, keep, send, after=()):
        rows, channels = keep.shape
        dims = (4, rows // 4, channels)
        shape = jax.ShapeDtypeStruct(dims[1:], BF16)
        pieces = call(
            share_near_kernel, "share_near", 0.3,
            near(keep.reshape(dims), swap([send], [1])[0].reshape(dims)),
            near(*[shape] * 4), [], after,
        )
        return [pieces[0]] + swap(pieces[1:], self.near_masks)

    def quarter(self, parts, after):
        shape = jax.ShapeDtypeStruct(parts[0].shape, BF16)
        (total,) = call(quarter_kernel, "quarter", 0.3, near(*parts), near(shape), [], after)
        return total

    def far(self, total):
        pieces = [total] + partners(total, self.far_masks)
        held = (len(pieces),) + total.shape if len(pieces) > 2 else (1, 16, LANES)
        return pieces, [pltpu.VMEM(held, BF16)]

    def middle(self, quarter, other, keep, send):
        pieces, scratch = self.far(quarter)
        rows, channels = quarter.shape
        shapes = [
            jax.ShapeDtypeStruct((rows + more, channels), BF16) for more in (0, keep.shape[0])
        ]
        return call(
            middle_kernel, "middle", 0.5,
            near(*pieces, other, keep, *swap([send], [1])), near(*shapes), scratch,
        )

    def exchange(self, total, after=()):
        pieces, scratch = self.far(total)
        shape = jax.ShapeDtypeStruct(total.shape, BF16)
        (total,) = call(far_kernel, "far", 0.3, near(*pieces), near(shape), scratch, after)
        return total

    def gather(self, total, quarter, after=()):
        rows, channels = total.shape
        shape = jax.ShapeDtypeStruct((3 * quarter + rows, channels), BF16)
        (whole,) = call(
            functools.partial(order_kernel, quarter), "order", 0.4,
            near(total, *partners(total, self.near_masks)), near(shape),
            [pltpu.VMEM((4, max(rows - quarter, 16), channels), BF16)], after,
        )
        return whole


def on_device(
    inputs,
    out_grad,
    kernel,
    norm_gain,
    up_weight,
    down_weight,
    layer_scale,
    seam_table,
    corner_table,
):
    tiles, edge, _, channels = inputs.shape
    layers, _, hidden = up_weight.shape
    sz = Sizes(tiles, edge, channels, hidden)
    columns = lax.axis_size("tile")
    plan = [(IN_SMEM, table.transpose((1, 2, 0))) for table in (seam_table, corner_table)]
    kern = kernel.transpose((1, 2, 0, 3))
    gain, lscale, up, down = norm_gain, layer_scale, up_weight, down_weight
    reduction = Reduction(columns)

    shape = jax.ShapeDtypeStruct
    image = shape(inputs.shape, BF16)
    strips_shape = shape((sz.pieces, REACH, edge, channels), BF16)
    slabs = shape((sz.slabs, sz.cells, LANES), F32)
    padded = shape((sz.slabs, sz.outer * PITCH, LANES), F32)
    inverses = shape((tiles, sz.cells, LANES), F32)
    narrow_short = shape((sz.rows, channels), BF16)
    wide_short = shape((sz.rows, hidden), BF16)
    narrow = shape((sz.rows, channels), F32)
    wide = shape((sz.rows, hidden), F32)
    sums = shape((edge, channels), F32)
    grad_slabs = shape((sz.slabs, edge * GRAD_PITCH, LANES), F32)
    own_shape = shape((sz.pieces, REACH, sz.lanes, edge, LANES), F32)
    pool = shape((3 * sz.pieces, REACH, edge, channels), BF16)
    grad_pool = shape((3 * sz.pieces, REACH, sz.lanes, edge, LANES), F32)
    taps = shape((sz.lanes, TAPS * 8, LANES), F32)
    tap_sums = shape((sz.lanes, TAPS * TAPS, 8, LANES), F32)
    small = shape((SMALL_ROWS, channels), F32)
    half = shape((hidden, channels), BF16)
    two_halves = shape((2, hidden, channels), BF16)

    def vmem(*shapes):
        return [pltpu.VMEM(one.shape, one.dtype) for one in shapes]

    def sems(count):
        return [pltpu.SemaphoreType.DMA((count,))]

    strips, inputs = call(
        functools.partial(strips_kernel, sz),
        "strips", 0.3,
        near(inputs),
        near(strips_shape, image),
        vmem(slabs),
    )
    below, above = pass_on(strips, 1), pass_on(strips, -1)
    fetched = (kern, gain, lscale, up, down)
    kern, gain, lscale, up, down = call(
        fetch_kernel,
        "fetch", 2.0,
        far(*fetched),
        near(*[shape(one.shape, one.dtype) for one in fetched]),
        sems(len(fetched)),
        (strips,),
    )
    middle, strips, pad_zero, normal, inverse, normed, slope, active, branch = call(
        functools.partial(forward_kernel, sz, 0),
        "forward", 8.7,
        plan + near(inputs, strips, below, above, kern, gain, lscale, up, down),
        near(
            image, strips_shape, padded, slabs, inverses,
            narrow_short, wide_short, wide_short, narrow,
        ),
        vmem(pool, taps, slabs, wide, slabs),
    )
    below, above = pass_on(strips, 1), pass_on(strips, -1)
    result, base, grad_own, grad_below, grad_above, *for_weights = call(
        functools.partial(turn_kernel, sz, 1),
        "turn", 15.4,
        plan + near(middle, strips, below, above, kern, gain, lscale, up, down, out_grad),
        far(image)
        + near(
            slabs, own_shape, strips_shape, strips_shape,
            padded, grad_slabs, narrow_short, wide_short, narrow_short, wide_short, sums, sums,
        ),
        vmem(
            pool, taps, slabs, wide, image, slabs, inverses, wide_short, narrow, grad_pool, padded
        )
        + sems(1),
    )
    from_below, from_above = pass_on(grad_above, 1), pass_on(grad_below, -1)
    keep_one, send_one, small_one = call(
        functools.partial(weights_kernel, sz),
        "weights", 2.8,
        near(*for_weights),
        near(half, half, small),
        vmem(tap_sums, two_halves),
    )
    keep_zero, send_zero, flat, up_in, scale_sums = call(
        functools.partial(backward_kernel, sz, 0),
        "backward", 2.9,
        near(
            base, grad_own, from_below, from_above, lscale, down, normed, slope, active, branch
        ),
        near(half, half, slabs, wide_short, sums),
        vmem(wide, narrow_short, two_halves),
    )
    parts_one = reduction.share(keep_one, send_one, (scale_sums,))
    parts_zero = reduction.share(keep_zero, send_zero)
    base, grad_own, grad_below, grad_above, grad_conv, gain_sums = call(
        functools.partial(spread_kernel, sz, 0),
        "spread", 6.0,
        plan + near(kern, gain, up, flat, up_in, normal, inverse),
        near(slabs, own_shape, strips_shape, strips_shape, grad_slabs, sums),
        vmem(taps, narrow, grad_pool, padded),
        (parts_zero[0], parts_one[0]),
    )
    quarter_one = reduction.quarter(parts_one, (gain_sums,))
    quarter_zero = reduction.quarter(parts_zero, (quarter_one,))
    from_below, from_above = pass_on(grad_above, 1), pass_on(grad_below, -1)
    small_keep, small_send = call(
        functools.partial(taps_kernel, sz),
        "taps", 2.1,
        near(pad_zero, grad_conv, gain_sums, scale_sums, small_one),
        near(*[shape(small.shape, BF16)] * 2),
        vmem(tap_sums, small, shape((2,) + small.shape, F32)),
        (quarter_zero,),
    )
    in_grad, token = call(
        functools.partial(last_kernel, sz),
        "last", 1.0,
        near(base, grad_own, from_below, from_above),
        far(image) + near(shape((8, LANES), F32)),
        vmem(slabs, image) + sems(1),
    )
    rows = hidden // 4
    total_one, total_zero = reduction.middle(quarter_one, quarter_zero, small_keep, small_send)
    total_zero = reduction.exchange(total_zero, (token,))
    mine_one = reduction.gather(total_one, rows, (total_zero,))
    theirs_one = partners(mine_one, [1])[0]
    weight_shapes = [shape(up_weight.shape, F32), shape(down_weight.shape, F32)]
    staged = shape((hidden, channels), F32)
    copies = [pltpu.SemaphoreType.DMA((2, hidden // channels))]
    grad_up, grad_down, token = call(
        functools.partial(unpack_layer_kernel, sz, 1),
        "unpack_one", 1.8,
        near(mine_one, theirs_one),
        far(*weight_shapes) + near(shape((8, LANES), F32)),
        vmem(staged, staged) + copies,
    )
    mine = reduction.gather(total_zero, rows, (token,))
    theirs = partners(mine, [1])[0]
    grad_up, grad_down = call(
        functools.partial(unpack_mine_kernel, sz, 0),
        "unpack_mine", 1.0,
        near(mine) + far(grad_up, grad_down),
        far(*weight_shapes),
        vmem(staged) + copies,
        aliases={1: 0, 2: 1},
    )
    grad_up, grad_down, grad_kernel, grad_gain, grad_scale = call(
        functools.partial(unpack_theirs_kernel, sz, 0),
        "unpack_theirs", 1.3,
        near(mine, theirs) + far(grad_up, grad_down),
        far(*weight_shapes)
        + near(
            shape(kern.shape, F32), shape(norm_gain.shape, F32), shape(norm_gain.shape, F32)
        ),
        vmem(staged, shape((2,) + small.shape, F32)) + copies,
        aliases={2: 0, 3: 1},
    )
    return (
        result, in_grad, grad_kernel.transpose((2, 0, 1, 3)),
        grad_gain, grad_up, grad_down, grad_scale,
    )


def solution(mesh):
    placed = (
        P(("groups", "tile"), None, None, None),
        P(("groups", "tile"), None, None, None),
        P(),
        P(),
        P(),
        P(),
        P(),
        P(),
        P(),
    )
    return jax.shard_map(
        on_device,
        mesh=mesh,
        in_specs=placed,
        out_specs=(
            P(("groups", "tile"), None, None, None),
            P(("groups", "tile"), None, None, None),
            P("groups", None, None, None),
            P("groups", None),
            P("groups", None, None),
            P("groups", None, None),
            P("groups", None),
        ),
        check_vma=False,
    )
```

```python
import functools

import jax
import jax.numpy as jnp
from jax import lax
from jax.experimental import pallas as pl
from jax.experimental.pallas import tpu as pltpu
from jax.sharding import PartitionSpec as P

epsilon = 1e-06
inverse_root_two = 0.7071067811865476
inverse_root_tau = 0.3989422804014327

LANES = 128
TAPS = 7
REACH = 3
PITCH = 24
GRAD_PITCH = 32
SMALL_ROWS = 64
F32 = jnp.float32
BF16 = jnp.bfloat16


def flip_rows(value):
    rows = value.shape[0]
    order = 7 - lax.broadcasted_iota(jnp.int32, (8, LANES), 0)
    parts = [
        jnp.take_along_axis(value[at : at + 8], order, axis=0, mode="promise_in_bounds")
        for at in range(0, rows, 8)
    ]
    return jnp.concatenate(parts[::-1], axis=0)


def halves(value):
    return [value[:, at : at + LANES] for at in range(0, value.shape[1], LANES)]


class Sizes:
    def __init__(self, tiles, edge, channels, hidden):
        self.tiles = tiles
        self.edge = edge
        self.channels = channels
        self.hidden = hidden
        self.lanes = channels // LANES
        self.cells = edge * edge
        self.rows = tiles * edge * edge
        self.pieces = tiles * 4
        self.outer = edge + 2 * REACH
        self.slabs = tiles * self.lanes

    def key(self):
        return (self.tiles, self.edge, self.channels, self.hidden)


def strip_window(edge, side, row):
    if side == 0:
        return pl.ds(row * edge, edge), False
    if side == 1:
        return pl.ds(edge - 1 - row, edge, stride=edge), False
    if side == 2:
        return pl.ds((edge - 1 - row) * edge, edge), True
    return pl.ds(row, edge, stride=edge), True


def margin_window(edge, side, row):
    last = edge + 2 * REACH - 1
    if side == 0:
        return pl.ds((2 - row) * PITCH + REACH, edge), True
    if side == 1:
        return pl.ds(REACH * PITCH + last - 2 + row, edge, stride=PITCH), True
    if side == 2:
        return pl.ds((last - 2 + row) * PITCH + REACH, edge), False
    return pl.ds(REACH * PITCH + 2 - row, edge, stride=PITCH), False


def corner_cell(edge, corner, row, column):
    last = edge + 2 * REACH - 1
    r, x = 2 - row, 2 - column
    if corner == 0:
        at = (r, x)
    elif corner == 1:
        at = (x, last - r)
    elif corner == 2:
        at = (last - r, last - x)
    else:
        at = (last - x, r)
    return at[0] * PITCH + at[1]


def read_plan(sz, table):
    columns = lax.axis_size("tile")
    device = lax.axis_index("tile")
    below = lax.rem(device + columns - 1, columns)
    plan = []
    for q in range(sz.tiles):
        for side in range(4):
            source = table[side, 0, device * sz.tiles + q]
            owner = lax.div(source, sz.tiles)
            local = (source - owner * sz.tiles) * 4 + table[side, 1, device * sz.tiles + q]
            shift = jnp.where(
                owner == device, 0, jnp.where(owner == below, sz.pieces, 2 * sz.pieces)
            )
            plan.append(shift + local)
    return plan


def digit_of(level):
    device = lax.axis_index("tile")
    if level == 0:
        return lax.rem(device, 2)
    if level == 1:
        return lax.rem(lax.div(device, 2), 4)
    return lax.div(device, 8)


def write_strips(sz, flat, strips_ref):
    for q in range(sz.tiles):
        for side in range(4):
            for row in range(REACH):
                window, turned = strip_window(sz.edge, side, row)
                parts = [flat[q * sz.lanes + h, window, :] for h in range(sz.lanes)]
                if turned:
                    parts = [flip_rows(part) for part in parts]
                strips_ref[q * 4 + side, row] = jnp.concatenate(parts, axis=1).astype(BF16)


def surround(sz, strip_at, corner_at, cur, own, below, above, pool, pad):
    pool[0 : sz.pieces] = own[...]
    pool[sz.pieces : 2 * sz.pieces] = below[...]
    pool[2 * sz.pieces : 3 * sz.pieces] = above[...]
    for q in range(sz.tiles):
        for i in range(sz.edge):
            for h, part in enumerate(halves(cur[q, i].astype(F32))):
                pad[q * sz.lanes + h, pl.ds((i + REACH) * PITCH + REACH, sz.edge), :] = part
    for q in range(sz.tiles):
        for side in range(4):
            piece = strip_at[q * 4 + side]
            for row in range(REACH):
                window, turned = margin_window(sz.edge, side, row)
                for h, part in enumerate(halves(pool[piece, row].astype(F32))):
                    pad[q * sz.lanes + h, window, :] = flip_rows(part) if turned else part
            piece = corner_at[q * 4 + side]
            for row in range(REACH):
                for h, part in enumerate(halves(pool[piece, row].astype(F32))):
                    for column in range(REACH):
                        at = corner_cell(sz.edge, side, row, column)
                        pad[q * sz.lanes + h, pl.ds(at, 1), :] = part[column : column + 1]


def hold_taps(sz, kern, layer, taps):
    for a in range(TAPS):
        for b in range(TAPS):
            for h, part in enumerate(halves(kern[a, b, layer : layer + 1])):
                taps[h, pl.ds(a * 8 + b, 1), :] = part


def tap(taps, h, a, b):
    return jnp.broadcast_to(taps[h, pl.ds(a * 8 + b, 1), :], (8, LANES))


def convolve(sz, pad, taps, conv):
    @pl.loop(0, sz.slabs)
    def _(slab):
        h = lax.rem(slab, sz.lanes)
        for g in range(sz.edge // 8):
            acc = [None] * sz.edge
            for b in range(TAPS):
                weights = [tap(taps, h, a, b) for a in range(TAPS)]
                for r in range(sz.outer):
                    x = pad[slab, pl.ds(r * PITCH + b + 8 * g, 8), :]
                    for a in range(TAPS):
                        i = r - a
                        if 0 <= i < sz.edge:
                            term = x * weights[a]
                            acc[i] = term if acc[i] is None else acc[i] + term
            for i in range(sz.edge):
                conv[slab, pl.ds(i * sz.edge + 8 * g, 8), :] = acc[i]


def normalise(sz, conv, gain, layer, normal, inverse, normed):
    scale = 1.0 / sz.channels
    for q in range(sz.tiles):

        @pl.loop(0, sz.edge, unroll=4)
        def _(i):
            at = pl.ds(pl.multiple_of(i * sz.edge, sz.edge), sz.edge)
            parts = [conv[q * sz.lanes + h, at, :] for h in range(sz.lanes)]
            mean = jnp.sum(sum(parts[1:], parts[0]), axis=-1, keepdims=True) * scale
            parts = [part - mean for part in parts]
            squares = [part * part for part in parts]
            variance = jnp.sum(sum(squares[1:], squares[0]), axis=-1, keepdims=True) * scale
            root = lax.rsqrt(variance + epsilon)
            inverse[q, at, :] = jnp.broadcast_to(root, (sz.edge, LANES))
            flat_at = pl.ds(pl.multiple_of(q * sz.cells + i * sz.edge, sz.edge), sz.edge)
            for h, part in enumerate(parts):
                part = part * root
                normal[q * sz.lanes + h, at, :] = part
                gains = gain[layer : layer + 1, h * LANES : (h + 1) * LANES]
                normed[flat_at, h * LANES : (h + 1) * LANES] = (part * gains).astype(BF16)


def activate(sz, upward, active, slope):
    width = 512

    @pl.loop(0, sz.rows // 16, unroll=2)
    def _(t):
        at = pl.ds(pl.multiple_of(t * 16, 16), 16)
        for start in range(0, sz.hidden, width):
            u = upward[at, start : start + width]
            chance = 0.5 * (1.0 + lax.erf(u * inverse_root_two))
            active[at, start : start + width] = (u * chance).astype(BF16)
            slope[at, start : start + width] = (
                chance + u * jnp.exp(-0.5 * u * u) * inverse_root_tau
            ).astype(slope.dtype)


def multiply(a, b, ca=1, cb=0):
    return lax.dot_general(a, b, (((ca,), (cb,)), ((), ())), preferred_element_type=F32)


def finish_forward(sz, cur, branch, lscale, layer, out, flat):
    for q in range(sz.tiles):

        @pl.loop(0, sz.edge, unroll=4)
        def _(i):
            at = pl.ds(pl.multiple_of(q * sz.cells + i * sz.edge, sz.edge), sz.edge)
            value = cur[q, i].astype(F32) + branch[at, :] * lscale[layer : layer + 1, :]
            value = value.astype(BF16)
            out[q, i] = value
            if flat is not None:
                local = pl.ds(pl.multiple_of(i * sz.edge, sz.edge), sz.edge)
                for h, part in enumerate(halves(value.astype(F32))):
                    flat[q * sz.lanes + h, local, :] = part


def scale_rows(sz, grad_row, branch, lscale, layer, down_in, sums):
    sums[...] = jnp.zeros_like(sums)
    for q in range(sz.tiles):

        @pl.loop(0, sz.edge, unroll=4)
        def _(i):
            at = pl.ds(pl.multiple_of(q * sz.cells + i * sz.edge, sz.edge), sz.edge)
            g = grad_row(q, i)
            down_in[at, :] = (g * lscale[layer : layer + 1, :]).astype(BF16)
            sums[...] += g * branch[at, :]


def slope_rows(sz, grad_active, slope, up_in):
    @pl.loop(0, sz.rows // 16, unroll=2)
    def _(t):
        at = pl.ds(pl.multiple_of(t * 16, 16), 16)
        up_in[at, :] = (grad_active[at, :] * slope[at, :].astype(F32)).astype(BF16)


def weight_gradients(sz, core, active, down_in, normed, up_in, both, keep, send):
    both[0] = multiply(active[...], down_in[...], 0, 0).astype(BF16)
    for k in range(sz.hidden // sz.channels):
        part = multiply(normed[...], up_in[:, k * sz.channels : (k + 1) * sz.channels], 0, 0)
        both[1, k * sz.channels : (k + 1) * sz.channels, :] = part.astype(BF16)
    keep[...] = both[core]
    send[...] = both[1 - core]


def norm_gradients(sz, grad_normed, normal, inverse, gain, layer, grad_conv, sums):
    scale = 1.0 / sz.channels
    sums[...] = jnp.zeros_like(sums)
    blank = jnp.zeros((8, LANES), F32)
    for q in range(sz.tiles):

        @pl.loop(0, sz.edge, unroll=4)
        def _(i):
            at = pl.ds(pl.multiple_of(q * sz.cells + i * sz.edge, sz.edge), sz.edge)
            local = pl.ds(pl.multiple_of(i * sz.edge, sz.edge), sz.edge)
            g = halves(grad_normed[at, :])
            n = [normal[q * sz.lanes + h, local, :] for h in range(sz.lanes)]
            sums[...] += jnp.concatenate([a * b for a, b in zip(g, n)], axis=1)
            s = [
                part * gain[layer : layer + 1, h * LANES : (h + 1) * LANES]
                for h, part in enumerate(g)
            ]
            products = [a * b for a, b in zip(s, n)]
            mean = jnp.sum(sum(s[1:], s[0]), axis=-1, keepdims=True) * scale
            slant = jnp.sum(sum(products[1:], products[0]), axis=-1, keepdims=True) * scale
            root = inverse[q, local, :]
            for h in range(sz.lanes):
                slab = q * sz.lanes + h
                base = pl.multiple_of(i * GRAD_PITCH, GRAD_PITCH)
                grad_conv[slab, pl.ds(base, 8), :] = blank
                grad_conv[slab, pl.ds(base + 8, sz.edge), :] = root * (s[h] - mean - n[h] * slant)
                grad_conv[slab, pl.ds(base + 8 + sz.edge, 8), :] = blank


def tap_gradients(sz, pad, grad_conv, tap_sums, small):
    tap_sums[...] = jnp.zeros_like(tap_sums)

    @pl.loop(0, sz.slabs)
    def _(slab):
        h = lax.rem(slab, sz.lanes)
        for b in range(TAPS):
            acc = [None] * TAPS
            for g in range(sz.edge // 8):
                grads = [
                    grad_conv[slab, pl.ds(i * GRAD_PITCH + 8 + 8 * g, 8), :]
                    for i in range(sz.edge)
                ]
                for r in range(sz.outer):
                    x = pad[slab, pl.ds(r * PITCH + b + 8 * g, 8), :]
                    for a in range(TAPS):
                        i = r - a
                        if 0 <= i < sz.edge:
                            term = x * grads[i]
                            acc[a] = term if acc[a] is None else acc[a] + term
            for a in range(TAPS):
                tap_sums[h, a * TAPS + b] += acc[a]

    for h in range(sz.lanes):
        for k in range(TAPS * TAPS):
            row = k // TAPS * 8 + k % TAPS
            small[row : row + 1, h * LANES : (h + 1) * LANES] = jnp.sum(
                tap_sums[h, k], axis=0, keepdims=True
            )


def spread_gradients(sz, grad_conv, taps, grad_pad):
    @pl.loop(0, sz.slabs)
    def _(slab):
        h = lax.rem(slab, sz.lanes)
        for g in range(PITCH // 8):
            acc = [None] * sz.outer
            for b in range(TAPS):
                start = 8 * g - b + 8
                if start >= 8 + sz.edge:
                    continue
                weights = [tap(taps, h, a, b) for a in range(TAPS)]
                for i in range(sz.edge):
                    x = grad_conv[slab, pl.ds(i * GRAD_PITCH + start, 8), :]
                    for a in range(TAPS):
                        term = x * weights[a]
                        acc[i + a] = term if acc[i + a] is None else acc[i + a] + term
            for p in range(sz.outer):
                grad_pad[slab, pl.ds(p * PITCH + 8 * g, 8), :] = acc[p]


def return_margins(sz, strip_at, corner_at, grad_pad, pool):
    pool[...] = jnp.zeros_like(pool)
    for q in range(sz.tiles):
        for side in range(4):
            piece = strip_at[q * 4 + side]
            for row in range(REACH):
                window, turned = margin_window(sz.edge, side, row)
                for h in range(sz.lanes):
                    part = grad_pad[q * sz.lanes + h, window, :]
                    pool[piece, row, h] = flip_rows(part) if turned else part
    for q in range(sz.tiles):
        for side in range(4):
            piece = corner_at[q * 4 + side]
            for row in range(REACH):
                for column in range(REACH):
                    at = corner_cell(sz.edge, side, row, column)
                    for h in range(sz.lanes):
                        pool[piece, row, h, pl.ds(column, 1), :] += grad_pad[
                            q * sz.lanes + h, pl.ds(at, 1), :
                        ]


def send_margins(sz, pool, own, below, above):
    own[...] = pool[0 : sz.pieces]
    for piece in range(sz.pieces):
        for row in range(REACH):
            for offset, ref in ((1, below), (2, above)):
                parts = [pool[offset * sz.pieces + piece, row, h] for h in range(sz.lanes)]
                ref[piece, row] = jnp.concatenate(parts, axis=1).astype(BF16)


def gather_inner(sz, grad_row, grad_pad, base):
    for q in range(sz.tiles):
        for i in range(sz.edge):
            for h, part in enumerate(halves(grad_row(q, i))):
                slab = q * sz.lanes + h
                base[slab, pl.ds(i * sz.edge, sz.edge), :] = (
                    part + grad_pad[slab, pl.ds((i + REACH) * PITCH + REACH, sz.edge), :]
                )


def add_strips(sz, base, own, first, second, flat):
    flat[...] = base[...]
    for q in range(sz.tiles):
        for side in range(4):
            piece = q * 4 + side
            for row in range(REACH):
                window, turned = strip_window(sz.edge, side, row)
                came = first[piece, row].astype(F32) + second[piece, row].astype(F32)
                for h, part in enumerate(halves(came)):
                    part = part + own[piece, row, h]
                    flat[q * sz.lanes + h, window, :] += flip_rows(part) if turned else part


def fill_small(small, gain_sums, scale_sums):
    small[TAPS * 8 : TAPS * 8 + 1, :] = jnp.sum(gain_sums[...], axis=0, keepdims=True)
    small[TAPS * 8 + 1 : TAPS * 8 + 2, :] = jnp.sum(scale_sums[...], axis=0, keepdims=True)


def flat_grad_row(sz, flat):
    def row(q, i):
        at = pl.ds(i * sz.edge, sz.edge)
        parts = [flat[q * sz.lanes + h, at, :] for h in range(sz.lanes)]
        return jnp.concatenate(parts, axis=1)

    return row


def fetch_kernel(*refs):
    count = (len(refs) - 1) // 2
    copies = [
        pltpu.make_async_copy(refs[k], refs[count + k], refs[-1].at[k]) for k in range(count)
    ]
    for copy in copies:
        copy.start()
    for copy in copies:
        copy.wait()


def strips_kernel(sz, cur, strips, held, flat):
    held[...] = cur[...]
    for q in range(sz.tiles):
        for i in range(sz.edge):
            for h, part in enumerate(halves(cur[q, i].astype(F32))):
                flat[q * sz.lanes + h, pl.ds(i * sz.edge, sz.edge), :] = part
    write_strips(sz, flat, strips)


def forward_kernel(
    sz, layer, seams, corners, cur, own, below, above, kern, gain, lscale, up, down,
    out, strips, pad, normal, inverse, normed, slope, active, branch,
    pool, taps, conv, upward, flat,
):
    strip_at, corner_at = read_plan(sz, seams), read_plan(sz, corners)
    surround(sz, strip_at, corner_at, cur, own, below, above, pool, pad)
    hold_taps(sz, kern, layer, taps)
    convolve(sz, pad, taps, conv)
    normalise(sz, conv, gain, layer, normal, inverse, normed)
    upward[...] = multiply(normed[...], up[layer])
    activate(sz, upward, active, slope)
    branch[...] = multiply(active[...], down[layer])
    finish_forward(sz, cur, branch, lscale, layer, out, flat)
    write_strips(sz, flat, strips)


def turn_kernel(
    sz, layer, seams, corners, cur, own, below, above, kern, gain, lscale, up, down, out_grad,
    out_hbm, base, grad_own, grad_below, grad_above,
    pad, grad_conv, normed, active, down_in, up_in, gain_sums, scale_sums,
    pool, taps, conv, upward, out, normal, inverse, slope, branch, grad_pool, grad_pad, out_sem,
):
    strip_at, corner_at = read_plan(sz, seams), read_plan(sz, corners)
    surround(sz, strip_at, corner_at, cur, own, below, above, pool, pad)
    hold_taps(sz, kern, layer, taps)
    convolve(sz, pad, taps, conv)
    normalise(sz, conv, gain, layer, normal, inverse, normed)
    upward[...] = multiply(normed[...], up[layer])
    activate(sz, upward, active, slope)
    branch[...] = multiply(active[...], down[layer])
    finish_forward(sz, cur, branch, lscale, layer, out, None)
    store = pltpu.make_async_copy(out, out_hbm, out_sem.at[0])
    store.start()

    def grad_row(q, i):
        return out_grad[q, i].astype(F32)

    scale_rows(sz, grad_row, branch, lscale, layer, down_in, scale_sums)
    upward[...] = multiply(down_in[...], down[layer], 1, 1)
    slope_rows(sz, upward, slope, up_in)
    branch[...] = multiply(up_in[...], up[layer], 1, 1)
    norm_gradients(sz, branch, normal, inverse, gain, layer, grad_conv, gain_sums)
    spread_gradients(sz, grad_conv, taps, grad_pad)
    return_margins(sz, strip_at, corner_at, grad_pad, grad_pool)
    send_margins(sz, grad_pool, grad_own, grad_below, grad_above)
    gather_inner(sz, grad_row, grad_pad, base)
    store.wait()


def weights_kernel(
    sz, pad, grad_conv, normed, active, down_in, up_in, gain_sums, scale_sums,
    keep, send, small, tap_sums, both,
):
    small[...] = jnp.zeros_like(small)
    weight_gradients(sz, digit_of(0), active, down_in, normed, up_in, both, keep, send)
    tap_gradients(sz, pad, grad_conv, tap_sums, small)
    fill_small(small, gain_sums, scale_sums)


def backward_kernel(
    sz, layer, base, own, first, second, lscale, down, normed, slope, active, branch,
    keep, send, flat, up_in, scale_sums,
    hidden, down_in, both,
):
    add_strips(sz, base, own, first, second, flat)
    for slab in range(sz.slabs):
        flat[slab] = flat[slab].astype(BF16).astype(F32)
    scale_rows(sz, flat_grad_row(sz, flat), branch, lscale, layer, down_in, scale_sums)
    hidden[...] = multiply(down_in[...], down[layer], 1, 1)
    slope_rows(sz, hidden, slope, up_in)
    weight_gradients(sz, digit_of(0), active, down_in, normed, up_in, both, keep, send)


def spread_kernel(
    sz, layer, seams, corners, kern, gain, up, flat, up_in, normal, inverse,
    base, grad_own, grad_below, grad_above, grad_conv, gain_sums,
    taps, branch, grad_pool, grad_pad,
):
    strip_at, corner_at = read_plan(sz, seams), read_plan(sz, corners)
    branch[...] = multiply(up_in[...], up[layer], 1, 1)
    norm_gradients(sz, branch, normal, inverse, gain, layer, grad_conv, gain_sums)
    hold_taps(sz, kern, layer, taps)
    spread_gradients(sz, grad_conv, taps, grad_pad)
    return_margins(sz, strip_at, corner_at, grad_pad, grad_pool)
    send_margins(sz, grad_pool, grad_own, grad_below, grad_above)
    gather_inner(sz, flat_grad_row(sz, flat), grad_pad, base)


def taps_kernel(
    sz, pad, grad_conv, gain_sums, scale_sums, other, keep, send, tap_sums, small, both
):
    small[...] = jnp.zeros_like(small)
    tap_gradients(sz, pad, grad_conv, tap_sums, small)
    fill_small(small, gain_sums, scale_sums)
    both[0] = small[...]
    both[1] = other[...]
    keep[...] = both[digit_of(0)].astype(BF16)
    send[...] = both[1 - digit_of(0)].astype(BF16)


def last_kernel(sz, base, own, first, second, out_hbm, token, flat, out, sems):
    token[...] = jnp.zeros_like(token)
    add_strips(sz, base, own, first, second, flat)
    row = flat_grad_row(sz, flat)
    for q in range(sz.tiles):
        for i in range(sz.edge):
            out[q, i] = row(q, i).astype(BF16)
    store = pltpu.make_async_copy(out, out_hbm, sems.at[0])
    store.start()
    store.wait()


def add_rows(out, parts):
    for start in range(0, out.shape[0], 16):
        rows = slice(start, start + 16)
        values = [part(rows).astype(F32) for part in parts]
        out[rows] = sum(values[1:], values[0]).astype(BF16)


def share_near_kernel(keep, came, *outs):
    for k, out in enumerate(outs):
        piece = digit_of(1) ^ k
        add_rows(out, [lambda rows: keep[piece, rows], lambda rows: came[piece, rows]])


def quarter_kernel(*refs):
    add_rows(refs[4], [lambda rows, array=array: array[rows] for array in refs[:4]])


def far_kernel(*refs):
    pieces, out, held = refs[:-2], refs[-2], refs[-1]
    if len(pieces) == 2:
        add_rows(out, [lambda rows: pieces[0][rows], lambda rows: pieces[1][rows]])
        return
    for k, piece in enumerate(pieces):
        held[digit_of(2) ^ k] = piece[...]
    add_rows(out, [lambda rows, k=k: held[k, rows] for k in range(len(pieces))])


def middle_kernel(*refs):
    total, payload, held = refs[-3:]
    pieces, quarter, small = refs[:-6], refs[-6], refs[-5:-3]
    far_kernel(*pieces, total, held)
    rows = quarter.shape[0]
    payload[0:rows] = quarter[...]
    add_rows(payload.at[rows:], [lambda rows, array=array: array[rows] for array in small])


def order_kernel(quarter, *refs):
    pieces, out, held = refs[:4], refs[4], refs[5]
    for k, piece in enumerate(pieces):
        place = digit_of(1) ^ k
        out[pl.ds(pl.multiple_of(place * quarter, quarter), quarter), :] = piece[0:quarter]
        if quarter < piece.shape[0]:
            held[place] = piece[quarter:]
    if out.shape[0] > 4 * quarter:
        add_rows(out.at[4 * quarter :], [lambda rows, k=k: held[k, rows] for k in range(4)])


def unpack_half(sz, half, layer, source, staged, up_hbm, down_hbm, sems):
    copies = []
    for k in range(sz.hidden // sz.channels):
        rows = slice(k * sz.channels, (k + 1) * sz.channels)
        staged[rows, :] = source[rows, :].astype(F32)
        place = down_hbm.at[layer, rows] if half == 0 else up_hbm.at[layer, :, rows]
        copy = pltpu.make_async_copy(staged.at[rows], place, sems.at[half, k])
        copy.start()
        copies.append(copy)
    return copies


def unpack_layer_kernel(sz, layer, mine, theirs, up_hbm, down_hbm, token, first, second, sems):
    token[...] = jnp.zeros_like(token)
    for half in range(2):

        @pl.when(digit_of(0) == half)
        def _(half=half):
            copies = unpack_half(sz, half, layer, mine, first, up_hbm, down_hbm, sems)
            copies += unpack_half(sz, 1 - half, layer, theirs, second, up_hbm, down_hbm, sems)
            for copy in copies:
                copy.wait()


def unpack_mine_kernel(sz, layer, mine, _up, _down, up_hbm, down_hbm, staged, sems):
    for half in range(2):

        @pl.when(digit_of(0) == half)
        def _(half=half):
            for copy in unpack_half(sz, half, layer, mine, staged, up_hbm, down_hbm, sems):
                copy.wait()


def unpack_theirs_kernel(
    sz, layer, mine, theirs, _up, _down, up_hbm, down_hbm, kernel_out, gain_out, scale_out,
    staged, small, sems,
):
    for half in range(2):

        @pl.when(digit_of(0) == 1 - half)
        def _(half=half):
            for copy in unpack_half(sz, half, layer, theirs, staged, up_hbm, down_hbm, sems):
                copy.wait()

    small[digit_of(0)] = mine[sz.hidden :].astype(F32)
    small[1 - digit_of(0)] = theirs[sz.hidden :].astype(F32)
    for layer in range(2):
        for a in range(TAPS):
            for b in range(TAPS):
                kernel_out[a, b, layer : layer + 1] = small[layer, pl.ds(a * 8 + b, 1), :]
        gain_out[layer : layer + 1] = small[layer, pl.ds(TAPS * 8, 1), :]
        scale_out[layer : layer + 1] = small[layer, pl.ds(TAPS * 8 + 1, 1), :]


IN_VMEM = pl.BlockSpec(memory_space=pltpu.VMEM)
IN_SMEM = pl.BlockSpec(memory_space=pltpu.SMEM)
IN_HBM = pl.BlockSpec(memory_space=pltpu.HBM)


def call(body, name, micros, ins, outs, scratch, after=(), aliases={}):
    count = len(ins)

    def run(*refs):
        body(*refs[:count], *refs[count + len(after) :])

    return pl.pallas_call(
        run,
        in_specs=[spec for spec, _ in ins] + [pl.BlockSpec(memory_space=pl.ANY)] * len(after),
        out_specs=[spec for spec, _ in outs],
        out_shape=[out for _, out in outs],
        scratch_shapes=scratch,
        compiler_params=pltpu.CompilerParams(vmem_limit_bytes=24 * 1024 * 1024),
        cost_estimate=pl.CostEstimate(
            flops=0, bytes_accessed=int(micros * 3.5e6), transcendentals=0
        ),
        input_output_aliases=aliases,
        name=name,
    )(*[array for _, array in ins], *after)


def near(*arrays):
    return [(IN_VMEM, array) for array in arrays]


def far(*arrays):
    return [(IN_HBM, array) for array in arrays]


def pass_on(shard, by):
    length = lax.axis_size("tile")
    return lax.ppermute(shard, "tile", [(i, (i + by) % length) for i in range(length)])


def partners(array, masks):
    length = lax.axis_size("tile")
    return [
        lax.ppermute(array, "tile", [(i, i ^ mask) for i in range(length)]) for mask in masks
    ]


def swap(arrays, masks):
    length = lax.axis_size("tile")
    return [
        lax.ppermute(array, "tile", [(i, i ^ mask) for i in range(length)])
        for array, mask in zip(arrays, masks)
    ]


class Reduction:
    def __init__(self, devices):
        self.near_masks = [2 * k for k in range(1, 4)]
        self.far_masks = [8 * k for k in range(1, devices // 8)]

    def share(self, keep, send, after=()):
        rows, channels = keep.shape
        dims = (4, rows // 4, channels)
        shape = jax.ShapeDtypeStruct(dims[1:], BF16)
        pieces = call(
            share_near_kernel, "share_near", 0.3,
            near(keep.reshape(dims), swap([send], [1])[0].reshape(dims)),
            near(*[shape] * 4), [], after,
        )
        return [pieces[0]] + swap(pieces[1:], self.near_masks)

    def quarter(self, parts, after):
        shape = jax.ShapeDtypeStruct(parts[0].shape, BF16)
        (total,) = call(quarter_kernel, "quarter", 0.3, near(*parts), near(shape), [], after)
        return total

    def far(self, total):
        pieces = [total] + partners(total, self.far_masks)
        held = (len(pieces),) + total.shape if len(pieces) > 2 else (1, 16, LANES)
        return pieces, [pltpu.VMEM(held, BF16)]

    def middle(self, quarter, other, keep, send):
        pieces, scratch = self.far(quarter)
        rows, channels = quarter.shape
        shapes = [
            jax.ShapeDtypeStruct((rows + more, channels), BF16) for more in (0, keep.shape[0])
        ]
        return call(
            middle_kernel, "middle", 0.5,
            near(*pieces, other, keep, *swap([send], [1])), near(*shapes), scratch,
        )

    def exchange(self, total, after=()):
        pieces, scratch = self.far(total)
        shape = jax.ShapeDtypeStruct(total.shape, BF16)
        (total,) = call(far_kernel, "far", 0.3, near(*pieces), near(shape), scratch, after)
        return total

    def gather(self, total, quarter, after=()):
        rows, channels = total.shape
        shape = jax.ShapeDtypeStruct((3 * quarter + rows, channels), BF16)
        (whole,) = call(
            functools.partial(order_kernel, quarter), "order", 0.4,
            near(total, *partners(total, self.near_masks)), near(shape),
            [pltpu.VMEM((4, max(rows - quarter, 16), channels), BF16)], after,
        )
        return whole


def on_device(
    inputs,
    out_grad,
    kernel,
    norm_gain,
    up_weight,
    down_weight,
    layer_scale,
    seam_table,
    corner_table,
):
    tiles, edge, _, channels = inputs.shape
    layers, _, hidden = up_weight.shape
    sz = Sizes(tiles, edge, channels, hidden)
    columns = lax.axis_size("tile")
    plan = [(IN_SMEM, table.transpose((1, 2, 0))) for table in (seam_table, corner_table)]
    kern = kernel.transpose((1, 2, 0, 3))
    gain, lscale, up, down = norm_gain, layer_scale, up_weight, down_weight
    reduction = Reduction(columns)

    shape = jax.ShapeDtypeStruct
    image = shape(inputs.shape, BF16)
    strips_shape = shape((sz.pieces, REACH, edge, channels), BF16)
    slabs = shape((sz.slabs, sz.cells, LANES), F32)
    padded = shape((sz.slabs, sz.outer * PITCH, LANES), F32)
    inverses = shape((tiles, sz.cells, LANES), F32)
    narrow_short = shape((sz.rows, channels), BF16)
    wide_short = shape((sz.rows, hidden), BF16)
    narrow = shape((sz.rows, channels), F32)
    wide = shape((sz.rows, hidden), F32)
    sums = shape((edge, channels), F32)
    grad_slabs = shape((sz.slabs, edge * GRAD_PITCH, LANES), F32)
    own_shape = shape((sz.pieces, REACH, sz.lanes, edge, LANES), F32)
    pool = shape((3 * sz.pieces, REACH, edge, channels), BF16)
    grad_pool = shape((3 * sz.pieces, REACH, sz.lanes, edge, LANES), F32)
    taps = shape((sz.lanes, TAPS * 8, LANES), F32)
    tap_sums = shape((sz.lanes, TAPS * TAPS, 8, LANES), F32)
    small = shape((SMALL_ROWS, channels), F32)
    half = shape((hidden, channels), BF16)
    two_halves = shape((2, hidden, channels), BF16)

    def vmem(*shapes):
        return [pltpu.VMEM(one.shape, one.dtype) for one in shapes]

    def sems(count):
        return [pltpu.SemaphoreType.DMA((count,))]

    strips, inputs = call(
        functools.partial(strips_kernel, sz),
        "strips", 0.3,
        near(inputs),
        near(strips_shape, image),
        vmem(slabs),
    )
    below, above = pass_on(strips, 1), pass_on(strips, -1)
    fetched = (kern, gain, lscale, up, down)
    kern, gain, lscale, up, down = call(
        fetch_kernel,
        "fetch", 2.0,
        far(*fetched),
        near(*[shape(one.shape, one.dtype) for one in fetched]),
        sems(len(fetched)),
        (strips,),
    )
    middle, strips, pad_zero, normal, inverse, normed, slope, active, branch = call(
        functools.partial(forward_kernel, sz, 0),
        "forward", 8.7,
        plan + near(inputs, strips, below, above, kern, gain, lscale, up, down),
        near(
            image, strips_shape, padded, slabs, inverses,
            narrow_short, wide_short, wide_short, narrow,
        ),
        vmem(pool, taps, slabs, wide, slabs),
    )
    below, above = pass_on(strips, 1), pass_on(strips, -1)
    result, base, grad_own, grad_below, grad_above, *for_weights = call(
        functools.partial(turn_kernel, sz, 1),
        "turn", 15.4,
        plan + near(middle, strips, below, above, kern, gain, lscale, up, down, out_grad),
        far(image)
        + near(
            slabs, own_shape, strips_shape, strips_shape,
            padded, grad_slabs, narrow_short, wide_short, narrow_short, wide_short, sums, sums,
        ),
        vmem(
            pool, taps, slabs, wide, image, slabs, inverses, wide_short, narrow, grad_pool, padded
        )
        + sems(1),
    )
    from_below, from_above = pass_on(grad_above, 1), pass_on(grad_below, -1)
    keep_one, send_one, small_one = call(
        functools.partial(weights_kernel, sz),
        "weights", 2.8,
        near(*for_weights),
        near(half, half, small),
        vmem(tap_sums, two_halves),
    )
    keep_zero, send_zero, flat, up_in, scale_sums = call(
        functools.partial(backward_kernel, sz, 0),
        "backward", 2.9,
        near(
            base, grad_own, from_below, from_above, lscale, down, normed, slope, active, branch
        ),
        near(half, half, slabs, wide_short, sums),
        vmem(wide, narrow_short, two_halves),
    )
    parts_one = reduction.share(keep_one, send_one, (scale_sums,))
    parts_zero = reduction.share(keep_zero, send_zero)
    base, grad_own, grad_below, grad_above, grad_conv, gain_sums = call(
        functools.partial(spread_kernel, sz, 0),
        "spread", 6.0,
        plan + near(kern, gain, up, flat, up_in, normal, inverse),
        near(slabs, own_shape, strips_shape, strips_shape, grad_slabs, sums),
        vmem(taps, narrow, grad_pool, padded),
        (parts_zero[0], parts_one[0]),
    )
    quarter_one = reduction.quarter(parts_one, (gain_sums,))
    quarter_zero = reduction.quarter(parts_zero, (quarter_one,))
    from_below, from_above = pass_on(grad_above, 1), pass_on(grad_below, -1)
    small_keep, small_send = call(
        functools.partial(taps_kernel, sz),
        "taps", 2.1,
        near(pad_zero, grad_conv, gain_sums, scale_sums, small_one),
        near(*[shape(small.shape, BF16)] * 2),
        vmem(tap_sums, small, shape((2,) + small.shape, F32)),
        (quarter_zero,),
    )
    in_grad, token = call(
        functools.partial(last_kernel, sz),
        "last", 1.0,
        near(base, grad_own, from_below, from_above),
        far(image) + near(shape((8, LANES), F32)),
        vmem(slabs, image) + sems(1),
    )
    rows = hidden // 4
    total_one, total_zero = reduction.middle(quarter_one, quarter_zero, small_keep, small_send)
    total_zero = reduction.exchange(total_zero, (token,))
    mine_one = reduction.gather(total_one, rows, (total_zero,))
    theirs_one = partners(mine_one, [1])[0]
    weight_shapes = [shape(up_weight.shape, F32), shape(down_weight.shape, F32)]
    staged = shape((hidden, channels), F32)
    copies = [pltpu.SemaphoreType.DMA((2, hidden // channels))]
    grad_up, grad_down, token = call(
        functools.partial(unpack_layer_kernel, sz, 1),
        "unpack_one", 1.8,
        near(mine_one, theirs_one),
        far(*weight_shapes) + near(shape((8, LANES), F32)),
        vmem(staged, staged) + copies,
    )
    mine = reduction.gather(total_zero, rows, (token,))
    theirs = partners(mine, [1])[0]
    grad_up, grad_down = call(
        functools.partial(unpack_mine_kernel, sz, 0),
        "unpack_mine", 1.0,
        near(mine) + far(grad_up, grad_down),
        far(*weight_shapes),
        vmem(staged) + copies,
        aliases={1: 0, 2: 1},
    )
    grad_up, grad_down, grad_kernel, grad_gain, grad_scale = call(
        functools.partial(unpack_theirs_kernel, sz, 0),
        "unpack_theirs", 1.3,
        near(mine, theirs) + far(grad_up, grad_down),
        far(*weight_shapes)
        + near(
            shape(kern.shape, F32), shape(norm_gain.shape, F32), shape(norm_gain.shape, F32)
        ),
        vmem(staged, shape((2,) + small.shape, F32)) + copies,
        aliases={2: 0, 3: 1},
    )
    return (
        result, in_grad, grad_kernel.transpose((2, 0, 1, 3)),
        grad_gain, grad_up, grad_down, grad_scale,
    )


def solution(mesh):
    placed = (
        P(("groups", "tile"), None, None, None),
        P(("groups", "tile"), None, None, None),
        P(),
        P(),
        P(),
        P(),
        P(),
        P(),
        P(),
    )
    return jax.shard_map(
        on_device,
        mesh=mesh,
        in_specs=placed,
        out_specs=(
            P(("groups", "tile"), None, None, None),
            P(("groups", "tile"), None, None, None),
            P("groups", None, None, None),
            P("groups", None),
            P("groups", None, None),
            P("groups", None, None),
            P("groups", None),
        ),
        check_vma=False,
    )
```
